32 devices in a mesh: img: 8 (over z, x), rows: 4 (over y, core).
Axes of the slice: x: 2, y: 2, z: 4, core: 2. Of those that a mesh axis runs over, the one named last changes fastest.
Arguments:
- small_images: bfloat16 [32, 224, 768], P('img', 'rows'), may hold values from -6 to 6
- large_images: bfloat16 [64, 576, 768], P('img', 'rows'), may hold values from -6 to 6
- w_qkv: float32 [768, 2304], P(('img', 'rows')), may hold values from -0.21875 to 0.21875
- w_out: float32 [768, 768], P(('img', 'rows')), may hold values from -0.875 to 0.875
- w_up: float32 [768, 3072], P(('img', 'rows')), may hold values from -0.21875 to 0.21875
- w_down: float32 [3072, 768], P(('img', 'rows')), may hold values from -0.109375 to 0.109375
- gains: float32 [768, 4], P(('img', 'rows')), may hold values from 0.5 to 1.5
- biases: float32 [768, 6], P(('img', 'rows')), may hold values from -3 to 3
- up_bias: float32 [3072], P(('img', 'rows')), may hold values from -3 to 3
- small_table: float32 [12, 729], replicated, may hold values from -6 to 6
- large_table: float32 [12, 2209], replicated, may hold values from -6 to 6
- small_cotangent: bfloat16 [32, 224, 768], P('img', 'rows'), may hold values from -6 to 6
- large_cotangent: bfloat16 [64, 576, 768], P('img', 'rows'), may hold values from -6 to 6
Outputs:
- small_out: bfloat16 [32, 224, 768], P('img', 'rows')
- large_out: bfloat16 [64, 576, 768], P('img', 'rows')
- small_grad: bfloat16 [32, 224, 768], P('img', 'rows')
- large_grad: bfloat16 [64, 576, 768], P('img', 'rows')
- grad_w_qkv: float32 [768, 2304], P(('img', 'rows'))
- grad_w_out: float32 [768, 768], P(('img', 'rows'))
- grad_w_up: float32 [768, 3072], P(('img', 'rows'))
- grad_w_down: float32 [3072, 768], P(('img', 'rows'))
- grad_gains: float32 [768, 4], P(('img', 'rows'))
- grad_biases: float32 [768, 6], P(('img', 'rows'))
- grad_up_bias: float32 [3072], P(('img', 'rows'))
- grad_small_table: float32 [12, 729], replicated
- grad_large_table: float32 [12, 2209], replicated
The draws below stay inside these ranges and needn't reach their ends.
All inputs are finite; a program needn't handle non-finite values.
Results may differ from the reference program's by a relative error of at most 0.015.
The reference program's roundings to bfloat16 on the way count: a program that leaves them out, or rounds other values in their place, can miss the bound.
Values may be sent and summed in bfloat16 or wider, within the bound.
A program may use at most 256 MiB of HBM per device.

```python
import jax
import jax.numpy as jnp
from jax import lax

D = 768
H = 12
HEAD = 64
FF = 3072
SIDE_S = 14
SIDE_L = 24
NS = 32
NL = 64
LEN_S = 224
LEN_L = 576
TS = 729
TL = 2209


def shard_levels(own_key, shape, shards, smallest, top_value):
    level, own = 1.0, jax.random.fold_in(own_key, 6)
    for axis_at, blocks in shards:
        draws = jnp.exp(jax.random.uniform(jax.random.fold_in(own, axis_at), (blocks,), jnp.float32, smallest / len(shards), top_value / len(shards)))
        level = level * jnp.repeat(draws, shape[axis_at] // blocks).reshape([-1 if axis == axis_at else 1 for axis in range(len(shape))])
    return level


def scatter_about(stream_key, shape, scale, reach, shards=(), kind=jnp.bfloat16):
    level = shard_levels(stream_key, shape, shards, -0.22, 0.18) if shards else 1.0
    values = jax.random.normal(stream_key, shape, jnp.float32) * scale * level
    return jnp.minimum(jnp.maximum(values, -reach), reach).astype(kind)


def setup_inputs(seed: int = 0) -> dict:
    key_list = jax.random.split(jax.random.key(seed), 14)
    return {
        "small_images": scatter_about(key_list[0], (NS, LEN_S, D), 1.0, 6.0, ((0, 8), (1, 4))),
        "large_images": scatter_about(key_list[1], (NL, LEN_L, D), 1.0, 6.0, ((0, 8), (1, 4))),
        "w_qkv": scatter_about(key_list[2], (D, 3 * D), D ** -0.5, 0.21875, ((0, 32),), jnp.float32),
        "w_out": scatter_about(key_list[3], (D, D), (D // 16) ** -0.5, 0.875, ((0, 32),), jnp.float32),
        "w_up": scatter_about(key_list[4], (D, FF), D ** -0.5, 0.21875, ((0, 32),), jnp.float32),
        "w_down": scatter_about(key_list[5], (FF, D), FF ** -0.5, 0.109375, ((0, 32),), jnp.float32),
        "gains": jnp.clip(1.0 + 0.1 * jax.random.normal(key_list[6], (D, 4), jnp.float32), 0.5, 1.5),
        "biases": scatter_about(key_list[7], (D, 6), 0.5, 3.0, ((0, 32),), jnp.float32),
        "up_bias": scatter_about(key_list[8], (FF,), 0.5, 3.0, ((0, 32),), jnp.float32),
        "small_table": scatter_about(key_list[9], (H, TS), 1.0, 6.0, (), jnp.float32),
        "large_table": scatter_about(key_list[10], (H, TL), 1.0, 6.0, (), jnp.float32),
        "small_cotangent": scatter_about(key_list[11], (NS, LEN_S, D), 1.0, 6.0, ((0, 8), (1, 4))),
        "large_cotangent": scatter_about(key_list[12], (NL, LEN_L, D), 1.0, 6.0, ((0, 8), (1, 4))),
    }


HIGH = lax.Precision.HIGHEST

@jax.custom_vjp
def low(v):
    return lax.optimization_barrier(v.astype(jnp.bfloat16)).astype(jnp.float32)

@jax.custom_vjp
def low_back(v):
    return v

def low_keep(v):
    return (low(v), None)

def low_pass(kept, grad):
    return (grad,)

def back_keep(v):
    return (v, None)

def back_low(kept, grad):
    return (low(grad),)
low.defvjp(low_keep, low_pass)
low_back.defvjp(back_keep, back_low)

def layer_norm(values, gain, shift):
    average = lax.optimization_barrier(jnp.mean(values, -1, keepdims=True))
    centered = values - average
    variance = lax.optimization_barrier(jnp.mean(centered * centered, -1, keepdims=True))
    return centered * lax.rsqrt(variance + 1e-06) * gain + shift

def relative_index(query_pos, key_pos, side):
    row_gap = jnp.clip(query_pos[:, None] // side - key_pos[None, :] // side, 1 - side, side - 1)
    col_gap = query_pos[:, None] % side - key_pos[None, :] % side
    return ((row_gap + side - 1) * (2 * side - 1) + col_gap + side - 1).astype(jnp.int32)

def product(left, right):
    return jnp.dot(left, right, precision=HIGH, preferred_element_type=jnp.float32)

def group_attention(merged, count, length, table, side):
    width = H * HEAD
    queries = merged[:, :width].reshape(count, length, H, HEAD)
    keys = merged[:, width:2 * width].reshape(count, length, H, HEAD)
    values = merged[:, 2 * width:].reshape(count, length, H, HEAD)
    positions = jnp.arange(length, dtype=jnp.int32)
    bias = table[:, relative_index(positions, positions, side)]
    keep = positions // side < side

    def attend(inputs):
        query_one, key_one, value_one = inputs
        scores = jnp.einsum('qhd,khd->hqk', query_one, key_one, precision=HIGH) * 0.125 + bias
        scores = low_back(jnp.where(keep[None, None, :], scores, -1e+30))
        probs = low(low_back(jax.nn.softmax(scores, -1)))
        return jnp.einsum('hqk,khd->qhd', probs, value_one, precision=HIGH)
    attended = lax.map(jax.checkpoint(attend), (queries, keys, values))
    return attended.reshape(count * length, width)

def forward(params, tables, small_x, large_x):
    w_qkv, w_out, w_up, w_down, gains, biases, up_bias = [low(item) for item in params]
    width = H * HEAD
    small_count = small_x.shape[0]
    large_count = large_x.shape[0]
    tokens = jnp.concatenate([small_x.reshape(-1, width), large_x.reshape(-1, width)], 0)
    split_at = small_count * LEN_S
    normed = low(layer_norm(tokens, gains[:, 0], biases[:, 0]))
    merged_bias = jnp.concatenate([biases[:, 2], jnp.zeros((width,), jnp.float32), biases[:, 3]])
    merged = low(low_back(product(normed, w_qkv) + merged_bias))
    attended = jnp.concatenate([group_attention(merged[:split_at], small_count, LEN_S, tables[0], SIDE_S), group_attention(merged[split_at:], large_count, LEN_L, tables[1], SIDE_L)], 0)
    attended = low(low_back(attended))
    branch = low_back(product(attended, w_out) + biases[:, 4])
    middle = tokens + gains[:, 2] * branch
    normed_mid = low(layer_norm(middle, gains[:, 1], biases[:, 1]))
    hidden = low_back(product(normed_mid, w_up) + up_bias)
    active = low(jax.nn.gelu(hidden, approximate=False))
    mlp_out = low_back(product(active, w_down) + biases[:, 5])
    result = middle + gains[:, 3] * mlp_out
    return (result[:split_at].reshape(small_x.shape), result[split_at:].reshape(large_x.shape))

def reference(small_images, large_images, w_qkv, w_out, w_up, w_down, gains, biases, up_bias, small_table, large_table, small_cotangent, large_cotangent):
    params = (w_qkv.astype(jnp.float32), w_out.astype(jnp.float32), w_up.astype(jnp.float32), w_down.astype(jnp.float32), gains.astype(jnp.float32), biases.astype(jnp.float32), up_bias.astype(jnp.float32))
    tables = (small_table.astype(jnp.float32), large_table.astype(jnp.float32))
    small_x = small_images.astype(jnp.float32)
    large_x = large_images.astype(jnp.float32)
    outputs, pull = jax.vjp(forward, params, tables, small_x, large_x)
    positions = jnp.arange(LEN_S, dtype=jnp.int32)
    valid = (positions // SIDE_S < SIDE_S).astype(jnp.float32)
    small_dy = small_cotangent.astype(jnp.float32) * valid[None, :, None]
    param_grads, table_grads, small_grad, large_grad = pull((small_dy, large_cotangent.astype(jnp.float32)))
    return (outputs[0].astype(jnp.bfloat16), outputs[1].astype(jnp.bfloat16), small_grad.astype(jnp.bfloat16), large_grad.astype(jnp.bfloat16), param_grads[0], param_grads[1], param_grads[2], param_grads[3], param_grads[4], param_grads[5], param_grads[6], table_grads[0], table_grads[1])
```

```python
import functools

import jax
import jax.numpy as jnp
from jax import lax
from jax.experimental import pallas as pl
from jax.experimental.pallas import tpu as pltpu
from jax.sharding import PartitionSpec as P

H = 12
SIDE_S = 14
SIDE_L = 24
LEN_S = 224
LEN_L = 576
WIDE_L = 1152
WIDE_S = 512

F32 = jnp.float32
BF = jnp.bfloat16
NN = (((1,), (0,)), ((), ()))
NT = (((1,), (1,)), ((), ()))
TN = (((0,), (0,)), ((), ()))
MESH = pl.DeviceIdType.MESH
ANY = pl.BlockSpec(memory_space=pl.ANY)
MIB = 1 << 20


def dot(left, right, dims):
    return lax.dot_general(left, right, dims, preferred_element_type=F32)


class Place:
    def __init__(self, img_size):
        self.img = lax.axis_index("img")
        self.row = lax.axis_index("rows")
        self.zs = img_size // 2
        self.z, self.x = self.img // 2, self.img % 2
        self.y, self.c = self.row // 2, self.row % 2

    def at(self, z=None, x=None, y=None, c=None):
        z = self.z if z is None else z
        x = self.x if x is None else x
        y = self.y if y is None else y
        c = self.c if c is None else c
        return (z * 2 + x, y * 2 + c)

    def z_other(self, step):
        return lax.rem(self.z + step, self.zs)

    def row_other(self, step):
        return lax.rem(self.row + step, 4)

    def partners(self):
        along_z = [self.at(z=self.z_other(s)) for s in range(1, self.zs)]
        in_rows = [(self.img, self.row_other(s)) for s in range(1, 4)]
        return along_z + in_rows + [self.at(x=1 - self.x)]


def greet(partners):
    barrier = pltpu.get_barrier_semaphore()
    for p in partners:
        pl.semaphore_signal(barrier, inc=1, device_id=p, device_id_type=MESH)
    pl.semaphore_wait(barrier, len(partners))


class Copies:
    def __init__(self, send, recv, local):
        self.send, self.recv, self.local = send, recv, local
        self.remotes, self.locals = 0, 0

    def remote(self, src, dst, device):
        i = self.remotes
        self.remotes += 1
        copy = pltpu.make_async_remote_copy(
            src_ref=src, dst_ref=dst, send_sem=self.send.at[i], recv_sem=self.recv.at[i],
            device_id=device, device_id_type=MESH,
        )
        copy.start()
        return copy

    def here(self, src, dst):
        i = self.locals
        self.locals += 1
        copy = pltpu.make_async_copy(src, dst, self.local.at[i])
        copy.start()
        return copy


def pipelined(units):
    depth = max(len(u) for u in units)
    for t in range(len(units) + depth - 1):
        for f in reversed(range(depth)):
            u = t - f
            if 0 <= u < len(units) and f < len(units[u]):
                units[u][f]()


def columns(start, size):
    return pl.ds(pl.multiple_of(start, 128), size)


class Gather:
    def __init__(self, place, copies, shard, full, both, low, chunks):
        self.p, self.copies = place, copies
        self.shard, self.full, self.both, self.low = shard, full, both, low
        self.k, self.cols = shard.shape
        self.half = self.cols // 2
        self.wide = self.half // chunks
        self.chunks = chunks
        self.state = [None] * chunks

    def exchange(self):
        p = self.p
        mine = pl.ds(pl.multiple_of(p.c * self.k, 8), self.k)
        self.kept = self.copies.here(self.shard.at[:, columns(p.c * self.half, self.half)], self.both.at[mine])
        self.swapped = self.copies.remote(
            self.shard.at[:, columns((1 - p.c) * self.half, self.half)], self.both.at[mine], p.at(c=1 - p.c)
        )

    def convert(self):
        self.kept.wait()
        self.swapped.wait_recv()
        self.low[...] = self.both[...].astype(BF)

    def along_z(self, u):
        if u == 0:
            self.convert()
        p = self.p
        src = self.low.at[:, pl.ds(u * self.wide, self.wide)]
        dst = self.full.at[p.z, p.x, p.y, :, self.part(u)]
        own = self.copies.here(src, dst)
        sent = [self.copies.remote(src, dst, p.at(z=p.z_other(s))) for s in range(1, p.zs)]
        self.state[u] = (own, sent, [])

    def part(self, u):
        return columns(self.p.c * self.half + u * self.wide, self.wide)

    def send(self, u, part, device):
        self.state[u][2].append(self.copies.remote(part, part, device))

    def along_y(self, u):
        p = self.p
        own, sent, _ = self.state[u]
        own.wait()
        for copy in sent:
            copy.wait_recv()
        self.send(u, self.full.at[:, p.x, p.y, :, self.part(u)], p.at(y=1 - p.y))

    def along_x(self, u):
        p = self.p
        self.state[u][2][-1].wait_recv()
        self.send(u, self.full.at[:, p.x, :, :, self.part(u)], p.at(x=1 - p.x))

    def along_c(self, u):
        p = self.p
        self.state[u][2][-1].wait_recv()
        self.send(u, self.full.at[:, :, :, :, self.part(u)], p.at(c=1 - p.c))

    def finish(self, u):
        own, sent, later = self.state[u]
        later[-1].wait_recv()
        for copy in sent + later:
            copy.wait_send()
        if u == 0:
            self.swapped.wait_send()

    def units(self):
        steps = (self.along_z, self.along_y, self.along_x, self.along_c, self.finish)
        return [[functools.partial(step, u) for step in steps] for u in range(self.chunks)]

    @staticmethod
    def scratch(shape):
        k, cols = shape
        return [pltpu.VMEM((2 * k, cols // 2), F32), pltpu.VMEM((2 * k, cols // 2), BF)]


class Spread:
    def __init__(self, place, copies, block, full):
        self.p, self.copies, self.block, self.full = place, copies, block, full
        self.sent = []

    def along_z(self):
        p = self.p
        dst = self.full.at[p.z, p.x, p.y, p.c]
        self.own = self.copies.here(self.block, dst)
        self.sent += [self.copies.remote(self.block, dst, p.at(z=p.z_other(s))) for s in range(1, p.zs)]

    def along_y(self):
        self.own.wait()
        for copy in self.sent:
            copy.wait_recv()
        p = self.p
        part = self.full.at[:, p.x, p.y, p.c]
        self.sent.append(self.copies.remote(part, part, p.at(y=1 - p.y)))

    def along_x(self):
        self.sent[-1].wait_recv()
        p = self.p
        part = self.full.at[:, p.x, :, p.c]
        self.sent.append(self.copies.remote(part, part, p.at(x=1 - p.x)))

    def along_c(self):
        self.sent[-1].wait_recv()
        p = self.p
        part = self.full.at[:, :, :, p.c]
        self.sent.append(self.copies.remote(part, part, p.at(c=1 - p.c)))

    def finish(self):
        self.sent[-1].wait_recv()
        for copy in self.sent:
            copy.wait_send()

    def units(self):
        return [[self.along_z, self.along_y, self.along_x, self.along_c, self.finish]]


class ToImages:
    def __init__(self, place, copies, blocks, whole):
        self.p, self.copies, self.blocks, self.whole = place, copies, blocks, whole
        self.n = blocks.shape[0] // 4

    def start(self):
        p, n = self.p, self.n
        dst = self.whole.at[:, p.row]
        self.sent = [
            self.copies.remote(self.blocks.at[pl.ds(p.row_other(s) * n, n)], dst, (p.img, p.row_other(s)))
            for s in (2, 3, 1)
        ]
        self.own = self.copies.here(self.blocks.at[pl.ds(p.row * n, n)], dst)

    def finish(self):
        self.own.wait()
        for copy in self.sent:
            copy.wait()


class ToBlocks(ToImages):
    def __init__(self, place, copies, whole, blocks):
        super().__init__(place, copies, blocks, whole)

    def start(self):
        p, n = self.p, self.n
        dst = self.blocks.at[pl.ds(p.row * n, n)]
        self.sent = [
            self.copies.remote(self.whole.at[:, p.row_other(s)], dst, (p.img, p.row_other(s))) for s in (2, 3, 1)
        ]
        self.own = self.copies.here(self.whole.at[:, p.row], dst)


class Scatter:
    def __init__(self, place, copies, grad, shard, own, from_c, from_x, from_y, from_z, summed, chunks):
        self.p, self.copies, self.grad, self.shard = place, copies, grad, shard
        self.own, self.from_c, self.from_x, self.from_y, self.from_z = own, from_c, from_x, from_y, from_z
        self.summed = summed
        self.k, self.cols = shard.shape
        self.half = self.cols // 2
        self.wide = self.half // chunks
        self.chunks = chunks
        self.sent = [[] for _ in range(chunks)]
        self.kept = [None] * chunks

    def send(self, u, src, dst, device):
        self.sent[u].append(self.copies.remote(src, dst, device))

    def along_c(self, u):
        p = self.p
        self.send(u, self.grad.at[:, :, :, :, columns((1 - p.c) * self.half + u * self.wide, self.wide)],
                  self.from_c.at[u], p.at(c=1 - p.c))
        self.kept[u] = self.copies.here(
            self.grad.at[:, :, :, :, columns(p.c * self.half + u * self.wide, self.wide)], self.own.at[u])

    def add(self, into, other):
        into[...] = (into[...].astype(F32) + other[...].astype(F32)).astype(BF)

    def along_x(self, u):
        p = self.p
        self.kept[u].wait()
        self.sent[u][-1].wait_recv()
        own, got = self.own.at[u], self.from_c.at[u]
        for z in range(p.zs):
            self.add(own.at[z, 1 - p.x], got.at[z, 1 - p.x])
        self.send(u, own.at[:, 1 - p.x], self.from_x.at[u], p.at(x=1 - p.x))
        for z in range(p.zs):
            self.add(own.at[z, p.x], got.at[z, p.x])

    def along_y(self, u):
        p = self.p
        self.sent[u][-1].wait_recv()
        own, got = self.own.at[u], self.from_x.at[u]
        for z in range(p.zs):
            self.add(own.at[z, p.x, 1 - p.y], got.at[z, 1 - p.y])
        self.send(u, own.at[:, p.x, 1 - p.y], self.from_y.at[u], p.at(y=1 - p.y))
        for z in range(p.zs):
            self.add(own.at[z, p.x, p.y], got.at[z, p.y])

    def along_z(self, u):
        p = self.p
        self.sent[u][-1].wait_recv()
        own, got = self.own.at[u], self.from_y.at[u]
        for z in range(p.zs):
            self.add(own.at[z, p.x, p.y], got.at[z])
        for s in range(1, p.zs):
            self.send(u, own.at[p.z_other(s), p.x, p.y], self.from_z.at[u, s - 1], p.at(z=p.z_other(s)))

    def finish(self, u):
        p = self.p
        for copy in self.sent[u][-(p.zs - 1):]:
            copy.wait_recv()
        total = self.own[u, p.z, p.x, p.y].astype(F32)
        for s in range(p.zs - 1):
            total += self.from_z[u, s].astype(F32)
        self.summed[:, pl.ds(u * self.wide, self.wide)] = total
        for copy in self.sent[u]:
            copy.wait_send()
        if u == self.chunks - 1:
            cols = columns(p.c * self.half, self.half)
            mine = pl.ds(pl.multiple_of(p.c * self.k, 8), self.k)
            theirs = pl.ds(pl.multiple_of((1 - p.c) * self.k, 8), self.k)
            self.last = [
                self.copies.remote(self.summed.at[theirs], self.shard.at[:, cols], p.at(c=1 - p.c)),
                self.copies.here(self.summed.at[mine], self.shard.at[:, cols]),
            ]

    def end(self):
        for copy in self.last:
            copy.wait()

    def units(self):
        steps = (self.along_c, self.along_x, self.along_y, self.along_z, self.finish)
        return [[functools.partial(step, u) for step in steps] for u in range(self.chunks)]

    @staticmethod
    def scratch(zs, k, cols, n):
        w = cols // 2 // n
        return [
            pltpu.VMEM((n, zs, 2, 2, 2 * k, w), BF),
            pltpu.VMEM((n, zs, 2, 2, 2 * k, w), BF),
            pltpu.VMEM((n, zs, 2, 2 * k, w), BF),
            pltpu.VMEM((n, zs, 2 * k, w), BF),
            pltpu.VMEM((n, zs - 1, 2 * k, w), BF),
            pltpu.VMEM((2 * k, cols // 2), F32),
        ]


class SmallSum:
    def __init__(self, place, copies, grad, shard, own, from_c, from_x, from_y, from_z):
        self.p, self.copies, self.grad, self.shard = place, copies, grad, shard
        self.own, self.from_c, self.from_x, self.from_y, self.from_z = own, from_c, from_x, from_y, from_z
        self.sent = []

    def along_c(self):
        p = self.p
        self.kept = self.copies.here(self.grad.at[:, :, :, p.c], self.own)
        self.sent.append(self.copies.remote(self.grad.at[:, :, :, 1 - p.c], self.from_c, p.at(c=1 - p.c)))

    def along_x(self):
        p = self.p
        self.kept.wait()
        self.sent[-1].wait_recv()
        self.own[...] = self.own[...] + self.from_c[...]
        self.sent.append(self.copies.remote(self.own.at[:, 1 - p.x], self.from_x, p.at(x=1 - p.x)))

    def along_y(self):
        p = self.p
        self.sent[-1].wait_recv()
        self.own[:, p.x] = self.own[:, p.x] + self.from_x[...]
        self.sent.append(self.copies.remote(self.own.at[:, p.x, 1 - p.y], self.from_y, p.at(y=1 - p.y)))

    def along_z(self):
        p = self.p
        self.sent[-1].wait_recv()
        self.own[:, p.x, p.y] = self.own[:, p.x, p.y] + self.from_y[...]
        self.sent += [
            self.copies.remote(self.own.at[p.z_other(s), p.x, p.y], self.from_z.at[s - 1], p.at(z=p.z_other(s)))
            for s in range(1, p.zs)
        ]

    def finish(self):
        p = self.p
        for copy in self.sent[-(p.zs - 1):]:
            copy.wait_recv()
        for copy in self.sent:
            copy.wait_send()
        total = self.own[p.z, p.x, p.y]
        for s in range(p.zs - 1):
            total += self.from_z[s]
        self.shard[...] = total

    def units(self):
        return [[self.along_c, self.along_x, self.along_y, self.along_z, self.finish]]

    @staticmethod
    def scratch(zs):
        return [
            pltpu.VMEM((zs, 2, 2, 8, 128), F32),
            pltpu.VMEM((zs, 2, 2, 8, 128), F32),
            pltpu.VMEM((zs, 2, 8, 128), F32),
            pltpu.VMEM((zs, 8, 128), F32),
            pltpu.VMEM((zs - 1, 8, 128), F32),
        ]


class TableSum:
    def __init__(self, place, copies, grad, result, got, work, from_z):
        self.p, self.copies, self.grad, self.result = place, copies, grad, result
        self.got, self.work, self.from_z = got, work, from_z
        self.sent = []

    def along_c(self):
        p = self.p
        self.kept = self.copies.here(self.grad.at[p.c], self.work)
        self.sent.append(self.copies.remote(self.grad.at[1 - p.c], self.got.at[0], p.at(c=1 - p.c)))

    def along_x(self):
        p = self.p
        self.kept.wait()
        self.sent[-1].wait_recv()
        self.work[...] = self.work[...] + self.got[0]
        self.sent.append(self.copies.remote(self.work, self.got.at[1], p.at(x=1 - p.x)))

    def along_y(self):
        p = self.p
        self.sent[-1].wait()
        self.work[...] = self.work[...] + self.got[1]
        self.sent.append(self.copies.remote(self.work, self.got.at[2], p.at(y=1 - p.y)))

    def along_z(self):
        p = self.p
        self.sent[-1].wait()
        self.from_z[p.z] = self.work[...] + self.got[2]
        mine = self.from_z.at[p.z]
        self.over_z = [self.copies.remote(mine, mine, p.at(z=p.z_other(s))) for s in range(1, p.zs)]

    def finish(self):
        p = self.p
        self.sent[0].wait_send()
        for copy in self.over_z:
            copy.wait()
        total = self.from_z[0]
        for z in range(1, p.zs):
            total += self.from_z[z]
        self.work[...] = total
        self.last = [
            self.copies.remote(self.work, self.result.at[p.c], p.at(c=1 - p.c)),
            self.copies.here(self.work, self.result.at[p.c]),
        ]

    def end(self):
        for copy in self.last:
            copy.wait()

    def units(self):
        return [[self.along_c, self.along_x, self.along_y, self.along_z, self.finish]]

    @staticmethod
    def scratch(zs, rows):
        return [pltpu.VMEM((3, rows, 128), F32), pltpu.VMEM((rows, 128), F32), pltpu.VMEM((zs, rows, 128), F32)]


def semaphores(remotes, locals_):
    return [
        pltpu.SemaphoreType.DMA((remotes,)),
        pltpu.SemaphoreType.DMA((remotes,)),
        pltpu.SemaphoreType.DMA((locals_,)),
    ]


def split_refs(refs, *sizes):
    parts, at = [], 0
    for size in sizes:
        parts.append(refs[at:at + size])
        at += size
    return parts + [refs[at:]]


def full_shape(img_size, shard):
    k, cols = shard.shape
    return (img_size // 2, 2, 2, 2 * k, cols)


def front(img_size, arrays, block, shards, chunks):
    na, nw = len(arrays), len(shards)
    zs = img_size // 2
    outs = [jax.ShapeDtypeStruct((a.shape[0] // 4, 4) + a.shape[1:], a.dtype) for a in arrays]
    outs += [jax.ShapeDtypeStruct((zs, 2, 2, 2, 8, 128), F32)]
    outs += [jax.ShapeDtypeStruct(full_shape(img_size, s), BF) for s in shards]

    def kernel(*refs):
        ins, blk, sh, whole, small, full, scr = split_refs(refs, na, 1, nw, na, 1, nw)
        p = Place(img_size)
        greet(p.partners())
        copies = Copies(*scr[-3:])
        gathers = [Gather(p, copies, sh[i], full[i], scr[2 * i], scr[2 * i + 1], chunks[i]) for i in range(nw)]
        moves = [ToImages(p, copies, a, b) for a, b in zip(ins, whole)]
        for g in gathers:
            g.exchange()
        for m in moves[:2]:
            m.start()
        units = Spread(p, copies, blk[0], small[0]).units()
        for i, g in enumerate(gathers):
            units += g.units()
        for m in moves[2:]:
            m.start()
        pipelined(units)
        for m in moves:
            m.finish()

    remotes = 3 * na + (zs + 2) + sum(1 + n * (zs + 2) for n in chunks)
    locals_ = na + 1 + sum(1 + n for n in chunks)
    return pl.pallas_call(
        kernel,
        out_shape=outs,
        in_specs=[ANY] * (na + 1 + nw),
        out_specs=[ANY] * len(outs),
        scratch_shapes=[s for w in shards for s in Gather.scratch(w.shape)] + semaphores(remotes, locals_),
        compiler_params=pltpu.CompilerParams(collective_id=0, has_side_effects=True, vmem_limit_bytes=40 * MIB),
        name="front",
    )(*arrays, block, *shards)


def finish(img_size, wholes, small, tables, grads, chunks):
    na, nw = len(wholes), len(grads)
    zs = img_size // 2
    outs = [jax.ShapeDtypeStruct((a.shape[0] * 4,) + a.shape[2:], a.dtype) for a in wholes]
    outs += [jax.ShapeDtypeStruct((8, 128), F32), jax.ShapeDtypeStruct(tables.shape, F32)]
    outs += [jax.ShapeDtypeStruct((g.shape[3] // 2, g.shape[4]), F32) for g in grads]

    def kernel(*refs):
        ins, sm, tb, gr, blocks, small_out, table_out, shard, scr = split_refs(refs, na, 1, 1, nw, na, 1, 1, nw)
        p = Place(img_size)
        greet(p.partners())
        copies = Copies(*scr[-3:])
        moves = [ToBlocks(p, copies, a, b) for a, b in zip(ins, blocks)]
        scatters = [Scatter(p, copies, gr[i], shard[i], *scr[6 * i:6 * i + 6], chunks[i]) for i in range(nw)]
        at = 6 * nw
        table = TableSum(p, copies, tb[0], table_out[0], *scr[at:at + 3])
        own = SmallSum(p, copies, sm[0], small_out[0], *scr[at + 3:at + 8])
        for m in moves:
            m.start()
        units = table.units() + own.units()
        for s in scatters:
            units += s.units()
        pipelined(units)
        for s in scatters:
            s.end()
        table.end()
        for m in moves:
            m.finish()

    remotes = 3 * na + (zs + 2) + (zs + 3) + sum(1 + n * (zs + 2) for n in chunks)
    locals_ = na + 1 + 2 + sum(1 + n for n in chunks)
    scratch = []
    for g, n in zip(grads, chunks):
        scratch += Scatter.scratch(zs, g.shape[3] // 2, g.shape[4], n)
    scratch += TableSum.scratch(zs, tables.shape[1]) + SmallSum.scratch(zs)
    vmem = pl.BlockSpec(memory_space=pltpu.VMEM)
    return pl.pallas_call(
        kernel,
        out_shape=outs,
        in_specs=[ANY] * (na + 2 + nw),
        out_specs=[ANY] * na + [vmem] + [ANY] * (1 + nw),
        scratch_shapes=scratch + semaphores(remotes, locals_),
        compiler_params=pltpu.CompilerParams(collective_id=1, has_side_effects=True, vmem_limit_bytes=56 * MIB),
        name="finish",
    )(*wholes, small, tables, *grads)


def table_rows(table, side, blocks, wide):
    span = 2 * side - 1
    square = table.reshape(H, span, span)
    square = jnp.concatenate([square] + [square[:, -1:]] * (blocks - span), 1)
    rows = []
    for turned in (square, square[:, ::-1, ::-1]):
        for part, pads in ((turned[:, :, :side], (0, 1)), (turned[:, :, side:], (1, 0))):
            part = jnp.pad(part, ((0, 0), pads, (0, side - part.shape[2])))
            flat = part.reshape(H, 1, (blocks + 1) * side)
            rows.append(jnp.roll(jnp.pad(flat, ((0, 0), (0, 0), (0, wide - flat.shape[2]))), 1 - side, 2))
    return jnp.concatenate(rows + [jnp.zeros((H, 4, wide), F32)], 1)


def table_sums(rows, side, blocks):
    span = 2 * side - 1
    rows = jnp.roll(rows, side - -(-side // 8) * 8, 2)
    parts = rows[:, :, :(blocks + 1) * side].reshape(H, 2, blocks + 1, side)
    square = jnp.concatenate([parts[:, 0, :blocks], parts[:, 1, 1:, :side - 1]], 2)
    square = jnp.concatenate([square[:, :span - 1], jnp.sum(square[:, span - 1:], 1, keepdims=True)], 1)
    return square.reshape(H, span * span)


def lower_offsets(side, rows, wide):
    lane = lax.rem(lax.broadcasted_iota(jnp.int32, (rows, wide), 1), side)
    return lane <= lax.broadcasted_iota(jnp.int32, (rows, wide), 0)


def spread_rows(rows_ref, h, first, side, rows, wide, lower):
    low = jnp.broadcast_to(rows_ref[h, first:first + 1, :], (rows, wide))
    high = jnp.broadcast_to(rows_ref[h, first + 1:first + 2, :], (rows, wide))
    return jnp.where(
        lower, pltpu.roll(low, 0, 1, stride=1, stride_axis=0), pltpu.roll(high, 0, 1, stride=1, stride_axis=0)
    )


def fill_bias(bias, h, spread, side, rows, first_offset):
    size = bias.shape[2]
    wide = spread.shape[1]
    window = -(-size // 128) * 128 + 128
    for r in range(rows):
        offset = (first_offset - r) * side
        base, rest = offset // 128 * 128, offset % 128
        part = spread[:, base:min(base + window, wide)]
        if part.shape[1] < window:
            part = jnp.concatenate([part, jnp.zeros((spread.shape[0], window - part.shape[1]), F32)], 1)
        if rest:
            part = pltpu.roll(part, window - rest, 1)
        bias[h, r * side:(r + 1) * side, :] = part[:side, :size]


def fold_bias(total, h, acc, side, rows, first_offset, lower, out_ref):
    size = total.shape[2]
    window = -(-size // 128) * 128 + 128
    height, wide = lower.shape
    acc[...] = jnp.zeros_like(acc)
    for r in range(rows):
        offset = (first_offset - r) * side
        base, rest = offset // 128 * 128, offset % 128
        part = total[h, r * side:(r + 1) * side, :]
        part = jnp.concatenate([part, jnp.zeros((side, window - size), F32)], 1)
        if rest:
            part = pltpu.roll(part, rest, 1)
        acc[:side, base:base + window] += part
    whole = acc[:, :wide]
    zero = jnp.zeros_like(whole)
    for at, part in enumerate((jnp.where(lower, whole, zero), jnp.where(lower, zero, whole))):
        turned = jnp.concatenate([part[j:j + 1] for j in reversed(range(height))], 0)
        out_ref[h, at:at + 1, :] = jnp.sum(pltpu.roll(turned, 0, 1, stride=1, stride_axis=0), 0, keepdims=True)


def head_part(full, mask, h):
    keep = mask if h == 0 else jnp.logical_not(mask)
    return jnp.where(keep, full, jnp.zeros_like(full))


def attend_kernel(large, small, q_ref, k_ref, v_ref, rows_l, rows_s, o_ref, bias_l, bias_s):
    mask = lax.broadcasted_iota(jnp.int32, (1, 128), 1) < 64
    lower_l = lower_offsets(SIDE_L, SIDE_L, WIDE_L)
    lower_s = lower_offsets(SIDE_S, 16, WIDE_S)
    for h in range(2):
        fill_bias(bias_l, h, spread_rows(rows_l, h, 2, SIDE_L, SIDE_L, WIDE_L, lower_l), SIDE_L, 24, 23)
        fill_bias(bias_s, h, spread_rows(rows_s, h, 2, SIDE_S, 16, WIDE_S, lower_s), SIDE_S, 16, 15)
    keep = lax.broadcasted_iota(jnp.int32, (1, LEN_S), 1) < SIDE_S * SIDE_S
    images = [(n * LEN_L, LEN_L, bias_l) for n in range(large)]
    images += [(large * LEN_L + n * LEN_S, LEN_S, bias_s) for n in range(small)]
    for at, size, bias in images:
        q, k, v = (ref[at:at + size, :] for ref in (q_ref, k_ref, v_ref))
        outs = []
        for h in range(2):
            s = dot(head_part(q, mask, h) * BF(0.125), k, NT) + bias[h]
            if size == LEN_S:
                s = jnp.where(keep, s, -1e30)
            e = jnp.exp(s - jnp.max(s, 1, keepdims=True))
            p = (e * (1.0 / jnp.sum(e, 1, keepdims=True))).astype(BF)
            outs.append(dot(p, v, NN))
        o_ref[at:at + size, :] = jnp.where(mask, outs[0], outs[1]).astype(BF)


def attend_back_kernel(large, small, q_ref, k_ref, v_ref, do_ref, rows_l, rows_s,
                       dq_ref, dk_ref, dv_ref, grad_l, grad_s, bias_l, bias_s, total_l, total_s, acc_l, acc_s):
    mask = lax.broadcasted_iota(jnp.int32, (1, 128), 1) < 64
    lower_l = lower_offsets(SIDE_L, SIDE_L, WIDE_L)
    lower_s = lower_offsets(SIDE_S, 16, WIDE_S)
    for h in range(2):
        fill_bias(bias_l, h, spread_rows(rows_l, h, 0, SIDE_L, SIDE_L, WIDE_L, lower_l), SIDE_L, 24, 23)
        fill_bias(bias_s, h, spread_rows(rows_s, h, 0, SIDE_S, 16, WIDE_S, lower_s), SIDE_S, 14, 13)
    keep = lax.broadcasted_iota(jnp.int32, (LEN_S, 1), 0) < SIDE_S * SIDE_S
    images = [(n * LEN_L, LEN_L, bias_l, total_l, n == 0) for n in range(large)]
    images += [(large * LEN_L + n * LEN_S, LEN_S, bias_s, total_s, n == 0) for n in range(small)]
    for at, size, bias, total, first in images:
        q, k, v, do = (ref[at:at + size, :] for ref in (q_ref, k_ref, v_ref, do_ref))
        got = []
        for h in range(2):
            s = dot(head_part(k, mask, h) * BF(0.125), q, NT) + bias[h]
            if size == LEN_S:
                s = jnp.where(keep, s, -1e30)
            e = jnp.exp(s - jnp.max(s, 0, keepdims=True))
            p = e * (1.0 / jnp.sum(e, 0, keepdims=True))
            dp = dot(head_part(v, mask, h), do, NT).astype(BF).astype(F32)
            pd = p * dp
            low = (pd - p * jnp.sum(pd, 0, keepdims=True)).astype(BF)
            got.append((dot(low, k, TN), dot(low, q, NN), dot(p.astype(BF), do, NN)))
            total[h] = low.astype(F32) if first else total[h] + low.astype(F32)
        for ref, a, b, scale in zip((dq_ref, dk_ref, dv_ref), got[0], got[1], (0.125, 0.125, 1.0)):
            ref[at:at + size, :] = (jnp.where(mask, a, b) * scale).astype(BF)
    for h in range(2):
        fold_bias(total_l, h, acc_l, SIDE_L, 24, 23, lower_l, grad_l)
        fold_bias(total_s, h, acc_s, SIDE_S, 14, 13, lower_s, grad_s)


def head_columns(rows, at):
    return pl.BlockSpec((rows, 128), lambda g: (0, g + at))


ROWS_L = pl.BlockSpec((2, 8, WIDE_L), lambda g: (g, 0, 0))
ROWS_S = pl.BlockSpec((2, 8, WIDE_S), lambda g: (g, 0, 0))


def attend(qkv, rows_l, rows_s, large, small):
    rows = qkv.shape[0]
    return pl.pallas_call(
        functools.partial(attend_kernel, large, small),
        grid=(H // 2,),
        out_shape=jax.ShapeDtypeStruct((rows, 64 * H), BF),
        in_specs=[head_columns(rows, H // 2 * i) for i in range(3)] + [ROWS_L, ROWS_S],
        out_specs=head_columns(rows, 0),
        scratch_shapes=[pltpu.VMEM((2, LEN_L, LEN_L), F32), pltpu.VMEM((2, LEN_S, LEN_S), F32)],
        compiler_params=pltpu.CompilerParams(vmem_limit_bytes=56 * MIB),
        name="attend",
    )(qkv, qkv, qkv, rows_l, rows_s)


def attend_back(qkv, d_att, rows_l, rows_s, large, small):
    rows = qkv.shape[0]
    flat = jax.ShapeDtypeStruct((rows, 64 * H), BF)
    return pl.pallas_call(
        functools.partial(attend_back_kernel, large, small),
        grid=(H // 2,),
        out_shape=[flat] * 3 + [jax.ShapeDtypeStruct((H, 8, WIDE_L), F32), jax.ShapeDtypeStruct((H, 8, WIDE_S), F32)],
        in_specs=[head_columns(rows, H // 2 * i) for i in range(3)] + [head_columns(rows, 0), ROWS_L, ROWS_S],
        out_specs=[head_columns(rows, 0)] * 3 + [ROWS_L, ROWS_S],
        scratch_shapes=[pltpu.VMEM((2, LEN_L, LEN_L), F32), pltpu.VMEM((2, LEN_S, LEN_S), F32)] * 2
        + [pltpu.VMEM((SIDE_L, WIDE_L + 128), F32), pltpu.VMEM((16, WIDE_S + 128), F32)],
        compiler_params=pltpu.CompilerParams(vmem_limit_bytes=56 * MIB),
        name="attend_back",
    )(qkv, qkv, qkv, d_att, rows_l, rows_s)


def layer_norm(values, gain, shift):
    average = jnp.mean(values, -1, keepdims=True)
    centered = values - average
    variance = jnp.mean(centered * centered, -1, keepdims=True)
    return centered * lax.rsqrt(variance + 1e-06) * gain + shift


def to_images(blocks):
    n = blocks.shape[0] // 4
    got = lax.all_to_all(blocks.reshape((4, n) + blocks.shape[1:]), "rows", 0, 0)
    return jnp.swapaxes(got, 0, 1)


def to_blocks(whole):
    got = lax.all_to_all(jnp.swapaxes(whole, 0, 1), "rows", 0, 0)
    return got.reshape((-1,) + got.shape[2:])


def front_plain(arrays, block, shards):
    axes = ("img", "rows")
    wholes = [to_images(a) for a in arrays]
    small = lax.all_gather(block, axes, axis=0)
    return wholes + [small] + [lax.all_gather(s.astype(BF), axes, axis=0, tiled=True) for s in shards]


def finish_plain(wholes, small, tables, grads):
    axes = ("img", "rows")
    blocks = [to_blocks(a) for a in wholes]
    own = lax.psum_scatter(small, axes, scatter_dimension=0, tiled=False)
    shards = [lax.psum_scatter(g.astype(F32), axes, scatter_dimension=0, tiled=True) for g in grads]
    return blocks + [own, lax.psum(tables, axes)] + shards


def on_device(img_size, small_images, large_images, w_qkv, w_out, w_up, w_down, gains, biases, up_bias,
              small_table, large_table, small_cotangent, large_cotangent):
    width = small_images.shape[2]
    shards = [w_qkv, w_out, w_up, w_down]
    own = gains.shape[0]
    own_up = up_bias.shape[0]
    own_len = 10 * own + own_up
    block = jnp.concatenate([gains.T.reshape(-1), biases.T.reshape(-1), up_bias])
    block = jnp.pad(block, (0, 1024 - own_len)).reshape(8, 128)
    arrays = [large_images, small_images, large_cotangent, small_cotangent]
    direct = own % 8 == 0
    if direct:
        got = front(img_size, arrays, block, shards, [3, 1, 3, 3])
    else:
        got = front_plain(arrays, block, shards)
    large_x, small_x, large_ct, small_ct = got[:4]
    vectors = got[4].reshape(-1, 1024).astype(BF).astype(F32)
    columns_ = jnp.swapaxes(vectors[:, :10 * own].reshape(-1, 10, own), 0, 1).reshape(10, width)
    up_vec = vectors[:, 10 * own:own_len].reshape(-1)
    gain_one, gain_two, scale_one, scale_two = (columns_[i] for i in range(4))
    shift_one, shift_two, q_bias, v_bias, out_bias, down_bias = (columns_[4 + i] for i in range(6))
    qkv_low, out_low, up_low, down_low = (g.reshape(-1, g.shape[-1]) for g in got[5:])

    large, small = large_x.shape[0], small_x.shape[0]
    split_at = large * LEN_L
    rows_l = table_rows(large_table, SIDE_L, 47, WIDE_L)
    rows_s = table_rows(small_table, SIDE_S, 29, WIDE_S)

    tokens = jnp.concatenate([large_x.reshape(-1, width), small_x.reshape(-1, width)], 0).astype(F32)
    normed = layer_norm(tokens, gain_one, shift_one).astype(BF)
    merged_bias = jnp.concatenate([q_bias, jnp.zeros((width,), F32), v_bias])
    merged = (jnp.dot(normed, qkv_low, preferred_element_type=F32) + merged_bias).astype(BF)
    attended = attend(merged, rows_l, rows_s, large, small)

    branch = jnp.dot(attended, out_low, preferred_element_type=F32) + out_bias
    middle = tokens + scale_one * branch
    normed_mid = layer_norm(middle, gain_two, shift_two).astype(BF)
    hidden = jnp.dot(normed_mid, up_low, preferred_element_type=F32) + up_vec
    active = jax.nn.gelu(hidden, approximate=False).astype(BF)
    mlp_out = jnp.dot(active, down_low, preferred_element_type=F32) + down_bias
    result = (middle + scale_two * mlp_out).astype(BF)

    valid = (jnp.arange(LEN_S) < SIDE_S * SIDE_S).astype(F32)
    small_dy = small_ct.reshape(small, LEN_S, width).astype(F32) * valid[None, :, None]
    d_result = jnp.concatenate([large_ct.reshape(-1, width).astype(F32), small_dy.reshape(-1, width)], 0)
    d_mlp = (scale_two * d_result).astype(BF)
    grad_scale_two = jnp.sum(mlp_out * d_result, 0)
    grad_down_bias = jnp.sum(d_mlp.astype(F32), 0)
    grad_w_down = jnp.einsum("rf,rd->fd", active, d_mlp, preferred_element_type=F32).astype(BF)
    d_active = jnp.einsum("rd,fd->rf", d_mlp, down_low, preferred_element_type=F32)
    _, gelu_pull = jax.vjp(lambda inner: jax.nn.gelu(inner, approximate=False), hidden)
    d_hidden = gelu_pull(d_active)[0].astype(BF)
    grad_up_bias = jnp.sum(d_hidden.astype(F32), 0)
    grad_w_up = jnp.einsum("rd,rf->df", normed_mid, d_hidden, preferred_element_type=F32).astype(BF)
    d_normed_mid = jnp.einsum("rf,df->rd", d_hidden, up_low, preferred_element_type=F32)
    _, norm_pull = jax.vjp(layer_norm, middle, gain_two, shift_two)
    d_middle_part, grad_gain_two, grad_shift_two = norm_pull(d_normed_mid)
    d_middle = d_result + d_middle_part
    d_branch = (scale_one * d_middle).astype(BF)
    grad_scale_one = jnp.sum(branch * d_middle, 0)
    grad_out_bias = jnp.sum(d_branch.astype(F32), 0)
    grad_w_out = jnp.einsum("re,rd->ed", attended, d_branch, preferred_element_type=F32).astype(BF)
    d_attended = jnp.einsum("rd,ed->re", d_branch, out_low, preferred_element_type=F32).astype(BF)

    dq, dk, dv, large_sums, small_sums = attend_back(merged, d_attended, rows_l, rows_s, large, small)
    d_merged = jnp.concatenate([dq, dk, dv], 1)
    grad_q_bias = jnp.sum(dq.astype(F32), 0)
    grad_v_bias = jnp.sum(dv.astype(F32), 0)
    grad_w_qkv = jnp.einsum("rd,re->de", normed, d_merged, preferred_element_type=F32).astype(BF)
    d_normed = jnp.einsum("re,de->rd", d_merged, qkv_low, preferred_element_type=F32)
    _, first_pull = jax.vjp(layer_norm, tokens, gain_one, shift_one)
    d_tokens_part, grad_gain_one, grad_shift_one = first_pull(d_normed)
    d_tokens = (d_middle + d_tokens_part).astype(BF)

    def whole(flat):
        return [flat[:split_at].reshape(large_x.shape), flat[split_at:].reshape(small_x.shape)]

    grad_columns = jnp.stack([
        grad_gain_one, grad_gain_two, grad_scale_one, grad_scale_two,
        grad_shift_one, grad_shift_two, grad_q_bias, grad_v_bias, grad_out_bias, grad_down_bias,
    ])
    devices = width // own
    packed = jnp.concatenate([
        jnp.swapaxes(grad_columns.reshape(10, devices, own), 0, 1).reshape(devices, 10 * own),
        grad_up_bias.reshape(devices, own_up),
        jnp.zeros((devices, 1024 - own_len), F32),
    ], 1)
    tables = jnp.concatenate([large_sums[:, :2].reshape(-1, 128), small_sums[:, :2].reshape(-1, 128)], 0)
    tables = jnp.pad(tables, ((0, 320 - tables.shape[0]), (0, 0))).reshape(2, 160, 128)
    wholes = whole(result) + whole(d_tokens)
    grads = [grad_w_qkv, grad_w_out, grad_w_up, grad_w_down]
    if direct:
        grads = [g.reshape(img_size // 2, 2, 2, 2 * s.shape[0], s.shape[1]) for g, s in zip(grads, shards)]
        done = finish(img_size, wholes, packed.reshape(img_size // 2, 2, 2, 2, 8, 128), tables, grads, [3, 1, 3, 3])
    else:
        done = finish_plain(wholes, packed, tables, grads)
    large_out, small_out, large_grad, small_grad, own_sums, table_total = done[:6]
    own_sums = own_sums.reshape(-1)
    own_columns = own_sums[:10 * own].reshape(10, own).T
    table_total = table_total.reshape(320, 128)
    count_l = H * 2 * WIDE_L // 128
    count_s = H * 2 * WIDE_S // 128
    grad_large_table = table_sums(table_total[:count_l].reshape(H, 2, WIDE_L), SIDE_L, 47)
    grad_small_table = table_sums(table_total[count_l:count_l + count_s].reshape(H, 2, WIDE_S), SIDE_S, 29)
    return (
        small_out, large_out, small_grad, large_grad, *done[6:],
        own_columns[:, :4], own_columns[:, 4:], own_sums[10 * own:own_len],
        grad_small_table, grad_large_table,
    )


def solution(mesh):
    images = P("img", "rows", None)
    matrix = P(("img", "rows"), None)
    vector = P(("img", "rows"))
    in_specs = (images, images) + (matrix,) * 6 + (vector, P(), P(), images, images)
    out_specs = (images,) * 4 + (matrix,) * 6 + (vector, P(), P())
    return jax.shard_map(
        functools.partial(on_device, mesh.shape["img"]),
        mesh=mesh, in_specs=in_specs, out_specs=out_specs, check_vma=False,
    )
```

```python
import functools

import jax
import jax.numpy as jnp
from jax import lax
from jax.experimental import pallas as pl
from jax.experimental.pallas import tpu as pltpu
from jax.sharding import PartitionSpec as P

H = 12
SIDE_S = 14
SIDE_L = 24
LEN_S = 224
LEN_L = 576
WIDE_L = 1152
WIDE_S = 512

F32 = jnp.float32
BF = jnp.bfloat16
NN = (((1,), (0,)), ((), ()))
NT = (((1,), (1,)), ((), ()))
TN = (((0,), (0,)), ((), ()))
MESH = pl.DeviceIdType.MESH
ANY = pl.BlockSpec(memory_space=pl.ANY)
MIB = 1 << 20


def dot(left, right, dims):
    return lax.dot_general(left, right, dims, preferred_element_type=F32)


class Place:
    def __init__(self, img_size):
        self.img = lax.axis_index("img")
        self.row = lax.axis_index("rows")
        self.zs = img_size // 2
        self.z, self.x = self.img // 2, self.img % 2
        self.y, self.c = self.row // 2, self.row % 2

    def at(self, z=None, x=None, y=None, c=None):
        z = self.z if z is None else z
        x = self.x if x is None else x
        y = self.y if y is None else y
        c = self.c if c is None else c
        return (z * 2 + x, y * 2 + c)

    def z_other(self, step):
        return lax.rem(self.z + step, self.zs)

    def row_other(self, step):
        return lax.rem(self.row + step, 4)

    def partners(self):
        along_z = [self.at(z=self.z_other(s)) for s in range(1, self.zs)]
        in_rows = [(self.img, self.row_other(s)) for s in range(1, 4)]
        return along_z + in_rows + [self.at(x=1 - self.x)]


def greet(partners):
    barrier = pltpu.get_barrier_semaphore()
    for p in partners:
        pl.semaphore_signal(barrier, inc=1, device_id=p, device_id_type=MESH)
    pl.semaphore_wait(barrier, len(partners))


class Remote:
    def __init__(self, copies, build):
        self.copies, self.build, self.at = copies, build, copies.remotes
        copies.remotes += 1

    def made(self):
        src, dst, device = self.build()
        return pltpu.make_async_remote_copy(
            src_ref=src, dst_ref=dst, send_sem=self.copies.send.at[self.at], recv_sem=self.copies.recv.at[self.at],
            device_id=device, device_id_type=MESH,
        )

    def start(self):
        self.made().start()
        return self

    def wait_send(self):
        self.made().wait_send()

    def wait_recv(self):
        self.made().wait_recv()


class Local:
    def __init__(self, copies, build):
        self.copies, self.build, self.at = copies, build, copies.locals
        copies.locals += 1

    def made(self):
        return pltpu.make_async_copy(*self.build(), self.copies.local.at[self.at])

    def start(self):
        self.made().start()
        return self

    def wait(self):
        self.made().wait()


class Copies:
    def __init__(self, send, recv, local):
        self.send, self.recv, self.local = send, recv, local
        self.remotes, self.locals = 0, 0

    def remote(self, build):
        return Remote(self, build)

    def here(self, build):
        return Local(self, build)


def pipelined(units):
    depth = max(len(u) for u in units)

    def step(t):
        for f in range(depth):
            u = t - f
            if 0 <= u < len(units) and f < len(units[u]):
                units[u][f]()

    return [functools.partial(step, t) for t in range(len(units) + depth - 1)]


def columns(start, size):
    return pl.ds(pl.multiple_of(start, 128), size)


class Gather:
    def __init__(self, place, copies, shard, full, both, low, pieces):
        self.p, self.copies = place, copies
        self.full, self.both, self.low = full, both, low
        self.k, self.cols = shard.shape
        self.half = self.cols // 2
        self.panels, self.wide = full.shape[0], full.shape[-1]
        self.tall = 2 * self.k // pieces
        self.pieces = pieces
        p = place

        def mine():
            return both.at[pl.ds(pl.multiple_of(p.c * self.k, 8), self.k)]

        self.kept = copies.here(lambda: (shard.at[:, columns(p.c * self.half, self.half)], mine()))
        self.swapped = copies.remote(
            lambda: (shard.at[:, columns((1 - p.c) * self.half, self.half)], mine(), p.at(c=1 - p.c)))

    def exchange(self):
        self.kept.start()
        self.swapped.start()

    def convert(self):
        self.kept.wait()
        self.swapped.wait_recv()
        self.low[...] = self.both[...].astype(BF)

    def unit(self, u, r):
        p, full = self.p, self.full
        rows = pl.ds(r * self.tall, self.tall)
        src = self.low.at[rows, pl.ds(u * self.wide, self.wide)]

        def dst():
            return full.at[u, p.c, p.z, p.x, p.y, rows]

        def twice(part, device):
            return self.copies.remote(lambda: (part(), part(), device()))

        own = self.copies.here(lambda: (src, dst()))
        over_z = [
            self.copies.remote(lambda s=s: (src, dst(), p.at(z=p.z_other(s)))) for s in range(1, p.zs)
        ]
        over_y = twice(lambda: full.at[u, p.c, :, p.x, p.y, rows], lambda: p.at(y=1 - p.y))
        over_x = twice(lambda: full.at[u, p.c, :, p.x, :, rows], lambda: p.at(x=1 - p.x))
        over_c = twice(lambda: full.at[u, p.c, :, :, :, rows], lambda: p.at(c=1 - p.c))

        def along_z():
            if u == 0 and r == 0:
                self.convert()
            for copy in [own] + over_z:
                copy.start()

        def along_y():
            own.wait()
            for copy in over_z:
                copy.wait_recv()
            over_y.start()

        def along_x():
            over_y.wait_recv()
            over_x.start()

        def along_c():
            over_x.wait_recv()
            over_c.start()

        def finish():
            over_c.wait_recv()
            for copy in over_z + [over_y, over_x, over_c]:
                copy.wait_send()
            if u == 0 and r == 0:
                self.swapped.wait_send()

        return [along_z, along_y, along_x, along_c, finish]

    def units(self):
        return [self.unit(u, r) for u in range(self.panels) for r in range(self.pieces)]

    @staticmethod
    def scratch(shape):
        k, cols = shape
        return [pltpu.VMEM((2 * k, cols // 2), F32), pltpu.VMEM((2 * k, cols // 2), BF)]


class Spread:
    def __init__(self, place, copies, block, full):
        p = place

        def dst():
            return full.at[p.z, p.x, p.y, p.c]

        def twice(part, device):
            return copies.remote(lambda: (part(), part(), device()))

        self.own = copies.here(lambda: (block, dst()))
        self.over_z = [copies.remote(lambda s=s: (block, dst(), p.at(z=p.z_other(s)))) for s in range(1, p.zs)]
        self.over_y = twice(lambda: full.at[:, p.x, p.y, p.c], lambda: p.at(y=1 - p.y))
        self.over_x = twice(lambda: full.at[:, p.x, :, p.c], lambda: p.at(x=1 - p.x))
        self.over_c = twice(lambda: full.at[:, :, :, p.c], lambda: p.at(c=1 - p.c))

    def along_z(self):
        for copy in [self.own] + self.over_z:
            copy.start()

    def along_y(self):
        self.own.wait()
        for copy in self.over_z:
            copy.wait_recv()
        self.over_y.start()

    def along_x(self):
        self.over_y.wait_recv()
        self.over_x.start()

    def along_c(self):
        self.over_x.wait_recv()
        self.over_c.start()

    def finish(self):
        self.over_c.wait_recv()
        for copy in self.over_z + [self.over_y, self.over_x, self.over_c]:
            copy.wait_send()

    def units(self):
        return [[self.along_z, self.along_y, self.along_x, self.along_c, self.finish]]


class Move:
    def __init__(self, place, copies, src, dst, to_images):
        p = place
        n = (src if to_images else dst).shape[0] // 4

        def part(row):
            if to_images:
                return src.at[pl.ds(row * n, n)], dst.at[:, p.row]
            return src.at[:, row], dst.at[pl.ds(p.row * n, n)]

        self.own = copies.here(lambda: part(p.row))
        self.sent = [
            copies.remote(lambda s=s: part(p.row_other(s)) + ((p.img, p.row_other(s)),)) for s in (2, 3, 1)
        ]

    def start(self):
        for copy in self.sent + [self.own]:
            copy.start()

    def finish(self):
        self.own.wait()
        for copy in self.sent:
            copy.wait_recv()
        for copy in self.sent:
            copy.wait_send()


class Scatter:
    def __init__(self, place, copies, grad, shard, scratch, pieces):
        self.p, self.copies, self.grad, self.shard = place, copies, grad, shard
        self.own, self.from_c, self.from_x, self.from_y, self.from_z, self.summed = scratch[:6]
        self.stage = scratch[6] if grad is None else None
        self.k, self.cols = shard.shape
        self.half = self.cols // 2
        self.pieces = pieces
        self.panels = self.own.shape[0] // pieces
        self.wide, self.tall = self.own.shape[-1], self.own.shape[-2]
        p = place

        def cols():
            return columns(p.c * self.half, self.half)

        def rows(c):
            return pl.ds(pl.multiple_of(c * self.k, 8), self.k)

        self.last = copies.remote(
            lambda: (self.summed.at[rows(1 - p.c)], shard.at[:, cols()], p.at(c=1 - p.c)))
        self.kept = copies.here(lambda: (self.summed.at[rows(p.c)], shard.at[:, cols()]))

    def unit(self, u, r):
        p, copies, grad = self.p, self.copies, self.grad
        at = u * self.pieces + r
        own, from_c, from_x = self.own.at[at], self.from_c.at[at], self.from_x.at[at]
        from_y, from_z = self.from_y.at[at], self.from_z.at[at]
        rows = pl.ds(r * self.tall, self.tall)
        if grad is None:
            over_c = copies.remote(lambda: (self.stage.at[at], from_c, p.at(c=1 - p.c)))
            loaded = None
        else:
            over_c = copies.remote(lambda: (grad.at[u, 1 - p.c, :, :, :, rows], from_c, p.at(c=1 - p.c)))
            loaded = copies.here(lambda: (grad.at[u, p.c, :, :, :, rows], own))
        over_x = copies.remote(lambda: (own.at[:, 1 - p.x], from_x, p.at(x=1 - p.x)))
        over_y = copies.remote(lambda: (own.at[:, p.x, 1 - p.y], from_y, p.at(y=1 - p.y)))
        over_z = [
            copies.remote(lambda s=s: (own.at[p.z_other(s), p.x, p.y], from_z.at[s - 1], p.at(z=p.z_other(s))))
            for s in range(1, p.zs)
        ]

        def add(into, other):
            into[...] = (into[...].astype(F32) + other[...].astype(F32)).astype(BF)

        def along_c():
            over_c.start()
            if loaded is not None:
                loaded.start()

        def along_x():
            if loaded is not None:
                loaded.wait()
            over_c.wait_recv()
            for z in range(p.zs):
                add(own.at[z, 1 - p.x], from_c.at[z, 1 - p.x])
            over_x.start()
            for z in range(p.zs):
                add(own.at[z, p.x], from_c.at[z, p.x])

        def along_y():
            over_x.wait_recv()
            for z in range(p.zs):
                add(own.at[z, p.x, 1 - p.y], from_x.at[z, 1 - p.y])
            over_y.start()
            for z in range(p.zs):
                add(own.at[z, p.x, p.y], from_x.at[z, p.y])

        def along_z():
            over_y.wait_recv()
            for z in range(p.zs):
                add(own.at[z, p.x, p.y], from_y.at[z])
            for copy in over_z:
                copy.start()

        def finish():
            for copy in over_z:
                copy.wait_recv()
            total = own[p.z, p.x, p.y].astype(F32)
            for s in range(p.zs - 1):
                total += from_z[s].astype(F32)
            self.summed[rows, pl.ds(u * self.wide, self.wide)] = total
            for copy in [over_c, over_x, over_y] + over_z:
                copy.wait_send()
            if at == self.panels * self.pieces - 1:
                self.last.start()
                self.kept.start()

        return [along_c, along_x, along_y, along_z, finish]

    def end(self):
        self.kept.wait()
        self.last.wait_recv()
        self.last.wait_send()

    def units(self):
        return [self.unit(u, r) for u in range(self.panels) for r in range(self.pieces)]

    @staticmethod
    def scratch(zs, k, cols, panels, pieces, staged=False):
        n, tall, w = panels * pieces, 2 * k // pieces, cols // 2 // panels
        shapes = [(n, zs, 2, 2, tall, w), (n, zs, 2, 2, tall, w), (n, zs, 2, tall, w), (n, zs, tall, w),
                  (n, zs - 1, tall, w)]
        return [pltpu.VMEM(s, BF) for s in shapes] + [pltpu.VMEM((2 * k, cols // 2), F32)] + (
            [pltpu.VMEM(shapes[0], BF)] if staged else [])

    @staticmethod
    def remotes(zs, panels, pieces):
        return 1 + panels * pieces * (zs + 2)


class Total:
    def __init__(self, place, copies, grad, result, got, work, from_z):
        self.p, self.grad, self.got, self.work, self.from_z = place, grad, got, work, from_z
        p = place
        self.kept = copies.here(lambda: (grad.at[p.c], work))
        self.over_c = copies.remote(lambda: (grad.at[1 - p.c], got.at[0], p.at(c=1 - p.c)))
        self.over_x = copies.remote(lambda: (work, got.at[1], p.at(x=1 - p.x)))
        self.over_y = copies.remote(lambda: (work, got.at[2], p.at(y=1 - p.y)))
        self.over_z = [
            copies.remote(lambda s=s: (from_z.at[p.z], from_z.at[p.z], p.at(z=p.z_other(s)))) for s in range(1, p.zs)
        ]
        self.last = [
            copies.remote(lambda: (work, result.at[p.c], p.at(c=1 - p.c))),
            copies.here(lambda: (work, result.at[p.c])),
        ]

    def along_c(self):
        self.kept.start()
        self.over_c.start()

    def along_x(self):
        self.kept.wait()
        self.over_c.wait_recv()
        self.work[...] = self.work[...] + self.got[0]
        self.over_x.start()

    def along_y(self):
        self.over_x.wait_recv()
        self.over_x.wait_send()
        self.work[...] = self.work[...] + self.got[1]
        self.over_y.start()

    def along_z(self):
        self.over_y.wait_recv()
        self.over_y.wait_send()
        self.from_z[self.p.z] = self.work[...] + self.got[2]
        for copy in self.over_z:
            copy.start()

    def finish(self):
        for copy in self.over_z:
            copy.wait_recv()
        for copy in [self.over_c] + self.over_z:
            copy.wait_send()
        total = self.from_z[0]
        for z in range(1, self.p.zs):
            total += self.from_z[z]
        self.work[...] = total
        for copy in self.last:
            copy.start()

    def end(self):
        self.last[1].wait()
        self.last[0].wait_recv()
        self.last[0].wait_send()

    def units(self):
        return [[self.along_c, self.along_x, self.along_y, self.along_z, self.finish]]

    @staticmethod
    def scratch(zs, rows, wide):
        return [pltpu.VMEM((3, rows, wide), F32), pltpu.VMEM((rows, wide), F32), pltpu.VMEM((zs, rows, wide), F32)]

    @staticmethod
    def remotes(zs):
        return zs + 3


def semaphores(remotes, locals_):
    return [
        pltpu.SemaphoreType.DMA((remotes,)),
        pltpu.SemaphoreType.DMA((remotes,)),
        pltpu.SemaphoreType.DMA((locals_,)),
    ]


def split_refs(refs, *sizes):
    parts, at = [], 0
    for size in sizes:
        parts.append(refs[at:at + size])
        at += size
    return parts + [refs[at:]]


def full_shape(img_size, shard, panels):
    k, cols = shard.shape
    return (panels, 2, img_size // 2, 2, 2, 2 * k, cols // 2 // panels)


def front(img_size, arrays, block, shards, cuts):
    na, nw = len(arrays), len(shards)
    zs = img_size // 2
    outs = [jax.ShapeDtypeStruct((a.shape[0] // 4, 4) + a.shape[1:], a.dtype) for a in arrays]
    outs += [jax.ShapeDtypeStruct((zs, 2, 2, 2, 8, 128), F32)]
    outs += [jax.ShapeDtypeStruct(full_shape(img_size, s, c[0]), BF) for s, c in zip(shards, cuts)]

    def kernel(*refs):
        ins, blk, sh, whole, small, full, scr = split_refs(refs, na, 1, nw, na, 1, nw)
        p = Place(img_size)
        greet(p.partners())
        copies = Copies(*scr[-3:])
        gathers = [Gather(p, copies, sh[i], full[i], scr[2 * i], scr[2 * i + 1], cuts[i][1]) for i in range(nw)]
        moves = [Move(p, copies, a, b, True) for a, b in zip(ins, whole)]
        for g in gathers:
            g.exchange()
        for m in moves:
            m.start()
        units = Spread(p, copies, blk[0], small[0]).units()
        for g in gathers:
            units += g.units()
        for step in pipelined(units):
            step()
        for m in moves:
            m.finish()

    count = sum(a * b for a, b in cuts)
    return pl.pallas_call(
        kernel,
        out_shape=outs,
        in_specs=[ANY] * (na + 1 + nw),
        out_specs=[ANY] * len(outs),
        scratch_shapes=[s for w in shards for s in Gather.scratch(w.shape)]
        + semaphores(3 * na + (zs + 2) * (1 + count) + nw, na + 1 + nw + count),
        compiler_params=pltpu.CompilerParams(collective_id=0, has_side_effects=True, vmem_limit_bytes=40 * MIB),
        name="front",
    )(*arrays, block, *shards)


def table_rows(table, side, blocks, wide):
    span = 2 * side - 1
    square = table.reshape(H, span, span)
    square = jnp.concatenate([square] + [square[:, -1:]] * (blocks - span), 1)
    rows = []
    for turned in (square, square[:, ::-1, ::-1]):
        for part, pads in ((turned[:, :, :side], (0, 1)), (turned[:, :, side:], (1, 0))):
            part = jnp.pad(part, ((0, 0), pads, (0, side - part.shape[2])))
            flat = part.reshape(H, 1, (blocks + 1) * side)
            rows.append(jnp.roll(jnp.pad(flat, ((0, 0), (0, 0), (0, wide - flat.shape[2]))), 1 - side, 2))
    return jnp.concatenate(rows + [jnp.zeros((H, 4, wide), F32)], 1)


def table_sums(rows, side, blocks):
    span = 2 * side - 1
    rows = jnp.roll(rows, side - -(-side // 8) * 8, 2)
    parts = rows[:, :, :(blocks + 1) * side].reshape(H, 2, blocks + 1, side)
    square = jnp.concatenate([parts[:, 0, :blocks], parts[:, 1, 1:, :side - 1]], 2)
    square = jnp.concatenate([square[:, :span - 1], jnp.sum(square[:, span - 1:], 1, keepdims=True)], 1)
    return square.reshape(H, span * span)


def lower_offsets(side, rows, wide):
    lane = lax.rem(lax.broadcasted_iota(jnp.int32, (rows, wide), 1), side)
    return lane <= lax.broadcasted_iota(jnp.int32, (rows, wide), 0)


def spread_rows(rows_ref, h, first, side, rows, wide, lower):
    low = jnp.broadcast_to(rows_ref[h, first:first + 1, :], (rows, wide))
    high = jnp.broadcast_to(rows_ref[h, first + 1:first + 2, :], (rows, wide))
    return jnp.where(
        lower, pltpu.roll(low, 0, 1, stride=1, stride_axis=0), pltpu.roll(high, 0, 1, stride=1, stride_axis=0)
    )


def fill_bias(bias, h, spread, side, rows, first_offset):
    size = bias.shape[2]
    wide = spread.shape[1]
    window = -(-size // 128) * 128 + 128
    for r in range(rows):
        offset = (first_offset - r) * side
        base, rest = offset // 128 * 128, offset % 128
        part = spread[:, base:min(base + window, wide)]
        if part.shape[1] < window:
            part = jnp.concatenate([part, jnp.zeros((spread.shape[0], window - part.shape[1]), F32)], 1)
        if rest:
            part = pltpu.roll(part, window - rest, 1)
        bias[h, r * side:(r + 1) * side, :] = part[:side, :size]


def fold_bias(total, h, acc, side, rows, first_offset, lower, out_ref, half, row):
    size = total.shape[2]
    window = -(-size // 128) * 128 + 128
    height, wide = lower.shape
    acc[...] = jnp.zeros_like(acc)
    for r in range(rows):
        offset = (first_offset - r) * side
        base, rest = offset // 128 * 128, offset % 128
        part = total[h, r * side:(r + 1) * side, :]
        part = jnp.concatenate([part, jnp.zeros((side, window - size), F32)], 1)
        if rest:
            part = pltpu.roll(part, rest, 1)
        acc[:side, base:base + window] += part
    whole = acc[:, :wide]
    zero = jnp.zeros_like(whole)
    for at, part in enumerate((jnp.where(lower, whole, zero), jnp.where(lower, zero, whole))):
        turned = jnp.concatenate([part[j:j + 1] for j in reversed(range(height))], 0)
        moved = pltpu.roll(turned, 0, 1, stride=1, stride_axis=0)
        out_ref[half, pl.ds(row + at, 1), :] = jnp.sum(moved, 0, keepdims=True)


def head_part(full, mask, h):
    keep = mask if h == 0 else jnp.logical_not(mask)
    return jnp.where(keep, full, jnp.zeros_like(full))


def attend_kernel(large, small, q_ref, k_ref, v_ref, rows_l, rows_s, o_ref, bias_l, bias_s):
    mask = lax.broadcasted_iota(jnp.int32, (1, 128), 1) < 64
    lower_l = lower_offsets(SIDE_L, SIDE_L, WIDE_L)
    lower_s = lower_offsets(SIDE_S, 16, WIDE_S)
    for h in range(2):
        fill_bias(bias_l, h, spread_rows(rows_l, h, 2, SIDE_L, SIDE_L, WIDE_L, lower_l), SIDE_L, 24, 23)
        fill_bias(bias_s, h, spread_rows(rows_s, h, 2, SIDE_S, 16, WIDE_S, lower_s), SIDE_S, 16, 15)
    keep = lax.broadcasted_iota(jnp.int32, (1, LEN_S), 1) < SIDE_S * SIDE_S
    images = [(n * LEN_L, LEN_L, bias_l) for n in range(large)]
    images += [(large * LEN_L + n * LEN_S, LEN_S, bias_s) for n in range(small)]
    for at, size, bias in images:
        q, k, v = (ref[at:at + size, :] for ref in (q_ref, k_ref, v_ref))
        outs = []
        for h in range(2):
            s = dot(head_part(q, mask, h) * BF(0.125), k, NT) + bias[h]
            if size == LEN_S:
                s = jnp.where(keep, s, -1e30)
            e = jnp.exp(s - jnp.max(s, 1, keepdims=True))
            p = (e * (1.0 / jnp.sum(e, 1, keepdims=True))).astype(BF)
            outs.append(dot(p, v, NN))
        o_ref[at:at + size, :] = jnp.where(mask, outs[0], outs[1]).astype(BF)


def loop_points(steps, every):
    return {t * every: step for t, step in enumerate(steps)}


def run_point(points, iteration, at, per, iterations):
    for i in range(iterations):
        step = points.get(i * per + at)
        if step is not None:
            pl.when(iteration == i)(step)


def run_rest(points, count):
    for at in sorted(points):
        if at >= count:
            points[at]()


def attend_back_pair(hp, qkv, do_ref, rows_l, rows_s, df, sums_l, sums_s, scratch, large, small, between):
    bias_l, bias_s, total_l, total_s, acc_l, acc_s = scratch
    mask = lax.broadcasted_iota(jnp.int32, (1, 128), 1) < 64
    lower_l = lower_offsets(SIDE_L, SIDE_L, WIDE_L)
    lower_s = lower_offsets(SIDE_S, 16, WIDE_S)
    for h in range(2):
        fill_bias(bias_l, h, spread_rows(rows_l, 2 * hp + h, 0, SIDE_L, SIDE_L, WIDE_L, lower_l), SIDE_L, 24, 23)
        fill_bias(bias_s, h, spread_rows(rows_s, 2 * hp + h, 0, SIDE_S, 16, WIDE_S, lower_s), SIDE_S, 14, 13)
    keep = lax.broadcasted_iota(jnp.int32, (LEN_S, 1), 0) < SIDE_S * SIDE_S
    images = [(n * LEN_L, LEN_L, bias_l, total_l, n == 0) for n in range(large)]
    images += [(large * LEN_L + n * LEN_S, LEN_S, bias_s, total_s, n == 0) for n in range(small)]
    cols = [columns(i * 64 * H + hp * 128, 128) for i in range(3)]
    for index, (at, size, bias, total, first) in enumerate(images):
        between(index)
        rows = slice(at, at + size)
        q, k, v = (qkv[rows, c] for c in cols)
        do = do_ref[rows, cols[0]]
        got = []
        for h in range(2):
            s = dot(head_part(k, mask, h) * BF(0.125), q, NT) + bias[h]
            if size == LEN_S:
                s = jnp.where(keep, s, -1e30)
            e = jnp.exp(s - jnp.max(s, 0, keepdims=True))
            p = e * (1.0 / jnp.sum(e, 0, keepdims=True))
            dp = dot(head_part(v, mask, h), do, NT).astype(BF).astype(F32)
            pd = p * dp
            low = (pd - p * jnp.sum(pd, 0, keepdims=True)).astype(BF)
            got.append((dot(low, k, TN), dot(low, q, NN), dot(p.astype(BF), do, NN)))
            total[h] = low.astype(F32) if first else total[h] + low.astype(F32)
        for c, a, b, scale in zip(cols, got[0], got[1], (0.125, 0.125, 1.0)):
            df[rows, c] = (jnp.where(mask, a, b) * scale).astype(BF)
    half, within = hp // 3, lax.rem(hp, 3)
    for h in range(2):
        fold_bias(total_l, h, acc_l, SIDE_L, 24, 23, lower_l, sums_l, half, 4 * within + 2 * h)
        fold_bias(total_s, h, acc_s, SIDE_S, 14, 13, lower_s, sums_s, half, 4 * within + 2 * h)


def back_scratch():
    return [pltpu.VMEM((2, LEN_L, LEN_L), F32), pltpu.VMEM((2, LEN_S, LEN_S), F32)] * 2 + [
        pltpu.VMEM((SIDE_L, WIDE_L + 128), F32), pltpu.VMEM((16, WIDE_S + 128), F32)]


VMEM = pl.BlockSpec(memory_space=pltpu.VMEM)


def attention_back(img_size, qkv, d_att, rows_l, rows_s, grads, cuts, wholes, large, small, every):
    zs = img_size // 2
    ng, nw = len(grads), len(wholes)
    rows = qkv.shape[0]
    shard_shapes = [(g.shape[5] // 2, g.shape[0] * 2 * g.shape[6]) for g in grads]

    def kernel(*refs):
        ins, gr, wh, outs, shards, blocks, scr = split_refs(refs, 4, ng, nw, 3, ng, nw)
        qkv_hbm, do_hbm, rl, rs = ins
        df_hbm, sums_l, sums_s = outs
        qkv_v, do_v, df_v = scr[:3]
        p = Place(img_size)
        copies = Copies(*scr[-3:])
        loads = [copies.here(lambda: (qkv_hbm, qkv_v)), copies.here(lambda: (do_hbm, do_v))]
        for copy in loads:
            copy.start()
        if ng + nw:
            greet(p.partners())
        at = 3 + 6
        scatters = []
        for i in range(ng):
            scatters.append(Scatter(p, copies, gr[i], shards[i], scr[at:at + 6], cuts[i]))
            at += 6
        moves = [Move(p, copies, a, b, False) for a, b in zip(wh, blocks)]
        units = [u for s in scatters for u in s.units()]
        points = loop_points(pipelined(units) if units else [], every)
        for m in moves:
            m.start()
        sums_l[...] = jnp.zeros_like(sums_l)
        sums_s[...] = jnp.zeros_like(sums_s)
        for copy in loads:
            copy.wait()

        def body(hp, carry):
            attend_back_pair(hp, qkv_v, do_v, rl, rs, df_v, sums_l, sums_s, scr[3:9], large, small,
                             lambda index: run_point(points, hp, index, large + small, H // 2))
            return carry

        lax.fori_loop(0, H // 2, body, 0)
        out = copies.here(lambda: (df_v, df_hbm))
        out.start()
        run_rest(points, (large + small) * (H // 2))
        for s in scatters:
            s.end()
        for m in moves:
            m.finish()
        out.wait()

    scratch = [pltpu.VMEM(qkv.shape, BF), pltpu.VMEM(d_att.shape, BF), pltpu.VMEM(qkv.shape, BF)] + back_scratch()
    for g, (k, cols), cut in zip(grads, shard_shapes, cuts):
        scratch += Scatter.scratch(zs, k, cols, g.shape[0], cut)
    remotes = 3 * nw + sum(Scatter.remotes(zs, g.shape[0], c) for g, c in zip(grads, cuts))
    locals_ = 3 + nw + sum(1 + g.shape[0] * c for g, c in zip(grads, cuts))
    remote = dict(collective_id=1, has_side_effects=True) if ng + nw else {}
    return pl.pallas_call(
        kernel,
        out_shape=[jax.ShapeDtypeStruct(qkv.shape, BF), jax.ShapeDtypeStruct((2, 16, WIDE_L), F32),
                   jax.ShapeDtypeStruct((2, 16, WIDE_S), F32)]
        + [jax.ShapeDtypeStruct(s, F32) for s in shard_shapes]
        + [jax.ShapeDtypeStruct((w.shape[0] * 4,) + w.shape[2:], w.dtype) for w in wholes],
        in_specs=[ANY, ANY, VMEM, VMEM] + [ANY] * (ng + nw),
        out_specs=[ANY, VMEM, VMEM] + [ANY] * (ng + nw),
        scratch_shapes=scratch + semaphores(max(remotes, 1), locals_),
        compiler_params=pltpu.CompilerParams(vmem_limit_bytes=60 * MIB, **remote),
        name="attention_back",
    )(qkv, d_att, rows_l, rows_s, *grads, *wholes)


def row_tiles(rows, tile, body):
    count = rows // tile

    def step(t, carry):
        body(pl.multiple_of(t * tile, 16), tile)
        return carry

    lax.fori_loop(0, count, step, 0)
    if rows % tile:
        body(count * tile, rows % tile)


def norm_parts(x):
    centered = x - jnp.mean(x, 1, keepdims=True)
    scale = lax.rsqrt(jnp.mean(centered * centered, 1, keepdims=True) + 1e-06)
    return centered * scale, scale


def norm_back(dn, hat, scale, gain):
    d_hat = dn * gain
    return scale * (d_hat - jnp.mean(d_hat, 1, keepdims=True) - hat * jnp.mean(d_hat * hat, 1, keepdims=True))


def fold8(values):
    return sum(values[i:i + 8] for i in range(0, values.shape[0], 8))


def place_small(ref, flat, at):
    for i in range(4):
        ref[at, i] = flat[i * 56:(i + 1) * 56].astype(ref.dtype)


def load_tokens(copies, large_hbm, small_hbm, flat, four):
    n, _, rows, _ = large_hbm.shape
    loads = [
        copies.here(lambda i=i, j=j: (large_hbm.at[i, j], flat.at[pl.ds((i * 4 + j) * rows, rows)]))
        for i in range(n) for j in range(4)
    ]
    return loads + [copies.here(lambda: (small_hbm, four))]


def join_small(flat, four, large):
    for n in range(four.shape[0]):
        rows = jnp.concatenate([four[n, i].astype(F32) for i in range(4)], 0)
        at = large * LEN_L + n * LEN_S
        flat[at:at + LEN_S, :] = rows.astype(flat.dtype)


def projection_back(img_size, df, dm, x_l, x_s, w_qkv, vectors, sums, tables, large, small):
    zs = img_size // 2
    rows, width = dm.shape
    panels, _, _, _, _, k2, wide = w_qkv.shape
    k, cols = k2 // 2, panels * 2 * wide
    nt = len(tables)

    def kernel(*refs):
        ins, tabs, outs, tab_outs, scr = split_refs(refs, 7, nt, 4, nt)
        df_hbm, dm_hbm, xl_hbm, xs_hbm, w_hbm, vec, sums_in = ins
        gl_out, gs_out, shard, sums_out = outs
        df_v, dm_v, flat, four, w_v, nt_v, dn, acc, own_sums, dl, ds = scr[:11]
        at = 11
        p = Place(img_size)
        copies = Copies(*scr[-3:])
        x_loads = load_tokens(copies, xl_hbm, xs_hbm, flat, four)
        df_load = copies.here(lambda: (df_hbm, df_v))
        later = [copies.here(lambda: (w_hbm, w_v)), copies.here(lambda: (dm_hbm, dm_v))]
        for copy in x_loads + [df_load] + later:
            copy.start()
        greet(p.partners())
        scatter = Scatter(p, copies, None, shard, scr[at:at + 7], 1)
        at += 7
        totals = []
        for a, b in zip(tabs, tab_outs):
            totals.append(Total(p, copies, a, b, *scr[at:at + 3]))
            at += 3
        last = Total(p, copies, own_sums, sums_out, *scr[at:at + 3])
        moves = [Move(p, copies, dl, gl_out, False), Move(p, copies, ds, gs_out, False)]
        for t in totals:
            t.along_c()
        for copy in x_loads:
            copy.wait()
        join_small(flat, four, large)
        gain, shift = vec[0:1, :], vec[4:5, :]

        def normed(start, size):
            hat, _ = norm_parts(flat[pl.ds(start, size), :].astype(F32))
            n1_v[pl.ds(start, size), :] = (hat * gain + shift).astype(BF)

        n1_v = scr[-4]
        row_tiles(rows, 96, normed)
        nt_v[...] = n1_v[...].T
        df_load.wait()
        units = scatter.units()
        for t in totals:
            t.along_x()
        for u in range(panels):
            def part(c):
                cols_ = columns(c * (cols // 2) + u * wide, wide)
                got = dot(nt_v[...], df_v[:, cols_], NN).astype(BF)
                return got.reshape(zs, 2, 2, k2, wide)
            scatter.stage[u] = part(1 - p.c)
            units[u][0]()
            scatter.own[u] = part(p.c)
            if u >= 1:
                units[u - 1][1]()
            if u >= 2:
                units[u - 2][2]()
            if u == 1:
                for t in totals:
                    t.along_y()
            if u == 2:
                for t in totals:
                    t.along_z()
        for copy in later:
            copy.wait()
        for u in range(panels):
            for c in range(2):
                cols_ = slice(c * (cols // 2) + u * wide, c * (cols // 2) + (u + 1) * wide)
                w = w_v[u, c].reshape(width, wide)
                got = dot(df_v[:, cols_], w, NT)
                dn[...] = got if u == 0 and c == 0 else dn[...] + got
            if u == 0:
                units[panels - 1][1]()
                units[panels - 2][2]()
        acc[...] = jnp.zeros_like(acc)

        def back(start, size):
            at_rows = pl.ds(start, size)
            hat, scale = norm_parts(flat[at_rows, :].astype(F32))
            d = dn[at_rows, :]
            acc[0] += fold8(d * hat)
            acc[1] += fold8(d)
            acc[2] += fold8(df_v[at_rows, :width].astype(F32))
            acc[3] += fold8(df_v[at_rows, 2 * width:].astype(F32))
            dm_v[at_rows, :] = dm_v[at_rows, :] + norm_back(d, hat, scale, gain)

        row_tiles(rows, 96, back)
        for i in range(large):
            for j in range(4):
                start = (i * 4 + j) * (LEN_L // 4)
                dl[i, j] = dm_v[start:start + LEN_L // 4, :].astype(BF)
        for n in range(small):
            start = large * LEN_L + n * LEN_S
            place_small(ds, dm_v[start:start + LEN_S, :], n)
        for m in moves:
            m.start()
        for i, row in ((0, 0), (1, 4), (2, 6), (3, 7)):
            own_sums[0, row:row + 1, :] = jnp.sum(acc[i], 0, keepdims=True)
        for row in (1, 2, 3, 5):
            own_sums[0, row:row + 1, :] = sums_in[0, row:row + 1, :]
        own_sums[1] = sums_in[1]
        last.along_c()
        units[panels - 1][2]()
        for f in (3, 4):
            for u in range(panels):
                units[u][f]()
            if f == 3:
                last.along_x()
                for t in totals:
                    t.finish()
        last.along_y()
        last.along_z()
        last.finish()
        scatter.end()
        for t in totals + [last]:
            t.end()
        for m in moves:
            m.finish()

    scratch = [
        pltpu.VMEM(df.shape, BF), pltpu.VMEM(dm.shape, F32), pltpu.VMEM((rows, width), BF),
        pltpu.VMEM(x_s.shape, BF), pltpu.VMEM(w_qkv.shape, BF), pltpu.VMEM((width, rows), BF),
        pltpu.VMEM((rows, width), F32), pltpu.VMEM((4, 8, width), F32), pltpu.VMEM((2, 8, width), F32),
        pltpu.VMEM(x_l.shape, BF), pltpu.VMEM(x_s.shape, BF),
    ] + Scatter.scratch(zs, k, cols, panels, 1, True)
    for t in list(tables) + [sums]:
        scratch += Total.scratch(zs, t.shape[1], t.shape[2])
    scratch += [pltpu.VMEM((rows, width), BF)]
    remotes = 6 + Scatter.remotes(zs, panels, 1) + Total.remotes(zs) * (nt + 1)
    locals_ = 4 * x_l.shape[0] + 1 + 3 + 2 + 1 + 2 * (nt + 1)
    f32 = lambda s: jax.ShapeDtypeStruct(s, F32)
    return pl.pallas_call(
        kernel,
        out_shape=[jax.ShapeDtypeStruct((4 * a.shape[0],) + a.shape[2:], BF) for a in (x_l, x_s)]
        + [f32((k, cols)), f32(sums.shape)] + [f32(t.shape) for t in tables],
        in_specs=[ANY] * 5 + [VMEM, VMEM] + [ANY] * nt,
        out_specs=[ANY] * (4 + nt),
        scratch_shapes=scratch + semaphores(remotes, locals_),
        compiler_params=pltpu.CompilerParams(collective_id=2, has_side_effects=True, vmem_limit_bytes=60 * MIB),
        name="projection_back",
    )(df, dm, x_l, x_s, w_qkv, vectors, sums, *tables)


def gelu_parts(u):
    bell = jnp.exp(-0.5 * (u * u))
    t = 1.0 / (1.0 + 0.2316418882663604 * jnp.abs(u))
    series = ((((1.061405429 * t - 1.453152027) * t + 1.421413741) * t - 0.284496736) * t + 0.254829592) * t
    tail = 0.5 * series * bell
    cdf = jnp.where(u >= 0.0, 1.0 - tail, tail)
    return u * cdf, cdf + 0.3989422804014327 * (u * bell)


def joined(w, *at):
    parts = [w[(at[0], c) + at[1:]] for c in range(2)]
    return jnp.concatenate([part.reshape(-1, part.shape[-1]) for part in parts], 1)


def image_rows(large, small):
    parts = [(n, j, (n * 4 + j) * (LEN_L // 4)) for n in range(large) for j in range(4)]
    return parts, [(n, large * LEN_L + n * LEN_S) for n in range(small)]


def forward_tail(att, x_l, x_s, ct_l, ct_s, w_out, w_up, w_down, vectors, up_vec):
    large, small = x_l.shape[0], x_s.shape[0]
    rows, width = att.shape
    chunks = up_vec.shape[0]
    half = rows // 2

    def kernel(att_hbm, xl_hbm, xs_hbm, cl_hbm, cs_hbm, wo_hbm, wu_hbm, wd_hbm, vec, upv,
               yl, ys, m_hbm, n2_hbm, e_hbm, g_hbm, dr_hbm, dy_hbm, sums,
               att_v, flat, four, ct_four, wo, wu, wd, m_v, n2_v, r_v, e_v, g_v, acc, local):
        copies = Copies(None, None, local)
        first = [copies.here(lambda: (att_hbm, att_v)), copies.here(lambda: (wo_hbm, wo))]
        first += load_tokens(copies, xl_hbm, xs_hbm, flat, four)
        second = [copies.here(lambda: (wu_hbm, wu))]
        third = [copies.here(lambda: (wd_hbm, wd))]
        for copy in first + second + third:
            copy.start()
        for copy in first:
            copy.wait()
        join_small(flat, four, large)
        g2, s1, s2, b2, bo, bd = (vec[i:i + 1, :] for i in (1, 2, 3, 5, 8, 9))

        def project(i, carry):
            at = pl.ds(pl.multiple_of(i * half, 16), half)
            m_v[at, :] = dot(att_v[at, :], joined(wo, 0), NN)
            return carry

        lax.fori_loop(0, 2, project, 0)

        def middle(start, size):
            at = pl.ds(start, size)
            m = flat[at, :].astype(F32) + s1 * (m_v[at, :] + bo)
            m_v[at, :] = m
            hat, _ = norm_parts(m)
            n2_v[at, :] = (hat * g2 + b2).astype(BF)

        row_tiles(rows, 96, middle)
        m_out = [copies.here(lambda: (m_v, m_hbm)), copies.here(lambda: (n2_v, n2_hbm))]
        for copy in m_out:
            copy.start()
        ct = load_tokens(copies, cl_hbm, cs_hbm, flat, ct_four)
        for copy in ct:
            copy.start()
        for copy in second + third:
            copy.wait()

        out_at = copies.locals
        copies.locals += 4

        def out(f, slot):
            return [
                pltpu.make_async_copy(v.at[slot], hbm.at[f], local.at[out_at + 2 * slot + i])
                for i, (v, hbm) in enumerate(((e_v, e_hbm), (g_v, g_hbm)))
            ]

        def chunk(f, carry):
            slot = lax.rem(f, 2)

            @pl.when(f >= 2)
            def _():
                for copy in out(f - 2, slot):
                    copy.wait()

            w1 = wu[lax.rem(f, 2), f // 2].reshape(width, width)
            w2 = jnp.concatenate([wd[0, c, f].reshape(width, width // 2) for c in range(2)], 1)
            for i in range(2):
                at = slice(i * half, (i + 1) * half)
                u = dot(n2_v[at, :], w1, NN) + upv[pl.ds(f, 1), :]
                e, g = gelu_parts(u)
                e = e.astype(BF)
                e_v[slot, at, :] = e
                g_v[slot, at, :] = g.astype(BF)
                r = dot(e, w2, NN)

                @pl.when(f == 0)
                def _():
                    r_v[at, :] = r

                @pl.when(f > 0)
                def _():
                    r_v[at, :] += r
            for copy in out(f, slot):
                copy.start()
            return carry

        lax.fori_loop(0, chunks, chunk, 0)
        for copy in ct:
            copy.wait()
        join_small(flat, ct_four, large)
        for n in range(small):
            at = large * LEN_L + n * LEN_S + SIDE_S * SIDE_S // 16 * 16
            keep = lax.broadcasted_iota(jnp.int32, (32, 1), 0) < SIDE_S * SIDE_S % 16
            flat[at:at + 32, :] = jnp.where(keep, flat[at:at + 32, :].astype(F32), 0.0).astype(BF)
        for copy in m_out:
            copy.wait()
        acc[...] = jnp.zeros_like(acc)

        def result(start, size):
            at = pl.ds(start, size)
            r = r_v[at, :] + bd
            dy = flat[at, :].astype(F32)
            dr = (s2 * dy).astype(BF)
            acc[0] += fold8(r * dy)
            acc[1] += fold8(dr.astype(F32))
            m_v[at, :] = m_v[at, :] + s2 * r
            n2_v[at, :] = dr

        row_tiles(rows, 96, result)
        last = [copies.here(lambda: (n2_v, dr_hbm)), copies.here(lambda: (flat, dy_hbm))]
        for copy in last:
            copy.start()
        for n, j, start in image_rows(large, small)[0]:
            yl[n, j] = m_v[start:start + LEN_L // 4, :].astype(BF)
        for n, start in image_rows(large, small)[1]:
            place_small(ys, m_v[start:start + LEN_S, :], n)
        for i in range(2):
            sums[i:i + 1, :] = jnp.sum(acc[i], 0, keepdims=True)
        for f in (chunks - 2, chunks - 1):
            for copy in out(f, f % 2):
                copy.wait()
        for copy in last:
            copy.wait()

    bf = lambda *s: jax.ShapeDtypeStruct(s, BF)
    return pl.pallas_call(
        kernel,
        out_shape=[bf(*x_l.shape), bf(*x_s.shape), jax.ShapeDtypeStruct((rows, width), F32), bf(rows, width),
                   bf(chunks, rows, width), bf(chunks, rows, width), bf(rows, width), bf(rows, width),
                   jax.ShapeDtypeStruct((8, width), F32)],
        in_specs=[ANY] * 8 + [VMEM, VMEM],
        out_specs=[VMEM, VMEM] + [ANY] * 6 + [VMEM],
        scratch_shapes=[
            pltpu.VMEM((rows, width), BF), pltpu.VMEM((rows, width), BF), pltpu.VMEM(x_s.shape, BF),
            pltpu.VMEM(x_s.shape, BF), pltpu.VMEM(w_out.shape, BF), pltpu.VMEM(w_up.shape, BF),
            pltpu.VMEM(w_down.shape, BF), pltpu.VMEM((rows, width), F32), pltpu.VMEM((rows, width), BF),
            pltpu.VMEM((rows, width), F32), pltpu.VMEM((2, rows, width), BF), pltpu.VMEM((2, rows, width), BF),
            pltpu.VMEM((2, 8, width), F32), pltpu.SemaphoreType.DMA((16 + 8 * large + 4,)),
        ],
        compiler_params=pltpu.CompilerParams(vmem_limit_bytes=60 * MIB),
        name="forward_tail",
    )(att, x_l, x_s, ct_l, ct_s, w_out, w_up, w_down, vectors, up_vec)


def backward_head(att, m, n2, e, g, dr, dy, w_out, w_up, w_down, vectors, sums_in):
    rows, width = att.shape
    chunks = e.shape[0]
    half = rows // 2

    def kernel(att_hbm, m_hbm, n2_hbm, e_hbm, g_hbm, dr_hbm, dy_hbm, wo_hbm, wu_hbm, wd_hbm, vec, s_in,
               go, gu, gd, dm_hbm, da_hbm, sums,
               att_v, m_v, n2_v, nt_v, e_v, g_v, dr_v, dy_v, wo, wu, wd, dn, du_v, gd_v, gu_v, go_v, acc, up_acc, local):
        copies = Copies(None, None, local)
        pairs = [(dr_hbm, dr_v), (n2_hbm, n2_v), (wd_hbm, wd), (wu_hbm, wu),
                 (m_hbm, m_v), (dy_hbm, dy_v), (att_hbm, att_v), (wo_hbm, wo)]
        loads = [copies.here(lambda a=a, b=b: (a, b)) for a, b in pairs]
        base = copies.locals
        copies.locals += 8

        def fetch(f, slot):
            return [pltpu.make_async_copy(h.at[f], v.at[slot], local.at[base + 2 * slot + i])
                    for i, (h, v) in enumerate(((e_hbm, e_v), (g_hbm, g_v)))]

        def put(f, slot):
            return [
                pltpu.make_async_copy(gd_v.at[slot], gd.at[0, :, f], local.at[base + 4 + 2 * slot]),
                pltpu.make_async_copy(gu_v.at[slot], gu.at[lax.rem(f, 2), f // 2], local.at[base + 5 + 2 * slot]),
            ]

        for copy in fetch(0, 0):
            copy.start()
        for copy in loads:
            copy.start()
        for copy in loads[:4]:
            copy.wait()
        nt_v[...] = n2_v[...].T
        g2, s1, b2, bo = (vec[i:i + 1, :] for i in (1, 2, 5, 8))

        def chunk(f, carry):
            slot = lax.rem(f, 2)
            for copy in fetch(f, slot):
                copy.wait()

            @pl.when(f + 1 < chunks)
            def _():
                for copy in fetch(f + 1, 1 - slot):
                    copy.start()

            @pl.when(f >= 2)
            def _():
                for copy in put(f - 2, slot):
                    copy.wait()

            w1 = wu[lax.rem(f, 2), f // 2].reshape(width, width)
            w2 = jnp.concatenate([wd[0, c, f].reshape(width, width // 2) for c in range(2)], 1)
            got = dot(e_v[slot], dr_v[...], TN).astype(BF)
            for c in range(2):
                part = got[:, c * (width // 2):(c + 1) * (width // 2)]
                gd_v[slot, c] = part.reshape(gd_v.shape[2:])
            total = jnp.zeros((8, width), F32)
            for i in range(2):
                at = slice(i * half, (i + 1) * half)
                de = dot(dr_v[at, :], w2, NT)
                du = (de * g_v[slot, at, :].astype(F32)).astype(BF)
                du_v[at, :] = du
                total += fold8(du.astype(F32))
                d = dot(du, w1, NT)

                @pl.when(f == 0)
                def _():
                    dn[at, :] = d

                @pl.when(f > 0)
                def _():
                    dn[at, :] += d
            up_acc[f] = total
            gu_v[slot] = dot(nt_v[...], du_v[...], NN).astype(BF).reshape(gu_v.shape[1:])
            for copy in put(f, slot):
                copy.start()
            return carry

        lax.fori_loop(0, chunks, chunk, 0)
        for copy in loads[4:]:
            copy.wait()
        acc[...] = jnp.zeros_like(acc)

        def norm(start, size):
            at = pl.ds(start, size)
            hat, scale = norm_parts(m_v[at, :])
            d = dn[at, :]
            acc[0] += fold8(d * hat)
            acc[1] += fold8(d)
            dm = dy_v[at, :].astype(F32) + norm_back(d, hat, scale, g2)
            da = (s1 * dm).astype(BF)
            acc[2] += fold8(da.astype(F32))
            m_v[at, :] = dm
            du_v[at, :] = da

        row_tiles(rows, 96, norm)
        out = [copies.here(lambda: (m_v, dm_hbm))]
        out[0].start()
        w = joined(wo, 0)
        got = dot(att_v[...], du_v[...], TN).astype(BF)
        for c in range(2):
            go_v[c] = got[:, c * (width // 2):(c + 1) * (width // 2)].reshape(go_v.shape[1:])
        out.append(copies.here(lambda: (go_v, go.at[0])))
        out[1].start()
        for i in range(2):
            at = slice(i * half, (i + 1) * half)
            n2_v[at, :] = dot(du_v[at, :], w, NT).astype(BF)
            a = dot(att_v[at, :], w, NN) + bo
            acc[3] += fold8(a * m_v[at, :])
        out.append(copies.here(lambda: (n2_v, da_hbm)))
        out[2].start()
        sums[...] = jnp.zeros_like(sums)
        for i, (part, row) in enumerate(((0, 1), (0, 5), (1, 0), (0, 2))):
            sums[part, row:row + 1, :] = jnp.sum(acc[i], 0, keepdims=True)
        sums[0, 3:4, :] = s_in[0:1, :]
        sums[1, 1:2, :] = s_in[1:2, :]
        for f in range(chunks):
            sums[1, 2 + f:3 + f, :] = jnp.sum(up_acc[f], 0, keepdims=True)
        for f in (chunks - 2, chunks - 1):
            for copy in put(f, f % 2):
                copy.wait()
        for copy in out:
            copy.wait()

    bf = lambda *s: jax.ShapeDtypeStruct(s, BF)
    f32 = lambda *s: jax.ShapeDtypeStruct(s, F32)
    vm = pltpu.VMEM
    flat = vm((rows, width), BF)
    return pl.pallas_call(
        kernel,
        out_shape=[bf(*w_out.shape), bf(*w_up.shape), bf(*w_down.shape), f32(rows, width), bf(rows, width),
                   f32(2, 8, width)],
        in_specs=[ANY] * 10 + [VMEM, VMEM],
        out_specs=[ANY] * 5 + [VMEM],
        scratch_shapes=[
            flat, vm((rows, width), F32), flat, vm((width, rows), BF), vm((2, rows, width), BF),
            vm((2, rows, width), BF), flat, flat, vm(w_out.shape, BF), vm(w_up.shape, BF), vm(w_down.shape, BF),
            vm((rows, width), F32), flat, vm((2, 2) + w_down.shape[3:], BF), vm((2,) + w_up.shape[2:], BF),
            vm(w_out.shape[1:], BF), vm((4, 8, width), F32), vm((chunks, 8, width), F32),
            pltpu.SemaphoreType.DMA((24,)),
        ],
        compiler_params=pltpu.CompilerParams(vmem_limit_bytes=60 * MIB),
        name="backward_head",
    )(att, m, n2, e, g, dr, dy, w_out, w_up, w_down, vectors, sums_in)


def project_in(x_l, x_s, w_qkv, vectors, merged_bias):
    large, small = x_l.shape[0], x_s.shape[0]
    rows, width = large * LEN_L + small * LEN_S, x_l.shape[3]
    panels, wide = w_qkv.shape[0], w_qkv.shape[-1]

    def kernel(xl_hbm, xs_hbm, w_hbm, vec, bias, out, flat, four, w_v, local):
        copies = Copies(None, None, local)
        loads = load_tokens(copies, xl_hbm, xs_hbm, flat, four) + [copies.here(lambda: (w_hbm, w_v))]
        for copy in loads:
            copy.start()
        for copy in loads[:-1]:
            copy.wait()
        join_small(flat, four, large)

        def normed(start, size):
            at = pl.ds(start, size)
            hat, _ = norm_parts(flat[at, :].astype(F32))
            flat[at, :] = (hat * vec[0:1, :] + vec[4:5, :]).astype(BF)

        row_tiles(rows, 96, normed)
        loads[-1].wait()
        for u in range(panels):
            for c in range(2):
                cols = slice((c * panels + u) * wide, (c * panels + u + 1) * wide)
                got = dot(flat[...], w_v[u, c].reshape(width, wide), NN) + bias[:, cols]
                out[:, cols] = got.astype(BF)

    return pl.pallas_call(
        kernel,
        out_shape=jax.ShapeDtypeStruct((rows, 3 * width), BF),
        in_specs=[ANY] * 3 + [VMEM, VMEM],
        out_specs=VMEM,
        scratch_shapes=[pltpu.VMEM((rows, width), BF), pltpu.VMEM(x_s.shape, BF), pltpu.VMEM(w_qkv.shape, BF),
                        pltpu.SemaphoreType.DMA((4 * large + 2,))],
        compiler_params=pltpu.CompilerParams(vmem_limit_bytes=40 * MIB),
        name="project_in",
    )(x_l, x_s, w_qkv, vectors, merged_bias)


def head_columns(rows, at):
    return pl.BlockSpec((rows, 128), lambda g: (0, g + at))


def attend(qkv, rows_l, rows_s, large, small):
    rows = qkv.shape[0]
    return pl.pallas_call(
        functools.partial(attend_kernel, large, small),
        grid=(H // 2,),
        out_shape=jax.ShapeDtypeStruct((rows, 64 * H), BF),
        in_specs=[head_columns(rows, H // 2 * i) for i in range(3)]
        + [pl.BlockSpec((2, 8, WIDE_L), lambda g: (g, 0, 0)), pl.BlockSpec((2, 8, WIDE_S), lambda g: (g, 0, 0))],
        out_specs=head_columns(rows, 0),
        scratch_shapes=[pltpu.VMEM((2, LEN_L, LEN_L), F32), pltpu.VMEM((2, LEN_S, LEN_S), F32)],
        compiler_params=pltpu.CompilerParams(vmem_limit_bytes=56 * MIB),
        name="attend",
    )(qkv, qkv, qkv, rows_l, rows_s)


def layer_norm(values, gain, shift):
    average = jnp.mean(values, -1, keepdims=True)
    centered = values - average
    variance = jnp.mean(centered * centered, -1, keepdims=True)
    return centered * lax.rsqrt(variance + 1e-06) * gain + shift


def to_images(blocks):
    n = blocks.shape[0] // 4
    got = lax.all_to_all(blocks.reshape((4, n) + blocks.shape[1:]), "rows", 0, 0)
    return jnp.swapaxes(got, 0, 1)


def to_blocks(whole):
    got = lax.all_to_all(jnp.swapaxes(whole, 0, 1), "rows", 0, 0)
    return got.reshape((-1,) + got.shape[2:])


def to_panels(full, panels):
    rows, cols = full.shape
    split = full.reshape(4, 2, 2, rows // 16, 2, panels, cols // 2 // panels)
    return split.transpose(5, 4, 0, 1, 2, 3, 6)


def from_panels(split):
    rows, cols = 16 * split.shape[5], split.shape[0] * 2 * split.shape[6]
    return split.transpose(2, 3, 4, 5, 1, 0, 6).reshape(rows, cols)


CUTS = ((3, 1), (1, 1), (2, 1), (1, 3))


def on_device(img_size, small_images, large_images, w_qkv, w_out, w_up, w_down, gains, biases, up_bias,
              small_table, large_table, small_cotangent, large_cotangent):
    width = small_images.shape[2]
    axes = ("img", "rows")
    shards = [w_qkv, w_out, w_up, w_down]
    own = gains.shape[0]
    own_up = up_bias.shape[0]
    own_len = 10 * own + own_up
    block = jnp.concatenate([gains.T.reshape(-1), biases.T.reshape(-1), up_bias])
    block = jnp.pad(block, (0, 1024 - own_len)).reshape(8, 128)
    arrays = [large_images, small_images, large_cotangent, small_cotangent]
    direct = own % 8 == 0
    if direct:
        got = front(img_size, arrays, block, shards, CUTS)
        full = got[5:]
    else:
        got = [to_images(a) for a in arrays] + [lax.all_gather(block, axes, axis=0)]
        full = [to_panels(lax.all_gather(s.astype(BF), axes, axis=0, tiled=True), c[0]) for s, c in zip(shards, CUTS)]
    large_x, small_x, large_ct, small_ct = got[:4]
    blocks = got[4].reshape(-1, 1024).astype(BF).astype(F32)
    vectors = jnp.swapaxes(blocks[:, :10 * own].reshape(-1, 10, own), 0, 1).reshape(10, width)
    merged_bias = jnp.concatenate([vectors[6:7], jnp.zeros((1, width), F32), vectors[7:8]], 1)
    up_vec = blocks[:, 10 * own:own_len].reshape(-1, width)
    vectors = jnp.pad(vectors, ((0, 6), (0, 0)))
    qkv_w, out_w, up_w, down_w = full

    large, small = large_x.shape[0], small_x.shape[0]
    rows_l = table_rows(large_table, SIDE_L, 47, WIDE_L)
    rows_s = table_rows(small_table, SIDE_S, 29, WIDE_S)

    qkv = project_in(large_x, small_x, qkv_w, vectors, merged_bias)
    attended = attend(qkv, rows_l, rows_s, large, small)
    large_y, small_y, m, n2, e, g, dr, dy, sums = forward_tail(
        attended, large_x, small_x, large_ct, small_ct, out_w, up_w, down_w, vectors, up_vec)
    grad_out, grad_up, grad_down, dm, d_att, sums = backward_head(
        attended, m, n2, e, g, dr, dy, out_w, up_w, down_w, vectors, sums)
    if direct:
        df, large_sums, small_sums, *more = attention_back(
            img_size, qkv, d_att, rows_l, rows_s, [grad_down, grad_out, grad_up], [CUTS[i][1] for i in (3, 1, 2)],
            [large_y, small_y], large, small, 1)
        own_down, own_out, own_up_w, large_out, small_out = more
        large_grad, small_grad, own_qkv, sums, large_sums, small_sums = projection_back(
            img_size, df, dm, large_x, small_x, qkv_w, vectors, sums, [large_sums, small_sums], large, small)
    else:
        df, large_sums, small_sums = attention_back(img_size, qkv, d_att, rows_l, rows_s, [], [], [], large, small, 1)
        split_at = large * LEN_L
        tokens = jnp.concatenate([large_x.reshape(-1, width), small_x.reshape(-1, width)], 0).astype(F32)
        normed, pull = jax.vjp(layer_norm, tokens, vectors[0], vectors[4])
        grad_qkv = jnp.einsum("rd,re->de", normed.astype(BF), df, preferred_element_type=F32)
        d_normed = jnp.einsum("re,de->rd", df, from_panels(qkv_w), preferred_element_type=F32)
        d_tokens, grad_gain, grad_shift = pull(d_normed)
        d_tokens = (dm + d_tokens).astype(BF)
        grad_q = jnp.sum(df[:, :width].astype(F32), 0)
        grad_v = jnp.sum(df[:, 2 * width:].astype(F32), 0)
        for row, value in ((0, grad_gain), (4, grad_shift), (6, grad_q), (7, grad_v)):
            sums = sums.at[0, row].set(value)
        sums, large_sums, small_sums = lax.psum((sums, large_sums, small_sums), axes)
        large_grad = to_blocks(d_tokens[:split_at].reshape(large_x.shape))
        small_grad = to_blocks(d_tokens[split_at:].reshape(small_x.shape))
        large_out, small_out = to_blocks(large_y), to_blocks(small_y)
        grads = [grad_qkv] + [from_panels(g).astype(F32) for g in (grad_out, grad_up, grad_down)]
        own_qkv, own_out, own_up_w, own_down = [
            lax.psum_scatter(g, axes, scatter_dimension=0, tiled=True) for g in grads]

    index = lax.axis_index("img") * 4 + lax.axis_index("rows")
    flat_sums = sums.reshape(16, width)
    own_columns = lax.dynamic_slice(flat_sums, (0, index * own), (10, own)).T
    own_up_sums = lax.dynamic_slice(flat_sums[10:14].reshape(-1), (index * own_up,), (own_up,))
    grad_large_table = table_sums(large_sums[:, :12].reshape(H, 2, WIDE_L), SIDE_L, 47)
    grad_small_table = table_sums(small_sums[:, :12].reshape(H, 2, WIDE_S), SIDE_S, 29)
    return (
        small_out, large_out, small_grad, large_grad, own_qkv, own_out, own_up_w, own_down,
        own_columns[:, :4], own_columns[:, 4:], own_up_sums, grad_small_table, grad_large_table,
    )


def solution(mesh):
    images = P("img", "rows", None)
    matrix = P(("img", "rows"), None)
    vector = P(("img", "rows"))
    in_specs = (images, images) + (matrix,) * 6 + (vector, P(), P(), images, images)
    out_specs = (images,) * 4 + (matrix,) * 6 + (vector, P(), P())
    return jax.shard_map(
        functools.partial(on_device, mesh.shape["img"]),
        mesh=mesh, in_specs=in_specs, out_specs=out_specs, check_vma=False,
    )
```

```python
import functools

import jax
import jax.numpy as jnp
from jax import lax
from jax.experimental import pallas as pl
from jax.experimental.pallas import tpu as pltpu
from jax.sharding import PartitionSpec as P

H = 12
SIDE_S = 14
SIDE_L = 24
LEN_S = 224
LEN_L = 576
WIDE_L = 1152
WIDE_S = 512

F32 = jnp.float32
BF = jnp.bfloat16
NN = (((1,), (0,)), ((), ()))
NT = (((1,), (1,)), ((), ()))
TN = (((0,), (0,)), ((), ()))
MESH = pl.DeviceIdType.MESH
ANY = pl.BlockSpec(memory_space=pl.ANY)
MIB = 1 << 20


def dot(left, right, dims):
    return lax.dot_general(left, right, dims, preferred_element_type=F32)


class Place:
    def __init__(self, img_size):
        self.img = lax.axis_index("img")
        self.row = lax.axis_index("rows")
        self.zs = img_size // 2
        self.z, self.x = self.img // 2, self.img % 2
        self.y, self.c = self.row // 2, self.row % 2

    def at(self, z=None, x=None, y=None, c=None):
        z = self.z if z is None else z
        x = self.x if x is None else x
        y = self.y if y is None else y
        c = self.c if c is None else c
        return (z * 2 + x, y * 2 + c)

    def z_other(self, step):
        return lax.rem(self.z + step, self.zs)

    def row_other(self, step):
        return lax.rem(self.row + step, 4)

    def partners(self):
        along_z = [self.at(z=self.z_other(s)) for s in range(1, self.zs)]
        in_rows = [(self.img, self.row_other(s)) for s in range(1, 4)]
        return along_z + in_rows + [self.at(x=1 - self.x)]


def greet(partners):
    barrier = pltpu.get_barrier_semaphore()
    for p in partners:
        pl.semaphore_signal(barrier, inc=1, device_id=p, device_id_type=MESH)
    pl.semaphore_wait(barrier, len(partners))


class Remote:
    def __init__(self, copies, build):
        self.copies, self.build, self.at = copies, build, copies.remotes
        copies.remotes += 1

    def made(self):
        src, dst, device = self.build()
        return pltpu.make_async_remote_copy(
            src_ref=src, dst_ref=dst, send_sem=self.copies.send.at[self.at], recv_sem=self.copies.recv.at[self.at],
            device_id=device, device_id_type=MESH,
        )

    def start(self):
        self.made().start()
        return self

    def wait_send(self):
        self.made().wait_send()

    def wait_recv(self):
        self.made().wait_recv()


class Local:
    def __init__(self, copies, build):
        self.copies, self.build, self.at = copies, build, copies.locals
        copies.locals += 1

    def made(self):
        return pltpu.make_async_copy(*self.build(), self.copies.local.at[self.at])

    def start(self):
        self.made().start()
        return self

    def wait(self):
        self.made().wait()


class Copies:
    def __init__(self, send, recv, local):
        self.send, self.recv, self.local = send, recv, local
        self.remotes, self.locals = 0, 0

    def remote(self, build):
        return Remote(self, build)

    def here(self, build):
        return Local(self, build)


def pipelined(units):
    depth = max(len(u) for u in units)

    def step(t):
        for f in range(depth):
            u = t - f
            if 0 <= u < len(units) and f < len(units[u]):
                units[u][f]()

    return [functools.partial(step, t) for t in range(len(units) + depth - 1)]


def columns(start, size):
    return pl.ds(pl.multiple_of(start, 128), size)


class Gather:
    def __init__(self, place, copies, shard, full, both, low, pieces):
        self.p, self.copies = place, copies
        self.full, self.both, self.low = full, both, low
        self.panels, self.wide = full.shape[0], full.shape[-1]
        self.k, self.half = full.shape[5] // 2, self.panels * self.wide
        self.tall = 2 * self.k // pieces
        self.pieces = pieces
        p = place

        def mine():
            return both.at[pl.ds(pl.multiple_of(p.c * self.k, 8), self.k)]

        if shard is not None:
            self.kept = copies.here(lambda: (shard.at[:, columns(p.c * self.half, self.half)], mine()))
            self.swapped = copies.remote(
                lambda: (shard.at[:, columns((1 - p.c) * self.half, self.half)], mine(), p.at(c=1 - p.c)))

    def exchange(self):
        self.kept.start()
        self.swapped.start()

    def convert(self):
        self.kept.wait()
        self.swapped.wait_recv()
        self.low[...] = self.both[...].astype(BF)

    def over_z(self, u, r):
        p = self.p
        rows = pl.ds(r * self.tall, self.tall)
        src = self.low.at[rows, pl.ds(u * self.wide, self.wide)]

        def dst():
            return self.full.at[u, p.c, p.z, p.x, p.y, rows]

        own = self.copies.here(lambda: (src, dst()))
        sent = [self.copies.remote(lambda s=s: (src, dst(), p.at(z=p.z_other(s)))) for s in range(1, p.zs)]

        def start():
            if u == 0 and r == 0:
                self.convert()
            for copy in [own] + sent:
                copy.start()

        def wait():
            own.wait()
            for copy in sent:
                copy.wait_recv()
            for copy in sent:
                copy.wait_send()
            if u == 0 and r == 0:
                self.swapped.wait_send()

        return [start, wait]

    def over_yx(self, u, r, x_first=False):
        p, full = self.p, self.full
        rows = pl.ds(r * self.tall, self.tall)
        one = lambda: full.at[u, p.c, :, p.x, p.y, rows]
        if x_first:
            first = self.twice(one, lambda: p.at(x=1 - p.x))
            second = self.twice(lambda: full.at[u, p.c, :, :, p.y, rows], lambda: p.at(y=1 - p.y))
        else:
            first = self.twice(one, lambda: p.at(y=1 - p.y))
            second = self.twice(lambda: full.at[u, p.c, :, p.x, :, rows], lambda: p.at(x=1 - p.x))
        third = self.twice(lambda: full.at[u, p.c, :, :, :, rows], lambda: p.at(c=1 - p.c))

        def next_(before, after):
            before.wait_recv()
            after.start()

        def finish():
            third.wait_recv()
            for copy in (first, second, third):
                copy.wait_send()

        return [first.start, functools.partial(next_, first, second), functools.partial(next_, second, third), finish]

    def unit(self, u, r, x_first=False):
        start, wait = self.over_z(u, r)
        after = self.over_yx(u, r, x_first)

        def second():
            wait()
            after[0]()

        return [start, second] + after[1:]

    def twice(self, part, device):
        return self.copies.remote(lambda: (part(), part(), device()))

    def units(self, kind=None, x_first=()):
        if kind is not None:
            return [kind(u, r) for u in range(self.panels) for r in range(self.pieces)]
        return [
            self.unit(u, r, u * self.pieces + r in x_first) for u in range(self.panels) for r in range(self.pieces)
        ]

    @staticmethod
    def scratch(shape):
        k, cols = shape
        return [pltpu.VMEM((2 * k, cols // 2), F32), pltpu.VMEM((2 * k, cols // 2), BF)]


class Spread:
    def __init__(self, place, copies, block, full):
        p = place

        def dst():
            return full.at[p.z, p.x, p.y, p.c]

        def twice(part, device):
            return copies.remote(lambda: (part(), part(), device()))

        self.own = copies.here(lambda: (block, dst()))
        self.over_z = [copies.remote(lambda s=s: (block, dst(), p.at(z=p.z_other(s)))) for s in range(1, p.zs)]
        self.over_y = twice(lambda: full.at[:, p.x, p.y, p.c], lambda: p.at(y=1 - p.y))
        self.over_x = twice(lambda: full.at[:, p.x, :, p.c], lambda: p.at(x=1 - p.x))
        self.over_c = twice(lambda: full.at[:, :, :, p.c], lambda: p.at(c=1 - p.c))

    def along_z(self):
        for copy in [self.own] + self.over_z:
            copy.start()

    def along_y(self):
        self.own.wait()
        for copy in self.over_z:
            copy.wait_recv()
        self.over_y.start()

    def along_x(self):
        self.over_y.wait_recv()
        self.over_x.start()

    def along_c(self):
        self.over_x.wait_recv()
        self.over_c.start()

    def finish(self):
        self.over_c.wait_recv()
        for copy in self.over_z + [self.over_y, self.over_x, self.over_c]:
            copy.wait_send()

    def units(self):
        return [[self.along_z, self.along_y, self.along_x, self.along_c, self.finish]]


class Move:
    def __init__(self, place, copies, src, dst, to_images):
        p = place
        n = (src if to_images else dst).shape[0] // 4

        def part(row):
            if to_images:
                return src.at[pl.ds(row * n, n)], dst.at[:, p.row]
            return src.at[:, row], dst.at[pl.ds(p.row * n, n)]

        self.own = copies.here(lambda: part(p.row))
        self.sent = [
            copies.remote(lambda s=s: part(p.row_other(s)) + ((p.img, p.row_other(s)),)) for s in (2, 3, 1)
        ]

    def start(self):
        for copy in self.sent + [self.own]:
            copy.start()

    def finish(self):
        self.own.wait()
        for copy in self.sent:
            copy.wait_recv()
        for copy in self.sent:
            copy.wait_send()


class Scatter:
    def __init__(self, place, copies, grad, shard, scratch, pieces):
        self.p, self.copies, self.grad, self.shard = place, copies, grad, shard
        self.own, self.from_c, self.from_x, self.from_y, self.from_z, self.summed = scratch[:6]
        self.stage = scratch[6] if grad is None else None
        self.k, self.cols = shard.shape
        self.half = self.cols // 2
        self.pieces = pieces
        self.panels = self.own.shape[0] // pieces
        self.wide, self.tall = self.own.shape[-1], self.own.shape[-2]
        p = place

        def cols():
            return columns(p.c * self.half, self.half)

        def rows(c):
            return pl.ds(pl.multiple_of(c * self.k, 8), self.k)

        self.last = copies.remote(
            lambda: (self.summed.at[rows(1 - p.c)], shard.at[:, cols()], p.at(c=1 - p.c)))
        self.kept = copies.here(lambda: (self.summed.at[rows(p.c)], shard.at[:, cols()]))

    def unit(self, u, r):
        p, copies, grad = self.p, self.copies, self.grad
        at = u * self.pieces + r
        own, from_c, from_x = self.own.at[at], self.from_c.at[at], self.from_x.at[at]
        from_y, from_z = self.from_y.at[at], self.from_z.at[at]
        rows = pl.ds(r * self.tall, self.tall)
        if grad is None:
            over_c = copies.remote(lambda: (self.stage.at[at], from_c, p.at(c=1 - p.c)))
            loaded = None
        else:
            over_c = copies.remote(lambda: (grad.at[u, 1 - p.c, :, :, :, rows], from_c, p.at(c=1 - p.c)))
            loaded = copies.here(lambda: (grad.at[u, p.c, :, :, :, rows], own))
        over_x = copies.remote(lambda: (own.at[:, 1 - p.x], from_x, p.at(x=1 - p.x)))
        over_y = copies.remote(lambda: (own.at[:, p.x, 1 - p.y], from_y, p.at(y=1 - p.y)))
        over_z = [
            copies.remote(lambda s=s: (own.at[p.z_other(s), p.x, p.y], from_z.at[s - 1], p.at(z=p.z_other(s))))
            for s in range(1, p.zs)
        ]

        def add(into, other):
            into[...] = (into[...].astype(F32) + other[...].astype(F32)).astype(BF)

        def along_c():
            over_c.start()
            if loaded is not None:
                loaded.start()

        def along_x():
            if loaded is not None:
                loaded.wait()
            over_c.wait_recv()
            for z in range(p.zs):
                add(own.at[z, 1 - p.x], from_c.at[z, 1 - p.x])
            over_x.start()
            for z in range(p.zs):
                add(own.at[z, p.x], from_c.at[z, p.x])

        def along_y():
            over_x.wait_recv()
            for z in range(p.zs):
                add(own.at[z, p.x, 1 - p.y], from_x.at[z, 1 - p.y])
            over_y.start()
            for z in range(p.zs):
                add(own.at[z, p.x, p.y], from_x.at[z, p.y])

        def along_z():
            over_y.wait_recv()
            for z in range(p.zs):
                add(own.at[z, p.x, p.y], from_y.at[z])
            for copy in over_z:
                copy.start()

        def finish():
            for copy in over_z:
                copy.wait_recv()
            total = own[p.z, p.x, p.y].astype(F32)
            for s in range(p.zs - 1):
                total += from_z[s].astype(F32)
            self.summed[rows, pl.ds(u * self.wide, self.wide)] = total
            for copy in [over_c, over_x, over_y] + over_z:
                copy.wait_send()
            if at == self.panels * self.pieces - 1:
                self.last.start()
                self.kept.start()

        return [along_c, along_x, along_y, along_z, finish]

    def end(self):
        self.kept.wait()
        self.last.wait_recv()
        self.last.wait_send()

    def units(self):
        return [self.unit(u, r) for u in range(self.panels) for r in range(self.pieces)]

    @staticmethod
    def scratch(zs, k, cols, panels, pieces, staged=False):
        n, tall, w = panels * pieces, 2 * k // pieces, cols // 2 // panels
        shapes = [(n, zs, 2, 2, tall, w), (n, zs, 2, 2, tall, w), (n, zs, 2, tall, w), (n, zs, tall, w),
                  (n, zs - 1, tall, w)]
        return [pltpu.VMEM(s, BF) for s in shapes] + [pltpu.VMEM((2 * k, cols // 2), F32)] + (
            [pltpu.VMEM(shapes[0], BF)] if staged else [])

    @staticmethod
    def remotes(zs, panels, pieces):
        return 1 + panels * pieces * (zs + 2)


class Total:
    def __init__(self, place, copies, grad, result, got, work, from_z):
        self.p, self.grad, self.got, self.work, self.from_z = place, grad, got, work, from_z
        p = place
        self.kept = copies.here(lambda: (grad.at[p.c], work))
        self.over_c = copies.remote(lambda: (grad.at[1 - p.c], got.at[0], p.at(c=1 - p.c)))
        self.over_x = copies.remote(lambda: (work, got.at[1], p.at(x=1 - p.x)))
        self.over_y = copies.remote(lambda: (work, got.at[2], p.at(y=1 - p.y)))
        self.over_z = [
            copies.remote(lambda s=s: (from_z.at[p.z], from_z.at[p.z], p.at(z=p.z_other(s)))) for s in range(1, p.zs)
        ]
        self.last = [
            copies.remote(lambda: (work, result.at[p.c], p.at(c=1 - p.c))),
            copies.here(lambda: (work, result.at[p.c])),
        ]

    def along_c(self):
        self.kept.start()
        self.over_c.start()

    def along_x(self):
        self.kept.wait()
        self.over_c.wait_recv()
        self.work[...] = self.work[...] + self.got[0]
        self.over_x.start()

    def along_y(self):
        self.over_x.wait_recv()
        self.over_x.wait_send()
        self.work[...] = self.work[...] + self.got[1]
        self.over_y.start()

    def along_z(self):
        self.over_y.wait_recv()
        self.over_y.wait_send()
        self.from_z[self.p.z] = self.work[...] + self.got[2]
        for copy in self.over_z:
            copy.start()

    def finish(self):
        for copy in self.over_z:
            copy.wait_recv()
        for copy in [self.over_c] + self.over_z:
            copy.wait_send()
        total = self.from_z[0]
        for z in range(1, self.p.zs):
            total += self.from_z[z]
        self.work[...] = total
        for copy in self.last:
            copy.start()

    def end(self):
        self.last[1].wait()
        self.last[0].wait_recv()
        self.last[0].wait_send()

    def units(self):
        return [[self.along_c, self.along_x, self.along_y, self.along_z, self.finish]]

    @staticmethod
    def scratch(zs, rows, wide):
        return [pltpu.VMEM((3, rows, wide), F32), pltpu.VMEM((rows, wide), F32), pltpu.VMEM((zs, rows, wide), F32)]

    @staticmethod
    def remotes(zs):
        return zs + 3


def semaphores(remotes, locals_):
    return [
        pltpu.SemaphoreType.DMA((remotes,)),
        pltpu.SemaphoreType.DMA((remotes,)),
        pltpu.SemaphoreType.DMA((locals_,)),
    ]


def split_refs(refs, *sizes):
    parts, at = [], 0
    for size in sizes:
        parts.append(refs[at:at + size])
        at += size
    return parts + [refs[at:]]


def full_shape(img_size, shard, panels):
    k, cols = shard.shape
    return (panels, 2, img_size // 2, 2, 2, 2 * k, cols // 2 // panels)


def table_rows(table, side, blocks, wide):
    span = 2 * side - 1
    square = table.reshape(H, span, span)
    square = jnp.concatenate([square] + [square[:, -1:]] * (blocks - span), 1)
    rows = []
    for turned in (square, square[:, ::-1, ::-1]):
        for part, pads in ((turned[:, :, :side], (0, 1)), (turned[:, :, side:], (1, 0))):
            part = jnp.pad(part, ((0, 0), pads, (0, side - part.shape[2])))
            flat = part.reshape(H, 1, (blocks + 1) * side)
            rows.append(jnp.roll(jnp.pad(flat, ((0, 0), (0, 0), (0, wide - flat.shape[2]))), 1 - side, 2))
    return jnp.concatenate(rows + [jnp.zeros((H, 4, wide), F32)], 1)


def table_sums(rows, side, blocks):
    span = 2 * side - 1
    rows = jnp.roll(rows, side - -(-side // 8) * 8, 2)
    parts = rows[:, :, :(blocks + 1) * side].reshape(H, 2, blocks + 1, side)
    square = jnp.concatenate([parts[:, 0, :blocks], parts[:, 1, 1:, :side - 1]], 2)
    square = jnp.concatenate([square[:, :span - 1], jnp.sum(square[:, span - 1:], 1, keepdims=True)], 1)
    return square.reshape(H, span * span)


def lower_offsets(side, rows, wide):
    lane = lax.rem(lax.broadcasted_iota(jnp.int32, (rows, wide), 1), side)
    return lane <= lax.broadcasted_iota(jnp.int32, (rows, wide), 0)


def spread_rows(rows_ref, h, first, side, rows, wide, lower):
    low = jnp.broadcast_to(rows_ref[h, first:first + 1, :], (rows, wide))
    high = jnp.broadcast_to(rows_ref[h, first + 1:first + 2, :], (rows, wide))
    return jnp.where(
        lower, pltpu.roll(low, 0, 1, stride=1, stride_axis=0), pltpu.roll(high, 0, 1, stride=1, stride_axis=0)
    )


def fill_bias(bias, h, spread, side, rows, first_offset):
    size = bias.shape[2]
    wide = spread.shape[1]
    window = -(-size // 128) * 128 + 128
    for r in range(rows):
        offset = (first_offset - r) * side
        base, rest = offset // 128 * 128, offset % 128
        part = spread[:, base:min(base + window, wide)]
        if part.shape[1] < window:
            part = jnp.concatenate([part, jnp.zeros((spread.shape[0], window - part.shape[1]), F32)], 1)
        if rest:
            part = pltpu.roll(part, window - rest, 1)
        bias[h, r * side:(r + 1) * side, :] = part[:side, :size]


def fold_bias(total, h, acc, side, rows, first_offset, lower, out_ref, half, row):
    size = total.shape[2]
    window = -(-size // 128) * 128 + 128
    height, wide = lower.shape
    acc[...] = jnp.zeros_like(acc)
    for r in range(rows):
        offset = (first_offset - r) * side
        base, rest = offset // 128 * 128, offset % 128
        part = total[h, r * side:(r + 1) * side, :]
        part = jnp.concatenate([part, jnp.zeros((side, window - size), F32)], 1)
        if rest:
            part = pltpu.roll(part, rest, 1)
        acc[:side, base:base + window] += part
    whole = acc[:, :wide]
    zero = jnp.zeros_like(whole)
    for at, part in enumerate((jnp.where(lower, whole, zero), jnp.where(lower, zero, whole))):
        turned = jnp.concatenate([part[j:j + 1] for j in reversed(range(height))], 0)
        moved = pltpu.roll(turned, 0, 1, stride=1, stride_axis=0)
        out_ref[half, pl.ds(row + at, 1), :] = jnp.sum(moved, 0, keepdims=True)


def head_part(full, mask, h):
    keep = mask if h == 0 else jnp.logical_not(mask)
    return jnp.where(keep, full, jnp.zeros_like(full))


def attend_kernel(large, small, q_ref, k_ref, v_ref, rows_l, rows_s, o_ref, bias_l, bias_s):
    mask = lax.broadcasted_iota(jnp.int32, (1, 128), 1) < 64
    lower_l = lower_offsets(SIDE_L, SIDE_L, WIDE_L)
    lower_s = lower_offsets(SIDE_S, 16, WIDE_S)
    for h in range(2):
        fill_bias(bias_l, h, spread_rows(rows_l, h, 2, SIDE_L, SIDE_L, WIDE_L, lower_l), SIDE_L, 24, 23)
        fill_bias(bias_s, h, spread_rows(rows_s, h, 2, SIDE_S, 16, WIDE_S, lower_s), SIDE_S, 16, 15)
    keep = lax.broadcasted_iota(jnp.int32, (1, LEN_S), 1) < SIDE_S * SIDE_S
    images = [(n * LEN_L, LEN_L, bias_l) for n in range(large)]
    images += [(large * LEN_L + n * LEN_S, LEN_S, bias_s) for n in range(small)]
    for at, size, bias in images:
        q, k, v = (ref[at:at + size, :] for ref in (q_ref, k_ref, v_ref))
        outs = []
        for h in range(2):
            s = dot(head_part(q, mask, h) * BF(0.125), k, NT) + bias[h]
            if size == LEN_S:
                s = jnp.where(keep, s, -1e30)
            e = jnp.exp(s - jnp.max(s, 1, keepdims=True))
            p = (e * (1.0 / jnp.sum(e, 1, keepdims=True))).astype(BF)
            outs.append(dot(p, v, NN))
        o_ref[at:at + size, :] = jnp.where(mask, outs[0], outs[1]).astype(BF)


def loop_points(steps, every):
    return {t * every: step for t, step in enumerate(steps)}


def run_point(points, iteration, at, per, iterations):
    for i in range(iterations):
        step = points.get(i * per + at)
        if step is not None:
            pl.when(iteration == i)(step)


def run_rest(points, count):
    for at in sorted(points):
        if at >= count:
            points[at]()


def attend_back_pair(hp, qkv, do_ref, rows_l, rows_s, df, sums_l, sums_s, scratch, large, small, between):
    bias_l, bias_s, total_l, total_s, acc_l, acc_s = scratch
    mask = lax.broadcasted_iota(jnp.int32, (1, 128), 1) < 64
    lower_l = lower_offsets(SIDE_L, SIDE_L, WIDE_L)
    lower_s = lower_offsets(SIDE_S, 16, WIDE_S)
    for h in range(2):
        fill_bias(bias_l, h, spread_rows(rows_l, 2 * hp + h, 0, SIDE_L, SIDE_L, WIDE_L, lower_l), SIDE_L, 24, 23)
        fill_bias(bias_s, h, spread_rows(rows_s, 2 * hp + h, 0, SIDE_S, 16, WIDE_S, lower_s), SIDE_S, 14, 13)
    keep = lax.broadcasted_iota(jnp.int32, (LEN_S, 1), 0) < SIDE_S * SIDE_S
    images = [(n * LEN_L, LEN_L, bias_l, total_l, n == 0) for n in range(large)]
    images += [(large * LEN_L + n * LEN_S, LEN_S, bias_s, total_s, n == 0) for n in range(small)]
    cols = [columns(i * 64 * H + hp * 128, 128) for i in range(3)]
    for index, (at, size, bias, total, first) in enumerate(images):
        between(index)
        rows = slice(at, at + size)
        q, k, v = (qkv[rows, c] for c in cols)
        do = do_ref[rows, cols[0]]
        got = []
        for h in range(2):
            s = dot(head_part(k, mask, h) * BF(0.125), q, NT) + bias[h]
            if size == LEN_S:
                s = jnp.where(keep, s, -1e30)
            e = jnp.exp(s - jnp.max(s, 0, keepdims=True))
            p = e * (1.0 / jnp.sum(e, 0, keepdims=True))
            dp = dot(head_part(v, mask, h), do, NT).astype(BF).astype(F32)
            pd = p * dp
            low = (pd - p * jnp.sum(pd, 0, keepdims=True)).astype(BF)
            got.append((dot(low, k, TN), dot(low, q, NN), dot(p.astype(BF), do, NN)))
            total[h] = low.astype(F32) if first else total[h] + low.astype(F32)
        for c, a, b, scale in zip(cols, got[0], got[1], (0.125, 0.125, 1.0)):
            df[rows, c] = (jnp.where(mask, a, b) * scale).astype(BF)
    half, within = hp // 3, lax.rem(hp, 3)
    for h in range(2):
        fold_bias(total_l, h, acc_l, SIDE_L, 24, 23, lower_l, sums_l, half, 4 * within + 2 * h)
        fold_bias(total_s, h, acc_s, SIDE_S, 14, 13, lower_s, sums_s, half, 4 * within + 2 * h)


def back_scratch():
    return [pltpu.VMEM((2, LEN_L, LEN_L), F32), pltpu.VMEM((2, LEN_S, LEN_S), F32)] * 2 + [
        pltpu.VMEM((SIDE_L, WIDE_L + 128), F32), pltpu.VMEM((16, WIDE_S + 128), F32)]


VMEM = pl.BlockSpec(memory_space=pltpu.VMEM)


def attention_back(img_size, qkv, d_att, rows_l, rows_s, grads, cuts, wholes, large, small, every):
    zs = img_size // 2
    ng, nw = len(grads), len(wholes)
    rows = qkv.shape[0]
    shard_shapes = [(g.shape[5] // 2, g.shape[0] * 2 * g.shape[6]) for g in grads]

    def kernel(*refs):
        ins, gr, wh, outs, shards, blocks, scr = split_refs(refs, 4, ng, nw, 3, ng, nw)
        qkv_hbm, do_hbm, rl, rs = ins
        df_hbm, sums_l, sums_s = outs
        qkv_v, do_v, df_v = scr[:3]
        p = Place(img_size)
        copies = Copies(*scr[-3:])
        loads = [copies.here(lambda: (qkv_hbm, qkv_v)), copies.here(lambda: (do_hbm, do_v))]
        for copy in loads:
            copy.start()
        if ng + nw:
            greet(p.partners())
        at = 3 + 6
        scatters = []
        for i in range(ng):
            scatters.append(Scatter(p, copies, gr[i], shards[i], scr[at:at + 6], cuts[i]))
            at += 6
        moves = [Move(p, copies, a, b, False) for a, b in zip(wh, blocks)]
        units = [u for s in scatters for u in s.units()]
        points = loop_points(pipelined(units) if units else [], every)
        for m in moves:
            m.start()
        sums_l[...] = jnp.zeros_like(sums_l)
        sums_s[...] = jnp.zeros_like(sums_s)
        for copy in loads:
            copy.wait()

        def body(hp, carry):
            attend_back_pair(hp, qkv_v, do_v, rl, rs, df_v, sums_l, sums_s, scr[3:9], large, small,
                             lambda index: run_point(points, hp, index, large + small, H // 2))
            return carry

        lax.fori_loop(0, H // 2, body, 0)
        out = copies.here(lambda: (df_v, df_hbm))
        out.start()
        run_rest(points, (large + small) * (H // 2))
        for s in scatters:
            s.end()
        for m in moves:
            m.finish()
        out.wait()

    scratch = [pltpu.VMEM(qkv.shape, BF), pltpu.VMEM(d_att.shape, BF), pltpu.VMEM(qkv.shape, BF)] + back_scratch()
    for g, (k, cols), cut in zip(grads, shard_shapes, cuts):
        scratch += Scatter.scratch(zs, k, cols, g.shape[0], cut)
    remotes = 3 * nw + sum(Scatter.remotes(zs, g.shape[0], c) for g, c in zip(grads, cuts))
    locals_ = 3 + nw + sum(1 + g.shape[0] * c for g, c in zip(grads, cuts))
    remote = dict(collective_id=1, has_side_effects=True) if ng + nw else {}
    return pl.pallas_call(
        kernel,
        out_shape=[jax.ShapeDtypeStruct(qkv.shape, BF), jax.ShapeDtypeStruct((2, 16, WIDE_L), F32),
                   jax.ShapeDtypeStruct((2, 16, WIDE_S), F32)]
        + [jax.ShapeDtypeStruct(s, F32) for s in shard_shapes]
        + [jax.ShapeDtypeStruct((w.shape[0] * 4,) + w.shape[2:], w.dtype) for w in wholes],
        in_specs=[ANY, ANY, VMEM, VMEM] + [ANY] * (ng + nw),
        out_specs=[ANY, VMEM, VMEM] + [ANY] * (ng + nw),
        scratch_shapes=scratch + semaphores(max(remotes, 1), locals_),
        compiler_params=pltpu.CompilerParams(vmem_limit_bytes=60 * MIB, **remote),
        name="attention_back",
    )(qkv, d_att, rows_l, rows_s, *grads, *wholes)


def row_tiles(rows, tile, body):
    count = rows // tile

    def step(t, carry):
        body(pl.multiple_of(t * tile, 16), tile)
        return carry

    lax.fori_loop(0, count, step, 0)
    if rows % tile:
        body(count * tile, rows % tile)


def norm_parts(x):
    centered = x - jnp.mean(x, 1, keepdims=True)
    scale = lax.rsqrt(jnp.mean(centered * centered, 1, keepdims=True) + 1e-06)
    return centered * scale, scale


def norm_back(dn, hat, scale, gain):
    d_hat = dn * gain
    return scale * (d_hat - jnp.mean(d_hat, 1, keepdims=True) - hat * jnp.mean(d_hat * hat, 1, keepdims=True))


def fold8(values):
    return sum(values[i:i + 8] for i in range(0, values.shape[0], 8))


def place_small(ref, flat, at):
    for i in range(4):
        ref[at, i] = flat[i * 56:(i + 1) * 56].astype(ref.dtype)


def load_tokens(copies, large_hbm, small_hbm, flat, four):
    n, _, rows, _ = large_hbm.shape
    loads = [
        copies.here(lambda i=i, j=j: (large_hbm.at[i, j], flat.at[pl.ds((i * 4 + j) * rows, rows)]))
        for i in range(n) for j in range(4)
    ]
    return loads + [copies.here(lambda: (small_hbm, four))]


def join_small(flat, four, large):
    for n in range(four.shape[0]):
        rows = jnp.concatenate([four[n, i].astype(F32) for i in range(4)], 0)
        at = large * LEN_L + n * LEN_S
        flat[at:at + LEN_S, :] = rows.astype(flat.dtype)


def projection_back(img_size, df, dm, n1, x_l, x_s, w_qkv, vectors, sums, tables, large, small):
    zs = img_size // 2
    rows, width = dm.shape
    panels, _, _, _, _, k2, wide = w_qkv.shape
    k, cols = k2 // 2, panels * 2 * wide
    nt = len(tables)

    def kernel(*refs):
        ins, tabs, outs, tab_outs, scr = split_refs(refs, 8, nt, 4, nt)
        df_hbm, dm_hbm, n1_hbm, xl_hbm, xs_hbm, w_hbm, vec, sums_in = ins
        gl_out, gs_out, shard, sums_out = outs
        df_v, dm_v, flat, four, w_v, n1_v, nt_v, dn, acc, own_sums, dl, ds, grad = scr[:13]
        at = 13
        p = Place(img_size)
        copies = Copies(*scr[-3:])
        first = [copies.here(lambda: (n1_hbm, n1_v)), copies.here(lambda: (df_hbm, df_v))]
        w_load = copies.here(lambda: (w_hbm, w_v))
        later = load_tokens(copies, xl_hbm, xs_hbm, flat, four) + [copies.here(lambda: (dm_hbm, dm_v))]
        for copy in first + [w_load] + later:
            copy.start()
        greet(p.partners())
        scatter = Scatter(p, copies, None, shard, scr[at:at + 7], 1)
        at += 7
        totals = []
        for a, b in zip(tabs, tab_outs):
            totals.append(Total(p, copies, a, b, *scr[at:at + 3]))
            at += 3
        last = Total(p, copies, own_sums, sums_out, *scr[at:at + 3])
        moves = [Move(p, copies, dl, gl_out, False), Move(p, copies, ds, gs_out, False)]
        units = scatter.units()
        first[0].wait()
        nt_v[...] = n1_v[...].T
        first[1].wait()

        def pair(ref, u):
            return jnp.concatenate(
                [ref[:, c * (cols // 2) + u * wide:c * (cols // 2) + (u + 1) * wide] for c in range(2)], 1)

        def gradient(u):
            grad[...] = dot(nt_v[...], pair(df_v, u), NN).astype(BF)
            for to, c in ((scatter.stage, 1 - p.c), (scatter.own, p.c)):
                to[u] = grad[:, columns(c * wide, wide)].reshape(zs, 2, 2, k2, wide)
            units[u][0]()

        def all_totals(phase):
            for t in totals:
                phase(t)

        gradient(0)
        all_totals(Total.along_c)
        w_load.wait()
        for u in range(panels):
            w = jnp.concatenate([w_v[u, c].reshape(width, wide) for c in range(2)], 1)
            got = dot(pair(df_v, u), w, NT)
            dn[...] = got if u == 0 else dn[...] + got
            if u == 0:
                units[0][1]()
                all_totals(Total.along_x)
        for copy in later:
            copy.wait()
        join_small(flat, four, large)
        acc[...] = jnp.zeros_like(acc)
        gain = vec[0:1, :]
        units[0][2]()

        def back(start, size):
            at_rows = pl.ds(start, size)
            hat, scale = norm_parts(flat[at_rows, :].astype(F32))
            d = dn[at_rows, :]
            acc[0] += fold8(d * hat)
            acc[1] += fold8(d)
            acc[2] += fold8(df_v[at_rows, :width].astype(F32))
            acc[3] += fold8(df_v[at_rows, 2 * width:].astype(F32))
            flat[at_rows, :] = (dm_v[at_rows, :] + norm_back(d, hat, scale, gain)).astype(BF)

        row_tiles(rows, 96, back)
        for i in range(large):
            for j in range(4):
                start = (i * 4 + j) * (LEN_L // 4)
                dl[i, j] = flat[start:start + LEN_L // 4, :]
        for n in range(small):
            start = large * LEN_L + n * LEN_S
            place_small(ds, flat[start:start + LEN_S, :].astype(F32), n)
        for m in moves:
            m.start()
        for i, row in ((0, 0), (1, 4), (2, 6), (3, 7)):
            own_sums[0, row:row + 1, :] = jnp.sum(acc[i], 0, keepdims=True)
        for row in (1, 2, 3, 5):
            own_sums[0, row:row + 1, :] = sums_in[0, row:row + 1, :]
        own_sums[1] = sums_in[1]
        last.along_c()
        for u in range(1, panels):
            gradient(u)
        all_totals(Total.along_y)
        units[1][1]()
        units[2][1]()
        units[0][3]()
        last.along_x()
        all_totals(Total.along_z)
        units[1][2]()
        last.along_y()
        units[0][4]()
        units[2][2]()
        units[1][3]()
        last.along_z()
        all_totals(Total.finish)
        units[2][3]()
        units[1][4]()
        last.finish()
        units[2][4]()
        scatter.end()
        for t in totals + [last]:
            t.end()
        for m in moves:
            m.finish()

    flat = pltpu.VMEM((rows, width), BF)
    scratch = [
        pltpu.VMEM(df.shape, BF), pltpu.VMEM(dm.shape, F32), flat, pltpu.VMEM(x_s.shape, BF),
        pltpu.VMEM(w_qkv.shape, BF), flat, pltpu.VMEM((width, rows), BF), pltpu.VMEM((rows, width), F32),
        pltpu.VMEM((4, 8, width), F32), pltpu.VMEM((2, 8, width), F32),
        pltpu.VMEM(x_l.shape, BF), pltpu.VMEM(x_s.shape, BF), pltpu.VMEM((width, 2 * wide), BF),
    ] + Scatter.scratch(zs, k, cols, panels, 1, True)
    for t in list(tables) + [sums]:
        scratch += Total.scratch(zs, t.shape[1], t.shape[2])
    remotes = 6 + Scatter.remotes(zs, panels, 1) + Total.remotes(zs) * (nt + 1)
    locals_ = 4 * x_l.shape[0] + 1 + 4 + 2 + 1 + 2 * (nt + 1)
    f32 = lambda s: jax.ShapeDtypeStruct(s, F32)
    return pl.pallas_call(
        kernel,
        out_shape=[jax.ShapeDtypeStruct((4 * a.shape[0],) + a.shape[2:], BF) for a in (x_l, x_s)]
        + [f32((k, cols)), f32(sums.shape)] + [f32(t.shape) for t in tables],
        in_specs=[ANY] * 6 + [VMEM, VMEM] + [ANY] * nt,
        out_specs=[ANY] * (4 + nt),
        scratch_shapes=scratch + semaphores(remotes, locals_),
        compiler_params=pltpu.CompilerParams(collective_id=2, has_side_effects=True, vmem_limit_bytes=60 * MIB),
        name="projection_back",
    )(df, dm, n1, x_l, x_s, w_qkv, vectors, sums, *tables)


def attend_pair(hp, qkv, bias_l, bias_s, out, large, small, between):
    mask = lax.broadcasted_iota(jnp.int32, (1, 128), 1) < 64
    keep = lax.broadcasted_iota(jnp.int32, (1, LEN_S), 1) < SIDE_S * SIDE_S
    images = [(n * LEN_L, LEN_L, bias_l) for n in range(large)]
    images += [(large * LEN_L + n * LEN_S, LEN_S, bias_s) for n in range(small)]
    cols = [columns(i * 64 * H + hp * 128, 128) for i in range(3)]
    between(0)
    for at, size, bias in images:
        rows = slice(at, at + size)
        q, k, v = (qkv[rows, c] for c in cols)
        outs = []
        for h in range(2):
            s = dot(head_part(q, mask, h) * BF(0.125), k, NT) + bias[2 * hp + h]
            if size == LEN_S:
                s = jnp.where(keep, s, -1e30)
            e = jnp.exp(s - jnp.max(s, 1, keepdims=True))
            outs.append(dot(e.astype(BF), v, NN) * (1.0 / jnp.sum(e, 1, keepdims=True)))
        out[rows, cols[0]] = jnp.where(mask, outs[0], outs[1]).astype(BF)


def fill_heads(start, stop, rows_l, rows_s, bias_l, bias_s):
    lower_l = lower_offsets(SIDE_L, SIDE_L, WIDE_L)
    lower_s = lower_offsets(SIDE_S, 16, WIDE_S)

    def body(h, carry):
        fill_bias(bias_l, h, spread_rows(rows_l, h, 2, SIDE_L, SIDE_L, WIDE_L, lower_l), SIDE_L, 24, 23)
        fill_bias(bias_s, h, spread_rows(rows_s, h, 2, SIDE_S, 16, WIDE_S, lower_s), SIDE_S, 16, 15)
        return carry

    lax.fori_loop(start, stop, body, 0)


def assemble(blocks, count, vectors, up_vec):
    row = lax.broadcasted_iota(jnp.int32, (16, 128), 0)
    vectors[...] = jnp.zeros_like(vectors)
    up_vec[...] = jnp.zeros_like(up_vec)
    width = vectors.shape[1] - 128
    own, own_up = width // count, 4 * width // count

    def shifted(part, offset):
        part = jnp.concatenate([part, jnp.zeros_like(part)], 1)
        return pltpu.roll(part, offset % 128, 1) if offset % 128 else part

    for d in range(count):
        block = blocks[d].astype(BF).astype(F32)
        offset = d * own
        base = offset // 128 * 128
        vectors[:, base:base + 256] += shifted(jnp.where(row < 10, block, 0.0), offset)
        at, offset = d * own_up // width, d * own_up % width
        base = offset // 128 * 128
        up_vec[at:at + 1, base:base + 256] += shifted(block[10:11], offset)


def front(img_size, arrays, block, shards, cuts, firsts, rows_l, rows_s):
    na, nw = len(arrays), len(shards)
    zs = img_size // 2
    large, small = arrays[0].shape[0] // 4, arrays[1].shape[0] // 4
    width = arrays[0].shape[2]
    rows = large * LEN_L + small * LEN_S
    count = 4 * img_size
    whole_shapes = [(a.shape[0] // 4, 4) + a.shape[1:] for a in arrays]
    full_shapes = [full_shape(img_size, s, c[0]) for s, c in zip(shards, cuts)]
    panels, wide = cuts[0][0], full_shapes[0][-1]

    def kernel(*refs):
        ins, blk, sh, tabs, whole, full, outs, scr = split_refs(refs, na, 1, nw, 2, na, nw, 5)
        qkv_hbm, n1_hbm, att, vec_out, up_out = outs
        flat, four, w_v, qkv, bias_l, bias_s, small_v, vectors, up_vec = scr[:9]
        gather_scr = scr[9:9 + 2 * nw]
        p = Place(img_size)
        greet(p.partners())
        copies = Copies(*scr[-3:])
        gathers = [
            Gather(p, copies, sh[i], full[i], gather_scr[2 * i], gather_scr[2 * i + 1], cuts[i][1]) for i in range(nw)
        ]
        moves = [Move(p, copies, a, b, True) for a, b in zip(ins, whole)]
        gathers[0].exchange()
        first = Spread(p, copies, blk[0], small_v).units() + gathers[0].units()
        rest = []
        for g, x_first in zip(gathers[1:-1], firsts):
            rest += g.units(None, x_first)
        last = gathers[-1].units(gathers[-1].over_z)
        steps = pipelined(rest + last)
        fill = functools.partial(fill_heads, rows_l=tabs[0], rows_s=tabs[1], bias_l=bias_l, bias_s=bias_s)
        for unit in first:
            unit[0]()
        for g in gathers[1:]:
            g.exchange()
        fill(0, 4)
        for unit in first:
            unit[1]()
        for m in moves:
            m.start()
        steps[0]()
        fill(4, 8)
        for unit in first:
            unit[2]()
        steps[1]()
        fill(8, 12)
        done = 2
        for unit in first:
            unit[3]()
            steps[done]()
            done += 1
        first[0][4]()
        assemble(small_v.reshape(count, 16, 128), count, vectors, up_vec)
        vec_out[...] = vectors[:, :width]
        up_out[...] = up_vec[:4, :width]
        for m in moves:
            m.finish()
        loads = load_tokens(copies, whole[0], whole[1], flat, four)
        for copy in loads:
            copy.start()
        for copy in loads:
            copy.wait()
        join_small(flat, four, large)
        gain, shift = vectors[0:1, :width], vectors[4:5, :width]

        def normed(start, size):
            at = pl.ds(start, size)
            hat, _ = norm_parts(flat[at, :].astype(F32))
            flat[at, :] = (hat * gain + shift).astype(BF)

        row_tiles(rows, 96, normed)
        for unit in first[1:]:
            unit[4]()
        w_loads = [copies.here(lambda u=u: (full[0].at[u], w_v.at[u])) for u in range(panels)]
        for copy in w_loads:
            copy.start()
        for u in range(panels):
            w_loads[u].wait()
            w = jnp.concatenate([w_v[u, c].reshape(width, wide) for c in range(2)], 1)
            got = dot(flat[...], w, NN)
            for c in range(2):
                at = (c * panels + u) * wide
                part = got[:, c * wide:(c + 1) * wide]
                if at + wide <= width:
                    part += vectors[6:7, at:at + wide]
                elif at >= 2 * width:
                    part += vectors[7:8, at - 2 * width:at - 2 * width + wide]
                qkv[:, at:at + wide] = part.astype(BF)
        out = [copies.here(lambda: (qkv, qkv_hbm)), copies.here(lambda: (flat, n1_hbm))]
        for copy in out:
            copy.start()
        points = loop_points(steps[done:], 1)

        def body(hp, carry):
            attend_pair(hp, qkv, bias_l, bias_s, att, large, small,
                        lambda index: run_point(points, hp, index, 1, H // 2))
            return carry

        lax.fori_loop(0, H // 2, body, 0)
        run_rest(points, H // 2)
        for copy in out:
            copy.wait()

    units = 1 + sum(a * b for a, b in cuts)
    vm = pltpu.VMEM
    return pl.pallas_call(
        kernel,
        out_shape=[jax.ShapeDtypeStruct(s, BF) for s in whole_shapes + full_shapes + [(rows, 3 * width), (rows, width), (rows, width)]]
        + [jax.ShapeDtypeStruct((16, width), F32), jax.ShapeDtypeStruct((4, width), F32)],
        in_specs=[ANY] * (na + 1 + nw) + [VMEM, VMEM],
        out_specs=[ANY] * (na + nw + 2) + [VMEM] * 3,
        scratch_shapes=[
            vm((rows, width), BF), vm(whole_shapes[1], BF), vm(full_shapes[0], BF), vm((rows, 3 * width), BF),
            vm((H, LEN_L, LEN_L), F32), vm((H, LEN_S, LEN_S), F32), vm((zs, 2, 2, 2, 16, 128), F32),
            vm((16, width + 128), F32), vm((8, width + 128), F32),
        ] + [s for w in shards for s in Gather.scratch(w.shape)]
        + semaphores(3 * na + (zs + 2) * units + nw, na + nw + units + 4 * large + 1 + panels + 2),
        compiler_params=pltpu.CompilerParams(collective_id=0, has_side_effects=True, vmem_limit_bytes=56 * MIB),
        name="front",
    )(*arrays, block, *shards, rows_l, rows_s)


def gelu_parts(u):
    bell = jnp.exp(-0.5 * (u * u))
    t = 1.0 / (1.0 + 0.2316418882663604 * jnp.abs(u))
    series = ((((1.061405429 * t - 1.453152027) * t + 1.421413741) * t - 0.284496736) * t + 0.254829592) * t
    tail = 0.5 * series * bell
    cdf = jnp.where(u >= 0.0, 1.0 - tail, tail)
    return u * cdf, cdf + 0.3989422804014327 * (u * bell)


def joined(w, *at):
    parts = [w[(at[0], c) + at[1:]] for c in range(2)]
    return jnp.concatenate([part.reshape(-1, part.shape[-1]) for part in parts], 1)


def image_rows(large, small):
    parts = [(n, j, (n * 4 + j) * (LEN_L // 4)) for n in range(large) for j in range(4)]
    return parts, [(n, large * LEN_L + n * LEN_S) for n in range(small)]


def forward_tail(img_size, att, x_l, x_s, ct_l, ct_s, w_out, w_up, w_down, cut, vectors, up_vec):
    large, small = x_l.shape[0], x_s.shape[0]
    rows, width = att.shape
    chunks = up_vec.shape[0]
    half = rows // 2
    direct = img_size is not None
    down_shape = w_down.shape
    bf = lambda *s: jax.ShapeDtypeStruct(s, BF)
    more = [bf(*down_shape), bf(*x_l.shape), bf(*x_s.shape)] if direct else []

    def kernel(att_hbm, xl_hbm, xs_hbm, cl_hbm, cs_hbm, wo_hbm, wu_hbm, wd_in, vec, upv, *refs):
        outs, extra, scr = split_refs(refs, 9, len(more))
        yl, ys, m_hbm, n2_hbm, e_hbm, g_hbm, dr_hbm, dy_hbm, sums = outs
        att_v, flat, four, ct_four, wo, wu, wd, m_v, n2_v, e_v, g_v, acc = scr[:12]
        copies = Copies(*scr[-3:])
        first = [copies.here(lambda: (att_hbm, att_v)), copies.here(lambda: (wo_hbm, wo))]
        first += load_tokens(copies, xl_hbm, xs_hbm, flat, four)
        second = copies.here(lambda: (wu_hbm, wu))
        for copy in first + [second]:
            copy.start()
        steps, moves = [], []
        wd_hbm, ct = wd_in, (cl_hbm, cs_hbm)
        if direct:
            p = Place(img_size)
            greet(p.partners())
            wd_hbm, ct = extra[0], extra[1:]
            gather = Gather(p, copies, None, wd_hbm, None, None, cut[1])
            moves = [Move(p, copies, a, b, True) for a, b in zip((cl_hbm, cs_hbm), ct)]
            units = gather.units(gather.over_yx)
            for unit in units:
                unit[0]()
            for m in moves:
                m.start()
            steps = [unit[f] for f in range(1, 4) for unit in units]
        for copy in first:
            copy.wait()
        join_small(flat, four, large)
        g2, s1, s2, b2, bo, bd = (vec[i:i + 1, :] for i in (1, 2, 3, 5, 8, 9))
        points = {t + 1: step for t, step in enumerate(steps[3:])}
        w = joined(wo, 0)
        for i in range(2):
            at = slice(i * half, (i + 1) * half)
            m_v[at, :] = dot(att_v[at, :], w, NN)
        for step in steps[:1]:
            step()

        def middle(start, size):
            at = pl.ds(start, size)
            m = flat[at, :].astype(F32) + s1 * (m_v[at, :] + bo)
            m_v[at, :] = m
            hat, _ = norm_parts(m)
            n2_v[at, :] = (hat * g2 + b2).astype(BF)

        row_tiles(rows, 96, middle)
        for step in steps[1:3]:
            step()
        m_out = [copies.here(lambda: (m_v, m_hbm)), copies.here(lambda: (n2_v, n2_hbm))]
        for copy in m_out:
            copy.start()
        second.wait()
        out_at = copies.locals
        copies.locals += chunks

        def out(f):
            return pltpu.make_async_copy(
                g_v.at[lax.rem(f, 2)], g_hbm.at[f], copies.local.at[out_at + f])

        def chunk(f, carry):
            run_point(points, f, 0, 1, chunks)

            @pl.when(f >= 2)
            def _():
                out(f - 2).wait()

            w1 = wu[lax.rem(f, 2), f // 2].reshape(width, width)
            for i in range(2):
                at = slice(i * half, (i + 1) * half)
                u = dot(n2_v[at, :], w1, NN) + upv[pl.ds(f, 1), :]
                e, g = gelu_parts(u)
                e_v[at, columns(f * width, width)] = e.astype(BF)
                g_v[lax.rem(f, 2), at, :] = g.astype(BF)
            out(f).start()
            return carry

        lax.fori_loop(0, chunks, chunk, 0)
        run_rest(points, chunks)
        e_out = copies.here(lambda: (e_v, e_hbm))
        e_out.start()
        third = copies.here(lambda: (wd_hbm, wd))
        third.start()
        for m in moves:
            m.finish()
        loads = load_tokens(copies, *ct, flat, ct_four)
        for copy in loads:
            copy.start()
        third.wait()
        for copy in m_out:
            copy.wait()
        for copy in loads:
            copy.wait()
        join_small(flat, ct_four, large)
        for n in range(small):
            at = large * LEN_L + n * LEN_S + SIDE_S * SIDE_S // 16 * 16
            keep = lax.broadcasted_iota(jnp.int32, (32, 1), 0) < SIDE_S * SIDE_S % 16
            flat[at:at + 32, :] = jnp.where(keep, flat[at:at + 32, :].astype(F32), 0.0).astype(BF)
        acc[...] = jnp.zeros_like(acc)
        w2 = joined(wd, 0)
        part = rows // 2
        for i in range(2):
            at = slice(i * part, (i + 1) * part)
            r = dot(e_v[at, :], w2, NN) + bd
            dy = flat[at, :].astype(F32)
            dr = (s2 * dy).astype(BF)
            acc[0] += fold8(r * dy)
            acc[1] += fold8(dr.astype(F32))
            m_v[at, :] = m_v[at, :] + s2 * r
            n2_v[at, :] = dr
        last = [copies.here(lambda: (n2_v, dr_hbm)), copies.here(lambda: (flat, dy_hbm))]
        for copy in last:
            copy.start()
        for n, j, start in image_rows(large, small)[0]:
            yl[n, j] = m_v[start:start + LEN_L // 4, :].astype(BF)
        for n, start in image_rows(large, small)[1]:
            place_small(ys, m_v[start:start + LEN_S, :], n)
        for i in range(2):
            sums[i:i + 1, :] = jnp.sum(acc[i], 0, keepdims=True)
        for f in (chunks - 2, chunks - 1):
            out(f).wait()
        for copy in last + [e_out]:
            copy.wait()

    vm = pltpu.VMEM
    flat = vm((rows, width), BF)
    scratch = [
        flat, flat, vm(x_s.shape, BF), vm(x_s.shape, BF), vm(w_out.shape, BF), vm(w_up.shape, BF),
        vm(down_shape, BF), vm((rows, width), F32), flat, vm((rows, chunks * width), BF),
        vm((2, rows, width), BF), vm((2, 8, width), F32),
    ]
    units = cut[0] * cut[1]
    scratch += semaphores(6 + 3 * units, 12 + 8 * large + 2 + chunks + units + 3)
    remote = dict(collective_id=3, has_side_effects=True) if direct else {}
    return pl.pallas_call(
        kernel,
        out_shape=[bf(*x_l.shape), bf(*x_s.shape), jax.ShapeDtypeStruct((rows, width), F32), bf(rows, width),
                   bf(rows, chunks * width), bf(chunks, rows, width), bf(rows, width), bf(rows, width),
                   jax.ShapeDtypeStruct((8, width), F32)] + more,
        in_specs=[ANY] * 8 + [VMEM, VMEM],
        out_specs=[VMEM, VMEM] + [ANY] * 6 + [VMEM] + [ANY] * len(more),
        scratch_shapes=scratch,
        input_output_aliases={7: 9} if direct else {},
        compiler_params=pltpu.CompilerParams(vmem_limit_bytes=60 * MIB, **remote),
        name="forward_tail",
    )(att, x_l, x_s, ct_l, ct_s, w_out, w_up, w_down, vectors, up_vec)


def backward_head(img_size, att, m, n2, e, g, dr, dy, w_out, w_up, w_down, cut, vectors, sums_in, wholes):
    rows, width = att.shape
    chunks = g.shape[0]
    half = rows // 2
    direct = img_size is not None
    zs = img_size // 2 if direct else 0
    nw = len(wholes)
    k2, wide = w_down.shape[5:]
    cols = w_down.shape[0] * 2 * wide
    tall = k2 // cut

    def kernel(*refs):
        ins, wh, outs, blocks, scr = split_refs(refs, 12, nw, 6, nw)
        att_hbm, m_hbm, n2_hbm, e_hbm, g_hbm, dr_hbm, dy_hbm, wo_hbm, wu_hbm, wd_hbm, vec, s_in = ins
        go, gu, gd, dm_hbm, da_hbm, sums = outs
        m_v, n2_v, nt_v, e_v, g_v, dr_v, wo, wu, wd, dn, du_v, gd_v, gu_v, go_v, acc, up_acc = scr[:16]
        copies = Copies(*scr[-3:])
        pairs = [(dr_hbm, dr_v), (n2_hbm, n2_v), (wd_hbm, wd), (wu_hbm, wu), (m_hbm, m_v), (wo_hbm, wo)]
        loads = [copies.here(lambda a=a, b=b: (a, b)) for a, b in pairs]
        at_e = copies.locals
        at_g = at_e + chunks
        at_gu = at_g + chunks
        copies.locals += 3 * chunks

        def fetch_e(f):
            return pltpu.make_async_copy(
                e_hbm.at[:, columns(f * width, width)], e_v.at[lax.rem(f, 2)], copies.local.at[at_e + f])

        def fetch_g(f):
            return pltpu.make_async_copy(g_hbm.at[f], g_v.at[lax.rem(f, 2)], copies.local.at[at_g + f])

        def put(f):
            return pltpu.make_async_copy(
                gu_v.at[lax.rem(f, 2)], gu.at[lax.rem(f, 2), f // 2], copies.local.at[at_gu + f])

        loads[0].start()
        fetch_e(0).start()
        fetch_e(1).start()
        for copy in loads[1:]:
            copy.start()
        fetch_g(0).start()
        moves, steps = [], []
        if direct:
            p = Place(img_size)
            greet(p.partners())
            moves = [Move(p, copies, a, b, False) for a, b in zip(wh, blocks)]
            scatter = Scatter(p, copies, None, gd, scr[16:23], cut)
            units = scatter.units()
            steps = pipelined(units)
        for m in moves:
            m.start()
        loads[0].wait()

        def down(f, carry):
            fetch_e(f).wait()
            gd_v[...] = dot(e_v[lax.rem(f, 2)], dr_v[...], TN).astype(BF)
            if direct:
                for to, c in ((scatter.own, p.c), (scatter.stage, 1 - p.c)):
                    got = gd_v[:, columns(c * wide, wide)].reshape(2, 2, cut, tall, wide)
                    for r in range(cut):
                        to[r, f] = got[:, :, r]
            else:
                for c in range(2):
                    gd[0, c, f] = gd_v[:, c * wide:(c + 1) * wide].reshape(2, 2, k2, wide)

            @pl.when(f + 2 < chunks)
            def _():
                fetch_e(f + 2).start()

            return carry

        lax.fori_loop(0, chunks, down, 0)
        for step in steps[:1]:
            step()
        late = [copies.here(lambda: (att_hbm, e_v.at[0])), copies.here(lambda: (dy_hbm, e_v.at[1]))]
        for copy in late:
            copy.start()
        for copy in loads[1:4]:
            copy.wait()
        nt_v[...] = n2_v[...].T
        dn[...] = jnp.zeros_like(dn)
        g2, s1, b2, bo = (vec[i:i + 1, :] for i in (1, 2, 5, 8))
        points = loop_points(steps[1:], 1)

        def chunk(f, carry):
            run_point(points, f, 0, 1, chunks)
            slot = lax.rem(f, 2)
            fetch_g(f).wait()

            @pl.when(f + 1 < chunks)
            def _():
                fetch_g(f + 1).start()

            @pl.when(f >= 2)
            def _():
                put(f - 2).wait()

            w1 = wu[slot, f // 2].reshape(width, width)
            w2 = jnp.concatenate([wd[0, c, f].reshape(width, wide) for c in range(2)], 1)
            total = jnp.zeros((8, width), F32)
            for i in range(2):
                at = slice(i * half, (i + 1) * half)
                de = dot(dr_v[at, :], w2, NT)
                du = (de * g_v[slot, at, :].astype(F32)).astype(BF)
                du_v[at, :] = du
                total += fold8(du.astype(F32))
            up_acc[f] = total
            dn[...] += dot(du_v[...], w1, NT)
            gu_v[slot] = dot(nt_v[...], du_v[...], NN).astype(BF).reshape(gu_v.shape[1:])
            put(f).start()
            return carry

        lax.fori_loop(0, chunks, chunk, 0)
        for copy in loads[4:] + late:
            copy.wait()
        acc[...] = jnp.zeros_like(acc)
        run_some = [points[t] for t in sorted(points) if t >= chunks]
        for step in run_some[:1]:
            step()

        def norm(start, size):
            at = pl.ds(start, size)
            hat, scale = norm_parts(m_v[at, :])
            d = dn[at, :]
            acc[0] += fold8(d * hat)
            acc[1] += fold8(d)
            dm = e_v[1, at, :].astype(F32) + norm_back(d, hat, scale, g2)
            da = (s1 * dm).astype(BF)
            acc[2] += fold8(da.astype(F32))
            m_v[at, :] = dm
            du_v[at, :] = da

        row_tiles(rows, 96, norm)
        out = [copies.here(lambda: (m_v, dm_hbm))]
        out[0].start()
        for step in run_some[1:]:
            step()
        w = joined(wo, 0)
        got = dot(e_v[0], du_v[...], TN).astype(BF)
        for c in range(2):
            go_v[c] = got[:, c * (width // 2):(c + 1) * (width // 2)].reshape(go_v.shape[1:])
        out.append(copies.here(lambda: (go_v, go.at[0])))
        out[1].start()
        for i in range(2):
            at = slice(i * half, (i + 1) * half)
            n2_v[at, :] = dot(du_v[at, :], w, NT).astype(BF)
            a = dot(e_v[0, at, :], w, NN) + bo
            acc[3] += fold8(a * m_v[at, :])
        out.append(copies.here(lambda: (n2_v, da_hbm)))
        out[2].start()
        sums[...] = jnp.zeros_like(sums)
        for i, (part, row) in enumerate(((0, 1), (0, 5), (1, 0), (0, 2))):
            sums[part, row:row + 1, :] = jnp.sum(acc[i], 0, keepdims=True)
        sums[0, 3:4, :] = s_in[0:1, :]
        sums[1, 1:2, :] = s_in[1:2, :]
        for f in range(chunks):
            sums[1, 2 + f:3 + f, :] = jnp.sum(up_acc[f], 0, keepdims=True)
        for f in (chunks - 2, chunks - 1):
            put(f).wait()
        if direct:
            scatter.end()
        for copy in moves:
            copy.finish()
        for copy in out:
            copy.wait()

    bf = lambda *s: jax.ShapeDtypeStruct(s, BF)
    f32 = lambda *s: jax.ShapeDtypeStruct(s, F32)
    vm = pltpu.VMEM
    flat = vm((rows, width), BF)
    scratch = [
        vm((rows, width), F32), flat, vm((width, rows), BF), vm((2, rows, width), BF),
        vm((2, rows, width), BF), flat, vm(w_out.shape, BF), vm(w_up.shape, BF), vm(w_down.shape, BF),
        vm((rows, width), F32), flat, vm((width, width), BF), vm((2,) + w_up.shape[2:], BF),
        vm(w_out.shape[1:], BF), vm((4, 8, width), F32), vm((chunks, 8, width), F32),
    ]
    if direct:
        scratch += Scatter.scratch(zs, k2 // 2, cols, 1, cut, True)
    scratch += semaphores(max(1, 3 * nw + Scatter.remotes(zs, 1, cut)), 6 + 3 * chunks + 2 + 3 + nw + 1)
    remote = dict(collective_id=4, has_side_effects=True) if direct else {}
    return pl.pallas_call(
        kernel,
        out_shape=[bf(*w_out.shape), bf(*w_up.shape), f32(k2 // 2, cols) if direct else bf(*w_down.shape),
                   f32(rows, width), bf(rows, width), f32(2, 8, width)]
        + [bf(w.shape[0] * 4, *w.shape[2:]) for w in wholes],
        in_specs=[ANY] * 10 + [VMEM, VMEM] + [ANY] * nw,
        out_specs=[ANY, ANY, ANY if direct else VMEM, ANY, ANY, VMEM] + [ANY] * nw,
        scratch_shapes=scratch,
        compiler_params=pltpu.CompilerParams(vmem_limit_bytes=61 * MIB, **remote),
        name="backward_head",
    )(att, m, n2, e, g, dr, dy, w_out, w_up, w_down, vectors, sums_in, *wholes)


def project_in(x_l, x_s, w_qkv, vectors, merged_bias):
    large, small = x_l.shape[0], x_s.shape[0]
    rows, width = large * LEN_L + small * LEN_S, x_l.shape[3]
    panels, wide = w_qkv.shape[0], w_qkv.shape[-1]

    def kernel(xl_hbm, xs_hbm, w_hbm, vec, bias, out, flat, four, w_v, local):
        copies = Copies(None, None, local)
        loads = load_tokens(copies, xl_hbm, xs_hbm, flat, four) + [copies.here(lambda: (w_hbm, w_v))]
        for copy in loads:
            copy.start()
        for copy in loads[:-1]:
            copy.wait()
        join_small(flat, four, large)

        def normed(start, size):
            at = pl.ds(start, size)
            hat, _ = norm_parts(flat[at, :].astype(F32))
            flat[at, :] = (hat * vec[0:1, :] + vec[4:5, :]).astype(BF)

        row_tiles(rows, 96, normed)
        loads[-1].wait()
        for u in range(panels):
            for c in range(2):
                cols = slice((c * panels + u) * wide, (c * panels + u + 1) * wide)
                got = dot(flat[...], w_v[u, c].reshape(width, wide), NN) + bias[:, cols]
                out[:, cols] = got.astype(BF)

    return pl.pallas_call(
        kernel,
        out_shape=jax.ShapeDtypeStruct((rows, 3 * width), BF),
        in_specs=[ANY] * 3 + [VMEM, VMEM],
        out_specs=VMEM,
        scratch_shapes=[pltpu.VMEM((rows, width), BF), pltpu.VMEM(x_s.shape, BF), pltpu.VMEM(w_qkv.shape, BF),
                        pltpu.SemaphoreType.DMA((4 * large + 2,))],
        compiler_params=pltpu.CompilerParams(vmem_limit_bytes=40 * MIB),
        name="project_in",
    )(x_l, x_s, w_qkv, vectors, merged_bias)


def head_columns(rows, at):
    return pl.BlockSpec((rows, 128), lambda g: (0, g + at))


def attend(qkv, rows_l, rows_s, large, small):
    rows = qkv.shape[0]
    return pl.pallas_call(
        functools.partial(attend_kernel, large, small),
        grid=(H // 2,),
        out_shape=jax.ShapeDtypeStruct((rows, 64 * H), BF),
        in_specs=[head_columns(rows, H // 2 * i) for i in range(3)]
        + [pl.BlockSpec((2, 8, WIDE_L), lambda g: (g, 0, 0)), pl.BlockSpec((2, 8, WIDE_S), lambda g: (g, 0, 0))],
        out_specs=head_columns(rows, 0),
        scratch_shapes=[pltpu.VMEM((2, LEN_L, LEN_L), F32), pltpu.VMEM((2, LEN_S, LEN_S), F32)],
        compiler_params=pltpu.CompilerParams(vmem_limit_bytes=56 * MIB),
        name="attend",
    )(qkv, qkv, qkv, rows_l, rows_s)


def layer_norm(values, gain, shift):
    average = jnp.mean(values, -1, keepdims=True)
    centered = values - average
    variance = jnp.mean(centered * centered, -1, keepdims=True)
    return centered * lax.rsqrt(variance + 1e-06) * gain + shift


def to_images(blocks):
    n = blocks.shape[0] // 4
    got = lax.all_to_all(blocks.reshape((4, n) + blocks.shape[1:]), "rows", 0, 0)
    return jnp.swapaxes(got, 0, 1)


def to_blocks(whole):
    got = lax.all_to_all(jnp.swapaxes(whole, 0, 1), "rows", 0, 0)
    return got.reshape((-1,) + got.shape[2:])


def to_panels(full, panels):
    rows, cols = full.shape
    split = full.reshape(4, 2, 2, rows // 16, 2, panels, cols // 2 // panels)
    return split.transpose(5, 4, 0, 1, 2, 3, 6)


def from_panels(split):
    rows, cols = 16 * split.shape[5], split.shape[0] * 2 * split.shape[6]
    return split.transpose(2, 3, 4, 5, 1, 0, 6).reshape(rows, cols)


CUTS = ((3, 1), (1, 1), (2, 3), (1, 3))


def on_device(img_size, small_images, large_images, w_qkv, w_out, w_up, w_down, gains, biases, up_bias,
              small_table, large_table, small_cotangent, large_cotangent):
    width = small_images.shape[2]
    axes = ("img", "rows")
    own = gains.shape[0]
    own_up = up_bias.shape[0]
    rows_l = table_rows(large_table, SIDE_L, 47, WIDE_L)
    rows_s = table_rows(small_table, SIDE_S, 29, WIDE_S)
    direct = own % 8 == 0
    if direct:
        block = jnp.concatenate([gains.T, biases.T], 0)
        block = jnp.pad(block, ((0, 0), (0, own_up - own)))
        block = jnp.pad(jnp.concatenate([block, up_bias[None]], 0), ((0, 5), (0, 128 - own_up)))
        large_x, small_x, qkv_w, up_w, out_w, down_w, qkv, n1, attended, vectors, up_vec = front(
            img_size, [large_images, small_images], block, [w_qkv, w_up, w_out, w_down],
            [CUTS[i] for i in (0, 2, 1, 3)], [(0, 3), (0,)], rows_l, rows_s)
        large, small = large_x.shape[0], small_x.shape[0]
        large_y, small_y, m, n2, e, g, dr, dy, sums, down_w, _, _ = forward_tail(
            img_size, attended, large_x, small_x, large_cotangent, small_cotangent, out_w, up_w, down_w, CUTS[3],
            vectors, up_vec)
        grad_out, grad_up, own_down, dm, d_att, sums, large_out, small_out = backward_head(
            img_size, attended, m, n2, e, g, dr, dy, out_w, up_w, down_w, CUTS[3][1], vectors, sums,
            [large_y, small_y])
        df, large_sums, small_sums, own_out, own_up_w = attention_back(
            img_size, qkv, d_att, rows_l, rows_s, [grad_out, grad_up], [1, 1], [], large, small, 3)
        large_grad, small_grad, own_qkv, sums, large_sums, small_sums = projection_back(
            img_size, df, dm, n1, large_x, small_x, qkv_w, vectors, sums, [large_sums, small_sums], large, small)
    else:
        large_x, small_x, large_ct, small_ct = [
            to_images(a) for a in (large_images, small_images, large_cotangent, small_cotangent)]
        large, small = large_x.shape[0], small_x.shape[0]
        qkv_w, out_w, up_w, down_w = [
            to_panels(lax.all_gather(s.astype(BF), axes, axis=0, tiled=True), c[0])
            for s, c in zip((w_qkv, w_out, w_up, w_down), CUTS)]
        vectors = lax.all_gather(jnp.concatenate([gains, biases], 1).astype(BF), axes, axis=0, tiled=True)
        vectors = jnp.pad(vectors.astype(F32).T, ((0, 6), (0, 0)))
        up_vec = lax.all_gather(up_bias.astype(BF), axes, axis=0, tiled=True).astype(F32).reshape(-1, width)
        merged_bias = jnp.concatenate([vectors[6:7], jnp.zeros((1, width), F32), vectors[7:8]], 1)
        qkv = project_in(large_x, small_x, qkv_w, vectors, merged_bias)
        attended = attend(qkv, rows_l, rows_s, large, small)
        large_y, small_y, m, n2, e, g, dr, dy, sums = forward_tail(
            None, attended, large_x, small_x, large_ct, small_ct, out_w, up_w, down_w, (1, 1), vectors, up_vec)
        grad_out, grad_up, grad_down, dm, d_att, sums = backward_head(
            None, attended, m, n2, e, g, dr, dy, out_w, up_w, down_w, 1, vectors, sums, [])
        df, large_sums, small_sums = attention_back(
            img_size, qkv, d_att, rows_l, rows_s, [], [], [], large, small, 1)
        split_at = large * LEN_L
        tokens = jnp.concatenate([large_x.reshape(-1, width), small_x.reshape(-1, width)], 0).astype(F32)
        normed, pull = jax.vjp(layer_norm, tokens, vectors[0], vectors[4])
        grad_qkv = jnp.einsum("rd,re->de", normed.astype(BF), df, preferred_element_type=F32)
        d_normed = jnp.einsum("re,de->rd", df, from_panels(qkv_w), preferred_element_type=F32)
        d_tokens, grad_gain, grad_shift = pull(d_normed)
        d_tokens = (dm + d_tokens).astype(BF)
        grad_q = jnp.sum(df[:, :width].astype(F32), 0)
        grad_v = jnp.sum(df[:, 2 * width:].astype(F32), 0)
        for row, value in ((0, grad_gain), (4, grad_shift), (6, grad_q), (7, grad_v)):
            sums = sums.at[0, row].set(value)
        sums, large_sums, small_sums = lax.psum((sums, large_sums, small_sums), axes)
        large_grad = to_blocks(d_tokens[:split_at].reshape(large_x.shape))
        small_grad = to_blocks(d_tokens[split_at:].reshape(small_x.shape))
        large_out, small_out = to_blocks(large_y), to_blocks(small_y)
        grads = [grad_qkv] + [from_panels(g).astype(F32) for g in (grad_out, grad_up, grad_down)]
        own_qkv, own_out, own_up_w, own_down = [
            lax.psum_scatter(g, axes, scatter_dimension=0, tiled=True) for g in grads]

    index = lax.axis_index("img") * 4 + lax.axis_index("rows")
    flat_sums = sums.reshape(16, width)
    own_columns = lax.dynamic_slice(flat_sums, (0, index * own), (10, own)).T
    own_up_sums = lax.dynamic_slice(flat_sums[10:14].reshape(-1), (index * own_up,), (own_up,))
    grad_large_table = table_sums(large_sums[:, :12].reshape(H, 2, WIDE_L), SIDE_L, 47)
    grad_small_table = table_sums(small_sums[:, :12].reshape(H, 2, WIDE_S), SIDE_S, 29)
    return (
        small_out, large_out, small_grad, large_grad, own_qkv, own_out, own_up_w, own_down,
        own_columns[:, :4], own_columns[:, 4:], own_up_sums, grad_small_table, grad_large_table,
    )


def solution(mesh):
    images = P("img", "rows", None)
    matrix = P(("img", "rows"), None)
    vector = P(("img", "rows"))
    in_specs = (images, images) + (matrix,) * 6 + (vector, P(), P(), images, images)
    out_specs = (images,) * 4 + (matrix,) * 6 + (vector, P(), P())
    return jax.shard_map(
        functools.partial(on_device, mesh.shape["img"]),
        mesh=mesh, in_specs=in_specs, out_specs=out_specs, check_vma=False,
    )
```

```python
import functools

import jax
import jax.numpy as jnp
from jax import lax
from jax.experimental import pallas as pl
from jax.experimental.pallas import tpu as pltpu
from jax.sharding import PartitionSpec as P

H = 12
SIDE_S = 14
SIDE_L = 24
LEN_S = 224
LEN_L = 576
WIDE_L = 1152
WIDE_S = 512

F32 = jnp.float32
BF = jnp.bfloat16
NN = (((1,), (0,)), ((), ()))
NT = (((1,), (1,)), ((), ()))
TN = (((0,), (0,)), ((), ()))
MESH = pl.DeviceIdType.MESH
ANY = pl.BlockSpec(memory_space=pl.ANY)
VMEM = pl.BlockSpec(memory_space=pltpu.VMEM)
HIGHEST = lax.Precision.HIGHEST
MIB = 1 << 20


def dot(left, right, dims):
    return lax.dot_general(left, right, dims, preferred_element_type=F32)


class Place:
    def __init__(self, img_size):
        self.img = lax.axis_index("img")
        self.row = lax.axis_index("rows")
        self.zs = img_size // 2
        self.z, self.x = self.img // 2, self.img % 2
        self.y, self.c = self.row // 2, self.row % 2

    def at(self, z=None, x=None, y=None, c=None):
        z = self.z if z is None else z
        x = self.x if x is None else x
        y = self.y if y is None else y
        c = self.c if c is None else c
        return (z * 2 + x, y * 2 + c)

    def z_other(self, step):
        return lax.rem(self.z + step, self.zs)

    def row_other(self, step):
        return lax.rem(self.row + step, 4)

    def partners(self):
        along_z = [self.at(z=self.z_other(s)) for s in range(1, self.zs)]
        in_rows = [(self.img, self.row_other(s)) for s in range(1, 4)]
        return along_z + in_rows + [self.at(x=1 - self.x)]


def greet(partners):
    barrier = pltpu.get_barrier_semaphore()
    for p in partners:
        pl.semaphore_signal(barrier, inc=1, device_id=p, device_id_type=MESH)
    pl.semaphore_wait(barrier, len(partners))


class Remote:
    def __init__(self, copies, build):
        self.copies, self.build, self.at = copies, build, copies.remotes
        copies.remotes += 1

    def made(self):
        src, dst, device = self.build()
        return pltpu.make_async_remote_copy(
            src_ref=src, dst_ref=dst, send_sem=self.copies.send.at[self.at], recv_sem=self.copies.recv.at[self.at],
            device_id=device, device_id_type=MESH,
        )

    def start(self):
        self.made().start()
        return self

    def wait_send(self):
        self.made().wait_send()

    def wait_recv(self):
        self.made().wait_recv()


class Local:
    def __init__(self, copies, build):
        self.copies, self.build, self.at = copies, build, copies.locals
        copies.locals += 1

    def made(self):
        return pltpu.make_async_copy(*self.build(), self.copies.local.at[self.at])

    def start(self):
        self.made().start()
        return self

    def wait(self):
        self.made().wait()


class Copies:
    def __init__(self, send, recv, local):
        self.send, self.recv, self.local = send, recv, local
        self.remotes, self.locals = 0, 0

    def remote(self, build):
        return Remote(self, build)

    def here(self, build):
        return Local(self, build)


def pipelined(units):
    depth = max(len(u) for u in units)

    def step(t):
        for f in range(depth):
            u = t - f
            if 0 <= u < len(units) and f < len(units[u]):
                units[u][f]()

    return [functools.partial(step, t) for t in range(len(units) + depth - 1)]


def in_turn(*phases):
    def step():
        for phase in phases:
            phase()

    return step


def columns(start, size):
    return pl.ds(pl.multiple_of(start, 128), size)


class Gather:
    def __init__(self, place, copies, shard, full, both, low, pieces):
        self.p, self.copies = place, copies
        self.full, self.both, self.low = full, both, low
        self.panels, self.wide = full.shape[0], full.shape[-1]
        self.k, self.half = full.shape[5] // 2, self.panels * self.wide
        self.tall = 2 * self.k // pieces
        self.pieces = pieces
        p = place

        def mine():
            return both.at[pl.ds(pl.multiple_of(p.c * self.k, 8), self.k)]

        if shard is not None:
            self.kept = copies.here(lambda: (shard.at[:, columns(p.c * self.half, self.half)], mine()))
            self.swapped = copies.remote(
                lambda: (shard.at[:, columns((1 - p.c) * self.half, self.half)], mine(), p.at(c=1 - p.c)))

    def exchange(self):
        self.kept.start()
        self.swapped.start()

    def convert(self):
        self.kept.wait()
        self.swapped.wait_recv()
        self.low[...] = self.both[...].astype(BF)

    def over_z(self, u, r):
        p = self.p
        rows = pl.ds(r * self.tall, self.tall)
        src = self.low.at[rows, pl.ds(u * self.wide, self.wide)]

        def dst():
            return self.full.at[u, p.c, p.z, p.x, p.y, rows]

        own = self.copies.here(lambda: (src, dst()))
        sent = [self.copies.remote(lambda s=s: (src, dst(), p.at(z=p.z_other(s)))) for s in range(1, p.zs)]

        def start():
            if u == 0 and r == 0:
                self.convert()
            for copy in [own] + sent:
                copy.start()

        def wait():
            own.wait()
            for copy in sent:
                copy.wait_recv()
            for copy in sent:
                copy.wait_send()
            if u == 0 and r == 0:
                self.swapped.wait_send()

        return [start, wait]

    def over_yx(self, u, r, x_first=False):
        p, full = self.p, self.full
        rows = pl.ds(r * self.tall, self.tall)
        one = lambda: full.at[u, p.c, :, p.x, p.y, rows]
        if x_first:
            first = self.twice(one, lambda: p.at(x=1 - p.x))
            second = self.twice(lambda: full.at[u, p.c, :, :, p.y, rows], lambda: p.at(y=1 - p.y))
        else:
            first = self.twice(one, lambda: p.at(y=1 - p.y))
            second = self.twice(lambda: full.at[u, p.c, :, p.x, :, rows], lambda: p.at(x=1 - p.x))
        third = self.twice(lambda: full.at[u, p.c, :, :, :, rows], lambda: p.at(c=1 - p.c))

        def next_(before, after):
            before.wait_recv()
            after.start()

        def finish():
            third.wait_recv()
            for copy in (first, second, third):
                copy.wait_send()

        return [first.start, functools.partial(next_, first, second), functools.partial(next_, second, third), finish]

    def unit(self, u, r, x_first=False):
        start, wait = self.over_z(u, r)
        after = self.over_yx(u, r, x_first)

        def second():
            wait()
            after[0]()

        return [start, second] + after[1:]

    def twice(self, part, device):
        return self.copies.remote(lambda: (part(), part(), device()))

    def units(self, kind=None, x_first=()):
        if kind is not None:
            return [kind(u, r) for u in range(self.panels) for r in range(self.pieces)]
        return [
            self.unit(u, r, u * self.pieces + r in x_first) for u in range(self.panels) for r in range(self.pieces)
        ]

    @staticmethod
    def scratch(shape):
        k, cols = shape
        return [pltpu.VMEM((2 * k, cols // 2), F32), pltpu.VMEM((2 * k, cols // 2), BF)]


class Spread:
    def __init__(self, place, copies, block, full):
        p = place

        def dst():
            return full.at[p.z, p.x, p.y, p.c]

        def twice(part, device):
            return copies.remote(lambda: (part(), part(), device()))

        self.own = copies.here(lambda: (block, dst()))
        self.over_z = [copies.remote(lambda s=s: (block, dst(), p.at(z=p.z_other(s)))) for s in range(1, p.zs)]
        self.over_y = twice(lambda: full.at[:, p.x, p.y, p.c], lambda: p.at(y=1 - p.y))
        self.over_x = twice(lambda: full.at[:, p.x, :, p.c], lambda: p.at(x=1 - p.x))
        self.over_c = twice(lambda: full.at[:, :, :, p.c], lambda: p.at(c=1 - p.c))

    def along_z(self):
        for copy in [self.own] + self.over_z:
            copy.start()

    def along_y(self):
        self.own.wait()
        for copy in self.over_z:
            copy.wait_recv()
        self.over_y.start()

    def along_x(self):
        self.over_y.wait_recv()
        self.over_x.start()

    def along_c(self):
        self.over_x.wait_recv()
        self.over_c.start()

    def finish(self):
        self.over_c.wait_recv()
        for copy in self.over_z + [self.over_y, self.over_x, self.over_c]:
            copy.wait_send()

    def units(self):
        return [[self.along_z, self.along_y, self.along_x, self.along_c, self.finish]]


class Move:
    def __init__(self, place, copies, src, dst, to_images, image=None):
        p = place
        n = (src if to_images else dst).shape[0] // 4

        def part(row):
            blocks, whole = (src, dst) if to_images else (dst, src)
            theirs, mine = (row, p.row) if to_images else (p.row, row)
            if image is None:
                found = blocks.at[pl.ds(theirs * n, n)], whole.at[:, mine]
            else:
                found = blocks.at[theirs * n + image], whole.at[image, mine]
            return found if to_images else found[::-1]

        self.own = copies.here(lambda: part(p.row))
        self.sent = [
            copies.remote(lambda s=s: part(p.row_other(s)) + ((p.img, p.row_other(s)),)) for s in (2, 3, 1)
        ]

    def start(self):
        for copy in self.sent + [self.own]:
            copy.start()

    def finish(self):
        self.own.wait()
        for copy in self.sent:
            copy.wait_recv()
        for copy in self.sent:
            copy.wait_send()


class Scatter:
    def __init__(self, place, copies, grad, shard, scratch, pieces):
        self.p, self.copies, self.grad, self.shard = place, copies, grad, shard
        self.own, self.from_c, self.from_x, self.from_y, self.from_z, self.summed = scratch[:6]
        self.stage = scratch[6] if grad is None else None
        self.k, self.cols = shard.shape
        self.half = self.cols // 2
        self.pieces = pieces
        self.panels = self.own.shape[0] // pieces
        self.wide, self.tall = self.own.shape[-1], self.own.shape[-2]
        p = place

        def cols():
            return columns(p.c * self.half, self.half)

        def rows(c):
            return pl.ds(pl.multiple_of(c * self.k, 8), self.k)

        self.last = copies.remote(
            lambda: (self.summed.at[rows(1 - p.c)], shard.at[:, cols()], p.at(c=1 - p.c)))
        self.kept = copies.here(lambda: (self.summed.at[rows(p.c)], shard.at[:, cols()]))

    def unit(self, u, r, y_first=False, given=False):
        p, copies, grad = self.p, self.copies, self.grad
        at = u * self.pieces + r
        own, from_c, from_x = self.own.at[at], self.from_c.at[at], self.from_x.at[at]
        from_y, from_z = self.from_y.at[at], self.from_z.at[at]
        rows = pl.ds(r * self.tall, self.tall)
        if grad is None:
            over_c = copies.remote(lambda: (self.stage.at[at], from_c, p.at(c=1 - p.c)))
            loaded = None
        else:
            over_c = copies.remote(lambda: (grad.at[u, 1 - p.c, :, :, :, rows], from_c, p.at(c=1 - p.c)))
            loaded = copies.here(lambda: (grad.at[u, p.c, :, :, :, rows], own))
        if y_first:
            over_x = copies.remote(lambda: (own.at[:, :, 1 - p.y], from_x, p.at(y=1 - p.y)))
            over_y = copies.remote(lambda: (own.at[:, 1 - p.x, p.y], from_y, p.at(x=1 - p.x)))
        else:
            over_x = copies.remote(lambda: (own.at[:, 1 - p.x], from_x, p.at(x=1 - p.x)))
            over_y = copies.remote(lambda: (own.at[:, p.x, 1 - p.y], from_y, p.at(y=1 - p.y)))
        over_z = [
            copies.remote(lambda s=s: (own.at[p.z_other(s), p.x, p.y], from_z.at[s - 1], p.at(z=p.z_other(s))))
            for s in range(1, p.zs)
        ]

        def add(into, other):
            into[...] = (into[...].astype(F32) + other[...].astype(F32)).astype(BF)

        def along_c():
            over_c.start()
            if loaded is not None:
                loaded.start()

        def along_x():
            if loaded is not None:
                loaded.wait()
            if not given:
                over_c.wait_recv()
            for theirs in (True, False):
                for z in range(p.zs):
                    for i in range(2):
                        where = (z, i, 1 - p.y if theirs else p.y) if y_first else (z, 1 - p.x if theirs else p.x, i)
                        add(own.at[where], from_c.at[where])
                if theirs:
                    over_x.start()

        def along_y():
            over_x.wait_recv()
            for theirs in (True, False):
                for z in range(p.zs):
                    i = p.x if y_first else p.y
                    i = 1 - i if theirs else i
                    add(own.at[(z, i, p.y) if y_first else (z, p.x, i)], from_x.at[z, i])
                if theirs:
                    over_y.start()

        def along_z():
            over_y.wait_recv()
            for z in range(p.zs):
                add(own.at[z, p.x, p.y], from_y.at[z])
            for copy in over_z:
                copy.start()

        def finish():
            for copy in over_z:
                copy.wait_recv()
            total = own[p.z, p.x, p.y].astype(F32)
            for s in range(p.zs - 1):
                total += from_z[s].astype(F32)
            self.summed[rows, pl.ds(u * self.wide, self.wide)] = total
            for copy in ([] if given else [over_c]) + [over_x, over_y] + over_z:
                copy.wait_send()
            if at == self.panels * self.pieces - 1:
                self.last.start()
                self.kept.start()

        return [along_c, along_x, along_y, along_z, finish]

    def unit_xzy(self, u):
        p, copies = self.p, self.copies
        own, from_c, from_x = self.own.at[u], self.from_c.at[u], self.from_x.at[u]
        from_z, from_y = self.from_y.at[u], self.from_z.at[u]
        over_c = copies.remote(lambda: (self.stage.at[u], from_c, p.at(c=1 - p.c)))
        over_x = copies.remote(lambda: (own.at[:, 1 - p.x], from_x, p.at(x=1 - p.x)))
        over_z = [
            copies.remote(lambda s=s: (own.at[p.z_other(s), p.x], from_z.at[s - 1], p.at(z=p.z_other(s))))
            for s in range(1, p.zs)
        ]
        over_y = copies.remote(lambda: (own.at[p.z, p.x, 1 - p.y], from_y, p.at(y=1 - p.y)))

        def add(into, other):
            into[...] = (into[...].astype(F32) + other[...].astype(F32)).astype(BF)

        def along_x():
            over_c.wait_recv()
            for x in (1 - p.x, p.x):
                for z in range(p.zs):
                    for y in range(2):
                        add(own.at[z, x, y], from_c.at[z, x, y])
                if x is not p.x:
                    over_x.start()

        def along_z():
            over_x.wait_recv()
            for s in range(1, p.zs):
                z = p.z_other(s)
                for y in range(2):
                    add(own.at[z, p.x, y], from_x.at[z, y])
                over_z[s - 1].start()
            for y in range(2):
                add(own.at[p.z, p.x, y], from_x.at[p.z, y])

        def along_y():
            for copy in over_z:
                copy.wait_recv()
            for y in (1 - p.y, p.y):
                mine = own.at[p.z, p.x, y]
                total = mine[...].astype(F32)
                for s in range(p.zs - 1):
                    total += from_z[s, y].astype(F32)
                mine[...] = total.astype(BF)
                if y is not p.y:
                    over_y.start()

        def finish():
            over_y.wait_recv()
            self.summed[:, pl.ds(u * self.wide, self.wide)] = (
                own[p.z, p.x, p.y].astype(F32) + from_y[...].astype(F32))
            for copy in [over_c, over_x, over_y] + over_z:
                copy.wait_send()
            if u == self.panels - 1:
                self.last.start()
                self.kept.start()

        return [over_c.start, along_x, along_z, along_y, finish]

    def end(self):
        self.kept.wait()
        self.last.wait_recv()
        self.last.wait_send()

    def units(self, y_first=(), given=False):
        return [
            self.unit(u, r, u * self.pieces + r in y_first, given)
            for u in range(self.panels) for r in range(self.pieces)
        ]

    @staticmethod
    def scratch(zs, k, cols, panels, pieces, staged=False):
        n, tall, w = panels * pieces, 2 * k // pieces, cols // 2 // panels
        shapes = [(n, zs, 2, 2, tall, w), (n, zs, 2, 2, tall, w), (n, zs, 2, tall, w), (n, zs, tall, w),
                  (n, zs - 1, tall, w)]
        return [pltpu.VMEM(s, BF) for s in shapes] + [pltpu.VMEM((2 * k, cols // 2), F32)] + (
            [pltpu.VMEM(shapes[0], BF)] if staged else [])

    @staticmethod
    def scratch_xzy(zs, k, cols, panels):
        w = cols // 2 // panels
        shapes = [(zs, 2, 2, 2 * k, w), (zs, 2, 2, 2 * k, w), (zs, 2, 2 * k, w), (zs - 1, 2, 2 * k, w), (2 * k, w)]
        return [pltpu.VMEM((panels,) + s, BF) for s in shapes] + [
            pltpu.VMEM((2 * k, cols // 2), F32), pltpu.VMEM((panels,) + shapes[0], BF)]

    @staticmethod
    def remotes(zs, panels, pieces):
        return 1 + panels * pieces * (zs + 2)


class Total:
    def __init__(self, place, copies, grad, result, got, work, from_z):
        self.p, self.grad, self.got, self.work, self.from_z = place, grad, got, work, from_z
        p = place
        self.kept = copies.here(lambda: (grad.at[p.c], work))
        self.over_c = copies.remote(lambda: (grad.at[1 - p.c], got.at[0], p.at(c=1 - p.c)))
        self.over_x = copies.remote(lambda: (work, got.at[1], p.at(x=1 - p.x)))
        self.over_y = copies.remote(lambda: (work, got.at[2], p.at(y=1 - p.y)))
        self.over_z = [
            copies.remote(lambda s=s: (from_z.at[p.z], from_z.at[p.z], p.at(z=p.z_other(s)))) for s in range(1, p.zs)
        ]
        self.last = [
            copies.remote(lambda: (work, result.at[p.c], p.at(c=1 - p.c))),
            copies.here(lambda: (work, result.at[p.c])),
        ]

    def along_c(self):
        self.kept.start()
        self.over_c.start()

    def along_x(self):
        self.kept.wait()
        self.over_c.wait_recv()
        self.work[...] = self.work[...] + self.got[0]
        self.over_x.start()

    def along_y(self):
        self.over_x.wait_recv()
        self.over_x.wait_send()
        self.work[...] = self.work[...] + self.got[1]
        self.over_y.start()

    def along_z(self):
        self.over_y.wait_recv()
        self.over_y.wait_send()
        self.from_z[self.p.z] = self.work[...] + self.got[2]
        for copy in self.over_z:
            copy.start()

    def finish(self):
        for copy in self.over_z:
            copy.wait_recv()
        for copy in [self.over_c] + self.over_z:
            copy.wait_send()
        total = self.from_z[0]
        for z in range(1, self.p.zs):
            total += self.from_z[z]
        self.work[...] = total
        for copy in self.last:
            copy.start()

    def end(self):
        self.last[1].wait()
        self.last[0].wait_recv()
        self.last[0].wait_send()

    def units(self):
        return [[self.along_c, self.along_x, self.along_y, self.along_z, self.finish]]

    @staticmethod
    def scratch(zs, rows, wide):
        return [pltpu.VMEM((3, rows, wide), F32), pltpu.VMEM((rows, wide), F32), pltpu.VMEM((zs, rows, wide), F32)]

    @staticmethod
    def remotes(zs):
        return zs + 3


def semaphores(remotes, locals_):
    return [
        pltpu.SemaphoreType.DMA((remotes,)),
        pltpu.SemaphoreType.DMA((remotes,)),
        pltpu.SemaphoreType.DMA((locals_,)),
    ]


def split_refs(refs, *sizes):
    parts, at = [], 0
    for size in sizes:
        parts.append(refs[at:at + size])
        at += size
    return parts + [refs[at:]]


def full_shape(img_size, shard, panels):
    k, cols = shard.shape
    return (panels, 2, img_size // 2, 2, 2, 2 * k, cols // 2 // panels)


def table_rows(table, side, blocks, wide):
    span = 2 * side - 1
    square = table.reshape(H, span, span)
    square = jnp.concatenate([square] + [square[:, -1:]] * (blocks - span), 1)
    rows = []
    for turned in (square, square[:, ::-1, ::-1]):
        for part, pads in ((turned[:, :, :side], (0, 1)), (turned[:, :, side:], (1, 0))):
            part = jnp.pad(part, ((0, 0), pads, (0, side - part.shape[2])))
            flat = part.reshape(H, 1, (blocks + 1) * side)
            rows.append(jnp.roll(jnp.pad(flat, ((0, 0), (0, 0), (0, wide - flat.shape[2]))), 1 - side, 2))
    return jnp.concatenate(rows + [jnp.zeros((H, 4, wide), F32)], 1)


def lower_offsets(side, rows, wide):
    lane = lax.rem(lax.broadcasted_iota(jnp.int32, (rows, wide), 1), side)
    return lane <= lax.broadcasted_iota(jnp.int32, (rows, wide), 0)


def spread_rows(low, high, rows, lower):
    low = jnp.broadcast_to(low, (rows, low.shape[1]))
    high = jnp.broadcast_to(high, (rows, high.shape[1]))
    return jnp.where(
        lower, pltpu.roll(low, 0, 1, stride=1, stride_axis=0), pltpu.roll(high, 0, 1, stride=1, stride_axis=0)
    )


def shifted_window(ref, source, target):
    base = source // 128 * 128
    shift = (target - source) % 128 if target % 128 >= source % 128 else target % 128 - source % 128 + 256
    part = ref[:, base:min(base + 256, ref.shape[1])]
    if part.shape[1] < 256:
        part = jnp.concatenate([part, jnp.zeros_like(part)], 1)
    return pltpu.roll(part, shift, 1) if shift else part


def window_masks(target, side):
    lane = lax.broadcasted_iota(jnp.int32, (16, 256), 1) - target % 128
    return (lane >= 0) & (lane < side), (lane >= side) & (lane < 2 * side - 1)


def turn_lanes(table, turned):
    swap = lax.broadcasted_iota(jnp.int32, (128, 128), 0) + lax.broadcasted_iota(jnp.int32, (128, 128), 1) == 127
    swap = jnp.where(swap, 1.0, 0.0)
    width = table.shape[1]
    for at in range(0, width, 128):
        turned[:, width - 128 - at:width - at] = lax.dot_general(
            table[:, at:at + 128], swap, NN, precision=HIGHEST, preferred_element_type=F32)


def make_rows(table, low, high, side, blocks, first, skip=0):
    span = 2 * side - 1
    wide = low.shape[1] - 256
    low[...] = jnp.zeros_like(low)
    high[...] = jnp.zeros_like(high)
    for a in range(blocks):
        source = min(max(a - first, 0), span - 1) * span + skip
        target = 128 + a * side - (side - 1)
        part = shifted_window(table, source, target)
        at = slice(target // 128 * 128, target // 128 * 128 + 256)
        for ref, mask in zip((low, high), window_masks(target, side)):
            ref[:, at] += jnp.where(mask, part, 0.0)
    for ref in (low, high):
        ref[:, wide:wide + 128] += ref[:, :128]
        ref[:, :wide] = ref[:, 128:128 + wide]


def make_table(low, high, table, side, blocks, height):
    span = 2 * side - 1
    table[...] = jnp.zeros_like(table)
    for a in range(blocks):
        source = a * side + height - side
        target = min(a, span - 1) * span
        at = slice(target // 128 * 128, target // 128 * 128 + 256)
        for ref, mask in zip((low, high), window_masks(target, side)):
            table[:, at] += jnp.where(mask, shifted_window(ref, source, target), 0.0)


def row_scratch():
    return [pltpu.VMEM((16, WIDE_L + 256), F32)] * 2 + [pltpu.VMEM((16, WIDE_S + 256), F32)] * 2


TABLE_L = 2560
TABLE_S = 1024


def padded_table(table, wide):
    return jnp.pad(table, ((0, 16 - H), (0, wide - table.shape[1])))


def fill_bias(bias, h, spread, side, rows, first_offset):
    size = bias.shape[2]
    wide = spread.shape[1]
    window = -(-size // 128) * 128 + 128
    for r in range(rows):
        offset = (first_offset - r) * side
        base, rest = offset // 128 * 128, offset % 128
        part = spread[:, base:min(base + window, wide)]
        if part.shape[1] < window:
            part = jnp.concatenate([part, jnp.zeros((spread.shape[0], window - part.shape[1]), F32)], 1)
        if rest:
            part = pltpu.roll(part, window - rest, 1)
        bias[h, r * side:(r + 1) * side, :] = part[:side, :size]


def fold_bias(total, h, acc, side, rows, first_offset, lower, out_ref, head):
    size = total.shape[2]
    window = -(-size // 128) * 128 + 128
    height, wide = lower.shape
    acc[...] = jnp.zeros_like(acc)
    for r in range(rows):
        offset = (first_offset - r) * side
        base, rest = offset // 128 * 128, offset % 128
        part = total[h, r * side:(r + 1) * side, :]
        part = jnp.concatenate([part, jnp.zeros((side, window - size), F32)], 1)
        if rest:
            part = pltpu.roll(part, rest, 1)
        acc[:side, base:base + window] += part
    whole = acc[:, :wide]
    zero = jnp.zeros_like(whole)
    for at, part in enumerate((jnp.where(lower, whole, zero), jnp.where(lower, zero, whole))):
        turned = jnp.concatenate([part[j:j + 1] for j in reversed(range(height))], 0)
        moved = pltpu.roll(turned, 0, 1, stride=1, stride_axis=0)
        out_ref[at, pl.ds(head, 1), :] = jnp.sum(moved, 0, keepdims=True)


def head_part(full, mask, h):
    keep = mask if h == 0 else jnp.logical_not(mask)
    return jnp.where(keep, full, jnp.zeros_like(full))


def softmax_product(s, v):
    top = jnp.max(s, 1, keepdims=True)
    e = jnp.exp(s - top)
    total = jnp.sum(e, 1, keepdims=True)
    lse = jnp.broadcast_to(top + jnp.log(total), (s.shape[0], 128)).T
    return dot(e.astype(BF), v, NN) * (1.0 / total), lse[0:1, :]


def attend_kernel(large, small, q_ref, k_ref, v_ref, rows_l, rows_s, o_ref, lse_ref, bias_l, bias_s):
    mask = lax.broadcasted_iota(jnp.int32, (1, 128), 1) < 64
    lower_l = lower_offsets(SIDE_L, SIDE_L, WIDE_L)
    lower_s = lower_offsets(SIDE_S, 16, WIDE_S)
    for h in range(2):
        fill_bias(bias_l, h, spread_rows(rows_l[h, 2:3, :], rows_l[h, 3:4, :], SIDE_L, lower_l), SIDE_L, 24, 23)
        fill_bias(bias_s, h, spread_rows(rows_s[h, 2:3, :], rows_s[h, 3:4, :], 16, lower_s), SIDE_S, 16, 15)
    keep = lax.broadcasted_iota(jnp.int32, (1, LEN_S), 1) < SIDE_S * SIDE_S
    images = [(n * LEN_L, LEN_L, bias_l) for n in range(large)]
    images += [(large * LEN_L + n * LEN_S, LEN_S, bias_s) for n in range(small)]
    for n, (at, size, bias) in enumerate(images):
        q, k, v = (ref[at:at + size, :] for ref in (q_ref, k_ref, v_ref))
        outs = []
        for h in range(2):
            s = dot(head_part(q, mask, h) * BF(0.125), k, NT) + bias[h]
            if size == LEN_S:
                s = jnp.where(keep, s, -1e30)
            out, lse = softmax_product(s, v)
            outs.append(out)
            lse_ref[n, pl.ds(2 * pl.program_id(0) + h, 1), :size] = lse
        o_ref[at:at + size, :] = jnp.where(mask, outs[0], outs[1]).astype(BF)


def loop_points(steps, every):
    return {t * every: step for t, step in enumerate(steps)}


def run_point(points, iteration, at, per, iterations):
    for i in range(iterations):
        step = points.get(i * per + at)
        if step is not None:
            pl.when(iteration == i)(step)


def run_rest(points, count):
    for at in sorted(points):
        if at >= count:
            points[at]()


def attend_back_pair(hp, qkv, do_ref, o_ref, lse_ref, rows, df, sums_l, sums_s, scratch, large, small, between):
    bias_l, bias_s, total_l, total_s, acc_l, acc_s = scratch
    mask = lax.broadcasted_iota(jnp.int32, (1, 128), 1) < 64
    lower_l = lower_offsets(SIDE_L, SIDE_L, WIDE_L)
    lower_s = lower_offsets(SIDE_S, 16, WIDE_S)
    low_l, high_l, low_s, high_s = rows
    for h in range(2):
        at = pl.ds(2 * hp + h, 1)
        fill_bias(bias_l, h, spread_rows(low_l[at, :WIDE_L], high_l[at, :WIDE_L], SIDE_L, lower_l), SIDE_L, 24, 23)
        fill_bias(bias_s, h, spread_rows(low_s[at, :WIDE_S], high_s[at, :WIDE_S], 16, lower_s), SIDE_S, 14, 13)
    keep = lax.broadcasted_iota(jnp.int32, (LEN_S, 1), 0) < SIDE_S * SIDE_S
    images = [(n * LEN_L, LEN_L, bias_l, total_l, n == 0) for n in range(large)]
    images += [(large * LEN_L + n * LEN_S, LEN_S, bias_s, total_s, n == 0) for n in range(small)]
    cols = [columns(i * 64 * H + hp * 128, 128) for i in range(3)]
    for index, (at, size, bias, total, first) in enumerate(images):
        between(index)
        rows = slice(at, at + size)
        q, k, v = (qkv[rows, c] for c in cols)
        do = do_ref[rows, cols[0]]
        products = do.astype(F32) * o_ref[rows, cols[0]].astype(F32)
        got = []
        for h in range(2):
            ones = jnp.broadcast_to(jnp.where(mask == (h == 0), 1.0, 0.0), (8, 128))
            row_dot = lax.dot_general(ones, products, NT, precision=HIGHEST, preferred_element_type=F32)[0:1, :]
            lse = lse_ref[index, pl.ds(2 * hp + h, 1), :size]
            s = dot(head_part(k, mask, h) * BF(0.125), q, NT) + bias[h]
            if size == LEN_S:
                s = jnp.where(keep, s, -1e30)
            p = jnp.exp(s - lse)
            ds = p * (dot(head_part(v, mask, h), do, NT) - row_dot)
            low = ds.astype(BF)
            got.append((dot(low, k, TN), dot(low, q, NN), dot(p.astype(BF), do, NN)))
            total[h] = ds if first else total[h] + ds
        for c, a, b, scale in zip(cols, got[0], got[1], (0.125, 0.125, 1.0)):
            df[rows, c] = (jnp.where(mask, a, b) * scale).astype(BF)
    for h in range(2):
        fold_bias(total_l, h, acc_l, SIDE_L, 24, 23, lower_l, sums_l, 2 * hp + h)
        fold_bias(total_s, h, acc_s, SIDE_S, 14, 13, lower_s, sums_s, 2 * hp + h)


def back_scratch():
    return [pltpu.VMEM((2, LEN_L, LEN_L), F32), pltpu.VMEM((2, LEN_S, LEN_S), F32)] * 2 + [
        pltpu.VMEM((SIDE_L, WIDE_L + 128), F32), pltpu.VMEM((16, WIDE_S + 128), F32)]


BACK_POINTS = {
    1: ((0, 1),), 3: ((1, 1),), 7: ((2, 1), (0, 2)), 9: ((1, 2), (0, 3)), 13: ((2, 2), (1, 3)), 15: ((2, 3),),
    17: ((0, 4), (1, 4)), 18: ((2, 4),),
}


def attention_back(img_size, qkv, d_att, att, lse, table_l, table_s, grads, cuts, wholes, large, small):
    zs = img_size // 2
    ng, nw = len(grads), len(wholes)
    rows = qkv.shape[0]
    shard_shapes = [(g.shape[5] // 2, g.shape[0] * 2 * g.shape[6]) for g in grads]

    def kernel(*refs):
        ins, gr, wh, outs, shards, blocks, scr = split_refs(refs, 6, ng, nw, 3, ng, nw)
        qkv_hbm, do_hbm, o_hbm, lse_v, tl, ts = ins
        df_hbm, sums_l, sums_s = outs
        qkv_v, do_v, df_v, o_v = scr[:4]
        rows_ = scr[4:8]
        p = Place(img_size)
        copies = Copies(*scr[-3:])
        loads = [copies.here(lambda a=a, b=b: (a, b)) for a, b in ((qkv_hbm, qkv_v), (do_hbm, do_v), (o_hbm, o_v))]
        for copy in loads:
            copy.start()
        if ng + nw:
            greet(p.partners())
        at = 8 + 6
        scatters = []
        for i in range(ng):
            scatters.append(Scatter(p, copies, gr[i], shards[i], scr[at:at + 6], cuts[i]))
            at += 6
        moves = [Move(p, copies, a, b, False) for a, b in zip(wh, blocks)]
        units = [u for s in scatters for u in s.units()]
        points = {}
        if units:
            points = {at: in_turn(*[units[u][f] for u, f in todo]) for at, todo in BACK_POINTS.items()}
        for unit in units:
            unit[0]()
        for m in moves:
            m.start()
        make_rows(tl, rows_[0], rows_[1], SIDE_L, 47, 0)
        make_rows(ts, rows_[2], rows_[3], SIDE_S, 29, 0)
        sums_l[...] = jnp.zeros_like(sums_l)
        sums_s[...] = jnp.zeros_like(sums_s)
        for copy in loads:
            copy.wait()

        def body(hp, carry):
            attend_back_pair(hp, qkv_v, do_v, o_v, lse_v, rows_, df_v, sums_l, sums_s, scr[8:14], large, small,
                             lambda index: run_point(points, hp, index, large + small, H // 2))
            return carry

        lax.fori_loop(0, H // 2, body, 0)
        out = copies.here(lambda: (df_v, df_hbm))
        out.start()
        run_rest(points, (large + small) * (H // 2))
        for s in scatters:
            s.end()
        for m in moves:
            m.finish()
        out.wait()

    scratch = [pltpu.VMEM(a.shape, BF) for a in (qkv, d_att, qkv, att)] + row_scratch() + back_scratch()
    for g, (k, cols), cut in zip(grads, shard_shapes, cuts):
        scratch += Scatter.scratch(zs, k, cols, g.shape[0], cut)
    remotes = 3 * nw + sum(Scatter.remotes(zs, g.shape[0], c) for g, c in zip(grads, cuts))
    locals_ = 4 + nw + sum(1 + g.shape[0] * c for g, c in zip(grads, cuts))
    remote = dict(collective_id=1, has_side_effects=True) if ng + nw else {}
    return pl.pallas_call(
        kernel,
        out_shape=[jax.ShapeDtypeStruct(qkv.shape, BF), jax.ShapeDtypeStruct((2, 16, WIDE_L), F32),
                   jax.ShapeDtypeStruct((2, 16, WIDE_S), F32)]
        + [jax.ShapeDtypeStruct(s, F32) for s in shard_shapes]
        + [jax.ShapeDtypeStruct((w.shape[0] * 4,) + w.shape[2:], w.dtype) for w in wholes],
        in_specs=[ANY] * 3 + [VMEM] * 3 + [ANY] * (ng + nw),
        out_specs=[ANY, VMEM, VMEM] + [ANY] * (ng + nw),
        scratch_shapes=scratch + semaphores(max(remotes, 1), locals_),
        compiler_params=pltpu.CompilerParams(vmem_limit_bytes=60 * MIB, **remote),
        name="attention_back",
    )(qkv, d_att, att, lse, table_l, table_s, *grads, *wholes)


def row_tiles(rows, tile, body):
    count = rows // tile

    def step(t, carry):
        body(pl.multiple_of(t * tile, 16), tile)
        return carry

    lax.fori_loop(0, count, step, 0)
    if rows % tile:
        body(count * tile, rows % tile)


def norm_parts(x):
    centered = x - jnp.mean(x, 1, keepdims=True)
    scale = lax.rsqrt(jnp.mean(centered * centered, 1, keepdims=True) + 1e-06)
    return centered * scale, scale


def norm_back(dn, hat, scale, gain):
    d_hat = dn * gain
    return scale * (d_hat - jnp.mean(d_hat, 1, keepdims=True) - hat * jnp.mean(d_hat * hat, 1, keepdims=True))


def fold8(values):
    return sum(values[i:i + 8] for i in range(0, values.shape[0], 8))


def place_small(ref, flat, at):
    for i in range(4):
        ref[at, i] = flat[i * 56:(i + 1) * 56].astype(ref.dtype)


def load_tokens(copies, large_hbm, small_hbm, flat, four):
    n, _, rows, _ = large_hbm.shape
    loads = [
        copies.here(lambda i=i, j=j: (large_hbm.at[i, j], flat.at[pl.ds((i * 4 + j) * rows, rows)]))
        for i in range(n) for j in range(4)
    ]
    return loads + [copies.here(lambda: (small_hbm, four))]


def join_small(flat, four, large):
    for n in range(four.shape[0]):
        rows = jnp.concatenate([four[n, i].astype(F32) for i in range(4)], 0)
        at = large * LEN_L + n * LEN_S
        flat[at:at + LEN_S, :] = rows.astype(flat.dtype)


def projection_back(img_size, df, dm, n1, x_l, x_s, w_qkv, vectors, sums, tables, large, small):
    zs = img_size // 2
    rows, width = dm.shape
    panels, _, _, _, _, k2, wide = w_qkv.shape
    k, cols = k2 // 2, panels * 2 * wide
    nt = len(tables)

    def kernel(*refs):
        ins, tabs, outs, tab_outs, scr = split_refs(refs, 8, nt, 4, nt)
        df_hbm, dm_hbm, n1_hbm, xl_hbm, xs_hbm, w_hbm, vec, sums_in = ins
        gl_out, gs_out, shard, sums_out = outs
        df_v, dm_v, flat, four, w_v, n1_v, nt_v, dn, acc, own_sums, dl, ds, grad = scr[:13]
        at = 13
        p = Place(img_size)
        copies = Copies(*scr[-3:])
        first = [copies.here(lambda: (n1_hbm, n1_v)), copies.here(lambda: (df_hbm, df_v))]
        w_load = copies.here(lambda: (w_hbm, w_v))
        later = load_tokens(copies, xl_hbm, xs_hbm, flat, four) + [copies.here(lambda: (dm_hbm, dm_v))]
        for copy in first + [w_load] + later:
            copy.start()
        greet(p.partners())
        scatter = Scatter(p, copies, None, shard, scr[at:at + 7], 1)
        at += 7
        totals = []
        for a, b in zip(tabs, scr[-3 - 2 * nt:-3 - nt]):
            totals.append(Total(p, copies, a, b, *scr[at:at + 3]))
            at += 3
        last = Total(p, copies, own_sums, sums_out, *scr[at:at + 3])
        moves = [Move(p, copies, dl, gl_out, False, n) for n in range(large)]
        moves.append(Move(p, copies, ds, gs_out, False))
        units = [scatter.unit_xzy(u) for u in range(panels)]
        first[0].wait()
        nt_v[...] = n1_v[...].T
        first[1].wait()

        def pair(ref, u, at):
            return jnp.concatenate(
                [ref[at, c * (cols // 2) + u * wide:c * (cols // 2) + (u + 1) * wide] for c in range(2)], 1)

        def gradient(u):
            grad[...] = dot(nt_v[...], pair(df_v, u, slice(None)), NN).astype(BF)
            for to, c in ((scatter.stage, 1 - p.c), (scatter.own, p.c)):
                to[u] = grad[:, columns(c * wide, wide)].reshape(zs, 2, 2, k2, wide)
            units[u][0]()

        def all_totals(phase):
            for t in totals:
                phase(t)

        gain = vec[0:1, :]

        def back(start, size):
            at_rows = pl.ds(start, size)
            hat, scale = norm_parts(flat[at_rows, :].astype(F32))
            d = dn[at_rows, :]
            acc[0] += fold8(d * hat)
            acc[1] += fold8(d)
            acc[2] += fold8(df_v[at_rows, :width].astype(F32))
            acc[3] += fold8(df_v[at_rows, 2 * width:].astype(F32))
            flat[at_rows, :] = (dm_v[at_rows, :] + norm_back(d, hat, scale, gain)).astype(BF)

        def image(start, size):
            at = slice(start, start + size)
            got = None
            for u in range(panels):
                w = jnp.concatenate([w_v[u, c].reshape(width, wide) for c in range(2)], 1)
                part = dot(pair(df_v, u, at), w, NT)
                got = part if got is None else got + part
            dn[at, :] = got
            row_tiles(size, 96, lambda at, n: back(start + at, n))

        acc[...] = jnp.zeros_like(acc)
        gradient(0)
        all_totals(Total.along_c)
        for copy in [w_load] + later:
            copy.wait()
        join_small(flat, four, large)
        for n in range(large):
            image(n * LEN_L, LEN_L)
            for j in range(4):
                start = (n * 4 + j) * (LEN_L // 4)
                dl[n, j] = flat[start:start + LEN_L // 4, :]
            moves[n].start()
            if n == 0:
                units[0][1]()
                all_totals(Total.along_x)
                gradient(1)
            if n == 1:
                units[1][1]()
                gradient(2)
                units[0][2]()
        for n in range(small):
            start = large * LEN_L + n * LEN_S
            image(start, LEN_S)
            place_small(ds, flat[start:start + LEN_S, :].astype(F32), n)
        moves[-1].start()
        units[2][1]()
        for i, row in ((0, 0), (1, 4), (2, 6), (3, 7)):
            own_sums[0, row:row + 1, :] = jnp.sum(acc[i], 0, keepdims=True)
        for row in (1, 2, 3, 5):
            own_sums[0, row:row + 1, :] = sums_in[0, row:row + 1, :]
        own_sums[1] = sums_in[1]
        last.along_c()
        units[1][2]()
        units[0][3]()
        all_totals(Total.along_y)
        last.along_x()
        units[2][2]()
        units[0][4]()
        units[1][3]()
        all_totals(Total.along_z)
        last.along_y()
        units[1][4]()
        units[2][3]()
        last.along_z()
        all_totals(Total.finish)
        units[2][4]()
        last.finish()
        for t in totals:
            t.end()
        for i, shape in enumerate(((SIDE_L, 47, 24), (SIDE_S, 29, 16))):
            result, whole = scr[-3 - 2 * nt + i], scr[-3 - nt + i]
            make_table(result.at[0], result.at[1], whole, *shape)
            tab_outs[i][...] = whole[:H, :tab_outs[i].shape[1]]
        scatter.end()
        last.end()
        for m in moves:
            m.finish()

    flat = pltpu.VMEM((rows, width), BF)
    scratch = [
        pltpu.VMEM(df.shape, BF), pltpu.VMEM(dm.shape, F32), flat, pltpu.VMEM(x_s.shape, BF),
        pltpu.VMEM(w_qkv.shape, BF), flat, pltpu.VMEM((width, rows), BF), pltpu.VMEM((rows, width), F32),
        pltpu.VMEM((4, 8, width), F32), pltpu.VMEM((2, 8, width), F32),
        pltpu.VMEM(x_l.shape, BF), pltpu.VMEM(x_s.shape, BF), pltpu.VMEM((width, 2 * wide), BF),
    ] + Scatter.scratch_xzy(zs, k, cols, panels)
    for t in list(tables) + [sums]:
        scratch += Total.scratch(zs, t.shape[1], t.shape[2])
    scratch += [pltpu.VMEM(t.shape, F32) for t in tables] + [pltpu.VMEM((16, w), F32) for w in (TABLE_L, TABLE_S)]
    remotes = 3 * (large + 1) + Scatter.remotes(zs, panels, 1) + Total.remotes(zs) * (nt + 1)
    locals_ = 4 * large + 1 + 4 + large + 1 + 1 + 2 * (nt + 1)
    f32 = lambda s: jax.ShapeDtypeStruct(s, F32)
    return pl.pallas_call(
        kernel,
        out_shape=[jax.ShapeDtypeStruct((4 * a.shape[0],) + a.shape[2:], BF) for a in (x_l, x_s)]
        + [f32((k, cols)), f32(sums.shape)] + [f32((H, (2 * side - 1) ** 2)) for side in (SIDE_L, SIDE_S)],
        in_specs=[ANY] * 6 + [VMEM, VMEM] + [ANY] * nt,
        out_specs=[ANY] * 4 + [VMEM] * nt,
        scratch_shapes=scratch + semaphores(remotes, locals_),
        compiler_params=pltpu.CompilerParams(collective_id=2, has_side_effects=True, vmem_limit_bytes=60 * MIB),
        name="projection_back",
    )(df, dm, n1, x_l, x_s, w_qkv, vectors, sums, *tables)


def attend_pair(hp, n, rows, size, qkv, bias, out, lse_out):
    mask = lax.broadcasted_iota(jnp.int32, (1, 128), 1) < 64
    cols = [columns(i * 64 * H + hp * 128, 128) for i in range(3)]
    q, k, v = (qkv[rows, c] for c in cols)
    outs = []
    for h in range(2):
        s = dot(head_part(q, mask, h) * BF(0.125), k, NT) + bias[2 * hp + h]
        if size == LEN_S:
            s = jnp.where(lax.broadcasted_iota(jnp.int32, (1, LEN_S), 1) < SIDE_S * SIDE_S, s, -1e30)
        o, lse = softmax_product(s, v)
        outs.append(o)
        lse_out[n, pl.ds(2 * hp + h, 1), :size] = lse
    out[rows, cols[0]] = jnp.where(mask, outs[0], outs[1]).astype(BF)


def fill_heads(start, stop, rows, bias_l, bias_s):
    low_l, high_l, low_s, high_s = rows
    lower_l = lower_offsets(SIDE_L, SIDE_L, WIDE_L)
    lower_s = lower_offsets(SIDE_S, 16, WIDE_S)

    def body(h, carry):
        at = pl.ds(h, 1)
        fill_bias(bias_l, h, spread_rows(low_l[at, :WIDE_L], high_l[at, :WIDE_L], SIDE_L, lower_l), SIDE_L, 24, 23)
        fill_bias(bias_s, h, spread_rows(low_s[at, :WIDE_S], high_s[at, :WIDE_S], 16, lower_s), SIDE_S, 16, 15)
        return carry

    lax.fori_loop(start, stop, body, 0)


def assemble(blocks, count, vectors, up_vec):
    row = lax.broadcasted_iota(jnp.int32, (16, 128), 0)
    vectors[...] = jnp.zeros_like(vectors)
    up_vec[...] = jnp.zeros_like(up_vec)
    width = vectors.shape[1] - 128
    own, own_up = width // count, 4 * width // count

    def shifted(part, offset):
        part = jnp.concatenate([part, jnp.zeros_like(part)], 1)
        return pltpu.roll(part, offset % 128, 1) if offset % 128 else part

    for d in range(count):
        block = blocks[d].astype(BF).astype(F32)
        offset = d * own
        base = offset // 128 * 128
        vectors[:, base:base + 256] += shifted(jnp.where(row < 10, block, 0.0), offset)
        at, offset = d * own_up // width, d * own_up % width
        base = offset // 128 * 128
        up_vec[at:at + 1, base:base + 256] += shifted(block[10:11], offset)


def front(img_size, arrays, block, shards, cuts, firsts, table_l, table_s):
    na, nw = len(arrays), len(shards)
    zs = img_size // 2
    large, small = arrays[0].shape[0] // 4, arrays[1].shape[0] // 4
    width = arrays[0].shape[2]
    rows = large * LEN_L + small * LEN_S
    count = 4 * img_size
    whole_shapes = [(a.shape[0] // 4, 4) + a.shape[1:] for a in arrays]
    full_shapes = [full_shape(img_size, s, c[0]) for s, c in zip(shards, cuts)]
    panels, wide = cuts[0][0], full_shapes[0][-1]

    def kernel(*refs):
        ins, blk, sh, tabs, whole, full, outs, scr = split_refs(refs, na, 1, nw, 2, na, nw, 6)
        qkv_hbm, n1_hbm, att, lse, vec_out, up_out = outs
        flat, four, w_v, qkv, bias_l, bias_s, small_v, vectors, up_vec = scr[:9]
        gather_scr = scr[13:13 + 2 * nw]
        p = Place(img_size)
        greet(p.partners())
        copies = Copies(*scr[-3:])
        gathers = [
            Gather(p, copies, sh[i], full[i], gather_scr[2 * i], gather_scr[2 * i + 1], cuts[i][1]) for i in range(nw)
        ]
        moves = [Move(p, copies, ins[0], whole[0], True, n) for n in range(large)]
        small_move = Move(p, copies, ins[1], whole[1], True)
        gathers[0].exchange()
        small_move.start()
        first = pipelined(Spread(p, copies, blk[0], small_v).units() + gathers[0].units())
        y_units, x_units = [], []
        for g, x_first in zip(gathers[1:-1], firsts):
            for at, unit in enumerate(g.units(None, x_first)):
                (x_units if at in x_first else y_units).append(unit)
        z_units = gathers[-1].units(gathers[-1].over_z)
        fill = functools.partial(fill_heads, rows=scr[9:13], bias_l=bias_l, bias_s=bias_s)
        for t in range(3):
            first[t]()
        for g in gathers[1:]:
            g.exchange()
        for table, turned, rows_, shape in (
            (tabs[0], scr[-5], scr[9:11], (SIDE_L, 47, 0)), (tabs[1], scr[-4], scr[11:13], (SIDE_S, 29, 2))
        ):
            turn_lanes(table, turned)
            make_rows(turned, *rows_, *shape, turned.shape[1] - (2 * shape[0] - 1) ** 2)
        fill(0, 4)
        first[3]()
        fill(4, 8)
        first[4]()
        moves[0].start()
        for unit in y_units + x_units:
            unit[0]()
        fill(8, 12)
        assemble(small_v.reshape(count, 16, 128), count, vectors, up_vec)
        vec_out[...] = vectors[:, :width]
        up_out[...] = up_vec[:4, :width]
        first[5]()
        for unit in y_units:
            unit[1]()
        first[6]()
        for m in moves[1:]:
            m.start()
        first[7]()
        w_load = copies.here(lambda: (full[0], w_v))
        w_load.start()
        for unit in x_units:
            unit[1]()
        half = (len(y_units) + 1) // 2
        groups = [[unit[2] for unit in y_units[:half]], [unit[2] for unit in x_units[:1]],
                  [unit[2] for unit in y_units[half:]], [unit[2] for unit in x_units[1:]],
                  [unit[0] for unit in z_units]]
        groups += [[unit[3]] for unit in y_units + x_units]
        groups.append([unit[4] for unit in y_units + x_units] + [unit[1] for unit in z_units])
        steps = [in_turn(*group) for group in groups]
        gain, shift = vectors[0:1, :width], vectors[4:5, :width]
        x_load = copies.locals
        copies.locals += 4 * large
        points = loop_points(steps, 1)

        def loads(n):
            return [
                pltpu.make_async_copy(
                    whole[0].at[n, j], flat.at[pl.ds((n * 4 + j) * (LEN_L // 4), LEN_L // 4)],
                    copies.local.at[x_load + n * 4 + j])
                for j in range(4)
            ]

        def project(start, size):
            rows_ = pl.ds(start, size)
            hat, _ = norm_parts(flat[rows_, :].astype(F32))
            n1 = (hat * gain + shift).astype(BF)
            flat[rows_, :] = n1
            for u in range(panels):
                w = jnp.concatenate([w_v[u, c].reshape(width, wide) for c in range(2)], 1)
                got = dot(n1, w, NN)
                for c in range(2):
                    at = (c * panels + u) * wide
                    part = got[:, c * wide:(c + 1) * wide]
                    if at + wide <= width:
                        part += vectors[6:7, at:at + wide]
                    elif at >= 2 * width:
                        part += vectors[7:8, at - 2 * width:at - 2 * width + wide]
                    qkv[rows_, at:at + wide] = part.astype(BF)

        def image(n, carry):
            for i in range(large):
                @pl.when(n == i)
                def _():
                    moves[i].finish()
                    for copy in loads(i):
                        copy.start()
                    for copy in loads(i):
                        copy.wait()
                    if i == 0:
                        w_load.wait()

            start = pl.multiple_of(n * LEN_L, 16)
            project(start, LEN_L)

            def body(hp, inner):
                run_point(points, n * (H // 2) + hp, 0, 1, large * (H // 2))
                attend_pair(hp, n, pl.ds(start, LEN_L), LEN_L, qkv, bias_l, att, lse)
                return inner

            lax.fori_loop(0, H // 2, body, 0)
            return carry

        lax.fori_loop(0, large, image, 0)
        small_move.finish()
        small_load = copies.here(lambda: (whole[1], four))
        small_load.start()
        small_load.wait()
        join_small(flat, four, large)
        for n in range(small):
            start = large * LEN_L + n * LEN_S
            project(start, LEN_S)

            def body(hp, inner):
                attend_pair(hp, large + n, pl.ds(start, LEN_S), LEN_S, qkv, bias_s, att, lse)
                return inner

            lax.fori_loop(0, H // 2, body, 0)
        out = [copies.here(lambda: (qkv, qkv_hbm)), copies.here(lambda: (flat, n1_hbm))]
        for copy in out:
            copy.start()
        run_rest(points, large * (H // 2))
        for copy in out:
            copy.wait()

    units = 1 + sum(a * b for a, b in cuts)
    vm = pltpu.VMEM
    return pl.pallas_call(
        kernel,
        out_shape=[jax.ShapeDtypeStruct(s, BF) for s in whole_shapes + full_shapes + [(rows, 3 * width), (rows, width), (rows, width)]]
        + [jax.ShapeDtypeStruct(s, F32) for s in ((large + small, 16, 640), (16, width), (4, width))],
        in_specs=[ANY] * (na + 1 + nw) + [VMEM, VMEM],
        out_specs=[ANY] * (na + nw + 2) + [VMEM] * 4,
        scratch_shapes=[
            vm((rows, width), BF), vm(whole_shapes[1], BF), vm(full_shapes[0], BF), vm((rows, 3 * width), BF),
            vm((H, LEN_L, LEN_L), F32), vm((H, LEN_S, LEN_S), F32), vm((zs, 2, 2, 2, 16, 128), F32),
            vm((16, width + 128), F32), vm((8, width + 128), F32),
        ] + row_scratch() + [s for w in shards for s in Gather.scratch(w.shape)]
        + [vm((16, TABLE_L), F32), vm((16, TABLE_S), F32)]
        + semaphores(3 * (large + 1) + (zs + 2) * units + nw, large + 1 + nw + units + 4 * large + 1 + 1 + 2),
        compiler_params=pltpu.CompilerParams(collective_id=0, has_side_effects=True, vmem_limit_bytes=56 * MIB),
        name="front",
    )(*arrays, block, *shards, table_l, table_s)


def gelu_parts(u):
    cdf = 0.5 * lax.erf(0.7071067811865476 * u) + 0.5
    bell = jnp.exp2(-0.7213475204444817 * (u * u))
    return u * cdf, cdf + u * (0.3989422804014327 * bell)


def joined(w, *at):
    parts = [w[(at[0], c) + at[1:]] for c in range(2)]
    return jnp.concatenate([part.reshape(-1, part.shape[-1]) for part in parts], 1)


def image_rows(large, small):
    parts = [(n, j, (n * 4 + j) * (LEN_L // 4)) for n in range(large) for j in range(4)]
    return parts, [(n, large * LEN_L + n * LEN_S) for n in range(small)]


def forward_tail(img_size, att, x_l, x_s, ct_l, ct_s, w_out, w_up, w_down, cut, vectors, up_vec):
    large, small = x_l.shape[0], x_s.shape[0]
    rows, width = att.shape
    chunks = up_vec.shape[0]
    half = rows // 2
    direct = img_size is not None
    down_shape = w_down.shape
    bf = lambda *s: jax.ShapeDtypeStruct(s, BF)
    more = [bf(*down_shape), bf(*x_l.shape), bf(*x_s.shape)] if direct else []

    def kernel(att_hbm, xl_hbm, xs_hbm, cl_hbm, cs_hbm, wo_hbm, wu_hbm, wd_in, vec, upv, *refs):
        outs, extra, scr = split_refs(refs, 9, len(more))
        yl, ys, m_hbm, n2_hbm, e_hbm, g_hbm, dr_hbm, dy_hbm, sums = outs
        att_v, flat, four, ct_four, wo, wu, wd, m_v, n2_v, e_v, g_v, acc = scr[:12]
        u_v = scr[12:14]
        copies = Copies(*scr[-3:])
        first = [copies.here(lambda: (att_hbm, att_v)), copies.here(lambda: (wo_hbm, wo))]
        first += load_tokens(copies, xl_hbm, xs_hbm, flat, four)
        second = copies.here(lambda: (wu_hbm, wu))
        for copy in first + [second]:
            copy.start()
        early, steps, moves = [], [], []
        wd_hbm, ct = wd_in, (cl_hbm, cs_hbm)
        if direct:
            p = Place(img_size)
            greet(p.partners())
            wd_hbm, ct = extra[0], extra[1:]
            gather = Gather(p, copies, None, wd_hbm, None, None, cut[1])
            moves = [Move(p, copies, a, b, True) for a, b in zip((cl_hbm, cs_hbm), ct)]
            units = gather.units(gather.over_yx)
            units[0][0]()
            early = [in_turn(units[t][1], units[t + 1][0]) for t in range(len(units) - 1)]
            early.append(in_turn(units[-1][1], *[m.start for m in moves]))
            steps = [unit[2] for unit in units[:-1]]
            steps.append(in_turn(units[-1][2], *[unit[3] for unit in units]))
        for copy in first:
            copy.wait()
        join_small(flat, four, large)
        g2, s1, s2, b2, bo, bd = (vec[i:i + 1, :] for i in (1, 2, 3, 5, 8, 9))
        points = {t + 2: step for t, step in enumerate(steps)}
        w = joined(wo, 0)
        for i in range(2):
            at = slice(i * half, (i + 1) * half)
            m_v[at, :] = dot(att_v[at, :], w, NN)
        for step in early[:1]:
            step()

        def middle(start, size):
            at = pl.ds(start, size)
            m = flat[at, :].astype(F32) + s1 * (m_v[at, :] + bo)
            m_v[at, :] = m
            hat, _ = norm_parts(m)
            n2_v[at, :] = (hat * g2 + b2).astype(BF)

        row_tiles(rows, 96, middle)
        for step in early[1:2]:
            step()
        m_out = [copies.here(lambda: (m_v, m_hbm)), copies.here(lambda: (n2_v, n2_hbm))]
        for copy in m_out:
            copy.start()
        second.wait()
        out_at = copies.locals
        copies.locals += chunks

        def out(f):
            return pltpu.make_async_copy(
                g_v.at[lax.rem(f, 2)], g_hbm.at[f], copies.local.at[out_at + f])

        tops = [slice(i * half, (i + 1) * half) for i in range(2)]

        def up(i, f):
            return dot(n2_v[tops[i], :], wu[lax.rem(f, 2), f // 2].reshape(width, width), NN)

        def activate(i, f):
            e, g = gelu_parts(u_v[i][...] + upv[pl.ds(f, 1), :])
            e_v[tops[i], columns(f * width, width)] = e.astype(BF)
            g_v[lax.rem(f, 2), tops[i], :] = g.astype(BF)

        u_v[0][...] = up(0, 0)
        for step in early[2:]:
            step()

        def chunk(f, carry):
            run_point(points, f, 0, 1, chunks)

            @pl.when(f >= 2)
            def _():
                out(f - 2).wait()

            u_v[1][...] = up(1, f)
            activate(0, f)
            u_v[0][...] = up(0, jnp.minimum(f + 1, chunks - 1))
            activate(1, f)
            out(f).start()
            return carry

        lax.fori_loop(0, chunks, chunk, 0)
        run_rest(points, chunks)
        e_out = copies.here(lambda: (e_v, e_hbm))
        e_out.start()
        third = copies.here(lambda: (wd_hbm, wd))
        third.start()
        for m in moves:
            m.finish()
        loads = load_tokens(copies, *ct, flat, ct_four)
        for copy in loads:
            copy.start()
        third.wait()
        for copy in m_out:
            copy.wait()
        for copy in loads:
            copy.wait()
        join_small(flat, ct_four, large)
        for n in range(small):
            at = large * LEN_L + n * LEN_S + SIDE_S * SIDE_S // 16 * 16
            keep = lax.broadcasted_iota(jnp.int32, (32, 1), 0) < SIDE_S * SIDE_S % 16
            flat[at:at + 32, :] = jnp.where(keep, flat[at:at + 32, :].astype(F32), 0.0).astype(BF)
        acc[...] = jnp.zeros_like(acc)
        w2 = joined(wd, 0)
        part = rows // 2
        for i in range(2):
            at = slice(i * part, (i + 1) * part)
            r = dot(e_v[at, :], w2, NN) + bd
            dy = flat[at, :].astype(F32)
            dr = (s2 * dy).astype(BF)
            acc[0] += fold8(r * dy)
            acc[1] += fold8(dr.astype(F32))
            m_v[at, :] = m_v[at, :] + s2 * r
            n2_v[at, :] = dr
        last = [copies.here(lambda: (n2_v, dr_hbm)), copies.here(lambda: (flat, dy_hbm))]
        for copy in last:
            copy.start()
        for n, j, start in image_rows(large, small)[0]:
            yl[n, j] = m_v[start:start + LEN_L // 4, :].astype(BF)
        for n, start in image_rows(large, small)[1]:
            place_small(ys, m_v[start:start + LEN_S, :], n)
        for i in range(2):
            sums[i:i + 1, :] = jnp.sum(acc[i], 0, keepdims=True)
        for f in (chunks - 2, chunks - 1):
            out(f).wait()
        for copy in last + [e_out]:
            copy.wait()

    vm = pltpu.VMEM
    flat = vm((rows, width), BF)
    scratch = [
        flat, flat, vm(x_s.shape, BF), vm(x_s.shape, BF), vm(w_out.shape, BF), vm(w_up.shape, BF),
        vm(down_shape, BF), vm((rows, width), F32), flat, vm((rows, chunks * width), BF),
        vm((2, rows, width), BF), vm((2, 8, width), F32), vm((half, width), F32), vm((half, width), F32),
    ]
    units = cut[0] * cut[1]
    scratch += semaphores(6 + 3 * units, 12 + 8 * large + 2 + chunks + units + 3)
    remote = dict(collective_id=3, has_side_effects=True) if direct else {}
    return pl.pallas_call(
        kernel,
        out_shape=[bf(*x_l.shape), bf(*x_s.shape), jax.ShapeDtypeStruct((rows, width), F32), bf(rows, width),
                   bf(rows, chunks * width), bf(chunks, rows, width), bf(rows, width), bf(rows, width),
                   jax.ShapeDtypeStruct((8, width), F32)] + more,
        in_specs=[ANY] * 8 + [VMEM, VMEM],
        out_specs=[VMEM, VMEM] + [ANY] * 6 + [VMEM] + [ANY] * len(more),
        scratch_shapes=scratch,
        input_output_aliases={7: 9} if direct else {},
        compiler_params=pltpu.CompilerParams(vmem_limit_bytes=60 * MIB, **remote),
        name="forward_tail",
    )(att, x_l, x_s, ct_l, ct_s, w_out, w_up, w_down, vectors, up_vec)


def backward_head(img_size, att, m, n2, e, g, dr, dy, w_out, w_up, w_down, cut, y_first, vectors, sums_in, wholes):
    rows, width = att.shape
    chunks = g.shape[0]
    half = rows // 2
    direct = img_size is not None
    zs = img_size // 2 if direct else 0
    nw = len(wholes)
    k2, wide = w_down.shape[5:]
    cols = w_down.shape[0] * 2 * wide
    tall = k2 // cut

    def kernel(*refs):
        ins, wh, outs, blocks, scr = split_refs(refs, 12, nw, 6, nw)
        att_hbm, m_hbm, n2_hbm, e_hbm, g_hbm, dr_hbm, dy_hbm, wo_hbm, wu_hbm, wd_hbm, vec, s_in = ins
        go, gu, gd, dm_hbm, da_hbm, sums = outs
        m_v, n2_v, nt_v, e_v, g_v, dr_v, wo, wu, wd, dn, du_v, gd_v, gu_v, go_v, acc, up_acc = scr[:16]
        copies = Copies(*scr[-3:])
        pairs = [(dr_hbm, dr_v), (n2_hbm, n2_v), (wd_hbm, wd), (wu_hbm, wu), (m_hbm, m_v), (wo_hbm, wo)]
        loads = [copies.here(lambda a=a, b=b: (a, b)) for a, b in pairs]
        at_e = copies.locals
        at_g = at_e + chunks
        at_gu = at_g + chunks
        copies.locals += 3 * chunks

        def fetch_e(f):
            return pltpu.make_async_copy(
                e_hbm.at[:, columns(f * width, width)], e_v.at[lax.rem(f, 2)], copies.local.at[at_e + f])

        def fetch_g(f):
            return pltpu.make_async_copy(g_hbm.at[f], g_v.at[lax.rem(f, 2)], copies.local.at[at_g + f])

        def put(f):
            return pltpu.make_async_copy(
                gu_v.at[lax.rem(f, 2)], gu.at[lax.rem(f, 2), f // 2], copies.local.at[at_gu + f])

        loads[0].start()
        fetch_e(0).start()
        fetch_e(1).start()
        for copy in loads[1:]:
            copy.start()
        fetch_g(0).start()
        moves, steps = [], []
        if direct:
            p = Place(img_size)
            greet(p.partners())
            moves = [Move(p, copies, a, b, False) for a, b in zip(wh, blocks)]
            scatter = Scatter(p, copies, None, gd, scr[16:23], cut)
            units = scatter.units(y_first, True)
            over_c = [
                copies.remote(lambda f=f: (scatter.stage.at[:, f], scatter.from_c.at[:, f], p.at(c=1 - p.c)))
                for f in range(chunks)
            ]
            steps = [in_turn(*[copy.wait_recv for copy in over_c], units[0][1], units[1][1])]
            steps += [units[2][1]] + [unit[2] for unit in units]
            steps.append(in_turn(*[unit[3] for unit in units]))
            steps.append(in_turn(*[unit[4] for unit in units]))
        for m in moves:
            m.start()
        loads[0].wait()

        def down(f):
            fetch_e(f).wait()
            gd_v[...] = dot(e_v[lax.rem(f, 2)], dr_v[...], TN).astype(BF)
            if direct:
                for to, c in ((scatter.own, p.c), (scatter.stage, 1 - p.c)):
                    got = gd_v[:, columns(c * wide, wide)].reshape(2, 2, cut, tall, wide)
                    for r in range(cut):
                        to[r, f] = got[:, :, r]
            else:
                for c in range(2):
                    gd[0, c, f] = gd_v[:, c * wide:(c + 1) * wide].reshape(2, 2, k2, wide)

            if f + 2 < chunks:
                fetch_e(f + 2).start()
            if direct:
                over_c[f].start()

        for f in range(chunks):
            down(f)
        for step in steps[:1]:
            step()
        late = [copies.here(lambda: (att_hbm, e_v.at[0])), copies.here(lambda: (dy_hbm, e_v.at[1]))]
        for copy in late:
            copy.start()
        for copy in loads[1:4]:
            copy.wait()
        nt_v[...] = n2_v[...].T
        dn[...] = jnp.zeros_like(dn)
        g2, s1, b2, bo = (vec[i:i + 1, :] for i in (1, 2, 5, 8))
        points = loop_points(steps[1:], 1)

        def chunk(f, carry):
            run_point(points, f, 0, 1, chunks)
            slot = lax.rem(f, 2)
            fetch_g(f).wait()

            @pl.when(f + 1 < chunks)
            def _():
                fetch_g(f + 1).start()

            @pl.when(f >= 2)
            def _():
                put(f - 2).wait()

            w1 = wu[slot, f // 2].reshape(width, width)
            w2 = jnp.concatenate([wd[0, c, f].reshape(width, wide) for c in range(2)], 1)
            total = jnp.zeros((8, width), F32)
            for i in range(2):
                at = slice(i * half, (i + 1) * half)
                de = dot(dr_v[at, :], w2, NT)
                du = (de * g_v[slot, at, :].astype(F32)).astype(BF)
                du_v[at, :] = du
                total += fold8(du.astype(F32))
            up_acc[f] = total
            dn[...] += dot(du_v[...], w1, NT)
            gu_v[slot] = dot(nt_v[...], du_v[...], NN).astype(BF).reshape(gu_v.shape[1:])
            put(f).start()
            return carry

        lax.fori_loop(0, chunks, chunk, 0)
        for copy in loads[4:] + late:
            copy.wait()
        acc[...] = jnp.zeros_like(acc)
        run_some = [points[t] for t in sorted(points) if t >= chunks]
        for step in run_some[:1]:
            step()

        def norm(start, size):
            at = pl.ds(start, size)
            hat, scale = norm_parts(m_v[at, :])
            d = dn[at, :]
            acc[0] += fold8(d * hat)
            acc[1] += fold8(d)
            dm = e_v[1, at, :].astype(F32) + norm_back(d, hat, scale, g2)
            da = (s1 * dm).astype(BF)
            acc[2] += fold8(da.astype(F32))
            m_v[at, :] = dm
            du_v[at, :] = da

        row_tiles(rows, 96, norm)
        out = [copies.here(lambda: (m_v, dm_hbm))]
        out[0].start()
        for step in run_some[1:]:
            step()
        w = joined(wo, 0)
        got = dot(e_v[0], du_v[...], TN).astype(BF)
        for c in range(2):
            go_v[c] = got[:, c * (width // 2):(c + 1) * (width // 2)].reshape(go_v.shape[1:])
        out.append(copies.here(lambda: (go_v, go.at[0])))
        out[1].start()
        for i in range(2):
            at = slice(i * half, (i + 1) * half)
            n2_v[at, :] = dot(du_v[at, :], w, NT).astype(BF)
            a = dot(e_v[0, at, :], w, NN) + bo
            acc[3] += fold8(a * m_v[at, :])
        out.append(copies.here(lambda: (n2_v, da_hbm)))
        out[2].start()
        sums[...] = jnp.zeros_like(sums)
        for i, (part, row) in enumerate(((0, 1), (0, 5), (1, 0), (0, 2))):
            sums[part, row:row + 1, :] = jnp.sum(acc[i], 0, keepdims=True)
        sums[0, 3:4, :] = s_in[0:1, :]
        sums[1, 1:2, :] = s_in[1:2, :]
        for f in range(chunks):
            sums[1, 2 + f:3 + f, :] = jnp.sum(up_acc[f], 0, keepdims=True)
        for f in (chunks - 2, chunks - 1):
            put(f).wait()
        if direct:
            for copy in over_c:
                copy.wait_send()
            scatter.end()
        for copy in moves:
            copy.finish()
        for copy in out:
            copy.wait()

    bf = lambda *s: jax.ShapeDtypeStruct(s, BF)
    f32 = lambda *s: jax.ShapeDtypeStruct(s, F32)
    vm = pltpu.VMEM
    flat = vm((rows, width), BF)
    scratch = [
        vm((rows, width), F32), flat, vm((width, rows), BF), vm((2, rows, width), BF),
        vm((2, rows, width), BF), flat, vm(w_out.shape, BF), vm(w_up.shape, BF), vm(w_down.shape, BF),
        vm((rows, width), F32), flat, vm((width, width), BF), vm((2,) + w_up.shape[2:], BF),
        vm(w_out.shape[1:], BF), vm((4, 8, width), F32), vm((chunks, 8, width), F32),
    ]
    if direct:
        scratch += Scatter.scratch(zs, k2 // 2, cols, 1, cut, True)
    scratch += semaphores(max(1, 3 * nw + Scatter.remotes(zs, 1, cut) + chunks), 6 + 3 * chunks + 2 + 3 + nw + 1)
    remote = dict(collective_id=4, has_side_effects=True) if direct else {}
    return pl.pallas_call(
        kernel,
        out_shape=[bf(*w_out.shape), bf(*w_up.shape), f32(k2 // 2, cols) if direct else bf(*w_down.shape),
                   f32(rows, width), bf(rows, width), f32(2, 8, width)]
        + [bf(w.shape[0] * 4, *w.shape[2:]) for w in wholes],
        in_specs=[ANY] * 10 + [VMEM, VMEM] + [ANY] * nw,
        out_specs=[ANY, ANY, ANY if direct else VMEM, ANY, ANY, VMEM] + [ANY] * nw,
        scratch_shapes=scratch,
        compiler_params=pltpu.CompilerParams(vmem_limit_bytes=61 * MIB, **remote),
        name="backward_head",
    )(att, m, n2, e, g, dr, dy, w_out, w_up, w_down, vectors, sums_in, *wholes)


def project_in(x_l, x_s, w_qkv, vectors, merged_bias):
    large, small = x_l.shape[0], x_s.shape[0]
    rows, width = large * LEN_L + small * LEN_S, x_l.shape[3]
    panels, wide = w_qkv.shape[0], w_qkv.shape[-1]

    def kernel(xl_hbm, xs_hbm, w_hbm, vec, bias, out, flat, four, w_v, local):
        copies = Copies(None, None, local)
        loads = load_tokens(copies, xl_hbm, xs_hbm, flat, four) + [copies.here(lambda: (w_hbm, w_v))]
        for copy in loads:
            copy.start()
        for copy in loads[:-1]:
            copy.wait()
        join_small(flat, four, large)

        def normed(start, size):
            at = pl.ds(start, size)
            hat, _ = norm_parts(flat[at, :].astype(F32))
            flat[at, :] = (hat * vec[0:1, :] + vec[4:5, :]).astype(BF)

        row_tiles(rows, 96, normed)
        loads[-1].wait()
        for u in range(panels):
            for c in range(2):
                cols = slice((c * panels + u) * wide, (c * panels + u + 1) * wide)
                got = dot(flat[...], w_v[u, c].reshape(width, wide), NN) + bias[:, cols]
                out[:, cols] = got.astype(BF)

    return pl.pallas_call(
        kernel,
        out_shape=jax.ShapeDtypeStruct((rows, 3 * width), BF),
        in_specs=[ANY] * 3 + [VMEM, VMEM],
        out_specs=VMEM,
        scratch_shapes=[pltpu.VMEM((rows, width), BF), pltpu.VMEM(x_s.shape, BF), pltpu.VMEM(w_qkv.shape, BF),
                        pltpu.SemaphoreType.DMA((4 * large + 2,))],
        compiler_params=pltpu.CompilerParams(vmem_limit_bytes=40 * MIB),
        name="project_in",
    )(x_l, x_s, w_qkv, vectors, merged_bias)


def head_columns(rows, at):
    return pl.BlockSpec((rows, 128), lambda g: (0, g + at))


def attend(qkv, rows_l, rows_s, large, small):
    rows = qkv.shape[0]
    return pl.pallas_call(
        functools.partial(attend_kernel, large, small),
        grid=(H // 2,),
        out_shape=[jax.ShapeDtypeStruct((rows, 64 * H), BF),
                   jax.ShapeDtypeStruct((large + small, 16, 640), F32)],
        in_specs=[head_columns(rows, H // 2 * i) for i in range(3)]
        + [pl.BlockSpec((2, 8, WIDE_L), lambda g: (g, 0, 0)), pl.BlockSpec((2, 8, WIDE_S), lambda g: (g, 0, 0))],
        out_specs=[head_columns(rows, 0), pl.BlockSpec((large + small, 16, 640), lambda g: (0, 0, 0))],
        scratch_shapes=[pltpu.VMEM((2, LEN_L, LEN_L), F32), pltpu.VMEM((2, LEN_S, LEN_S), F32)],
        compiler_params=pltpu.CompilerParams(vmem_limit_bytes=56 * MIB),
        name="attend",
    )(qkv, qkv, qkv, rows_l, rows_s)


def layer_norm(values, gain, shift):
    average = jnp.mean(values, -1, keepdims=True)
    centered = values - average
    variance = jnp.mean(centered * centered, -1, keepdims=True)
    return centered * lax.rsqrt(variance + 1e-06) * gain + shift


def table_sums(rows, side, blocks):
    span = 2 * side - 1
    rows = jnp.roll(rows[:, :H], side - -(-side // 8) * 8, 2)
    low, high = rows[:, :, :(blocks + 1) * side].reshape(2, H, blocks + 1, side)
    square = jnp.concatenate([low[:, :blocks], high[:, 1:, :side - 1]], 2)
    square = jnp.concatenate([square[:, :span - 1], jnp.sum(square[:, span - 1:], 1, keepdims=True)], 1)
    return square.reshape(H, span * span)


def to_images(blocks):
    n = blocks.shape[0] // 4
    got = lax.all_to_all(blocks.reshape((4, n) + blocks.shape[1:]), "rows", 0, 0)
    return jnp.swapaxes(got, 0, 1)


def to_blocks(whole):
    got = lax.all_to_all(jnp.swapaxes(whole, 0, 1), "rows", 0, 0)
    return got.reshape((-1,) + got.shape[2:])


def to_panels(full, panels):
    rows, cols = full.shape
    split = full.reshape(4, 2, 2, rows // 16, 2, panels, cols // 2 // panels)
    return split.transpose(5, 4, 0, 1, 2, 3, 6)


def from_panels(split):
    rows, cols = 16 * split.shape[5], split.shape[0] * 2 * split.shape[6]
    return split.transpose(2, 3, 4, 5, 1, 0, 6).reshape(rows, cols)


CUTS = ((3, 1), (1, 1), (2, 3), (1, 3))


def on_device(img_size, small_images, large_images, w_qkv, w_out, w_up, w_down, gains, biases, up_bias,
              small_table, large_table, small_cotangent, large_cotangent):
    width = small_images.shape[2]
    axes = ("img", "rows")
    own = gains.shape[0]
    own_up = up_bias.shape[0]
    table_l, table_s = padded_table(large_table, TABLE_L), padded_table(small_table, TABLE_S)
    direct = own % 8 == 0
    if direct:
        block = jnp.concatenate([gains.T, biases.T], 0)
        block = jnp.pad(block, ((0, 0), (0, own_up - own)))
        block = jnp.pad(jnp.concatenate([block, up_bias[None]], 0), ((0, 5), (0, 128 - own_up)))
        large_x, small_x, qkv_w, up_w, out_w, down_w, qkv, n1, attended, lse, vectors, up_vec = front(
            img_size, [large_images, small_images], block, [w_qkv, w_up, w_out, w_down],
            [CUTS[i] for i in (0, 2, 1, 3)], [(3, 4, 5), (0,)], table_l, table_s)
        large, small = large_x.shape[0], small_x.shape[0]
        large_y, small_y, m, n2, e, g, dr, dy, sums, down_w, _, _ = forward_tail(
            img_size, attended, large_x, small_x, large_cotangent, small_cotangent, out_w, up_w, down_w, CUTS[3],
            vectors, up_vec)
        grad_out, grad_up, own_down, dm, d_att, sums = backward_head(
            img_size, attended, m, n2, e, g, dr, dy, out_w, up_w, down_w, CUTS[3][1], (1,), vectors,
            sums, [])
        df, large_sums, small_sums, own_out, own_up_w, large_out, small_out = attention_back(
            img_size, qkv, d_att, attended, lse, table_l, table_s, [grad_out, grad_up], [1, 1],
            [large_y, small_y], large, small)
        large_grad, small_grad, own_qkv, sums, grad_large_table, grad_small_table = projection_back(
            img_size, df, dm, n1, large_x, small_x, qkv_w, vectors, sums, [large_sums, small_sums], large, small)
    else:
        large_x, small_x, large_ct, small_ct = [
            to_images(a) for a in (large_images, small_images, large_cotangent, small_cotangent)]
        large, small = large_x.shape[0], small_x.shape[0]
        qkv_w, out_w, up_w, down_w = [
            to_panels(lax.all_gather(s.astype(BF), axes, axis=0, tiled=True), c[0])
            for s, c in zip((w_qkv, w_out, w_up, w_down), CUTS)]
        vectors = lax.all_gather(jnp.concatenate([gains, biases], 1).astype(BF), axes, axis=0, tiled=True)
        vectors = jnp.pad(vectors.astype(F32).T, ((0, 6), (0, 0)))
        up_vec = lax.all_gather(up_bias.astype(BF), axes, axis=0, tiled=True).astype(F32).reshape(-1, width)
        merged_bias = jnp.concatenate([vectors[6:7], jnp.zeros((1, width), F32), vectors[7:8]], 1)
        qkv = project_in(large_x, small_x, qkv_w, vectors, merged_bias)
        attended, lse = attend(
            qkv, table_rows(large_table, SIDE_L, 47, WIDE_L), table_rows(small_table, SIDE_S, 29, WIDE_S), large, small)
        large_y, small_y, m, n2, e, g, dr, dy, sums = forward_tail(
            None, attended, large_x, small_x, large_ct, small_ct, out_w, up_w, down_w, (1, 1), vectors, up_vec)
        grad_out, grad_up, grad_down, dm, d_att, sums = backward_head(
            None, attended, m, n2, e, g, dr, dy, out_w, up_w, down_w, 1, (), vectors, sums, [])
        df, large_sums, small_sums = attention_back(
            img_size, qkv, d_att, attended, lse, table_l, table_s, [], [], [], large, small)
        split_at = large * LEN_L
        tokens = jnp.concatenate([large_x.reshape(-1, width), small_x.reshape(-1, width)], 0).astype(F32)
        normed, pull = jax.vjp(layer_norm, tokens, vectors[0], vectors[4])
        grad_qkv = jnp.einsum("rd,re->de", normed.astype(BF), df, preferred_element_type=F32)
        d_normed = jnp.einsum("re,de->rd", df, from_panels(qkv_w), preferred_element_type=F32)
        d_tokens, grad_gain, grad_shift = pull(d_normed)
        d_tokens = (dm + d_tokens).astype(BF)
        grad_q = jnp.sum(df[:, :width].astype(F32), 0)
        grad_v = jnp.sum(df[:, 2 * width:].astype(F32), 0)
        for row, value in ((0, grad_gain), (4, grad_shift), (6, grad_q), (7, grad_v)):
            sums = sums.at[0, row].set(value)
        sums, large_sums, small_sums = lax.psum((sums, large_sums, small_sums), axes)
        grad_large_table = table_sums(large_sums, SIDE_L, 47)
        grad_small_table = table_sums(small_sums, SIDE_S, 29)
        large_grad = to_blocks(d_tokens[:split_at].reshape(large_x.shape))
        small_grad = to_blocks(d_tokens[split_at:].reshape(small_x.shape))
        large_out, small_out = to_blocks(large_y), to_blocks(small_y)
        grads = [grad_qkv] + [from_panels(g).astype(F32) for g in (grad_out, grad_up, grad_down)]
        own_qkv, own_out, own_up_w, own_down = [
            lax.psum_scatter(g, axes, scatter_dimension=0, tiled=True) for g in grads]

    index = lax.axis_index("img") * 4 + lax.axis_index("rows")
    flat_sums = sums.reshape(16, width)
    own_columns = lax.dynamic_slice(flat_sums, (0, index * own), (10, own)).T
    own_up_sums = lax.dynamic_slice(flat_sums[10:14].reshape(-1), (index * own_up,), (own_up,))
    return (
        small_out, large_out, small_grad, large_grad, own_qkv, own_out, own_up_w, own_down,
        own_columns[:, :4], own_columns[:, 4:], own_up_sums, grad_small_table, grad_large_table,
    )


def solution(mesh):
    images = P("img", "rows", None)
    matrix = P(("img", "rows"), None)
    vector = P(("img", "rows"))
    in_specs = (images, images) + (matrix,) * 6 + (vector, P(), P(), images, images)
    out_specs = (images,) * 4 + (matrix,) * 6 + (vector, P(), P())
    return jax.shard_map(
        functools.partial(on_device, mesh.shape["img"]),
        mesh=mesh, in_specs=in_specs, out_specs=out_specs, check_vma=False,
    )
```

```python
import functools

import jax
import jax.numpy as jnp
from jax import lax
from jax.experimental import pallas as pl
from jax.experimental.pallas import tpu as pltpu
from jax.sharding import PartitionSpec as P

H = 12
SIDE_S = 14
SIDE_L = 24
LEN_S = 224
LEN_L = 576
WIDE_L = 1152
WIDE_S = 512

F32 = jnp.float32
BF = jnp.bfloat16
NN = (((1,), (0,)), ((), ()))
NT = (((1,), (1,)), ((), ()))
TN = (((0,), (0,)), ((), ()))
MESH = pl.DeviceIdType.MESH
ANY = pl.BlockSpec(memory_space=pl.ANY)
VMEM = pl.BlockSpec(memory_space=pltpu.VMEM)
HIGHEST = lax.Precision.HIGHEST
MIB = 1 << 20


def dot(left, right, dims):
    return lax.dot_general(left, right, dims, preferred_element_type=F32)


class Place:
    def __init__(self, img_size):
        self.img = lax.axis_index("img")
        self.row = lax.axis_index("rows")
        self.zs = img_size // 2
        self.z, self.x = self.img // 2, self.img % 2
        self.y, self.c = self.row // 2, self.row % 2

    def at(self, z=None, x=None, y=None, c=None):
        z = self.z if z is None else z
        x = self.x if x is None else x
        y = self.y if y is None else y
        c = self.c if c is None else c
        return (z * 2 + x, y * 2 + c)

    def z_other(self, step):
        return lax.rem(self.z + step, self.zs)

    def row_other(self, step):
        return lax.rem(self.row + step, 4)

    def partners(self):
        along_z = [self.at(z=self.z_other(s)) for s in range(1, self.zs)]
        in_rows = [(self.img, self.row_other(s)) for s in range(1, 4)]
        return along_z + in_rows + [self.at(x=1 - self.x)]


def announce(partners):
    barrier = pltpu.get_barrier_semaphore()
    for p in partners:
        pl.semaphore_signal(barrier, inc=1, device_id=p, device_id_type=MESH)


def await_partners(partners):
    pl.semaphore_wait(pltpu.get_barrier_semaphore(), len(partners))


def greet(partners):
    announce(partners)
    await_partners(partners)


class Remote:
    def __init__(self, copies, build):
        self.copies, self.build, self.at = copies, build, copies.remotes
        copies.remotes += 1

    def made(self):
        src, dst, device = self.build()
        return pltpu.make_async_remote_copy(
            src_ref=src, dst_ref=dst, send_sem=self.copies.send.at[self.at], recv_sem=self.copies.recv.at[self.at],
            device_id=device, device_id_type=MESH,
        )

    def start(self):
        self.made().start()
        return self

    def wait_send(self):
        self.made().wait_send()

    def wait_recv(self):
        self.made().wait_recv()


class Local:
    def __init__(self, copies, build):
        self.copies, self.build, self.at = copies, build, copies.locals
        copies.locals += 1

    def made(self):
        return pltpu.make_async_copy(*self.build(), self.copies.local.at[self.at])

    def start(self):
        self.made().start()
        return self

    def wait(self):
        self.made().wait()


class Copies:
    def __init__(self, send, recv, local):
        self.send, self.recv, self.local = send, recv, local
        self.remotes, self.locals = 0, 0

    def remote(self, build):
        return Remote(self, build)

    def here(self, build):
        return Local(self, build)


def pipelined(units):
    depth = max(len(u) for u in units)

    def step(t):
        for f in range(depth):
            u = t - f
            if 0 <= u < len(units) and f < len(units[u]):
                units[u][f]()

    return [functools.partial(step, t) for t in range(len(units) + depth - 1)]


def in_turn(*phases):
    def step():
        for phase in phases:
            phase()

    return step


def columns(start, size):
    return pl.ds(pl.multiple_of(start, 128), size)


class Gather:
    def __init__(self, place, copies, shard, full, both, low, pieces):
        self.p, self.copies = place, copies
        self.full, self.both, self.low = full, both, low
        self.panels, self.wide = full.shape[0], full.shape[-1]
        self.k, self.half = full.shape[5] // 2, self.panels * self.wide
        self.tall = 2 * self.k // pieces
        self.pieces = pieces
        p = place

        def mine():
            return both.at[pl.ds(pl.multiple_of(p.c * self.k, 8), self.k)]

        if shard is not None:
            self.kept = copies.here(lambda: (shard.at[:, columns(p.c * self.half, self.half)], mine()))
            self.swapped = copies.remote(
                lambda: (shard.at[:, columns((1 - p.c) * self.half, self.half)], mine(), p.at(c=1 - p.c)))

    def exchange(self):
        self.kept.start()
        self.swapped.start()

    def convert(self):
        self.kept.wait()
        self.swapped.wait_recv()
        self.low[...] = self.both[...].astype(BF)

    def over_z(self, u, r):
        p = self.p
        rows = pl.ds(r * self.tall, self.tall)
        src = self.low.at[rows, pl.ds(u * self.wide, self.wide)]

        def dst():
            return self.full.at[u, p.c, p.z, p.x, p.y, rows]

        own = self.copies.here(lambda: (src, dst()))
        sent = [self.copies.remote(lambda s=s: (src, dst(), p.at(z=p.z_other(s)))) for s in range(1, p.zs)]

        def start():
            if u == 0 and r == 0:
                self.convert()
            for copy in [own] + sent:
                copy.start()

        def wait():
            own.wait()
            for copy in sent:
                copy.wait_recv()
            for copy in sent:
                copy.wait_send()
            if u == 0 and r == 0:
                self.swapped.wait_send()

        return [start, wait]

    def over_yx(self, u, r, x_first=False):
        p, full = self.p, self.full
        rows = pl.ds(r * self.tall, self.tall)
        one = lambda: full.at[u, p.c, :, p.x, p.y, rows]
        if x_first:
            first = self.twice(one, lambda: p.at(x=1 - p.x))
            second = self.twice(lambda: full.at[u, p.c, :, :, p.y, rows], lambda: p.at(y=1 - p.y))
        else:
            first = self.twice(one, lambda: p.at(y=1 - p.y))
            second = self.twice(lambda: full.at[u, p.c, :, p.x, :, rows], lambda: p.at(x=1 - p.x))
        third = self.twice(lambda: full.at[u, p.c, :, :, :, rows], lambda: p.at(c=1 - p.c))

        def next_(before, after):
            before.wait_recv()
            after.start()

        def finish():
            third.wait_recv()
            for copy in (first, second, third):
                copy.wait_send()

        return [first.start, functools.partial(next_, first, second), functools.partial(next_, second, third), finish]

    def unit(self, u, r, x_first=False):
        start, wait = self.over_z(u, r)
        after = self.over_yx(u, r, x_first)

        def second():
            wait()
            after[0]()

        return [start, second] + after[1:]

    def twice(self, part, device):
        return self.copies.remote(lambda: (part(), part(), device()))

    def units(self, kind=None, x_first=()):
        if kind is not None:
            return [kind(u, r) for u in range(self.panels) for r in range(self.pieces)]
        return [
            self.unit(u, r, u * self.pieces + r in x_first) for u in range(self.panels) for r in range(self.pieces)
        ]

    @staticmethod
    def scratch(shape):
        k, cols = shape
        return [pltpu.VMEM((2 * k, cols // 2), F32), pltpu.VMEM((2 * k, cols // 2), BF)]


class Spread:
    def __init__(self, place, copies, block, full):
        p = place

        def dst():
            return full.at[p.z, p.x, p.y, p.c]

        def twice(part, device):
            return copies.remote(lambda: (part(), part(), device()))

        self.own = copies.here(lambda: (block, dst()))
        self.over_z = [copies.remote(lambda s=s: (block, dst(), p.at(z=p.z_other(s)))) for s in range(1, p.zs)]
        self.over_y = twice(lambda: full.at[:, p.x, p.y, p.c], lambda: p.at(y=1 - p.y))
        self.over_x = twice(lambda: full.at[:, p.x, :, p.c], lambda: p.at(x=1 - p.x))
        self.over_c = twice(lambda: full.at[:, :, :, p.c], lambda: p.at(c=1 - p.c))

    def along_z(self):
        for copy in [self.own] + self.over_z:
            copy.start()

    def along_y(self):
        self.own.wait()
        for copy in self.over_z:
            copy.wait_recv()
        self.over_y.start()

    def along_x(self):
        self.over_y.wait_recv()
        self.over_x.start()

    def along_c(self):
        self.over_x.wait_recv()
        self.over_c.start()

    def finish(self):
        self.over_c.wait_recv()
        for copy in self.over_z + [self.over_y, self.over_x, self.over_c]:
            copy.wait_send()

    def units(self):
        return [[self.along_z, self.along_y, self.along_x, self.along_c, self.finish]]


class Move:
    def __init__(self, place, copies, src, dst, to_images, image=None):
        p = place
        n = (src if to_images else dst).shape[0] // 4

        def part(row):
            blocks, whole = (src, dst) if to_images else (dst, src)
            theirs, mine = (row, p.row) if to_images else (p.row, row)
            if image is None:
                found = blocks.at[pl.ds(theirs * n, n)], whole.at[:, mine]
            else:
                found = blocks.at[theirs * n + image], whole.at[image, mine]
            return found if to_images else found[::-1]

        self.own = copies.here(lambda: part(p.row))
        self.sent = [
            copies.remote(lambda s=s: part(p.row_other(s)) + ((p.img, p.row_other(s)),)) for s in (2, 3, 1)
        ]

    def start(self):
        for copy in self.sent + [self.own]:
            copy.start()

    def finish(self):
        self.own.wait()
        for copy in self.sent:
            copy.wait_recv()
        for copy in self.sent:
            copy.wait_send()


class Scatter:
    def __init__(self, place, copies, grad, shard, scratch, pieces):
        self.p, self.copies, self.grad, self.shard = place, copies, grad, shard
        self.own, self.from_c, self.from_x, self.from_y, self.from_z, self.summed = scratch[:6]
        self.stage = scratch[6] if grad is None else None
        self.k, self.cols = shard.shape
        self.half = self.cols // 2
        self.pieces = pieces
        self.panels = self.own.shape[0] // pieces
        self.wide, self.tall = self.own.shape[-1], self.own.shape[-2]
        p = place

        def cols():
            return columns(p.c * self.half, self.half)

        def rows(c):
            return pl.ds(pl.multiple_of(c * self.k, 8), self.k)

        self.last = copies.remote(
            lambda: (self.summed.at[rows(1 - p.c)], shard.at[:, cols()], p.at(c=1 - p.c)))
        self.kept = copies.here(lambda: (self.summed.at[rows(p.c)], shard.at[:, cols()]))

    def unit(self, u, r, y_first=False, given=False):
        p, copies, grad = self.p, self.copies, self.grad
        at = u * self.pieces + r
        own, from_c, from_x = self.own.at[at], self.from_c.at[at], self.from_x.at[at]
        from_y, from_z = self.from_y.at[at], self.from_z.at[at]
        rows = pl.ds(r * self.tall, self.tall)
        if grad is None:
            over_c = copies.remote(lambda: (self.stage.at[at], from_c, p.at(c=1 - p.c)))
            loaded = None
        else:
            over_c = copies.remote(lambda: (grad.at[u, 1 - p.c, :, :, :, rows], from_c, p.at(c=1 - p.c)))
            loaded = copies.here(lambda: (grad.at[u, p.c, :, :, :, rows], own))
        if y_first:
            over_x = copies.remote(lambda: (own.at[:, :, 1 - p.y], from_x, p.at(y=1 - p.y)))
            over_y = copies.remote(lambda: (own.at[:, 1 - p.x, p.y], from_y, p.at(x=1 - p.x)))
        else:
            over_x = copies.remote(lambda: (own.at[:, 1 - p.x], from_x, p.at(x=1 - p.x)))
            over_y = copies.remote(lambda: (own.at[:, p.x, 1 - p.y], from_y, p.at(y=1 - p.y)))
        over_z = [
            copies.remote(lambda s=s: (own.at[p.z_other(s), p.x, p.y], from_z.at[s - 1], p.at(z=p.z_other(s))))
            for s in range(1, p.zs)
        ]

        def add(into, other):
            into[...] = (into[...].astype(F32) + other[...].astype(F32)).astype(BF)

        def along_c():
            over_c.start()
            if loaded is not None:
                loaded.start()

        def along_x():
            if loaded is not None:
                loaded.wait()
            if not given:
                over_c.wait_recv()
            for theirs in (True, False):
                for z in range(p.zs):
                    for i in range(2):
                        where = (z, i, 1 - p.y if theirs else p.y) if y_first else (z, 1 - p.x if theirs else p.x, i)
                        add(own.at[where], from_c.at[where])
                if theirs:
                    over_x.start()

        def along_y():
            over_x.wait_recv()
            for theirs in (True, False):
                for z in range(p.zs):
                    i = p.x if y_first else p.y
                    i = 1 - i if theirs else i
                    add(own.at[(z, i, p.y) if y_first else (z, p.x, i)], from_x.at[z, i])
                if theirs:
                    over_y.start()

        def along_z():
            over_y.wait_recv()
            for z in range(p.zs):
                add(own.at[z, p.x, p.y], from_y.at[z])
            for copy in over_z:
                copy.start()

        def finish():
            for copy in over_z:
                copy.wait_recv()
            total = own[p.z, p.x, p.y].astype(F32)
            for s in range(p.zs - 1):
                total += from_z[s].astype(F32)
            self.summed[rows, pl.ds(u * self.wide, self.wide)] = total
            for copy in ([] if given else [over_c]) + [over_x, over_y] + over_z:
                copy.wait_send()
            if at == self.panels * self.pieces - 1:
                self.last.start()
                self.kept.start()

        return [along_c, along_x, along_y, along_z, finish]

    def unit_xzy(self, u):
        p, copies = self.p, self.copies
        own, from_c, from_x = self.own.at[u], self.from_c.at[u], self.from_x.at[u]
        from_z, from_y = self.from_y.at[u], self.from_z.at[u]
        over_c = copies.remote(lambda: (self.stage.at[u], from_c, p.at(c=1 - p.c)))
        over_x = copies.remote(lambda: (own.at[:, 1 - p.x], from_x, p.at(x=1 - p.x)))
        over_z = [
            copies.remote(lambda s=s: (own.at[p.z_other(s), p.x], from_z.at[s - 1], p.at(z=p.z_other(s))))
            for s in range(1, p.zs)
        ]
        over_y = copies.remote(lambda: (own.at[p.z, p.x, 1 - p.y], from_y, p.at(y=1 - p.y)))

        def add(into, other):
            into[...] = (into[...].astype(F32) + other[...].astype(F32)).astype(BF)

        def along_x():
            over_c.wait_recv()
            for x in (1 - p.x, p.x):
                for z in range(p.zs):
                    for y in range(2):
                        add(own.at[z, x, y], from_c.at[z, x, y])
                if x is not p.x:
                    over_x.start()

        def along_z():
            over_x.wait_recv()
            for s in range(1, p.zs):
                z = p.z_other(s)
                for y in range(2):
                    add(own.at[z, p.x, y], from_x.at[z, y])
                over_z[s - 1].start()
            for y in range(2):
                add(own.at[p.z, p.x, y], from_x.at[p.z, y])

        def along_y():
            for copy in over_z:
                copy.wait_recv()
            for y in (1 - p.y, p.y):
                mine = own.at[p.z, p.x, y]
                total = mine[...].astype(F32)
                for s in range(p.zs - 1):
                    total += from_z[s, y].astype(F32)
                mine[...] = total.astype(BF)
                if y is not p.y:
                    over_y.start()

        def finish():
            over_y.wait_recv()
            self.summed[:, pl.ds(u * self.wide, self.wide)] = (
                own[p.z, p.x, p.y].astype(F32) + from_y[...].astype(F32))
            for copy in [over_c, over_x, over_y] + over_z:
                copy.wait_send()
            if u == self.panels - 1:
                self.last.start()
                self.kept.start()

        return [over_c.start, along_x, along_z, along_y, finish]

    def end(self):
        self.kept.wait()
        self.last.wait_recv()
        self.last.wait_send()

    def units(self, y_first=(), given=False):
        return [
            self.unit(u, r, u * self.pieces + r in y_first, given)
            for u in range(self.panels) for r in range(self.pieces)
        ]

    @staticmethod
    def scratch(zs, k, cols, panels, pieces, staged=False):
        n, tall, w = panels * pieces, 2 * k // pieces, cols // 2 // panels
        shapes = [(n, zs, 2, 2, tall, w), (n, zs, 2, 2, tall, w), (n, zs, 2, tall, w), (n, zs, tall, w),
                  (n, zs - 1, tall, w)]
        return [pltpu.VMEM(s, BF) for s in shapes] + [pltpu.VMEM((2 * k, cols // 2), F32)] + (
            [pltpu.VMEM(shapes[0], BF)] if staged else [])

    @staticmethod
    def scratch_xzy(zs, k, cols, panels):
        w = cols // 2 // panels
        shapes = [(zs, 2, 2, 2 * k, w), (zs, 2, 2, 2 * k, w), (zs, 2, 2 * k, w), (zs - 1, 2, 2 * k, w), (2 * k, w)]
        return [pltpu.VMEM((panels,) + s, BF) for s in shapes] + [
            pltpu.VMEM((2 * k, cols // 2), F32), pltpu.VMEM((panels,) + shapes[0], BF)]

    @staticmethod
    def remotes(zs, panels, pieces):
        return 1 + panels * pieces * (zs + 2)


class Total:
    def __init__(self, place, copies, grad, result, got, work, from_z):
        self.p, self.grad, self.got, self.work, self.from_z = place, grad, got, work, from_z
        p = place
        self.kept = copies.here(lambda: (grad.at[p.c], work))
        self.over_c = copies.remote(lambda: (grad.at[1 - p.c], got.at[0], p.at(c=1 - p.c)))
        self.over_x = copies.remote(lambda: (work, got.at[1], p.at(x=1 - p.x)))
        self.over_y = copies.remote(lambda: (work, got.at[2], p.at(y=1 - p.y)))
        self.over_z = [
            copies.remote(lambda s=s: (from_z.at[p.z], from_z.at[p.z], p.at(z=p.z_other(s)))) for s in range(1, p.zs)
        ]
        self.last = [
            copies.remote(lambda: (work, result.at[p.c], p.at(c=1 - p.c))),
            copies.here(lambda: (work, result.at[p.c])),
        ]

    def along_c(self):
        self.kept.start()
        self.over_c.start()

    def along_x(self):
        self.kept.wait()
        self.over_c.wait_recv()
        self.work[...] = self.work[...] + self.got[0]
        self.over_x.start()

    def along_y(self):
        self.over_x.wait_recv()
        self.over_x.wait_send()
        self.work[...] = self.work[...] + self.got[1]
        self.over_y.start()

    def along_z(self):
        self.over_y.wait_recv()
        self.over_y.wait_send()
        self.from_z[self.p.z] = self.work[...] + self.got[2]
        for copy in self.over_z:
            copy.start()

    def finish(self):
        for copy in self.over_z:
            copy.wait_recv()
        for copy in [self.over_c] + self.over_z:
            copy.wait_send()
        total = self.from_z[0]
        for z in range(1, self.p.zs):
            total += self.from_z[z]
        self.work[...] = total
        for copy in self.last:
            copy.start()

    def end(self):
        self.last[1].wait()
        self.last[0].wait_recv()
        self.last[0].wait_send()

    def units(self):
        return [[self.along_c, self.along_x, self.along_y, self.along_z, self.finish]]

    @staticmethod
    def scratch(zs, rows, wide):
        return [pltpu.VMEM((3, rows, wide), F32), pltpu.VMEM((rows, wide), F32), pltpu.VMEM((zs, rows, wide), F32)]

    @staticmethod
    def remotes(zs):
        return zs + 3


def semaphores(remotes, locals_):
    return [
        pltpu.SemaphoreType.DMA((remotes,)),
        pltpu.SemaphoreType.DMA((remotes,)),
        pltpu.SemaphoreType.DMA((locals_,)),
    ]


def split_refs(refs, *sizes):
    parts, at = [], 0
    for size in sizes:
        parts.append(refs[at:at + size])
        at += size
    return parts + [refs[at:]]


def full_shape(img_size, shard, panels):
    k, cols = shard.shape
    return (panels, 2, img_size // 2, 2, 2, 2 * k, cols // 2 // panels)


def table_rows(table, side, blocks, wide):
    span = 2 * side - 1
    square = table.reshape(H, span, span)
    square = jnp.concatenate([square] + [square[:, -1:]] * (blocks - span), 1)
    rows = []
    for turned in (square, square[:, ::-1, ::-1]):
        for part, pads in ((turned[:, :, :side], (0, 1)), (turned[:, :, side:], (1, 0))):
            part = jnp.pad(part, ((0, 0), pads, (0, side - part.shape[2])))
            flat = part.reshape(H, 1, (blocks + 1) * side)
            rows.append(jnp.roll(jnp.pad(flat, ((0, 0), (0, 0), (0, wide - flat.shape[2]))), 1 - side, 2))
    return jnp.concatenate(rows + [jnp.zeros((H, 4, wide), F32)], 1)


def lower_offsets(side, rows, wide):
    lane = lax.rem(lax.broadcasted_iota(jnp.int32, (rows, wide), 1), side)
    return lane <= lax.broadcasted_iota(jnp.int32, (rows, wide), 0)


def spread_rows(low, high, rows, lower):
    low = jnp.broadcast_to(low, (rows, low.shape[1]))
    high = jnp.broadcast_to(high, (rows, high.shape[1]))
    return jnp.where(
        lower, pltpu.roll(low, 0, 1, stride=1, stride_axis=0), pltpu.roll(high, 0, 1, stride=1, stride_axis=0)
    )


def shifted_window(ref, source, target):
    base = source // 128 * 128
    shift = (target - source) % 128 if target % 128 >= source % 128 else target % 128 - source % 128 + 256
    part = ref[:, base:min(base + 256, ref.shape[1])]
    if part.shape[1] < 256:
        part = jnp.concatenate([part, jnp.zeros_like(part)], 1)
    return pltpu.roll(part, shift, 1) if shift else part


def window_masks(target, side):
    lane = lax.broadcasted_iota(jnp.int32, (16, 256), 1) - target % 128
    return (lane >= 0) & (lane < side), (lane >= side) & (lane < 2 * side - 1)


def turn_lanes(table, turned):
    swap = lax.broadcasted_iota(jnp.int32, (128, 128), 0) + lax.broadcasted_iota(jnp.int32, (128, 128), 1) == 127
    swap = jnp.where(swap, 1.0, 0.0)
    width = table.shape[1]
    for at in range(0, width, 128):
        turned[:, width - 128 - at:width - at] = lax.dot_general(
            table[:, at:at + 128], swap, NN, precision=HIGHEST, preferred_element_type=F32)


def make_rows(table, low, high, side, blocks, first, skip=0):
    span = 2 * side - 1
    wide = low.shape[1] - 256
    low[...] = jnp.zeros_like(low)
    high[...] = jnp.zeros_like(high)
    for a in range(blocks):
        source = min(max(a - first, 0), span - 1) * span + skip
        target = 128 + a * side - (side - 1)
        part = shifted_window(table, source, target)
        at = slice(target // 128 * 128, target // 128 * 128 + 256)
        for ref, mask in zip((low, high), window_masks(target, side)):
            ref[:, at] += jnp.where(mask, part, 0.0)
    for ref in (low, high):
        ref[:, wide:wide + 128] += ref[:, :128]
        ref[:, :wide] = ref[:, 128:128 + wide]


def make_table(low, high, table, side, blocks, height):
    span = 2 * side - 1
    table[...] = jnp.zeros_like(table)
    for a in range(blocks):
        source = a * side + height - side
        target = min(a, span - 1) * span
        at = slice(target // 128 * 128, target // 128 * 128 + 256)
        for ref, mask in zip((low, high), window_masks(target, side)):
            table[:, at] += jnp.where(mask, shifted_window(ref, source, target), 0.0)


def row_scratch():
    return [pltpu.VMEM((16, WIDE_L + 256), F32)] * 2 + [pltpu.VMEM((16, WIDE_S + 256), F32)] * 2


TABLE_L = 2560
TABLE_S = 1024


def padded_table(table, wide):
    return jnp.pad(table, ((0, 16 - H), (0, wide - table.shape[1])))


def fill_bias(bias, h, spread, side, rows, first_offset):
    size = bias.shape[2]
    wide = spread.shape[1]
    window = -(-size // 128) * 128 + 128
    for r in range(rows):
        offset = (first_offset - r) * side
        base, rest = offset // 128 * 128, offset % 128
        part = spread[:, base:min(base + window, wide)]
        if part.shape[1] < window:
            part = jnp.concatenate([part, jnp.zeros((spread.shape[0], window - part.shape[1]), F32)], 1)
        if rest:
            part = pltpu.roll(part, window - rest, 1)
        bias[h, r * side:(r + 1) * side, :] = part[:side, :size]


def fold_bias(total, h, acc, side, rows, first_offset, lower, out_ref, head):
    size = total.shape[2]
    window = -(-size // 128) * 128 + 128
    height, wide = lower.shape
    acc[...] = jnp.zeros_like(acc)
    for r in range(rows):
        offset = (first_offset - r) * side
        base, rest = offset // 128 * 128, offset % 128
        part = total[h, r * side:(r + 1) * side, :]
        part = jnp.concatenate([part, jnp.zeros((side, window - size), F32)], 1)
        if rest:
            part = pltpu.roll(part, rest, 1)
        acc[:side, base:base + window] += part
    whole = acc[:, :wide]
    zero = jnp.zeros_like(whole)
    for at, part in enumerate((jnp.where(lower, whole, zero), jnp.where(lower, zero, whole))):
        turned = jnp.concatenate([part[j:j + 1] for j in reversed(range(height))], 0)
        moved = pltpu.roll(turned, 0, 1, stride=1, stride_axis=0)
        out_ref[at, pl.ds(head, 1), :] = jnp.sum(moved, 0, keepdims=True)


def head_part(full, mask, h):
    keep = mask if h == 0 else jnp.logical_not(mask)
    return jnp.where(keep, full, jnp.zeros_like(full))


def softmax_product(s, v):
    top = jnp.max(s, 1, keepdims=True)
    e = jnp.exp(s - top)
    total = jnp.sum(e, 1, keepdims=True)
    lse = jnp.broadcast_to(top + jnp.log(total), (s.shape[0], 128)).T
    return dot(e.astype(BF), v, NN) * (1.0 / total), lse[0:1, :]


def attend_kernel(large, small, q_ref, k_ref, v_ref, rows_l, rows_s, o_ref, lse_ref, bias_l, bias_s):
    mask = lax.broadcasted_iota(jnp.int32, (1, 128), 1) < 64
    lower_l = lower_offsets(SIDE_L, SIDE_L, WIDE_L)
    lower_s = lower_offsets(SIDE_S, 16, WIDE_S)
    for h in range(2):
        fill_bias(bias_l, h, spread_rows(rows_l[h, 2:3, :], rows_l[h, 3:4, :], SIDE_L, lower_l), SIDE_L, 24, 23)
        fill_bias(bias_s, h, spread_rows(rows_s[h, 2:3, :], rows_s[h, 3:4, :], 16, lower_s), SIDE_S, 16, 15)
    keep = lax.broadcasted_iota(jnp.int32, (1, LEN_S), 1) < SIDE_S * SIDE_S
    images = [(n * LEN_L, LEN_L, bias_l) for n in range(large)]
    images += [(large * LEN_L + n * LEN_S, LEN_S, bias_s) for n in range(small)]
    for n, (at, size, bias) in enumerate(images):
        q, k, v = (ref[at:at + size, :] for ref in (q_ref, k_ref, v_ref))
        outs = []
        for h in range(2):
            s = dot(head_part(q, mask, h) * BF(0.125), k, NT) + bias[h]
            if size == LEN_S:
                s = jnp.where(keep, s, -1e30)
            out, lse = softmax_product(s, v)
            outs.append(out)
            lse_ref[n, pl.ds(2 * pl.program_id(0) + h, 1), :size] = lse
        o_ref[at:at + size, :] = jnp.where(mask, outs[0], outs[1]).astype(BF)


def loop_points(steps, every):
    return {t * every: step for t, step in enumerate(steps)}


def run_point(points, iteration, at, per, iterations):
    for i in range(iterations):
        step = points.get(i * per + at)
        if step is not None:
            pl.when(iteration == i)(step)


def run_rest(points, count):
    for at in sorted(points):
        if at >= count:
            points[at]()


def attend_back_pair(hp, qkv, do_ref, o_ref, lse_ref, rows, df, sums_l, sums_s, scratch, large, small, between):
    bias_l, bias_s, total_l, total_s, acc_l, acc_s = scratch
    mask = lax.broadcasted_iota(jnp.int32, (1, 128), 1) < 64
    lower_l = lower_offsets(SIDE_L, SIDE_L, WIDE_L)
    lower_s = lower_offsets(SIDE_S, 16, WIDE_S)
    low_l, high_l, low_s, high_s = rows
    for h in range(2):
        at = pl.ds(2 * hp + h, 1)
        fill_bias(bias_l, h, spread_rows(low_l[at, :WIDE_L], high_l[at, :WIDE_L], SIDE_L, lower_l), SIDE_L, 24, 23)
        fill_bias(bias_s, h, spread_rows(low_s[at, :WIDE_S], high_s[at, :WIDE_S], 16, lower_s), SIDE_S, 14, 13)
    keep = lax.broadcasted_iota(jnp.int32, (LEN_S, 1), 0) < SIDE_S * SIDE_S
    images = [(n * LEN_L, LEN_L, bias_l, total_l, n == 0) for n in range(large)]
    images += [(large * LEN_L + n * LEN_S, LEN_S, bias_s, total_s, n == 0) for n in range(small)]
    cols = [columns(i * 64 * H + hp * 128, 128) for i in range(3)]
    for index, (at, size, bias, total, first) in enumerate(images):
        between(index)
        rows = slice(at, at + size)
        q, k, v = (qkv[rows, c] for c in cols)
        do = do_ref[rows, cols[0]]
        products = do.astype(F32) * o_ref[rows, cols[0]].astype(F32)
        sides = lax.broadcasted_iota(jnp.int32, (8, 128), 0) == lax.broadcasted_iota(jnp.int32, (8, 128), 1) // 64
        row_dots = lax.dot_general(
            jnp.where(sides, 1.0, 0.0), products, NT, precision=HIGHEST, preferred_element_type=F32)
        got = []
        for h in range(2):
            row_dot = row_dots[h:h + 1, :]
            lse = lse_ref[index, pl.ds(2 * hp + h, 1), :size]
            s = dot(head_part(k, mask, h) * BF(0.125), q, NT) + bias[h]
            if size == LEN_S:
                s = jnp.where(keep, s, -1e30)
            p = jnp.exp(s - lse)
            ds = p * (dot(head_part(v, mask, h), do, NT) - row_dot)
            low = ds.astype(BF)
            got.append((dot(low, k, TN), dot(low, q, NN), dot(p.astype(BF), do, NN)))
            total[h] = ds if first else total[h] + ds
        for c, a, b, scale in zip(cols, got[0], got[1], (0.125, 0.125, 1.0)):
            df[rows, c] = (jnp.where(mask, a, b) * scale).astype(BF)
    for h in range(2):
        fold_bias(total_l, h, acc_l, SIDE_L, 24, 23, lower_l, sums_l, 2 * hp + h)
        fold_bias(total_s, h, acc_s, SIDE_S, 14, 13, lower_s, sums_s, 2 * hp + h)


def back_scratch():
    return [pltpu.VMEM((2, LEN_L, LEN_L), F32), pltpu.VMEM((2, LEN_S, LEN_S), F32)] * 2 + [
        pltpu.VMEM((SIDE_L, WIDE_L + 128), F32), pltpu.VMEM((16, WIDE_S + 128), F32)]


BACK_POINTS = {
    1: ((0, 1),), 3: ((1, 1),), 7: ((2, 1), (0, 2)), 9: ((1, 2), (0, 3)), 13: ((2, 2), (1, 3)), 15: ((2, 3),),
    17: ((0, 4), (1, 4)), 18: ((2, 4),),
}


def attention_back(img_size, qkv, d_att, att, lse, table_l, table_s, grads, cuts, wholes, large, small):
    zs = img_size // 2
    ng, nw = len(grads), len(wholes)
    rows = qkv.shape[0]
    shard_shapes = [(g.shape[5] // 2, g.shape[0] * 2 * g.shape[6]) for g in grads]

    def kernel(*refs):
        ins, gr, wh, outs, shards, blocks, scr = split_refs(refs, 6, ng, nw, 3, ng, nw)
        qkv_hbm, do_hbm, o_hbm, lse_v, tl, ts = ins
        df_hbm, sums_l, sums_s = outs
        qkv_v, do_v, df_v, o_v = scr[:4]
        rows_ = scr[4:8]
        p = Place(img_size)
        copies = Copies(*scr[-3:])
        loads = [copies.here(lambda a=a, b=b: (a, b)) for a, b in ((qkv_hbm, qkv_v), (do_hbm, do_v), (o_hbm, o_v))]
        for copy in loads:
            copy.start()
        if ng + nw:
            announce(p.partners())
        at = 8 + 6
        scatters = []
        for i in range(ng):
            scatters.append(Scatter(p, copies, gr[i], shards[i], scr[at:at + 6], cuts[i]))
            at += 6
        moves = [Move(p, copies, a, b, False) for a, b in zip(wh, blocks)]
        units = [u for s in scatters for u in s.units()]
        points = {}
        if units:
            points = {at: in_turn(*[units[u][f] for u, f in todo]) for at, todo in BACK_POINTS.items()}
        make_rows(tl, rows_[0], rows_[1], SIDE_L, 47, 0)
        make_rows(ts, rows_[2], rows_[3], SIDE_S, 29, 0)
        sums_l[...] = jnp.zeros_like(sums_l)
        sums_s[...] = jnp.zeros_like(sums_s)
        if ng + nw:
            await_partners(p.partners())
        for unit in units:
            unit[0]()
        for m in moves:
            m.start()
        for copy in loads:
            copy.wait()

        out_at = copies.locals
        copies.locals += 3 * (H // 2)

        def out(hp):
            cols = [columns(i * 64 * H + hp * 128, 128) for i in range(3)]
            return [
                pltpu.make_async_copy(df_v.at[:, c], df_hbm.at[:, c], copies.local.at[out_at + 3 * hp + i])
                for i, c in enumerate(cols)
            ]

        def body(hp, carry):
            attend_back_pair(hp, qkv_v, do_v, o_v, lse_v, rows_, df_v, sums_l, sums_s, scr[8:14], large, small,
                             lambda index: run_point(points, hp, index, large + small, H // 2))
            for copy in out(hp):
                copy.start()
            return carry

        lax.fori_loop(0, H // 2, body, 0)
        run_rest(points, (large + small) * (H // 2))
        for s in scatters:
            s.end()
        for m in moves:
            m.finish()
        for hp in range(H // 2):
            for copy in out(hp):
                copy.wait()

    scratch = [pltpu.VMEM(a.shape, BF) for a in (qkv, d_att, qkv, att)] + row_scratch() + back_scratch()
    for g, (k, cols), cut in zip(grads, shard_shapes, cuts):
        scratch += Scatter.scratch(zs, k, cols, g.shape[0], cut)
    remotes = 3 * nw + sum(Scatter.remotes(zs, g.shape[0], c) for g, c in zip(grads, cuts))
    locals_ = 3 + 3 * (H // 2) + nw + sum(1 + g.shape[0] * c for g, c in zip(grads, cuts))
    remote = dict(collective_id=1, has_side_effects=True) if ng + nw else {}
    return pl.pallas_call(
        kernel,
        out_shape=[jax.ShapeDtypeStruct(qkv.shape, BF), jax.ShapeDtypeStruct((2, 16, WIDE_L), F32),
                   jax.ShapeDtypeStruct((2, 16, WIDE_S), F32)]
        + [jax.ShapeDtypeStruct(s, F32) for s in shard_shapes]
        + [jax.ShapeDtypeStruct((w.shape[0] * 4,) + w.shape[2:], w.dtype) for w in wholes],
        in_specs=[ANY] * 3 + [VMEM] * 3 + [ANY] * (ng + nw),
        out_specs=[ANY, VMEM, VMEM] + [ANY] * (ng + nw),
        scratch_shapes=scratch + semaphores(max(remotes, 1), locals_),
        compiler_params=pltpu.CompilerParams(vmem_limit_bytes=60 * MIB, **remote),
        name="attention_back",
    )(qkv, d_att, att, lse, table_l, table_s, *grads, *wholes)


def row_tiles(rows, tile, body):
    count = rows // tile

    def step(t, carry):
        body(pl.multiple_of(t * tile, 16), tile)
        return carry

    lax.fori_loop(0, count, step, 0)
    if rows % tile:
        body(count * tile, rows % tile)


def norm_parts(x):
    centered = x - jnp.mean(x, 1, keepdims=True)
    scale = lax.rsqrt(jnp.mean(centered * centered, 1, keepdims=True) + 1e-06)
    return centered * scale, scale


def norm_back(dn, hat, scale, gain):
    d_hat = dn * gain
    return scale * (d_hat - jnp.mean(d_hat, 1, keepdims=True) - hat * jnp.mean(d_hat * hat, 1, keepdims=True))


def fold8(values):
    return sum(values[i:i + 8] for i in range(0, values.shape[0], 8))


def place_small(ref, flat, at):
    for i in range(4):
        ref[at, i] = flat[i * 56:(i + 1) * 56].astype(ref.dtype)


def load_tokens(copies, large_hbm, small_hbm, flat, four):
    n, _, rows, _ = large_hbm.shape
    loads = [
        copies.here(lambda i=i, j=j: (large_hbm.at[i, j], flat.at[pl.ds((i * 4 + j) * rows, rows)]))
        for i in range(n) for j in range(4)
    ]
    return loads + [copies.here(lambda: (small_hbm, four))]


def join_small(flat, four, large):
    for n in range(four.shape[0]):
        rows = jnp.concatenate([four[n, i].astype(F32) for i in range(4)], 0)
        at = large * LEN_L + n * LEN_S
        flat[at:at + LEN_S, :] = rows.astype(flat.dtype)


def projection_back(img_size, df, dm, n1, x_l, x_s, w_qkv, vectors, sums, tables, large, small):
    zs = img_size // 2
    rows, width = dm.shape
    panels, _, _, _, _, k2, wide = w_qkv.shape
    k, cols = k2 // 2, panels * 2 * wide
    nt = len(tables)

    def kernel(*refs):
        ins, tabs, outs, tab_outs, scr = split_refs(refs, 8, nt, 4, nt)
        df_hbm, dm_hbm, n1_hbm, xl_hbm, xs_hbm, w_hbm, vec, sums_in = ins
        gl_out, gs_out, shard, sums_out = outs
        df_v, dm_v, flat, four, w_v, n1_v, nt_v, dn, acc, own_sums, dl, ds, grad = scr[:13]
        at = 13
        p = Place(img_size)
        copies = Copies(*scr[-3:])
        first = [copies.here(lambda: (n1_hbm, n1_v)), copies.here(lambda: (df_hbm, df_v))]
        w_load = copies.here(lambda: (w_hbm, w_v))
        later = load_tokens(copies, xl_hbm, xs_hbm, flat, four) + [copies.here(lambda: (dm_hbm, dm_v))]
        for copy in first + [w_load] + later:
            copy.start()
        greet(p.partners())
        scatter = Scatter(p, copies, None, shard, scr[at:at + 7], 1)
        at += 7
        totals = []
        for a, b in zip(tabs, scr[-3 - 2 * nt:-3 - nt]):
            totals.append(Total(p, copies, a, b, *scr[at:at + 3]))
            at += 3
        last = Total(p, copies, own_sums, sums_out, *scr[at:at + 3])
        moves = [Move(p, copies, dl, gl_out, False, n) for n in range(large)]
        moves.append(Move(p, copies, ds, gs_out, False))
        units = [scatter.unit_xzy(u) for u in range(panels)]
        for t in totals:
            t.along_c()
        first[0].wait()
        nt_v[...] = n1_v[...].T
        first[1].wait()

        def pair(ref, u, at):
            return jnp.concatenate(
                [ref[at, c * (cols // 2) + u * wide:c * (cols // 2) + (u + 1) * wide] for c in range(2)], 1)

        def gradient(u):
            grad[...] = dot(nt_v[...], pair(df_v, u, slice(None)), NN).astype(BF)
            for to, c in ((scatter.stage, 1 - p.c), (scatter.own, p.c)):
                to[u] = grad[:, columns(c * wide, wide)].reshape(zs, 2, 2, k2, wide)
            units[u][0]()

        def all_totals(phase):
            for t in totals:
                phase(t)

        gain = vec[0:1, :]

        def back(start, size):
            at_rows = pl.ds(start, size)
            hat, scale = norm_parts(flat[at_rows, :].astype(F32))
            d = dn[at_rows, :]
            acc[0] += fold8(d * hat)
            acc[1] += fold8(d)
            acc[2] += fold8(df_v[at_rows, :width].astype(F32))
            acc[3] += fold8(df_v[at_rows, 2 * width:].astype(F32))
            flat[at_rows, :] = (dm_v[at_rows, :] + norm_back(d, hat, scale, gain)).astype(BF)

        def image(start, size):
            at = slice(start, start + size)
            got = None
            for u in range(panels):
                w = jnp.concatenate([w_v[u, c].reshape(width, wide) for c in range(2)], 1)
                part = dot(pair(df_v, u, at), w, NT)
                got = part if got is None else got + part
            dn[at, :] = got
            row_tiles(size, 96, lambda at, n: back(start + at, n))

        acc[...] = jnp.zeros_like(acc)
        all_totals(Total.along_x)
        gradient(0)
        all_totals(Total.along_y)
        gradient(1)
        units[0][1]()
        all_totals(Total.along_z)
        for copy in [w_load] + later:
            copy.wait()
        join_small(flat, four, large)
        for n in range(large):
            image(n * LEN_L, LEN_L)
            for j in range(4):
                start = (n * 4 + j) * (LEN_L // 4)
                dl[n, j] = flat[start:start + LEN_L // 4, :]
            moves[n].start()
            if n == 0:
                units[1][1]()
                gradient(2)
                units[0][2]()
                all_totals(Total.finish)
            if n == 1:
                units[2][1]()
                units[1][2]()
        for n in range(small):
            start = large * LEN_L + n * LEN_S
            image(start, LEN_S)
            place_small(ds, flat[start:start + LEN_S, :].astype(F32), n)
        moves[-1].start()
        for i, row in ((0, 0), (1, 4), (2, 6), (3, 7)):
            own_sums[0, row:row + 1, :] = jnp.sum(acc[i], 0, keepdims=True)
        for row in (1, 2, 3, 5):
            own_sums[0, row:row + 1, :] = sums_in[0, row:row + 1, :]
        own_sums[1] = sums_in[1]
        last.along_c()

        def table_out(i, *shape):
            result, whole = scr[-3 - 2 * nt + i], scr[-3 - nt + i]
            make_table(result.at[0], result.at[1], whole, *shape)
            tab_outs[i][...] = whole[:H, :tab_outs[i].shape[1]]

        units[0][3]()
        for t in totals:
            t.end()
        last.along_x()
        table_out(0, SIDE_L, 47, 24)
        units[2][2]()
        units[0][4]()
        last.along_y()
        table_out(1, SIDE_S, 29, 16)
        units[1][3]()
        last.along_z()
        units[1][4]()
        units[2][3]()
        last.finish()
        units[2][4]()
        scatter.end()
        last.end()
        for m in moves:
            m.finish()

    flat = pltpu.VMEM((rows, width), BF)
    scratch = [
        pltpu.VMEM(df.shape, BF), pltpu.VMEM(dm.shape, F32), flat, pltpu.VMEM(x_s.shape, BF),
        pltpu.VMEM(w_qkv.shape, BF), flat, pltpu.VMEM((width, rows), BF), pltpu.VMEM((rows, width), F32),
        pltpu.VMEM((4, 8, width), F32), pltpu.VMEM((2, 8, width), F32),
        pltpu.VMEM(x_l.shape, BF), pltpu.VMEM(x_s.shape, BF), pltpu.VMEM((width, 2 * wide), BF),
    ] + Scatter.scratch_xzy(zs, k, cols, panels)
    for t in list(tables) + [sums]:
        scratch += Total.scratch(zs, t.shape[1], t.shape[2])
    scratch += [pltpu.VMEM(t.shape, F32) for t in tables] + [pltpu.VMEM((16, w), F32) for w in (TABLE_L, TABLE_S)]
    remotes = 3 * (large + 1) + Scatter.remotes(zs, panels, 1) + Total.remotes(zs) * (nt + 1)
    locals_ = 4 * large + 1 + 4 + large + 1 + 1 + 2 * (nt + 1)
    f32 = lambda s: jax.ShapeDtypeStruct(s, F32)
    return pl.pallas_call(
        kernel,
        out_shape=[jax.ShapeDtypeStruct((4 * a.shape[0],) + a.shape[2:], BF) for a in (x_l, x_s)]
        + [f32((k, cols)), f32(sums.shape)] + [f32((H, (2 * side - 1) ** 2)) for side in (SIDE_L, SIDE_S)],
        in_specs=[ANY] * 6 + [VMEM, VMEM] + [ANY] * nt,
        out_specs=[ANY] * 4 + [VMEM] * nt,
        scratch_shapes=scratch + semaphores(remotes, locals_),
        compiler_params=pltpu.CompilerParams(collective_id=2, has_side_effects=True, vmem_limit_bytes=60 * MIB),
        name="projection_back",
    )(df, dm, n1, x_l, x_s, w_qkv, vectors, sums, *tables)


def attend_pair(hp, n, rows, size, qkv, bias, out, lse_out):
    mask = lax.broadcasted_iota(jnp.int32, (1, 128), 1) < 64
    cols = [columns(i * 64 * H + hp * 128, 128) for i in range(3)]
    q, k, v = (qkv[rows, c] for c in cols)
    scores = [dot(head_part(q, mask, h) * BF(0.125), k, NT) for h in range(2)]
    outs = []
    for h in range(2):
        s = scores[h] + bias[2 * hp + h]
        if size == LEN_S:
            s = jnp.where(lax.broadcasted_iota(jnp.int32, (1, LEN_S), 1) < SIDE_S * SIDE_S, s, -1e30)
        o, lse = softmax_product(s, v)
        outs.append(o)
        lse_out[n, pl.ds(2 * hp + h, 1), :size] = lse
    out[rows, cols[0]] = jnp.where(mask, outs[0], outs[1]).astype(BF)


def fill_heads(start, stop, rows, bias_l, bias_s):
    low_l, high_l, low_s, high_s = rows
    lower_l = lower_offsets(SIDE_L, SIDE_L, WIDE_L)
    lower_s = lower_offsets(SIDE_S, 16, WIDE_S)

    def body(h, carry):
        at = pl.ds(h, 1)
        fill_bias(bias_l, h, spread_rows(low_l[at, :WIDE_L], high_l[at, :WIDE_L], SIDE_L, lower_l), SIDE_L, 24, 23)
        fill_bias(bias_s, h, spread_rows(low_s[at, :WIDE_S], high_s[at, :WIDE_S], 16, lower_s), SIDE_S, 16, 15)
        return carry

    lax.fori_loop(start, stop, body, 0)


def assemble(blocks, count, vectors, up_vec):
    row = lax.broadcasted_iota(jnp.int32, (16, 128), 0)
    vectors[...] = jnp.zeros_like(vectors)
    up_vec[...] = jnp.zeros_like(up_vec)
    width = vectors.shape[1] - 128
    own, own_up = width // count, 4 * width // count

    def shifted(part, offset):
        part = jnp.concatenate([part, jnp.zeros_like(part)], 1)
        return pltpu.roll(part, offset % 128, 1) if offset % 128 else part

    for d in range(count):
        block = blocks[d].astype(BF).astype(F32)
        offset = d * own
        base = offset // 128 * 128
        vectors[:, base:base + 256] += shifted(jnp.where(row < 10, block, 0.0), offset)
        at, offset = d * own_up // width, d * own_up % width
        base = offset // 128 * 128
        up_vec[at:at + 1, base:base + 256] += shifted(block[10:11], offset)


def front(img_size, arrays, block, shards, cuts, firsts, table_l, table_s):
    na, nw = len(arrays), len(shards)
    zs = img_size // 2
    large, small = arrays[0].shape[0] // 4, arrays[1].shape[0] // 4
    width = arrays[0].shape[2]
    rows = large * LEN_L + small * LEN_S
    count = 4 * img_size
    whole_shapes = [(a.shape[0] // 4, 4) + a.shape[1:] for a in arrays]
    full_shapes = [full_shape(img_size, s, c[0]) for s, c in zip(shards, cuts)]
    panels, wide = cuts[0][0], full_shapes[0][-1]

    def kernel(*refs):
        ins, blk, sh, tabs, whole, full, outs, scr = split_refs(refs, na, 1, nw, 2, na, nw, 6)
        qkv_hbm, n1_hbm, att, lse, vec_out, up_out = outs
        flat, four, w_v, qkv, bias_l, bias_s, small_v, vectors, up_vec = scr[:9]
        gather_scr = scr[13:13 + 2 * nw]
        p = Place(img_size)
        greet(p.partners())
        copies = Copies(*scr[-3:])
        gathers = [
            Gather(p, copies, sh[i], full[i], gather_scr[2 * i], gather_scr[2 * i + 1], cuts[i][1]) for i in range(nw)
        ]
        moves = [Move(p, copies, ins[0], whole[0], True, n) for n in range(large)]
        small_move = Move(p, copies, ins[1], whole[1], True)
        ct_moves = [Move(p, copies, ins[2], whole[2], True, 0), Move(p, copies, ins[3], whole[3], True)]
        gathers[0].exchange()
        small_move.start()
        first = pipelined(Spread(p, copies, blk[0], small_v).units() + gathers[0].units())
        y_units, x_units = [], []
        for g, x_first in zip(gathers[1:-1], firsts):
            for at, unit in enumerate(g.units(None, x_first)):
                (x_units if at in x_first else y_units).append(unit)
        z_units = gathers[-1].units(gathers[-1].over_z)
        fill = functools.partial(fill_heads, rows=scr[9:13], bias_l=bias_l, bias_s=bias_s)
        for t in range(3):
            first[t]()
        for g in gathers[1:]:
            g.exchange()
        for table, turned, rows_, shape in (
            (tabs[0], scr[-5], scr[9:11], (SIDE_L, 47, 0)), (tabs[1], scr[-4], scr[11:13], (SIDE_S, 29, 2))
        ):
            turn_lanes(table, turned)
            make_rows(turned, *rows_, *shape, turned.shape[1] - (2 * shape[0] - 1) ** 2)
        fill(0, 4)
        first[3]()
        fill(4, 8)
        first[4]()
        moves[0].start()
        for unit in y_units + x_units:
            unit[0]()
        fill(8, 12)
        assemble(small_v.reshape(count, 16, 128), count, vectors, up_vec)
        vec_out[...] = vectors[:, :width]
        up_out[...] = up_vec[:4, :width]
        first[5]()
        for unit in y_units:
            unit[1]()
        first[6]()
        for m in moves[1:]:
            m.start()
        first[7]()
        w_load = copies.here(lambda: (full[0], w_v))
        w_load.start()
        for unit in x_units:
            unit[1]()
        half = (len(y_units) + 1) // 2
        groups = [[unit[2] for unit in y_units[:half]], [unit[2] for unit in x_units[:1]],
                  [unit[2] for unit in y_units[half:]], [unit[2] for unit in x_units[1:]],
                  [unit[0] for unit in z_units]]
        groups += [[unit[3]] for unit in y_units + x_units]
        groups[6] = groups[6] + [m.start for m in ct_moves]
        groups.append([unit[4] for unit in y_units + x_units] + [unit[1] for unit in z_units] + [m.finish for m in ct_moves])
        steps = [in_turn(*group) for group in groups]
        gain, shift = vectors[0:1, :width], vectors[4:5, :width]
        x_load = copies.locals
        copies.locals += 4 * large
        points = loop_points(steps, 1)

        def loads(n):
            return [
                pltpu.make_async_copy(
                    whole[0].at[n, j], flat.at[pl.ds((n * 4 + j) * (LEN_L // 4), LEN_L // 4)],
                    copies.local.at[x_load + n * 4 + j])
                for j in range(4)
            ]

        def project(start, size):
            rows_ = pl.ds(start, size)
            hat, _ = norm_parts(flat[rows_, :].astype(F32))
            n1 = (hat * gain + shift).astype(BF)
            flat[rows_, :] = n1
            for u in range(panels):
                w = jnp.concatenate([w_v[u, c].reshape(width, wide) for c in range(2)], 1)
                got = dot(n1, w, NN)
                for c in range(2):
                    at = (c * panels + u) * wide
                    part = got[:, c * wide:(c + 1) * wide]
                    if at + wide <= width:
                        part += vectors[6:7, at:at + wide]
                    elif at >= 2 * width:
                        part += vectors[7:8, at - 2 * width:at - 2 * width + wide]
                    qkv[rows_, at:at + wide] = part.astype(BF)

        out_at = copies.locals
        copies.locals += 2 * (large + small)

        def outs_of(n, rows_):
            return [
                pltpu.make_async_copy(src.at[rows_], dst.at[rows_], copies.local.at[out_at + 2 * n + i])
                for i, (src, dst) in enumerate(((qkv, qkv_hbm), (flat, n1_hbm)))
            ]

        def image(n, carry):
            for i in range(large):
                @pl.when(n == i)
                def _():
                    moves[i].finish()
                    for copy in loads(i):
                        copy.start()
                    for copy in loads(i):
                        copy.wait()
                    if i == 0:
                        w_load.wait()

            start = pl.multiple_of(n * LEN_L, 16)
            project(start, LEN_L)
            for copy in outs_of(n, pl.ds(start, LEN_L)):
                copy.start()

            def body(hp, inner):
                run_point(points, n * (H // 2) + hp, 0, 1, large * (H // 2))
                attend_pair(hp, n, pl.ds(start, LEN_L), LEN_L, qkv, bias_l, att, lse)
                return inner

            lax.fori_loop(0, H // 2, body, 0)
            return carry

        lax.fori_loop(0, large, image, 0)
        small_move.finish()
        small_load = copies.here(lambda: (whole[1], four))
        small_load.start()
        small_load.wait()
        join_small(flat, four, large)
        for n in range(small):
            start = large * LEN_L + n * LEN_S
            project(start, LEN_S)
            for copy in outs_of(large + n, pl.ds(start, LEN_S)):
                copy.start()

            def body(hp, inner):
                attend_pair(hp, large + n, pl.ds(start, LEN_S), LEN_S, qkv, bias_s, att, lse)
                return inner

            lax.fori_loop(0, H // 2, body, 0)
        run_rest(points, large * (H // 2))
        for n in range(large + small):
            rows_ = pl.ds(n * LEN_L, LEN_L) if n < large else pl.ds(large * LEN_L + (n - large) * LEN_S, LEN_S)
            for copy in outs_of(n, rows_):
                copy.wait()

    units = 1 + sum(a * b for a, b in cuts)
    vm = pltpu.VMEM
    return pl.pallas_call(
        kernel,
        out_shape=[jax.ShapeDtypeStruct(s, BF) for s in whole_shapes + full_shapes + [(rows, 3 * width), (rows, width), (rows, width)]]
        + [jax.ShapeDtypeStruct(s, F32) for s in ((large + small, 16, 640), (16, width), (4, width))],
        in_specs=[ANY] * (na + 1 + nw) + [VMEM, VMEM],
        out_specs=[ANY] * (na + nw + 2) + [VMEM] * 4,
        scratch_shapes=[
            vm((rows, width), BF), vm(whole_shapes[1], BF), vm(full_shapes[0], BF), vm((rows, 3 * width), BF),
            vm((H, LEN_L, LEN_L), F32), vm((H, LEN_S, LEN_S), F32), vm((zs, 2, 2, 2, 16, 128), F32),
            vm((16, width + 128), F32), vm((8, width + 128), F32),
        ] + row_scratch() + [s for w in shards for s in Gather.scratch(w.shape)]
        + [vm((16, TABLE_L), F32), vm((16, TABLE_S), F32)]
        + semaphores(3 * (large + 3) + (zs + 2) * units + nw, large + 3 + nw + units + 4 * large + 1 + 1 + 2 * (large + small)),
        compiler_params=pltpu.CompilerParams(collective_id=0, has_side_effects=True, vmem_limit_bytes=56 * MIB),
        name="front",
    )(*arrays, block, *shards, table_l, table_s)


def gelu_parts(u):
    cdf = 0.5 * lax.erf(0.7071067811865476 * u) + 0.5
    bell = jnp.exp2(-0.7213475204444817 * (u * u))
    return u * cdf, cdf + u * (0.3989422804014327 * bell)


def joined(w, *at):
    parts = [w[(at[0], c) + at[1:]] for c in range(2)]
    return jnp.concatenate([part.reshape(-1, part.shape[-1]) for part in parts], 1)


def image_rows(large, small):
    parts = [(n, j, (n * 4 + j) * (LEN_L // 4)) for n in range(large) for j in range(4)]
    return parts, [(n, large * LEN_L + n * LEN_S) for n in range(small)]


def forward_tail(img_size, att, x_l, x_s, ct_l, ct_s, ct_part, w_out, w_up, w_down, cut, vectors, up_vec):
    large, small = x_l.shape[0], x_s.shape[0]
    rows, width = att.shape
    chunks = up_vec.shape[0]
    half = rows // 2
    direct = img_size is not None
    down_shape = w_down.shape
    bf = lambda *s: jax.ShapeDtypeStruct(s, BF)
    more = [bf(*down_shape), bf(*x_l.shape)] if direct else []

    def kernel(att_hbm, xl_hbm, xs_hbm, cl_hbm, cs_hbm, wo_hbm, wu_hbm, wd_in, vec, upv, *refs):
        refs = refs[1:] if direct else refs
        outs, extra, scr = split_refs(refs, 9, len(more))
        yl, ys, m_hbm, n2_hbm, e_hbm, g_hbm, dr_hbm, dy_hbm, sums = outs
        att_v, flat, four, ct_four, wo, wu, wd, m_v, n2_v, e_v, g_v, acc = scr[:12]
        u_v = scr[12:14]
        copies = Copies(*scr[-3:])
        first = [copies.here(lambda: (att_hbm, att_v)), copies.here(lambda: (wo_hbm, wo))]
        first += load_tokens(copies, xl_hbm, xs_hbm, flat, four)
        second = copies.here(lambda: (wu_hbm, wu))
        for copy in first + [second]:
            copy.start()
        early, steps, moves = [], [], []
        wd_hbm, ct = wd_in, (cl_hbm, cs_hbm)
        if direct:
            p = Place(img_size)
            greet(p.partners())
            wd_hbm, ct = extra[0], (extra[1], cs_hbm)
            gather = Gather(p, copies, None, wd_hbm, None, None, cut[1])
            moves = [Move(p, copies, cl_hbm, ct[0], True, n) for n in range(1, large)]
            units = [gather.over_yx(0, r, r == 1) for r in range(cut[1])]
            units[0][0]()
            units[1][0]()
            early = [in_turn(units[0][1], units[2][0]), in_turn(units[1][1], *[m.start for m in moves]), units[2][1]]
            steps = [units[0][2], units[1][2], in_turn(units[2][2], *[unit[3] for unit in units])]
        for copy in first:
            copy.wait()
        join_small(flat, four, large)
        g2, s1, s2, b2, bo, bd = (vec[i:i + 1, :] for i in (1, 2, 3, 5, 8, 9))
        points = {t + 2: step for t, step in enumerate(steps)}
        w = joined(wo, 0)
        for i in range(2):
            at = slice(i * half, (i + 1) * half)
            m_v[at, :] = dot(att_v[at, :], w, NN)
        for step in early[:1]:
            step()

        def middle(start, size):
            at = pl.ds(start, size)
            m = flat[at, :].astype(F32) + s1 * (m_v[at, :] + bo)
            m_v[at, :] = m
            hat, _ = norm_parts(m)
            n2_v[at, :] = (hat * g2 + b2).astype(BF)

        row_tiles(rows, 96, middle)
        for step in early[1:2]:
            step()
        m_out = [copies.here(lambda: (m_v, m_hbm)), copies.here(lambda: (n2_v, n2_hbm))]
        for copy in m_out:
            copy.start()
        second.wait()
        out_at = copies.locals
        copies.locals += chunks

        def out(f):
            return pltpu.make_async_copy(
                g_v.at[lax.rem(f, 2)], g_hbm.at[f], copies.local.at[out_at + f])

        tops = [slice(i * half, (i + 1) * half) for i in range(2)]

        def up(i, f):
            return dot(n2_v[tops[i], :], wu[lax.rem(f, 2), f // 2].reshape(width, width), NN)

        def activate(i, f):
            e, g = gelu_parts(u_v[i][...] + upv[pl.ds(f, 1), :])
            e_v[tops[i], columns(f * width, width)] = e.astype(BF)
            g_v[lax.rem(f, 2), tops[i], :] = g.astype(BF)

        u_v[0][...] = up(0, 0)
        for step in early[2:]:
            step()

        def chunk(f, carry):
            run_point(points, f, 0, 1, chunks)

            @pl.when(f >= 2)
            def _():
                out(f - 2).wait()

            u_v[1][...] = up(1, f)
            activate(0, f)
            u_v[0][...] = up(0, jnp.minimum(f + 1, chunks - 1))
            activate(1, f)
            out(f).start()
            return carry

        lax.fori_loop(0, chunks, chunk, 0)
        run_rest(points, chunks)
        e_out = copies.here(lambda: (e_v, e_hbm))
        e_out.start()
        third = copies.here(lambda: (wd_hbm, wd))
        third.start()
        for m in moves:
            m.finish()
        loads = load_tokens(copies, *ct, flat, ct_four)
        for copy in loads:
            copy.start()
        third.wait()
        for copy in m_out:
            copy.wait()
        for copy in loads:
            copy.wait()
        join_small(flat, ct_four, large)
        for n in range(small):
            at = large * LEN_L + n * LEN_S + SIDE_S * SIDE_S // 16 * 16
            keep = lax.broadcasted_iota(jnp.int32, (32, 1), 0) < SIDE_S * SIDE_S % 16
            flat[at:at + 32, :] = jnp.where(keep, flat[at:at + 32, :].astype(F32), 0.0).astype(BF)
        acc[...] = jnp.zeros_like(acc)
        w2 = joined(wd, 0)
        part = rows // 2
        for i in range(2):
            at = slice(i * part, (i + 1) * part)
            r = dot(e_v[at, :], w2, NN) + bd
            dy = flat[at, :].astype(F32)
            dr = (s2 * dy).astype(BF)
            acc[0] += fold8(r * dy)
            acc[1] += fold8(dr.astype(F32))
            m_v[at, :] = m_v[at, :] + s2 * r
            n2_v[at, :] = dr
        last = [copies.here(lambda: (n2_v, dr_hbm)), copies.here(lambda: (flat, dy_hbm))]
        for copy in last:
            copy.start()
        for n, j, start in image_rows(large, small)[0]:
            yl[n, j] = m_v[start:start + LEN_L // 4, :].astype(BF)
        for n, start in image_rows(large, small)[1]:
            place_small(ys, m_v[start:start + LEN_S, :], n)
        for i in range(2):
            sums[i:i + 1, :] = jnp.sum(acc[i], 0, keepdims=True)
        for f in (chunks - 2, chunks - 1):
            out(f).wait()
        for copy in last + [e_out]:
            copy.wait()

    vm = pltpu.VMEM
    flat = vm((rows, width), BF)
    scratch = [
        flat, flat, vm(x_s.shape, BF), vm(x_s.shape, BF), vm(w_out.shape, BF), vm(w_up.shape, BF),
        vm(down_shape, BF), vm((rows, width), F32), flat, vm((rows, chunks * width), BF),
        vm((2, rows, width), BF), vm((2, 8, width), F32), vm((half, width), F32), vm((half, width), F32),
    ]
    units = cut[0] * cut[1]
    scratch += semaphores(6 + 3 * units, 12 + 8 * large + 2 + chunks + units + 3)
    remote = dict(collective_id=3, has_side_effects=True) if direct else {}
    return pl.pallas_call(
        kernel,
        out_shape=[bf(*x_l.shape), bf(*x_s.shape), jax.ShapeDtypeStruct((rows, width), F32), bf(rows, width),
                   bf(rows, chunks * width), bf(chunks, rows, width), bf(rows, width), bf(rows, width),
                   jax.ShapeDtypeStruct((8, width), F32)] + more,
        in_specs=[ANY] * 8 + [VMEM, VMEM] + [ANY] * direct,
        out_specs=[VMEM, VMEM] + [ANY] * 6 + [VMEM] + [ANY] * len(more),
        scratch_shapes=scratch,
        input_output_aliases={7: 9, 10: 10} if direct else {},
        compiler_params=pltpu.CompilerParams(vmem_limit_bytes=60 * MIB, **remote),
        name="forward_tail",
    )(att, x_l, x_s, ct_l, ct_s, w_out, w_up, w_down, vectors, up_vec, *([ct_part] if direct else []))


def backward_head(img_size, att, m, n2, e, g, dr, dy, w_out, w_up, w_down, cut, y_first, vectors, sums_in, wholes):
    rows, width = att.shape
    chunks = g.shape[0]
    half = rows // 2
    direct = img_size is not None
    zs = img_size // 2 if direct else 0
    nw = len(wholes)
    k2, wide = w_down.shape[5:]
    cols = w_down.shape[0] * 2 * wide
    tall = k2 // cut

    def kernel(*refs):
        ins, wh, outs, blocks, scr = split_refs(refs, 12, nw, 6, nw)
        att_hbm, m_hbm, n2_hbm, e_hbm, g_hbm, dr_hbm, dy_hbm, wo_hbm, wu_hbm, wd_hbm, vec, s_in = ins
        go, gu, gd, dm_hbm, da_hbm, sums = outs
        m_v, n2_v, nt_v, e_v, g_v, dr_v, wo, wu, wd, dn, du_v, gd_v, gu_v, go_v, acc, up_acc = scr[:16]
        copies = Copies(*scr[-3:])
        pairs = [(dr_hbm, dr_v), (n2_hbm, n2_v), (wd_hbm, wd), (wu_hbm, wu), (m_hbm, m_v), (wo_hbm, wo)]
        loads = [copies.here(lambda a=a, b=b: (a, b)) for a, b in pairs]
        at_e = copies.locals
        at_g = at_e + chunks
        at_gu = at_g + chunks
        copies.locals += 3 * chunks

        def fetch_e(f):
            return pltpu.make_async_copy(
                e_hbm.at[:, columns(f * width, width)], e_v.at[lax.rem(f, 2)], copies.local.at[at_e + f])

        def fetch_g(f):
            return pltpu.make_async_copy(g_hbm.at[f], g_v.at[lax.rem(f, 2)], copies.local.at[at_g + f])

        def put(f):
            return pltpu.make_async_copy(
                gu_v.at[lax.rem(f, 2)], gu.at[lax.rem(f, 2), f // 2], copies.local.at[at_gu + f])

        loads[0].start()
        fetch_e(0).start()
        fetch_e(1).start()
        for copy in loads[1:]:
            copy.start()
        fetch_g(0).start()
        moves, steps = [], []
        if direct:
            p = Place(img_size)
            announce(p.partners())
            moves = [Move(p, copies, a, b, False) for a, b in zip(wh, blocks)]
            scatter = Scatter(p, copies, None, gd, scr[16:23], cut)
            units = scatter.units(y_first, True)
            over_c = [
                copies.remote(lambda f=f: (scatter.stage.at[:, f], scatter.from_c.at[:, f], p.at(c=1 - p.c)))
                for f in range(chunks)
            ]
            steps = [in_turn(*[copy.wait_recv for copy in over_c], units[0][1], units[1][1])]
            steps += [units[2][1], in_turn(units[0][2], units[1][2]), in_turn(units[0][3], units[1][3], units[2][2])]
            steps += [units[2][3], in_turn(*[unit[4] for unit in units])]
        loads[0].wait()

        def down(f):
            fetch_e(f).wait()
            gd_v[...] = dot(e_v[lax.rem(f, 2)], dr_v[...], TN).astype(BF)
            if direct:
                for to, c in ((scatter.own, p.c), (scatter.stage, 1 - p.c)):
                    got = gd_v[:, columns(c * wide, wide)].reshape(2, 2, cut, tall, wide)
                    for r in range(cut):
                        to[r, f] = got[:, :, r]
            else:
                for c in range(2):
                    gd[0, c, f] = gd_v[:, c * wide:(c + 1) * wide].reshape(2, 2, k2, wide)

            if f + 2 < chunks:
                fetch_e(f + 2).start()
            if direct:
                if f == 0:
                    await_partners(p.partners())
                    for m in moves:
                        m.start()
                over_c[f].start()

        for f in range(chunks):
            down(f)
        for step in steps[:1]:
            step()
        late = [copies.here(lambda: (att_hbm, e_v.at[0])), copies.here(lambda: (dy_hbm, e_v.at[1]))]
        for copy in late:
            copy.start()
        for copy in loads[1:4]:
            copy.wait()
        nt_v[...] = n2_v[...].T
        dn[...] = jnp.zeros_like(dn)
        g2, s1, b2, bo = (vec[i:i + 1, :] for i in (1, 2, 5, 8))
        points = {t + 1: step for t, step in enumerate(steps[1:])}

        def chunk(f, carry):
            run_point(points, f, 0, 1, chunks)
            slot = lax.rem(f, 2)
            fetch_g(f).wait()

            @pl.when(f + 1 < chunks)
            def _():
                fetch_g(f + 1).start()

            @pl.when(f >= 2)
            def _():
                put(f - 2).wait()

            w1 = wu[slot, f // 2].reshape(width, width)
            w2 = jnp.concatenate([wd[0, c, f].reshape(width, wide) for c in range(2)], 1)
            total = jnp.zeros((8, width), F32)
            for i in range(2):
                at = slice(i * half, (i + 1) * half)
                de = dot(dr_v[at, :], w2, NT)
                du = (de * g_v[slot, at, :].astype(F32)).astype(BF)
                du_v[at, :] = du
                total += fold8(du.astype(F32))
            up_acc[f] = total
            dn[...] += dot(du_v[...], w1, NT)
            gu_v[slot] = dot(nt_v[...], du_v[...], NN).astype(BF).reshape(gu_v.shape[1:])
            put(f).start()
            return carry

        lax.fori_loop(0, chunks, chunk, 0)
        for copy in loads[4:] + late:
            copy.wait()
        acc[...] = jnp.zeros_like(acc)
        run_some = [points[t] for t in sorted(points) if t >= chunks]
        for step in run_some[:1]:
            step()

        def norm(start, size):
            at = pl.ds(start, size)
            hat, scale = norm_parts(m_v[at, :])
            d = dn[at, :]
            acc[0] += fold8(d * hat)
            acc[1] += fold8(d)
            dm = e_v[1, at, :].astype(F32) + norm_back(d, hat, scale, g2)
            da = (s1 * dm).astype(BF)
            acc[2] += fold8(da.astype(F32))
            m_v[at, :] = dm
            du_v[at, :] = da

        row_tiles(rows, 96, norm)
        out = [copies.here(lambda: (m_v, dm_hbm))]
        out[0].start()
        for step in run_some[1:]:
            step()
        w = joined(wo, 0)
        got = dot(e_v[0], du_v[...], TN).astype(BF)
        for c in range(2):
            go_v[c] = got[:, c * (width // 2):(c + 1) * (width // 2)].reshape(go_v.shape[1:])
        out.append(copies.here(lambda: (go_v, go.at[0])))
        out[1].start()
        for i in range(2):
            at = slice(i * half, (i + 1) * half)
            n2_v[at, :] = dot(du_v[at, :], w, NT).astype(BF)
            a = dot(e_v[0, at, :], w, NN) + bo
            acc[3] += fold8(a * m_v[at, :])
        out.append(copies.here(lambda: (n2_v, da_hbm)))
        out[2].start()
        sums[...] = jnp.zeros_like(sums)
        for i, (part, row) in enumerate(((0, 1), (0, 5), (1, 0), (0, 2))):
            sums[part, row:row + 1, :] = jnp.sum(acc[i], 0, keepdims=True)
        sums[0, 3:4, :] = s_in[0:1, :]
        sums[1, 1:2, :] = s_in[1:2, :]
        for f in range(chunks):
            sums[1, 2 + f:3 + f, :] = jnp.sum(up_acc[f], 0, keepdims=True)
        for f in (chunks - 2, chunks - 1):
            put(f).wait()
        if direct:
            for copy in over_c:
                copy.wait_send()
            scatter.end()
        for copy in moves:
            copy.finish()
        for copy in out:
            copy.wait()

    bf = lambda *s: jax.ShapeDtypeStruct(s, BF)
    f32 = lambda *s: jax.ShapeDtypeStruct(s, F32)
    vm = pltpu.VMEM
    flat = vm((rows, width), BF)
    scratch = [
        vm((rows, width), F32), flat, vm((width, rows), BF), vm((2, rows, width), BF),
        vm((2, rows, width), BF), flat, vm(w_out.shape, BF), vm(w_up.shape, BF), vm(w_down.shape, BF),
        vm((rows, width), F32), flat, vm((width, width), BF), vm((2,) + w_up.shape[2:], BF),
        vm(w_out.shape[1:], BF), vm((4, 8, width), F32), vm((chunks, 8, width), F32),
    ]
    if direct:
        scratch += Scatter.scratch(zs, k2 // 2, cols, 1, cut, True)
    scratch += semaphores(max(1, 3 * nw + Scatter.remotes(zs, 1, cut) + chunks), 6 + 3 * chunks + 2 + 3 + nw + 1)
    remote = dict(collective_id=4, has_side_effects=True) if direct else {}
    return pl.pallas_call(
        kernel,
        out_shape=[bf(*w_out.shape), bf(*w_up.shape), f32(k2 // 2, cols) if direct else bf(*w_down.shape),
                   f32(rows, width), bf(rows, width), f32(2, 8, width)]
        + [bf(w.shape[0] * 4, *w.shape[2:]) for w in wholes],
        in_specs=[ANY] * 10 + [VMEM, VMEM] + [ANY] * nw,
        out_specs=[ANY, ANY, ANY if direct else VMEM, ANY, ANY, VMEM] + [ANY] * nw,
        scratch_shapes=scratch,
        compiler_params=pltpu.CompilerParams(vmem_limit_bytes=61 * MIB, **remote),
        name="backward_head",
    )(att, m, n2, e, g, dr, dy, w_out, w_up, w_down, vectors, sums_in, *wholes)


def project_in(x_l, x_s, w_qkv, vectors, merged_bias):
    large, small = x_l.shape[0], x_s.shape[0]
    rows, width = large * LEN_L + small * LEN_S, x_l.shape[3]
    panels, wide = w_qkv.shape[0], w_qkv.shape[-1]

    def kernel(xl_hbm, xs_hbm, w_hbm, vec, bias, out, flat, four, w_v, local):
        copies = Copies(None, None, local)
        loads = load_tokens(copies, xl_hbm, xs_hbm, flat, four) + [copies.here(lambda: (w_hbm, w_v))]
        for copy in loads:
            copy.start()
        for copy in loads[:-1]:
            copy.wait()
        join_small(flat, four, large)

        def normed(start, size):
            at = pl.ds(start, size)
            hat, _ = norm_parts(flat[at, :].astype(F32))
            flat[at, :] = (hat * vec[0:1, :] + vec[4:5, :]).astype(BF)

        row_tiles(rows, 96, normed)
        loads[-1].wait()
        for u in range(panels):
            for c in range(2):
                cols = slice((c * panels + u) * wide, (c * panels + u + 1) * wide)
                got = dot(flat[...], w_v[u, c].reshape(width, wide), NN) + bias[:, cols]
                out[:, cols] = got.astype(BF)

    return pl.pallas_call(
        kernel,
        out_shape=jax.ShapeDtypeStruct((rows, 3 * width), BF),
        in_specs=[ANY] * 3 + [VMEM, VMEM],
        out_specs=VMEM,
        scratch_shapes=[pltpu.VMEM((rows, width), BF), pltpu.VMEM(x_s.shape, BF), pltpu.VMEM(w_qkv.shape, BF),
                        pltpu.SemaphoreType.DMA((4 * large + 2,))],
        compiler_params=pltpu.CompilerParams(vmem_limit_bytes=40 * MIB),
        name="project_in",
    )(x_l, x_s, w_qkv, vectors, merged_bias)


def head_columns(rows, at):
    return pl.BlockSpec((rows, 128), lambda g: (0, g + at))


def attend(qkv, rows_l, rows_s, large, small):
    rows = qkv.shape[0]
    return pl.pallas_call(
        functools.partial(attend_kernel, large, small),
        grid=(H // 2,),
        out_shape=[jax.ShapeDtypeStruct((rows, 64 * H), BF),
                   jax.ShapeDtypeStruct((large + small, 16, 640), F32)],
        in_specs=[head_columns(rows, H // 2 * i) for i in range(3)]
        + [pl.BlockSpec((2, 8, WIDE_L), lambda g: (g, 0, 0)), pl.BlockSpec((2, 8, WIDE_S), lambda g: (g, 0, 0))],
        out_specs=[head_columns(rows, 0), pl.BlockSpec((large + small, 16, 640), lambda g: (0, 0, 0))],
        scratch_shapes=[pltpu.VMEM((2, LEN_L, LEN_L), F32), pltpu.VMEM((2, LEN_S, LEN_S), F32)],
        compiler_params=pltpu.CompilerParams(vmem_limit_bytes=56 * MIB),
        name="attend",
    )(qkv, qkv, qkv, rows_l, rows_s)


def layer_norm(values, gain, shift):
    average = jnp.mean(values, -1, keepdims=True)
    centered = values - average
    variance = jnp.mean(centered * centered, -1, keepdims=True)
    return centered * lax.rsqrt(variance + 1e-06) * gain + shift


def table_sums(rows, side, blocks):
    span = 2 * side - 1
    rows = jnp.roll(rows[:, :H], side - -(-side // 8) * 8, 2)
    low, high = rows[:, :, :(blocks + 1) * side].reshape(2, H, blocks + 1, side)
    square = jnp.concatenate([low[:, :blocks], high[:, 1:, :side - 1]], 2)
    square = jnp.concatenate([square[:, :span - 1], jnp.sum(square[:, span - 1:], 1, keepdims=True)], 1)
    return square.reshape(H, span * span)


def to_images(blocks):
    n = blocks.shape[0] // 4
    got = lax.all_to_all(blocks.reshape((4, n) + blocks.shape[1:]), "rows", 0, 0)
    return jnp.swapaxes(got, 0, 1)


def to_blocks(whole):
    got = lax.all_to_all(jnp.swapaxes(whole, 0, 1), "rows", 0, 0)
    return got.reshape((-1,) + got.shape[2:])


def to_panels(full, panels):
    rows, cols = full.shape
    split = full.reshape(4, 2, 2, rows // 16, 2, panels, cols // 2 // panels)
    return split.transpose(5, 4, 0, 1, 2, 3, 6)


def from_panels(split):
    rows, cols = 16 * split.shape[5], split.shape[0] * 2 * split.shape[6]
    return split.transpose(2, 3, 4, 5, 1, 0, 6).reshape(rows, cols)


CUTS = ((3, 1), (1, 1), (2, 3), (1, 3))


def on_device(img_size, small_images, large_images, w_qkv, w_out, w_up, w_down, gains, biases, up_bias,
              small_table, large_table, small_cotangent, large_cotangent):
    width = small_images.shape[2]
    axes = ("img", "rows")
    own = gains.shape[0]
    own_up = up_bias.shape[0]
    table_l, table_s = padded_table(large_table, TABLE_L), padded_table(small_table, TABLE_S)
    direct = own % 8 == 0
    if direct:
        block = jnp.concatenate([gains.T, biases.T], 0)
        block = jnp.pad(block, ((0, 0), (0, own_up - own)))
        block = jnp.pad(jnp.concatenate([block, up_bias[None]], 0), ((0, 5), (0, 128 - own_up)))
        large_x, small_x, large_ct, small_ct, qkv_w, up_w, out_w, down_w, qkv, n1, attended, lse, vectors, up_vec = front(
            img_size, [large_images, small_images, large_cotangent, small_cotangent], block, [w_qkv, w_up, w_out, w_down],
            [CUTS[i] for i in (0, 2, 1, 3)], [(3, 4, 5), (0,)], table_l, table_s)
        large, small = large_x.shape[0], small_x.shape[0]
        large_y, small_y, m, n2, e, g, dr, dy, sums, down_w, _ = forward_tail(
            img_size, attended, large_x, small_x, large_cotangent, small_ct, large_ct, out_w, up_w, down_w, CUTS[3],
            vectors, up_vec)
        grad_out, grad_up, own_down, dm, d_att, sums = backward_head(
            img_size, attended, m, n2, e, g, dr, dy, out_w, up_w, down_w, CUTS[3][1], (1,), vectors,
            sums, [])
        df, large_sums, small_sums, own_out, own_up_w, large_out, small_out = attention_back(
            img_size, qkv, d_att, attended, lse, table_l, table_s, [grad_out, grad_up], [1, 1],
            [large_y, small_y], large, small)
        large_grad, small_grad, own_qkv, sums, grad_large_table, grad_small_table = projection_back(
            img_size, df, dm, n1, large_x, small_x, qkv_w, vectors, sums, [large_sums, small_sums], large, small)
    else:
        large_x, small_x, large_ct, small_ct = [
            to_images(a) for a in (large_images, small_images, large_cotangent, small_cotangent)]
        large, small = large_x.shape[0], small_x.shape[0]
        qkv_w, out_w, up_w, down_w = [
            to_panels(lax.all_gather(s.astype(BF), axes, axis=0, tiled=True), c[0])
            for s, c in zip((w_qkv, w_out, w_up, w_down), CUTS)]
        vectors = lax.all_gather(jnp.concatenate([gains, biases], 1).astype(BF), axes, axis=0, tiled=True)
        vectors = jnp.pad(vectors.astype(F32).T, ((0, 6), (0, 0)))
        up_vec = lax.all_gather(up_bias.astype(BF), axes, axis=0, tiled=True).astype(F32).reshape(-1, width)
        merged_bias = jnp.concatenate([vectors[6:7], jnp.zeros((1, width), F32), vectors[7:8]], 1)
        qkv = project_in(large_x, small_x, qkv_w, vectors, merged_bias)
        attended, lse = attend(
            qkv, table_rows(large_table, SIDE_L, 47, WIDE_L), table_rows(small_table, SIDE_S, 29, WIDE_S), large, small)
        large_y, small_y, m, n2, e, g, dr, dy, sums = forward_tail(
            None, attended, large_x, small_x, large_ct, small_ct, None, out_w, up_w, down_w, (1, 1), vectors, up_vec)
        grad_out, grad_up, grad_down, dm, d_att, sums = backward_head(
            None, attended, m, n2, e, g, dr, dy, out_w, up_w, down_w, 1, (), vectors, sums, [])
        df, large_sums, small_sums = attention_back(
            img_size, qkv, d_att, attended, lse, table_l, table_s, [], [], [], large, small)
        split_at = large * LEN_L
        tokens = jnp.concatenate([large_x.reshape(-1, width), small_x.reshape(-1, width)], 0).astype(F32)
        normed, pull = jax.vjp(layer_norm, tokens, vectors[0], vectors[4])
        grad_qkv = jnp.einsum("rd,re->de", normed.astype(BF), df, preferred_element_type=F32)
        d_normed = jnp.einsum("re,de->rd", df, from_panels(qkv_w), preferred_element_type=F32)
        d_tokens, grad_gain, grad_shift = pull(d_normed)
        d_tokens = (dm + d_tokens).astype(BF)
        grad_q = jnp.sum(df[:, :width].astype(F32), 0)
        grad_v = jnp.sum(df[:, 2 * width:].astype(F32), 0)
        for row, value in ((0, grad_gain), (4, grad_shift), (6, grad_q), (7, grad_v)):
            sums = sums.at[0, row].set(value)
        sums, large_sums, small_sums = lax.psum((sums, large_sums, small_sums), axes)
        grad_large_table = table_sums(large_sums, SIDE_L, 47)
        grad_small_table = table_sums(small_sums, SIDE_S, 29)
        large_grad = to_blocks(d_tokens[:split_at].reshape(large_x.shape))
        small_grad = to_blocks(d_tokens[split_at:].reshape(small_x.shape))
        large_out, small_out = to_blocks(large_y), to_blocks(small_y)
        grads = [grad_qkv] + [from_panels(g).astype(F32) for g in (grad_out, grad_up, grad_down)]
        own_qkv, own_out, own_up_w, own_down = [
            lax.psum_scatter(g, axes, scatter_dimension=0, tiled=True) for g in grads]

    index = lax.axis_index("img") * 4 + lax.axis_index("rows")
    flat_sums = sums.reshape(16, width)
    own_columns = lax.dynamic_slice(flat_sums, (0, index * own), (10, own)).T
    own_up_sums = lax.dynamic_slice(flat_sums[10:14].reshape(-1), (index * own_up,), (own_up,))
    return (
        small_out, large_out, small_grad, large_grad, own_qkv, own_out, own_up_w, own_down,
        own_columns[:, :4], own_columns[:, 4:], own_up_sums, grad_small_table, grad_large_table,
    )


def solution(mesh):
    images = P("img", "rows", None)
    matrix = P(("img", "rows"), None)
    vector = P(("img", "rows"))
    in_specs = (images, images) + (matrix,) * 6 + (vector, P(), P(), images, images)
    out_specs = (images,) * 4 + (matrix,) * 6 + (vector, P(), P())
    return jax.shard_map(
        functools.partial(on_device, mesh.shape["img"]),
        mesh=mesh, in_specs=in_specs, out_specs=out_specs, check_vma=False,
    )
```

```python
import functools

import jax
import jax.numpy as jnp
from jax import lax
from jax.experimental import pallas as pl
from jax.experimental.pallas import tpu as pltpu
from jax.sharding import PartitionSpec as P

H = 12
SIDE_S = 14
SIDE_L = 24
LEN_S = 224
LEN_L = 576
WIDE_L = 1152
WIDE_S = 512

F32 = jnp.float32
BF = jnp.bfloat16
NN = (((1,), (0,)), ((), ()))
NT = (((1,), (1,)), ((), ()))
TN = (((0,), (0,)), ((), ()))
MESH = pl.DeviceIdType.MESH
ANY = pl.BlockSpec(memory_space=pl.ANY)
VMEM = pl.BlockSpec(memory_space=pltpu.VMEM)
HIGHEST = lax.Precision.HIGHEST
MIB = 1 << 20


def dot(left, right, dims):
    return lax.dot_general(left, right, dims, preferred_element_type=F32)


class Place:
    def __init__(self, img_size):
        self.img = lax.axis_index("img")
        self.row = lax.axis_index("rows")
        self.zs = img_size // 2
        self.z, self.x = self.img // 2, self.img % 2
        self.y, self.c = self.row // 2, self.row % 2

    def at(self, z=None, x=None, y=None, c=None):
        z = self.z if z is None else z
        x = self.x if x is None else x
        y = self.y if y is None else y
        c = self.c if c is None else c
        return (z * 2 + x, y * 2 + c)

    def z_other(self, step):
        return lax.rem(self.z + step, self.zs)

    def row_other(self, step):
        return lax.rem(self.row + step, 4)

    def partners(self):
        along_z = [self.at(z=self.z_other(s)) for s in range(1, self.zs)]
        in_rows = [(self.img, self.row_other(s)) for s in range(1, 4)]
        return along_z + in_rows + [self.at(x=1 - self.x)]


def announce(partners):
    barrier = pltpu.get_barrier_semaphore()
    for p in partners:
        pl.semaphore_signal(barrier, inc=1, device_id=p, device_id_type=MESH)


def await_partners(partners):
    pl.semaphore_wait(pltpu.get_barrier_semaphore(), len(partners))


def greet(partners):
    announce(partners)
    await_partners(partners)


class Remote:
    def __init__(self, copies, build):
        self.copies, self.build, self.at = copies, build, copies.remotes
        copies.remotes += 1

    def made(self):
        src, dst, device = self.build()
        return pltpu.make_async_remote_copy(
            src_ref=src, dst_ref=dst, send_sem=self.copies.send.at[self.at], recv_sem=self.copies.recv.at[self.at],
            device_id=device, device_id_type=MESH,
        )

    def start(self):
        self.made().start()
        return self

    def wait_send(self):
        self.made().wait_send()

    def wait_recv(self):
        self.made().wait_recv()


class Local:
    def __init__(self, copies, build):
        self.copies, self.build, self.at = copies, build, copies.locals
        copies.locals += 1

    def made(self):
        return pltpu.make_async_copy(*self.build(), self.copies.local.at[self.at])

    def start(self):
        self.made().start()
        return self

    def wait(self):
        self.made().wait()


class Copies:
    def __init__(self, send, recv, local):
        self.send, self.recv, self.local = send, recv, local
        self.remotes, self.locals = 0, 0

    def remote(self, build):
        return Remote(self, build)

    def here(self, build):
        return Local(self, build)


def pipelined(units):
    depth = max(len(u) for u in units)

    def step(t):
        for f in range(depth):
            u = t - f
            if 0 <= u < len(units) and f < len(units[u]):
                units[u][f]()

    return [functools.partial(step, t) for t in range(len(units) + depth - 1)]


def in_turn(*phases):
    def step():
        for phase in phases:
            phase()

    return step


def columns(start, size):
    return pl.ds(pl.multiple_of(start, 128), size)


class Gather:
    def __init__(self, place, copies, shard, full, both, low, pieces):
        self.p, self.copies = place, copies
        self.full, self.both, self.low = full, both, low
        self.panels, self.wide = full.shape[0], full.shape[-1]
        self.k, self.half = full.shape[5] // 2, self.panels * self.wide
        self.tall = 2 * self.k // pieces
        self.pieces = pieces
        p = place

        def mine():
            return both.at[pl.ds(pl.multiple_of(p.c * self.k, 8), self.k)]

        if shard is not None:
            self.kept = copies.here(lambda: (shard.at[:, columns(p.c * self.half, self.half)], mine()))
            self.swapped = copies.remote(
                lambda: (shard.at[:, columns((1 - p.c) * self.half, self.half)], mine(), p.at(c=1 - p.c)))

    def exchange(self):
        self.kept.start()
        self.swapped.start()

    def convert(self):
        self.kept.wait()
        self.swapped.wait_recv()
        self.low[...] = self.both[...].astype(BF)

    def over_z(self, u, r):
        p = self.p
        rows = pl.ds(r * self.tall, self.tall)
        src = self.low.at[rows, pl.ds(u * self.wide, self.wide)]

        def dst():
            return self.full.at[u, p.c, p.z, p.x, p.y, rows]

        own = self.copies.here(lambda: (src, dst()))
        sent = [self.copies.remote(lambda s=s: (src, dst(), p.at(z=p.z_other(s)))) for s in range(1, p.zs)]

        def start():
            if u == 0 and r == 0:
                self.convert()
            for copy in [own] + sent:
                copy.start()

        def wait():
            own.wait()
            for copy in sent:
                copy.wait_recv()
            for copy in sent:
                copy.wait_send()
            if u == 0 and r == 0:
                self.swapped.wait_send()

        return [start, wait]

    def over_yx(self, u, r, x_first=False):
        p, full = self.p, self.full
        rows = pl.ds(r * self.tall, self.tall)
        one = lambda: full.at[u, p.c, :, p.x, p.y, rows]
        if x_first:
            first = self.twice(one, lambda: p.at(x=1 - p.x))
            second = self.twice(lambda: full.at[u, p.c, :, :, p.y, rows], lambda: p.at(y=1 - p.y))
        else:
            first = self.twice(one, lambda: p.at(y=1 - p.y))
            second = self.twice(lambda: full.at[u, p.c, :, p.x, :, rows], lambda: p.at(x=1 - p.x))
        third = self.twice(lambda: full.at[u, p.c, :, :, :, rows], lambda: p.at(c=1 - p.c))

        def next_(before, after):
            before.wait_recv()
            after.start()

        def finish():
            third.wait_recv()
            for copy in (first, second, third):
                copy.wait_send()

        return [first.start, functools.partial(next_, first, second), functools.partial(next_, second, third), finish]

    def unit(self, u, r, x_first=False):
        start, wait = self.over_z(u, r)
        after = self.over_yx(u, r, x_first)

        def second():
            wait()
            after[0]()

        return [start, second] + after[1:]

    def twice(self, part, device):
        return self.copies.remote(lambda: (part(), part(), device()))

    def units(self, kind=None, x_first=()):
        if kind is not None:
            return [kind(u, r) for u in range(self.panels) for r in range(self.pieces)]
        return [
            self.unit(u, r, u * self.pieces + r in x_first) for u in range(self.panels) for r in range(self.pieces)
        ]

    @staticmethod
    def scratch(shape):
        k, cols = shape
        return [pltpu.VMEM((2 * k, cols // 2), F32), pltpu.VMEM((2 * k, cols // 2), BF)]


class Spread:
    def __init__(self, place, copies, block, full):
        p = place

        def dst():
            return full.at[p.z, p.x, p.y, p.c]

        def twice(part, device):
            return copies.remote(lambda: (part(), part(), device()))

        self.own = copies.here(lambda: (block, dst()))
        self.over_z = [copies.remote(lambda s=s: (block, dst(), p.at(z=p.z_other(s)))) for s in range(1, p.zs)]
        self.over_y = twice(lambda: full.at[:, p.x, p.y, p.c], lambda: p.at(y=1 - p.y))
        self.over_x = twice(lambda: full.at[:, p.x, :, p.c], lambda: p.at(x=1 - p.x))
        self.over_c = twice(lambda: full.at[:, :, :, p.c], lambda: p.at(c=1 - p.c))

    def along_z(self):
        for copy in [self.own] + self.over_z:
            copy.start()

    def along_y(self):
        self.own.wait()
        for copy in self.over_z:
            copy.wait_recv()
        self.over_y.start()

    def along_x(self):
        self.over_y.wait_recv()
        self.over_x.start()

    def along_c(self):
        self.over_x.wait_recv()
        self.over_c.start()

    def finish(self):
        self.over_c.wait_recv()
        for copy in self.over_z + [self.over_y, self.over_x, self.over_c]:
            copy.wait_send()

    def units(self):
        return [[self.along_z, self.along_y, self.along_x, self.along_c, self.finish]]


class Move:
    def __init__(self, place, copies, src, dst, to_images, image=None):
        p = place
        n = (src if to_images else dst).shape[0] // 4

        def part(row):
            blocks, whole = (src, dst) if to_images else (dst, src)
            theirs, mine = (row, p.row) if to_images else (p.row, row)
            if image is None:
                found = blocks.at[pl.ds(theirs * n, n)], whole.at[:, mine]
            else:
                found = blocks.at[theirs * n + image], whole.at[image, mine]
            return found if to_images else found[::-1]

        self.own = copies.here(lambda: part(p.row))
        self.sent = [
            copies.remote(lambda s=s: part(p.row_other(s)) + ((p.img, p.row_other(s)),)) for s in (2, 3, 1)
        ]

    def start(self):
        for copy in self.sent + [self.own]:
            copy.start()

    def finish(self):
        self.own.wait()
        for copy in self.sent:
            copy.wait_recv()
        for copy in self.sent:
            copy.wait_send()


class Scatter:
    def __init__(self, place, copies, grad, shard, scratch, pieces):
        self.p, self.copies, self.grad, self.shard = place, copies, grad, shard
        self.own, self.from_c, self.from_x, self.from_y, self.from_z, self.summed = scratch[:6]
        self.stage = scratch[6] if grad is None else None
        self.k, self.cols = shard.shape
        self.half = self.cols // 2
        self.pieces = pieces
        self.panels = self.own.shape[0] // pieces
        self.wide, self.tall = self.own.shape[-1], self.own.shape[-2]
        p = place

        def cols():
            return columns(p.c * self.half, self.half)

        def rows(c):
            return pl.ds(pl.multiple_of(c * self.k, 8), self.k)

        self.last = copies.remote(
            lambda: (self.summed.at[rows(1 - p.c)], shard.at[:, cols()], p.at(c=1 - p.c)))
        self.kept = copies.here(lambda: (self.summed.at[rows(p.c)], shard.at[:, cols()]))

    def unit(self, u, r, y_first=False, given=False):
        p, copies, grad = self.p, self.copies, self.grad
        at = u * self.pieces + r
        own, from_c, from_x = self.own.at[at], self.from_c.at[at], self.from_x.at[at]
        from_y, from_z = self.from_y.at[at], self.from_z.at[at]
        rows = pl.ds(r * self.tall, self.tall)
        if grad is None:
            over_c = copies.remote(lambda: (self.stage.at[at], from_c, p.at(c=1 - p.c)))
            loaded = None
        else:
            over_c = copies.remote(lambda: (grad.at[u, 1 - p.c, :, :, :, rows], from_c, p.at(c=1 - p.c)))
            loaded = copies.here(lambda: (grad.at[u, p.c, :, :, :, rows], own))
        if y_first:
            over_x = copies.remote(lambda: (own.at[:, :, 1 - p.y], from_x, p.at(y=1 - p.y)))
            over_y = copies.remote(lambda: (own.at[:, 1 - p.x, p.y], from_y, p.at(x=1 - p.x)))
        else:
            over_x = copies.remote(lambda: (own.at[:, 1 - p.x], from_x, p.at(x=1 - p.x)))
            over_y = copies.remote(lambda: (own.at[:, p.x, 1 - p.y], from_y, p.at(y=1 - p.y)))
        over_z = [
            copies.remote(lambda s=s: (own.at[p.z_other(s), p.x, p.y], from_z.at[s - 1], p.at(z=p.z_other(s))))
            for s in range(1, p.zs)
        ]

        def add(into, other):
            into[...] = (into[...].astype(F32) + other[...].astype(F32)).astype(BF)

        def along_c():
            over_c.start()
            if loaded is not None:
                loaded.start()

        def along_x():
            if loaded is not None:
                loaded.wait()
            if not given:
                over_c.wait_recv()
            for theirs in (True, False):
                for z in range(p.zs):
                    for i in range(2):
                        where = (z, i, 1 - p.y if theirs else p.y) if y_first else (z, 1 - p.x if theirs else p.x, i)
                        add(own.at[where], from_c.at[where])
                if theirs:
                    over_x.start()

        def along_y():
            over_x.wait_recv()
            for theirs in (True, False):
                for z in range(p.zs):
                    i = p.x if y_first else p.y
                    i = 1 - i if theirs else i
                    add(own.at[(z, i, p.y) if y_first else (z, p.x, i)], from_x.at[z, i])
                if theirs:
                    over_y.start()

        def along_z():
            over_y.wait_recv()
            for z in range(p.zs):
                add(own.at[z, p.x, p.y], from_y.at[z])
            for copy in over_z:
                copy.start()

        def finish():
            for copy in over_z:
                copy.wait_recv()
            total = own[p.z, p.x, p.y].astype(F32)
            for s in range(p.zs - 1):
                total += from_z[s].astype(F32)
            self.summed[rows, pl.ds(u * self.wide, self.wide)] = total
            for copy in ([] if given else [over_c]) + [over_x, over_y] + over_z:
                copy.wait_send()
            if at == self.panels * self.pieces - 1:
                self.last.start()
                self.kept.start()

        return [along_c, along_x, along_y, along_z, finish]

    def unit_xzy(self, u):
        p, copies = self.p, self.copies
        own, from_c, from_x = self.own.at[u], self.from_c.at[u], self.from_x.at[u]
        from_z, from_y = self.from_y.at[u], self.from_z.at[u]
        over_c = copies.remote(lambda: (self.stage.at[u], from_c, p.at(c=1 - p.c)))
        over_x = copies.remote(lambda: (own.at[:, 1 - p.x], from_x, p.at(x=1 - p.x)))
        over_z = [
            copies.remote(lambda s=s: (own.at[p.z_other(s), p.x], from_z.at[s - 1], p.at(z=p.z_other(s))))
            for s in range(1, p.zs)
        ]
        over_y = copies.remote(lambda: (own.at[p.z, p.x, 1 - p.y], from_y, p.at(y=1 - p.y)))

        def add(into, other):
            into[...] = (into[...].astype(F32) + other[...].astype(F32)).astype(BF)

        def along_x():
            over_c.wait_recv()
            for x in (1 - p.x, p.x):
                for z in range(p.zs):
                    for y in range(2):
                        add(own.at[z, x, y], from_c.at[z, x, y])
                if x is not p.x:
                    over_x.start()

        def along_z():
            over_x.wait_recv()
            for s in range(1, p.zs):
                z = p.z_other(s)
                for y in range(2):
                    add(own.at[z, p.x, y], from_x.at[z, y])
                over_z[s - 1].start()
            for y in range(2):
                add(own.at[p.z, p.x, y], from_x.at[p.z, y])

        def along_y():
            for copy in over_z:
                copy.wait_recv()
            for y in (1 - p.y, p.y):
                mine = own.at[p.z, p.x, y]
                total = mine[...].astype(F32)
                for s in range(p.zs - 1):
                    total += from_z[s, y].astype(F32)
                mine[...] = total.astype(BF)
                if y is not p.y:
                    over_y.start()

        def finish():
            over_y.wait_recv()
            self.summed[:, pl.ds(u * self.wide, self.wide)] = (
                own[p.z, p.x, p.y].astype(F32) + from_y[...].astype(F32))
            for copy in [over_c, over_x, over_y] + over_z:
                copy.wait_send()
            if u == self.panels - 1:
                self.last.start()
                self.kept.start()

        return [over_c.start, along_x, along_z, along_y, finish]

    def end(self):
        self.kept.wait()
        self.last.wait_recv()
        self.last.wait_send()

    def units(self, y_first=(), given=False):
        return [
            self.unit(u, r, u * self.pieces + r in y_first, given)
            for u in range(self.panels) for r in range(self.pieces)
        ]

    @staticmethod
    def scratch(zs, k, cols, panels, pieces, staged=False):
        n, tall, w = panels * pieces, 2 * k // pieces, cols // 2 // panels
        shapes = [(n, zs, 2, 2, tall, w), (n, zs, 2, 2, tall, w), (n, zs, 2, tall, w), (n, zs, tall, w),
                  (n, zs - 1, tall, w)]
        return [pltpu.VMEM(s, BF) for s in shapes] + [pltpu.VMEM((2 * k, cols // 2), F32)] + (
            [pltpu.VMEM(shapes[0], BF)] if staged else [])

    @staticmethod
    def scratch_xzy(zs, k, cols, panels):
        w = cols // 2 // panels
        shapes = [(zs, 2, 2, 2 * k, w), (zs, 2, 2, 2 * k, w), (zs, 2, 2 * k, w), (zs - 1, 2, 2 * k, w), (2 * k, w)]
        return [pltpu.VMEM((panels,) + s, BF) for s in shapes] + [
            pltpu.VMEM((2 * k, cols // 2), F32), pltpu.VMEM((panels,) + shapes[0], BF)]

    @staticmethod
    def remotes(zs, panels, pieces):
        return 1 + panels * pieces * (zs + 2)


class Total:
    def __init__(self, place, copies, grad, result, got, work, from_z):
        self.p, self.grad, self.got, self.work, self.from_z = place, grad, got, work, from_z
        p = place
        self.kept = copies.here(lambda: (grad.at[p.c], work))
        self.over_c = copies.remote(lambda: (grad.at[1 - p.c], got.at[0], p.at(c=1 - p.c)))
        self.over_x = copies.remote(lambda: (work, got.at[1], p.at(x=1 - p.x)))
        self.over_y = copies.remote(lambda: (work, got.at[2], p.at(y=1 - p.y)))
        self.over_z = [
            copies.remote(lambda s=s: (from_z.at[p.z], from_z.at[p.z], p.at(z=p.z_other(s)))) for s in range(1, p.zs)
        ]
        self.last = [
            copies.remote(lambda: (work, result.at[p.c], p.at(c=1 - p.c))),
            copies.here(lambda: (work, result.at[p.c])),
        ]

    def along_c(self):
        self.kept.start()
        self.over_c.start()

    def along_x(self):
        self.kept.wait()
        self.over_c.wait_recv()
        self.work[...] = self.work[...] + self.got[0]
        self.over_x.start()

    def along_y(self):
        self.over_x.wait_recv()
        self.over_x.wait_send()
        self.work[...] = self.work[...] + self.got[1]
        self.over_y.start()

    def along_z(self):
        self.over_y.wait_recv()
        self.over_y.wait_send()
        self.from_z[self.p.z] = self.work[...] + self.got[2]
        for copy in self.over_z:
            copy.start()

    def finish(self):
        for copy in self.over_z:
            copy.wait_recv()
        for copy in [self.over_c] + self.over_z:
            copy.wait_send()
        total = self.from_z[0]
        for z in range(1, self.p.zs):
            total += self.from_z[z]
        self.work[...] = total
        for copy in self.last:
            copy.start()

    def end(self):
        self.last[1].wait()
        self.last[0].wait_recv()
        self.last[0].wait_send()

    def units(self):
        return [[self.along_c, self.along_x, self.along_y, self.along_z, self.finish]]

    @staticmethod
    def scratch(zs, rows, wide):
        return [pltpu.VMEM((3, rows, wide), F32), pltpu.VMEM((rows, wide), F32), pltpu.VMEM((zs, rows, wide), F32)]

    @staticmethod
    def remotes(zs):
        return zs + 3


def semaphores(remotes, locals_):
    return [
        pltpu.SemaphoreType.DMA((remotes,)),
        pltpu.SemaphoreType.DMA((remotes,)),
        pltpu.SemaphoreType.DMA((locals_,)),
    ]


def split_refs(refs, *sizes):
    parts, at = [], 0
    for size in sizes:
        parts.append(refs[at:at + size])
        at += size
    return parts + [refs[at:]]


def full_shape(img_size, shard, panels):
    k, cols = shard.shape
    return (panels, 2, img_size // 2, 2, 2, 2 * k, cols // 2 // panels)


def table_rows(table, side, blocks, wide):
    span = 2 * side - 1
    square = table.reshape(H, span, span)
    square = jnp.concatenate([square] + [square[:, -1:]] * (blocks - span), 1)
    rows = []
    for turned in (square, square[:, ::-1, ::-1]):
        for part, pads in ((turned[:, :, :side], (0, 1)), (turned[:, :, side:], (1, 0))):
            part = jnp.pad(part, ((0, 0), pads, (0, side - part.shape[2])))
            flat = part.reshape(H, 1, (blocks + 1) * side)
            rows.append(jnp.roll(jnp.pad(flat, ((0, 0), (0, 0), (0, wide - flat.shape[2]))), 1 - side, 2))
    return jnp.concatenate(rows + [jnp.zeros((H, 4, wide), F32)], 1)


def lower_offsets(side, rows, wide):
    lane = lax.rem(lax.broadcasted_iota(jnp.int32, (rows, wide), 1), side)
    return lane <= lax.broadcasted_iota(jnp.int32, (rows, wide), 0)


def spread_rows(low, high, rows, lower):
    low = jnp.broadcast_to(low, (rows, low.shape[1]))
    high = jnp.broadcast_to(high, (rows, high.shape[1]))
    return jnp.where(
        lower, pltpu.roll(low, 0, 1, stride=1, stride_axis=0), pltpu.roll(high, 0, 1, stride=1, stride_axis=0)
    )


def shifted_window(ref, source, target):
    base = source // 128 * 128
    shift = (target - source) % 128 if target % 128 >= source % 128 else target % 128 - source % 128 + 256
    part = ref[:, base:min(base + 256, ref.shape[1])]
    if part.shape[1] < 256:
        part = jnp.concatenate([part, jnp.zeros_like(part)], 1)
    return pltpu.roll(part, shift, 1) if shift else part


def window_masks(target, side):
    lane = lax.broadcasted_iota(jnp.int32, (16, 256), 1) - target % 128
    return (lane >= 0) & (lane < side), (lane >= side) & (lane < 2 * side - 1)


def turn_lanes(table, turned):
    swap = lax.broadcasted_iota(jnp.int32, (128, 128), 0) + lax.broadcasted_iota(jnp.int32, (128, 128), 1) == 127
    swap = jnp.where(swap, 1.0, 0.0)
    width = table.shape[1]
    for at in range(0, width, 128):
        turned[:, width - 128 - at:width - at] = lax.dot_general(
            table[:, at:at + 128], swap, NN, precision=HIGHEST, preferred_element_type=F32)


def make_rows(table, low, high, side, blocks, first, skip=0):
    span = 2 * side - 1
    wide = low.shape[1] - 256
    low[...] = jnp.zeros_like(low)
    high[...] = jnp.zeros_like(high)
    for a in range(blocks):
        source = min(max(a - first, 0), span - 1) * span + skip
        target = 128 + a * side - (side - 1)
        part = shifted_window(table, source, target)
        at = slice(target // 128 * 128, target // 128 * 128 + 256)
        for ref, mask in zip((low, high), window_masks(target, side)):
            ref[:, at] += jnp.where(mask, part, 0.0)
    for ref in (low, high):
        ref[:, wide:wide + 128] += ref[:, :128]
        ref[:, :wide] = ref[:, 128:128 + wide]


def make_table(low, high, table, side, blocks, height):
    span = 2 * side - 1
    table[...] = jnp.zeros_like(table)
    for a in range(blocks):
        source = a * side + height - side
        target = min(a, span - 1) * span
        at = slice(target // 128 * 128, target // 128 * 128 + 256)
        for ref, mask in zip((low, high), window_masks(target, side)):
            table[:, at] += jnp.where(mask, shifted_window(ref, source, target), 0.0)


def row_scratch():
    return [pltpu.VMEM((16, WIDE_L + 256), F32)] * 2 + [pltpu.VMEM((16, WIDE_S + 256), F32)] * 2


TABLE_L = 2560
TABLE_S = 1024


def padded_table(table, wide):
    return jnp.pad(table, ((0, 16 - H), (0, wide - table.shape[1])))


def fill_bias(bias, h, spread, side, rows, first_offset):
    size = bias.shape[2]
    wide = spread.shape[1]
    window = -(-size // 128) * 128 + 128
    for r in range(rows):
        offset = (first_offset - r) * side
        base, rest = offset // 128 * 128, offset % 128
        part = spread[:, base:min(base + window, wide)]
        if part.shape[1] < window:
            part = jnp.concatenate([part, jnp.zeros((spread.shape[0], window - part.shape[1]), F32)], 1)
        if rest:
            part = pltpu.roll(part, window - rest, 1)
        bias[h, r * side:(r + 1) * side, :] = part[:side, :size]


def fold_bias(total, h, acc, side, rows, first_offset, lower, out_ref, head):
    size = total.shape[2]
    window = -(-size // 128) * 128 + 128
    height, wide = lower.shape
    acc[...] = jnp.zeros_like(acc)
    for r in range(rows):
        offset = (first_offset - r) * side
        base, rest = offset // 128 * 128, offset % 128
        part = total[h, r * side:(r + 1) * side, :]
        part = jnp.concatenate([part, jnp.zeros((side, window - size), F32)], 1)
        if rest:
            part = pltpu.roll(part, rest, 1)
        acc[:side, base:base + window] += part
    whole = acc[:, :wide]
    zero = jnp.zeros_like(whole)
    for at, part in enumerate((jnp.where(lower, whole, zero), jnp.where(lower, zero, whole))):
        turned = jnp.concatenate([part[j:j + 1] for j in reversed(range(height))], 0)
        moved = pltpu.roll(turned, 0, 1, stride=1, stride_axis=0)
        out_ref[at, pl.ds(head, 1), :] = jnp.sum(moved, 0, keepdims=True)


def head_part(full, mask, h):
    keep = mask if h == 0 else jnp.logical_not(mask)
    return jnp.where(keep, full, jnp.zeros_like(full))


def softmax_product(s, v):
    top = jnp.max(s, 1, keepdims=True)
    e = jnp.exp(s - top)
    total = jnp.sum(e, 1, keepdims=True)
    lse = jnp.broadcast_to(top + jnp.log(total), (s.shape[0], 128)).T
    return dot(e.astype(BF), v, NN) * (1.0 / total), lse[0:1, :]


def attend_kernel(large, small, q_ref, k_ref, v_ref, rows_l, rows_s, o_ref, lse_ref, bias_l, bias_s):
    mask = lax.broadcasted_iota(jnp.int32, (1, 128), 1) < 64
    lower_l = lower_offsets(SIDE_L, SIDE_L, WIDE_L)
    lower_s = lower_offsets(SIDE_S, 16, WIDE_S)
    for h in range(2):
        fill_bias(bias_l, h, spread_rows(rows_l[h, 2:3, :], rows_l[h, 3:4, :], SIDE_L, lower_l), SIDE_L, 24, 23)
        fill_bias(bias_s, h, spread_rows(rows_s[h, 2:3, :], rows_s[h, 3:4, :], 16, lower_s), SIDE_S, 16, 15)
    keep = lax.broadcasted_iota(jnp.int32, (1, LEN_S), 1) < SIDE_S * SIDE_S
    images = [(n * LEN_L, LEN_L, bias_l) for n in range(large)]
    images += [(large * LEN_L + n * LEN_S, LEN_S, bias_s) for n in range(small)]
    for n, (at, size, bias) in enumerate(images):
        q, k, v = (ref[at:at + size, :] for ref in (q_ref, k_ref, v_ref))
        outs = []
        for h in range(2):
            s = dot(head_part(q, mask, h) * BF(0.125), k, NT) + bias[h]
            if size == LEN_S:
                s = jnp.where(keep, s, -1e30)
            out, lse = softmax_product(s, v)
            outs.append(out)
            lse_ref[n, pl.ds(2 * pl.program_id(0) + h, 1), :size] = lse
        o_ref[at:at + size, :] = jnp.where(mask, outs[0], outs[1]).astype(BF)


def loop_points(steps, every):
    return {t * every: step for t, step in enumerate(steps)}


def run_point(points, iteration, at, per, iterations):
    for i in range(iterations):
        step = points.get(i * per + at)
        if step is not None:
            pl.when(iteration == i)(step)


def run_rest(points, count):
    for at in sorted(points):
        if at >= count:
            points[at]()


def attend_back_pair(hp, qkv, do_ref, o_ref, lse_ref, rows, df, sums_l, sums_s, scratch, large, small, between):
    bias_l, bias_s, total_l, total_s, acc_l, acc_s = scratch
    mask = lax.broadcasted_iota(jnp.int32, (1, 128), 1) < 64
    lower_l = lower_offsets(SIDE_L, SIDE_L, WIDE_L)
    lower_s = lower_offsets(SIDE_S, 16, WIDE_S)
    low_l, high_l, low_s, high_s = rows
    for h in range(2):
        at = pl.ds(2 * hp + h, 1)
        fill_bias(bias_l, h, spread_rows(low_l[at, :WIDE_L], high_l[at, :WIDE_L], SIDE_L, lower_l), SIDE_L, 24, 23)
        fill_bias(bias_s, h, spread_rows(low_s[at, :WIDE_S], high_s[at, :WIDE_S], 16, lower_s), SIDE_S, 14, 13)
    keep = lax.broadcasted_iota(jnp.int32, (LEN_S, 1), 0) < SIDE_S * SIDE_S
    images = [(n * LEN_L, LEN_L, bias_l, total_l, n == 0) for n in range(large)]
    images += [(large * LEN_L + n * LEN_S, LEN_S, bias_s, total_s, n == 0) for n in range(small)]
    cols = [columns(i * 64 * H + hp * 128, 128) for i in range(3)]
    for index, (at, size, bias, total, first) in enumerate(images):
        between(index)
        rows = slice(at, at + size)
        q, k, v = (qkv[rows, c] for c in cols)
        do = do_ref[rows, cols[0]]
        products = do.astype(F32) * o_ref[rows, cols[0]].astype(F32)
        sides = lax.broadcasted_iota(jnp.int32, (8, 128), 0) == lax.broadcasted_iota(jnp.int32, (8, 128), 1) // 64
        row_dots = lax.dot_general(
            jnp.where(sides, 1.0, 0.0), products, NT, precision=HIGHEST, preferred_element_type=F32)
        got = []
        for h in range(2):
            row_dot = row_dots[h:h + 1, :]
            lse = lse_ref[index, pl.ds(2 * hp + h, 1), :size]
            s = dot(head_part(k, mask, h) * BF(0.125), q, NT) + bias[h]
            if size == LEN_S:
                s = jnp.where(keep, s, -1e30)
            p = jnp.exp(s - lse)
            ds = p * (dot(head_part(v, mask, h), do, NT) - row_dot)
            low = ds.astype(BF)
            got.append((dot(low, k, TN), dot(low, q, NN), dot(p.astype(BF), do, NN)))
            total[h] = ds if first else total[h] + ds
        for c, a, b, scale in zip(cols, got[0], got[1], (0.125, 0.125, 1.0)):
            df[rows, c] = (jnp.where(mask, a, b) * scale).astype(BF)
    for h in range(2):
        fold_bias(total_l, h, acc_l, SIDE_L, 24, 23, lower_l, sums_l, 2 * hp + h)
        fold_bias(total_s, h, acc_s, SIDE_S, 14, 13, lower_s, sums_s, 2 * hp + h)


def back_scratch():
    return [pltpu.VMEM((2, LEN_L, LEN_L), F32), pltpu.VMEM((2, LEN_S, LEN_S), F32)] * 2 + [
        pltpu.VMEM((SIDE_L, WIDE_L + 128), F32), pltpu.VMEM((16, WIDE_S + 128), F32)]


BACK_POINTS = {
    1: ((0, 1),), 3: ((1, 1),), 7: ((2, 1), (0, 2)), 9: ((1, 2), (0, 3)), 13: ((2, 2), (1, 3)), 15: ((2, 3),),
    17: ((0, 4), (1, 4)), 18: ((2, 4),),
}


def attention_back(img_size, qkv, d_att, att, lse, table_l, table_s, grads, cuts, wholes, large, small):
    zs = img_size // 2
    ng, nw = len(grads), len(wholes)
    rows = qkv.shape[0]
    shard_shapes = [(g.shape[5] // 2, g.shape[0] * 2 * g.shape[6]) for g in grads]

    def kernel(*refs):
        ins, gr, wh, outs, shards, blocks, scr = split_refs(refs, 6, ng, nw, 3, ng, nw)
        qkv_hbm, do_hbm, o_hbm, lse_v, tl, ts = ins
        df_hbm, sums_l, sums_s = outs
        qkv_v, do_v, df_v, o_v = scr[:4]
        rows_ = scr[4:8]
        p = Place(img_size)
        copies = Copies(*scr[-3:])
        loads = [copies.here(lambda a=a, b=b: (a, b)) for a, b in ((qkv_hbm, qkv_v), (do_hbm, do_v), (o_hbm, o_v))]
        for copy in loads:
            copy.start()
        if ng + nw:
            announce(p.partners())
        at = 8 + 6
        scatters = []
        for i in range(ng):
            scatters.append(Scatter(p, copies, gr[i], shards[i], scr[at:at + 6], cuts[i]))
            at += 6
        moves = [Move(p, copies, a, b, False) for a, b in zip(wh, blocks)]
        units = [u for s in scatters for u in s.units()]
        points = {}
        if units:
            points = {at: in_turn(*[units[u][f] for u, f in todo]) for at, todo in BACK_POINTS.items()}
        make_rows(tl, rows_[0], rows_[1], SIDE_L, 47, 0)
        make_rows(ts, rows_[2], rows_[3], SIDE_S, 29, 0)
        sums_l[...] = jnp.zeros_like(sums_l)
        sums_s[...] = jnp.zeros_like(sums_s)
        if ng + nw:
            await_partners(p.partners())
        for unit in units:
            unit[0]()
        for m in moves:
            m.start()
        for copy in loads:
            copy.wait()

        out_at = copies.locals
        copies.locals += 3 * (H // 2)

        def out(hp):
            cols = [columns(i * 64 * H + hp * 128, 128) for i in range(3)]
            return [
                pltpu.make_async_copy(df_v.at[:, c], df_hbm.at[:, c], copies.local.at[out_at + 3 * hp + i])
                for i, c in enumerate(cols)
            ]

        def body(hp, carry):
            attend_back_pair(hp, qkv_v, do_v, o_v, lse_v, rows_, df_v, sums_l, sums_s, scr[8:14], large, small,
                             lambda index: run_point(points, hp, index, large + small, H // 2))
            for copy in out(hp):
                copy.start()
            return carry

        lax.fori_loop(0, H // 2, body, 0)
        run_rest(points, (large + small) * (H // 2))
        for s in scatters:
            s.end()
        for m in moves:
            m.finish()
        for hp in range(H // 2):
            for copy in out(hp):
                copy.wait()

    scratch = [pltpu.VMEM(a.shape, BF) for a in (qkv, d_att, qkv, att)] + row_scratch() + back_scratch()
    for g, (k, cols), cut in zip(grads, shard_shapes, cuts):
        scratch += Scatter.scratch(zs, k, cols, g.shape[0], cut)
    remotes = 3 * nw + sum(Scatter.remotes(zs, g.shape[0], c) for g, c in zip(grads, cuts))
    locals_ = 3 + 3 * (H // 2) + nw + sum(1 + g.shape[0] * c for g, c in zip(grads, cuts))
    remote = dict(collective_id=1, has_side_effects=True) if ng + nw else {}
    return pl.pallas_call(
        kernel,
        out_shape=[jax.ShapeDtypeStruct(qkv.shape, BF), jax.ShapeDtypeStruct((2, 16, WIDE_L), F32),
                   jax.ShapeDtypeStruct((2, 16, WIDE_S), F32)]
        + [jax.ShapeDtypeStruct(s, F32) for s in shard_shapes]
        + [jax.ShapeDtypeStruct((w.shape[0] * 4,) + w.shape[2:], w.dtype) for w in wholes],
        in_specs=[ANY] * 3 + [VMEM] * 3 + [ANY] * (ng + nw),
        out_specs=[ANY, VMEM, VMEM] + [ANY] * (ng + nw),
        scratch_shapes=scratch + semaphores(max(remotes, 1), locals_),
        compiler_params=pltpu.CompilerParams(vmem_limit_bytes=60 * MIB, **remote),
        name="attention_back",
    )(qkv, d_att, att, lse, table_l, table_s, *grads, *wholes)


def row_tiles(rows, tile, body):
    count = rows // tile

    def step(t, carry):
        body(pl.multiple_of(t * tile, 16), tile)
        return carry

    lax.fori_loop(0, count, step, 0)
    if rows % tile:
        body(count * tile, rows % tile)


def norm_parts(x):
    centered = x - jnp.mean(x, 1, keepdims=True)
    scale = lax.rsqrt(jnp.mean(centered * centered, 1, keepdims=True) + 1e-06)
    return centered * scale, scale


def norm_back(dn, hat, scale, gain):
    d_hat = dn * gain
    return scale * (d_hat - jnp.mean(d_hat, 1, keepdims=True) - hat * jnp.mean(d_hat * hat, 1, keepdims=True))


def fold8(values):
    return sum(values[i:i + 8] for i in range(0, values.shape[0], 8))


def place_small(ref, flat, at):
    for i in range(4):
        ref[at, i] = flat[i * 56:(i + 1) * 56].astype(ref.dtype)


def load_tokens(copies, large_hbm, small_hbm, flat, four):
    n, _, rows, _ = large_hbm.shape
    loads = [
        copies.here(lambda i=i, j=j: (large_hbm.at[i, j], flat.at[pl.ds((i * 4 + j) * rows, rows)]))
        for i in range(n) for j in range(4)
    ]
    return loads + [copies.here(lambda: (small_hbm, four))]


def join_small(flat, four, large):
    for n in range(four.shape[0]):
        rows = jnp.concatenate([four[n, i].astype(F32) for i in range(4)], 0)
        at = large * LEN_L + n * LEN_S
        flat[at:at + LEN_S, :] = rows.astype(flat.dtype)


def projection_back(img_size, df, dm, n1, x_l, x_s, w_qkv, vectors, sums, tables, large, small):
    zs = img_size // 2
    rows, width = dm.shape
    panels, _, _, _, _, k2, wide = w_qkv.shape
    k, cols = k2 // 2, panels * 2 * wide
    nt = len(tables)

    def kernel(*refs):
        ins, tabs, outs, tab_outs, scr = split_refs(refs, 8, nt, 4, nt)
        df_hbm, dm_hbm, n1_hbm, xl_hbm, xs_hbm, w_hbm, vec, sums_in = ins
        gl_out, gs_out, shard, sums_out = outs
        df_v, dm_v, flat, four, w_v, n1_v, nt_v, dn, acc, own_sums, dl, ds, grad = scr[:13]
        at = 13
        p = Place(img_size)
        copies = Copies(*scr[-3:])
        first = [copies.here(lambda: (n1_hbm, n1_v)), copies.here(lambda: (df_hbm, df_v))]
        w_load = copies.here(lambda: (w_hbm, w_v))
        later = load_tokens(copies, xl_hbm, xs_hbm, flat, four) + [copies.here(lambda: (dm_hbm, dm_v))]
        for copy in first + [w_load] + later:
            copy.start()
        greet(p.partners())
        scatter = Scatter(p, copies, None, shard, scr[at:at + 7], 1)
        at += 7
        totals = []
        for a, b in zip(tabs, scr[-3 - 2 * nt:-3 - nt]):
            totals.append(Total(p, copies, a, b, *scr[at:at + 3]))
            at += 3
        last = Total(p, copies, own_sums, sums_out, *scr[at:at + 3])
        moves = [Move(p, copies, dl, gl_out, False, n) for n in range(large)]
        moves.append(Move(p, copies, ds, gs_out, False))
        units = [scatter.unit_xzy(u) for u in range(panels)]
        for t in totals:
            t.along_c()
        first[0].wait()
        nt_v[...] = n1_v[...].T
        first[1].wait()

        def pair(ref, u, at):
            return jnp.concatenate(
                [ref[at, c * (cols // 2) + u * wide:c * (cols // 2) + (u + 1) * wide] for c in range(2)], 1)

        def gradient(u):
            grad[...] = dot(nt_v[...], pair(df_v, u, slice(None)), NN).astype(BF)
            for to, c in ((scatter.stage, 1 - p.c), (scatter.own, p.c)):
                to[u] = grad[:, columns(c * wide, wide)].reshape(zs, 2, 2, k2, wide)
            units[u][0]()

        def all_totals(phase):
            for t in totals:
                phase(t)

        gain = vec[0:1, :]

        def back(start, size):
            at_rows = pl.ds(start, size)
            hat, scale = norm_parts(flat[at_rows, :].astype(F32))
            d = dn[at_rows, :]
            acc[0] += fold8(d * hat)
            acc[1] += fold8(d)
            acc[2] += fold8(df_v[at_rows, :width].astype(F32))
            acc[3] += fold8(df_v[at_rows, 2 * width:].astype(F32))
            flat[at_rows, :] = (dm_v[at_rows, :] + norm_back(d, hat, scale, gain)).astype(BF)

        def image(start, size):
            at = slice(start, start + size)
            got = None
            for u in range(panels):
                w = jnp.concatenate([w_v[u, c].reshape(width, wide) for c in range(2)], 1)
                part = dot(pair(df_v, u, at), w, NT)
                got = part if got is None else got + part
            dn[at, :] = got
            row_tiles(size, 96, lambda at, n: back(start + at, n))

        acc[...] = jnp.zeros_like(acc)
        all_totals(Total.along_x)
        gradient(0)
        all_totals(Total.along_y)
        gradient(1)
        units[0][1]()
        all_totals(Total.along_z)
        for copy in [w_load] + later:
            copy.wait()
        join_small(flat, four, large)
        for n in range(large):
            image(n * LEN_L, LEN_L)
            for j in range(4):
                start = (n * 4 + j) * (LEN_L // 4)
                dl[n, j] = flat[start:start + LEN_L // 4, :]
            moves[n].start()
            if n == 0:
                units[1][1]()
                gradient(2)
                units[0][2]()
                all_totals(Total.finish)
            if n == 1:
                units[2][1]()
                units[1][2]()
        for n in range(small):
            start = large * LEN_L + n * LEN_S
            image(start, LEN_S)
            place_small(ds, flat[start:start + LEN_S, :].astype(F32), n)
        moves[-1].start()
        for i, row in ((0, 0), (1, 4), (2, 6), (3, 7)):
            own_sums[0, row:row + 1, :] = jnp.sum(acc[i], 0, keepdims=True)
        for row in (1, 2, 3, 5):
            own_sums[0, row:row + 1, :] = sums_in[0, row:row + 1, :]
        own_sums[1] = sums_in[1]
        last.along_c()

        def table_out(i, *shape):
            result, whole = scr[-3 - 2 * nt + i], scr[-3 - nt + i]
            make_table(result.at[0], result.at[1], whole, *shape)
            tab_outs[i][...] = whole[:H, :tab_outs[i].shape[1]]

        units[0][3]()
        for t in totals:
            t.end()
        last.along_x()
        table_out(0, SIDE_L, 47, 24)
        units[2][2]()
        units[0][4]()
        last.along_y()
        table_out(1, SIDE_S, 29, 16)
        units[1][3]()
        last.along_z()
        units[1][4]()
        units[2][3]()
        last.finish()
        units[2][4]()
        scatter.end()
        last.end()
        for m in moves:
            m.finish()

    flat = pltpu.VMEM((rows, width), BF)
    scratch = [
        pltpu.VMEM(df.shape, BF), pltpu.VMEM(dm.shape, F32), flat, pltpu.VMEM(x_s.shape, BF),
        pltpu.VMEM(w_qkv.shape, BF), flat, pltpu.VMEM((width, rows), BF), pltpu.VMEM((rows, width), F32),
        pltpu.VMEM((4, 8, width), F32), pltpu.VMEM((2, 8, width), F32),
        pltpu.VMEM(x_l.shape, BF), pltpu.VMEM(x_s.shape, BF), pltpu.VMEM((width, 2 * wide), BF),
    ] + Scatter.scratch_xzy(zs, k, cols, panels)
    for t in list(tables) + [sums]:
        scratch += Total.scratch(zs, t.shape[1], t.shape[2])
    scratch += [pltpu.VMEM(t.shape, F32) for t in tables] + [pltpu.VMEM((16, w), F32) for w in (TABLE_L, TABLE_S)]
    remotes = 3 * (large + 1) + Scatter.remotes(zs, panels, 1) + Total.remotes(zs) * (nt + 1)
    locals_ = 4 * large + 1 + 4 + large + 1 + 1 + 2 * (nt + 1)
    f32 = lambda s: jax.ShapeDtypeStruct(s, F32)
    return pl.pallas_call(
        kernel,
        out_shape=[jax.ShapeDtypeStruct((4 * a.shape[0],) + a.shape[2:], BF) for a in (x_l, x_s)]
        + [f32((k, cols)), f32(sums.shape)] + [f32((H, (2 * side - 1) ** 2)) for side in (SIDE_L, SIDE_S)],
        in_specs=[ANY] * 6 + [VMEM, VMEM] + [ANY] * nt,
        out_specs=[ANY] * 4 + [VMEM] * nt,
        scratch_shapes=scratch + semaphores(remotes, locals_),
        compiler_params=pltpu.CompilerParams(collective_id=2, has_side_effects=True, vmem_limit_bytes=60 * MIB),
        name="projection_back",
    )(df, dm, n1, x_l, x_s, w_qkv, vectors, sums, *tables)


def attend_pair(hp, n, rows, size, qkv, bias, out, lse_out):
    mask = lax.broadcasted_iota(jnp.int32, (1, 128), 1) < 64
    cols = [columns(i * 64 * H + hp * 128, 128) for i in range(3)]
    q, k, v = (qkv[rows, c] for c in cols)
    scores = [dot(head_part(q, mask, h) * BF(0.125), k, NT) for h in range(2)]
    outs = []
    for h in range(2):
        s = scores[h] + bias[2 * hp + h]
        if size == LEN_S:
            s = jnp.where(lax.broadcasted_iota(jnp.int32, (1, LEN_S), 1) < SIDE_S * SIDE_S, s, -1e30)
        o, lse = softmax_product(s, v)
        outs.append(o)
        lse_out[n, pl.ds(2 * hp + h, 1), :size] = lse
    out[rows, cols[0]] = jnp.where(mask, outs[0], outs[1]).astype(BF)


def fill_heads(start, stop, rows, bias_l, bias_s):
    low_l, high_l, low_s, high_s = rows
    lower_l = lower_offsets(SIDE_L, SIDE_L, WIDE_L)
    lower_s = lower_offsets(SIDE_S, 16, WIDE_S)

    def body(h, carry):
        at = pl.ds(h, 1)
        fill_bias(bias_l, h, spread_rows(low_l[at, :WIDE_L], high_l[at, :WIDE_L], SIDE_L, lower_l), SIDE_L, 24, 23)
        fill_bias(bias_s, h, spread_rows(low_s[at, :WIDE_S], high_s[at, :WIDE_S], 16, lower_s), SIDE_S, 16, 15)
        return carry

    lax.fori_loop(start, stop, body, 0)


def assemble(blocks, count, vectors, up_vec):
    row = lax.broadcasted_iota(jnp.int32, (16, 128), 0)
    vectors[...] = jnp.zeros_like(vectors)
    up_vec[...] = jnp.zeros_like(up_vec)
    width = vectors.shape[1] - 128
    own, own_up = width // count, 4 * width // count

    def shifted(part, offset):
        part = jnp.concatenate([part, jnp.zeros_like(part)], 1)
        return pltpu.roll(part, offset % 128, 1) if offset % 128 else part

    for d in range(count):
        block = blocks[d].astype(BF).astype(F32)
        offset = d * own
        base = offset // 128 * 128
        vectors[:, base:base + 256] += shifted(jnp.where(row < 10, block, 0.0), offset)
        at, offset = d * own_up // width, d * own_up % width
        base = offset // 128 * 128
        up_vec[at:at + 1, base:base + 256] += shifted(block[10:11], offset)


CT_GROUP = 3


def front(img_size, arrays, block, shards, cuts, firsts, table_l, table_s):
    na, nw = len(arrays), len(shards)
    zs = img_size // 2
    large, small = arrays[0].shape[0] // 4, arrays[1].shape[0] // 4
    width = arrays[0].shape[2]
    rows = large * LEN_L + small * LEN_S
    count = 4 * img_size
    whole_shapes = [(a.shape[0] // 4, 4) + a.shape[1:] for a in arrays]
    full_shapes = [full_shape(img_size, s, c[0]) for s, c in zip(shards, cuts)]
    panels, wide = cuts[0][0], full_shapes[0][-1]

    def kernel(*refs):
        ins, blk, sh, tabs, whole, full, outs, scr = split_refs(refs, na, 1, nw, 2, na, nw, 6)
        qkv_hbm, n1_hbm, att, lse, vec_out, up_out = outs
        flat, four, w_v, qkv, bias_l, bias_s, small_v, vectors, up_vec = scr[:9]
        gather_scr = scr[13:13 + 2 * nw]
        p = Place(img_size)
        greet(p.partners())
        copies = Copies(*scr[-3:])
        gathers = [
            Gather(p, copies, sh[i], full[i], gather_scr[2 * i], gather_scr[2 * i + 1], cuts[i][1]) for i in range(nw)
        ]
        moves = [Move(p, copies, ins[0], whole[0], True, n) for n in range(large)]
        small_move = Move(p, copies, ins[1], whole[1], True)
        ct_moves = [Move(p, copies, ins[2], whole[2], True, 0), Move(p, copies, ins[3], whole[3], True)]
        gathers[0].exchange()
        small_move.start()
        first = pipelined(Spread(p, copies, blk[0], small_v).units() + gathers[0].units())
        y_units, x_units = [], []
        for g, x_first in zip(gathers[1:-1], firsts):
            for at, unit in enumerate(g.units(None, x_first)):
                (x_units if at in x_first else y_units).append(unit)
        z_units = gathers[-1].units(gathers[-1].over_z)
        fill = functools.partial(fill_heads, rows=scr[9:13], bias_l=bias_l, bias_s=bias_s)
        for t in range(3):
            first[t]()
        for g in gathers[1:]:
            g.exchange()
        for table, turned, rows_, shape in (
            (tabs[0], scr[-5], scr[9:11], (SIDE_L, 47, 0)), (tabs[1], scr[-4], scr[11:13], (SIDE_S, 29, 2))
        ):
            turn_lanes(table, turned)
            make_rows(turned, *rows_, *shape, turned.shape[1] - (2 * shape[0] - 1) ** 2)
        fill(0, 4)
        first[3]()
        fill(4, 8)
        first[4]()
        moves[0].start()
        for unit in y_units + x_units:
            unit[0]()
        fill(8, 12)
        assemble(small_v.reshape(count, 16, 128), count, vectors, up_vec)
        vec_out[...] = vectors[:, :width]
        up_out[...] = up_vec[:4, :width]
        first[5]()
        for unit in y_units:
            unit[1]()
        first[6]()
        for m in moves[1:]:
            m.start()
        first[7]()
        w_load = copies.here(lambda: (full[0], w_v))
        w_load.start()
        for unit in x_units:
            unit[1]()
        half = (len(y_units) + 1) // 2
        groups = [[unit[2] for unit in y_units[:half]], [unit[2] for unit in x_units[:1]],
                  [unit[2] for unit in y_units[half:]], [unit[2] for unit in x_units[1:]],
                  [unit[0] for unit in z_units]]
        groups += [[unit[3]] for unit in y_units + x_units]
        groups[CT_GROUP] = groups[CT_GROUP] + [m.start for m in ct_moves]
        groups.append([unit[4] for unit in y_units + x_units] + [unit[1] for unit in z_units] + [m.finish for m in ct_moves])
        steps = [in_turn(*group) for group in groups]
        gain, shift = vectors[0:1, :width], vectors[4:5, :width]
        x_load = copies.locals
        copies.locals += 4 * large
        points = loop_points(steps, 1)

        def loads(n):
            return [
                pltpu.make_async_copy(
                    whole[0].at[n, j], flat.at[pl.ds((n * 4 + j) * (LEN_L // 4), LEN_L // 4)],
                    copies.local.at[x_load + n * 4 + j])
                for j in range(4)
            ]

        def project(start, size):
            rows_ = pl.ds(start, size)
            hat, _ = norm_parts(flat[rows_, :].astype(F32))
            n1 = (hat * gain + shift).astype(BF)
            flat[rows_, :] = n1
            for u in range(panels):
                w = jnp.concatenate([w_v[u, c].reshape(width, wide) for c in range(2)], 1)
                got = dot(n1, w, NN)
                for c in range(2):
                    at = (c * panels + u) * wide
                    part = got[:, c * wide:(c + 1) * wide]
                    if at + wide <= width:
                        part += vectors[6:7, at:at + wide]
                    elif at >= 2 * width:
                        part += vectors[7:8, at - 2 * width:at - 2 * width + wide]
                    qkv[rows_, at:at + wide] = part.astype(BF)

        out_at = copies.locals
        copies.locals += 2 * (large + small)

        def outs_of(n, rows_):
            return [
                pltpu.make_async_copy(src.at[rows_], dst.at[rows_], copies.local.at[out_at + 2 * n + i])
                for i, (src, dst) in enumerate(((qkv, qkv_hbm), (flat, n1_hbm)))
            ]

        def image(n, carry):
            for i in range(large):
                @pl.when(n == i)
                def _():
                    moves[i].finish()
                    for copy in loads(i):
                        copy.start()
                    for copy in loads(i):
                        copy.wait()
                    if i == 0:
                        w_load.wait()

            start = pl.multiple_of(n * LEN_L, 16)
            project(start, LEN_L)
            for copy in outs_of(n, pl.ds(start, LEN_L)):
                copy.start()

            def body(hp, inner):
                run_point(points, n * (H // 2) + hp, 0, 1, large * (H // 2))
                attend_pair(hp, n, pl.ds(start, LEN_L), LEN_L, qkv, bias_l, att, lse)
                return inner

            lax.fori_loop(0, H // 2, body, 0)
            return carry

        lax.fori_loop(0, large, image, 0)
        small_move.finish()
        small_load = copies.here(lambda: (whole[1], four))
        small_load.start()
        small_load.wait()
        join_small(flat, four, large)
        for n in range(small):
            start = large * LEN_L + n * LEN_S
            project(start, LEN_S)
            for copy in outs_of(large + n, pl.ds(start, LEN_S)):
                copy.start()

            def body(hp, inner):
                attend_pair(hp, large + n, pl.ds(start, LEN_S), LEN_S, qkv, bias_s, att, lse)
                return inner

            lax.fori_loop(0, H // 2, body, 0)
        run_rest(points, large * (H // 2))
        for n in range(large + small):
            rows_ = pl.ds(n * LEN_L, LEN_L) if n < large else pl.ds(large * LEN_L + (n - large) * LEN_S, LEN_S)
            for copy in outs_of(n, rows_):
                copy.wait()

    units = 1 + sum(a * b for a, b in cuts)
    vm = pltpu.VMEM
    return pl.pallas_call(
        kernel,
        out_shape=[jax.ShapeDtypeStruct(s, BF) for s in whole_shapes + full_shapes + [(rows, 3 * width), (rows, width), (rows, width)]]
        + [jax.ShapeDtypeStruct(s, F32) for s in ((large + small, 16, 640), (16, width), (4, width))],
        in_specs=[ANY] * (na + 1 + nw) + [VMEM, VMEM],
        out_specs=[ANY] * (na + nw + 2) + [VMEM] * 4,
        scratch_shapes=[
            vm((rows, width), BF), vm(whole_shapes[1], BF), vm(full_shapes[0], BF), vm((rows, 3 * width), BF),
            vm((H, LEN_L, LEN_L), F32), vm((H, LEN_S, LEN_S), F32), vm((zs, 2, 2, 2, 16, 128), F32),
            vm((16, width + 128), F32), vm((8, width + 128), F32),
        ] + row_scratch() + [s for w in shards for s in Gather.scratch(w.shape)]
        + [vm((16, TABLE_L), F32), vm((16, TABLE_S), F32)]
        + semaphores(3 * (large + 3) + (zs + 2) * units + nw, large + 3 + nw + units + 4 * large + 1 + 1 + 2 * (large + small)),
        compiler_params=pltpu.CompilerParams(collective_id=0, has_side_effects=True, vmem_limit_bytes=56 * MIB),
        name="front",
    )(*arrays, block, *shards, table_l, table_s)


def gelu_parts(u):
    cdf = 0.5 * lax.erf(0.7071067811865476 * u) + 0.5
    bell = jnp.exp2(-0.7213475204444817 * (u * u))
    return u * cdf, cdf + u * (0.3989422804014327 * bell)


def joined(w, *at):
    parts = [w[(at[0], c) + at[1:]] for c in range(2)]
    return jnp.concatenate([part.reshape(-1, part.shape[-1]) for part in parts], 1)


def image_rows(large, small):
    parts = [(n, j, (n * 4 + j) * (LEN_L // 4)) for n in range(large) for j in range(4)]
    return parts, [(n, large * LEN_L + n * LEN_S) for n in range(small)]


def forward_tail(img_size, att, x_l, x_s, ct_l, ct_s, ct_part, w_out, w_up, w_down, cut, vectors, up_vec):
    large, small = x_l.shape[0], x_s.shape[0]
    rows, width = att.shape
    chunks = up_vec.shape[0]
    half = rows // 2
    direct = img_size is not None
    down_shape = w_down.shape
    bf = lambda *s: jax.ShapeDtypeStruct(s, BF)
    more = [bf(*down_shape), bf(*x_l.shape)] if direct else []

    def kernel(att_hbm, xl_hbm, xs_hbm, cl_hbm, cs_hbm, wo_hbm, wu_hbm, wd_in, vec, upv, *refs):
        refs = refs[1:] if direct else refs
        outs, extra, scr = split_refs(refs, 9, len(more))
        yl, ys, m_hbm, n2_hbm, e_hbm, g_hbm, dr_hbm, dy_hbm, sums = outs
        att_v, flat, four, ct_four, wo, wu, wd, m_v, n2_v, e_v, g_v, acc = scr[:12]
        u_v = scr[12:14]
        copies = Copies(*scr[-3:])
        first = [copies.here(lambda: (att_hbm, att_v)), copies.here(lambda: (wo_hbm, wo))]
        first += load_tokens(copies, xl_hbm, xs_hbm, flat, four)
        second = copies.here(lambda: (wu_hbm, wu))
        for copy in first + [second]:
            copy.start()
        early, steps, moves = [], [], []
        wd_hbm, ct = wd_in, (cl_hbm, cs_hbm)
        if direct:
            p = Place(img_size)
            greet(p.partners())
            wd_hbm, ct = extra[0], (extra[1], cs_hbm)
            gather = Gather(p, copies, None, wd_hbm, None, None, cut[1])
            moves = [Move(p, copies, cl_hbm, ct[0], True, n) for n in range(1, large)]
            units = [gather.over_yx(0, r, r == 1) for r in range(cut[1])]
            units[0][0]()
            units[1][0]()
            early = [in_turn(units[0][1], units[2][0]), in_turn(units[1][1], *[m.start for m in moves]), units[2][1]]
            steps = [units[0][2], units[1][2], in_turn(units[2][2], *[unit[3] for unit in units])]
        for copy in first:
            copy.wait()
        join_small(flat, four, large)
        g2, s1, s2, b2, bo, bd = (vec[i:i + 1, :] for i in (1, 2, 3, 5, 8, 9))
        points = {t + 2: step for t, step in enumerate(steps)}
        w = joined(wo, 0)
        for i in range(2):
            at = slice(i * half, (i + 1) * half)
            m_v[at, :] = dot(att_v[at, :], w, NN)
        for step in early[:1]:
            step()

        def middle(start, size):
            at = pl.ds(start, size)
            m = flat[at, :].astype(F32) + s1 * (m_v[at, :] + bo)
            m_v[at, :] = m
            hat, _ = norm_parts(m)
            n2_v[at, :] = (hat * g2 + b2).astype(BF)

        row_tiles(rows, 96, middle)
        for step in early[1:2]:
            step()
        m_out = [copies.here(lambda: (m_v, m_hbm)), copies.here(lambda: (n2_v, n2_hbm))]
        for copy in m_out:
            copy.start()
        second.wait()
        out_at = copies.locals
        copies.locals += chunks

        def out(f):
            return pltpu.make_async_copy(
                g_v.at[lax.rem(f, 2)], g_hbm.at[f], copies.local.at[out_at + f])

        tops = [slice(i * half, (i + 1) * half) for i in range(2)]

        def up(i, f):
            return dot(n2_v[tops[i], :], wu[lax.rem(f, 2), f // 2].reshape(width, width), NN)

        def activate(i, f):
            e, g = gelu_parts(u_v[i][...] + upv[pl.ds(f, 1), :])
            e_v[tops[i], columns(f * width, width)] = e.astype(BF)
            g_v[lax.rem(f, 2), tops[i], :] = g.astype(BF)

        u_v[0][...] = up(0, 0)
        for step in early[2:]:
            step()

        def chunk(f, carry):
            run_point(points, f, 0, 1, chunks)

            @pl.when(f >= 2)
            def _():
                out(f - 2).wait()

            u_v[1][...] = up(1, f)
            activate(0, f)
            u_v[0][...] = up(0, jnp.minimum(f + 1, chunks - 1))
            activate(1, f)
            out(f).start()
            return carry

        lax.fori_loop(0, chunks, chunk, 0)
        run_rest(points, chunks)
        e_out = copies.here(lambda: (e_v, e_hbm))
        e_out.start()
        third = copies.here(lambda: (wd_hbm, wd))
        third.start()
        for m in moves:
            m.finish()
        loads = load_tokens(copies, *ct, flat, ct_four)
        for copy in loads:
            copy.start()
        third.wait()
        for copy in m_out:
            copy.wait()
        for copy in loads:
            copy.wait()
        join_small(flat, ct_four, large)
        for n in range(small):
            at = large * LEN_L + n * LEN_S + SIDE_S * SIDE_S // 16 * 16
            keep = lax.broadcasted_iota(jnp.int32, (32, 1), 0) < SIDE_S * SIDE_S % 16
            flat[at:at + 32, :] = jnp.where(keep, flat[at:at + 32, :].astype(F32), 0.0).astype(BF)
        acc[...] = jnp.zeros_like(acc)
        w2 = joined(wd, 0)
        part = rows // 2
        for i in range(2):
            at = slice(i * part, (i + 1) * part)
            r = dot(e_v[at, :], w2, NN) + bd
            dy = flat[at, :].astype(F32)
            dr = (s2 * dy).astype(BF)
            acc[0] += fold8(r * dy)
            acc[1] += fold8(dr.astype(F32))
            m_v[at, :] = m_v[at, :] + s2 * r
            n2_v[at, :] = dr
        last = [copies.here(lambda: (n2_v, dr_hbm)), copies.here(lambda: (flat, dy_hbm))]
        for copy in last:
            copy.start()
        for n, j, start in image_rows(large, small)[0]:
            yl[n, j] = m_v[start:start + LEN_L // 4, :].astype(BF)
        for n, start in image_rows(large, small)[1]:
            place_small(ys, m_v[start:start + LEN_S, :], n)
        for i in range(2):
            sums[i:i + 1, :] = jnp.sum(acc[i], 0, keepdims=True)
        for f in (chunks - 2, chunks - 1):
            out(f).wait()
        for copy in last + [e_out]:
            copy.wait()

    vm = pltpu.VMEM
    flat = vm((rows, width), BF)
    scratch = [
        flat, flat, vm(x_s.shape, BF), vm(x_s.shape, BF), vm(w_out.shape, BF), vm(w_up.shape, BF),
        vm(down_shape, BF), vm((rows, width), F32), flat, vm((rows, chunks * width), BF),
        vm((2, rows, width), BF), vm((2, 8, width), F32), vm((half, width), F32), vm((half, width), F32),
    ]
    units = cut[0] * cut[1]
    scratch += semaphores(6 + 3 * units, 12 + 8 * large + 2 + chunks + units + 3)
    remote = dict(collective_id=3, has_side_effects=True) if direct else {}
    return pl.pallas_call(
        kernel,
        out_shape=[bf(*x_l.shape), bf(*x_s.shape), jax.ShapeDtypeStruct((rows, width), F32), bf(rows, width),
                   bf(rows, chunks * width), bf(chunks, rows, width), bf(rows, width), bf(rows, width),
                   jax.ShapeDtypeStruct((8, width), F32)] + more,
        in_specs=[ANY] * 8 + [VMEM, VMEM] + [ANY] * direct,
        out_specs=[VMEM, VMEM] + [ANY] * 6 + [VMEM] + [ANY] * len(more),
        scratch_shapes=scratch,
        input_output_aliases={7: 9, 10: 10} if direct else {},
        compiler_params=pltpu.CompilerParams(vmem_limit_bytes=60 * MIB, **remote),
        name="forward_tail",
    )(att, x_l, x_s, ct_l, ct_s, w_out, w_up, w_down, vectors, up_vec, *([ct_part] if direct else []))


def backward_head(img_size, att, m, n2, e, g, dr, dy, w_out, w_up, w_down, cut, y_first, vectors, sums_in, wholes):
    rows, width = att.shape
    chunks = g.shape[0]
    half = rows // 2
    direct = img_size is not None
    zs = img_size // 2 if direct else 0
    nw = len(wholes)
    k2, wide = w_down.shape[5:]
    cols = w_down.shape[0] * 2 * wide
    tall = k2 // cut

    def kernel(*refs):
        ins, wh, outs, blocks, scr = split_refs(refs, 12, nw, 6, nw)
        att_hbm, m_hbm, n2_hbm, e_hbm, g_hbm, dr_hbm, dy_hbm, wo_hbm, wu_hbm, wd_hbm, vec, s_in = ins
        go, gu, gd, dm_hbm, da_hbm, sums = outs
        m_v, n2_v, nt_v, e_v, g_v, dr_v, wo, wu, wd, dn, du_v, gd_v, gu_v, go_v, acc, up_acc = scr[:16]
        copies = Copies(*scr[-3:])
        pairs = [(dr_hbm, dr_v), (n2_hbm, n2_v), (wd_hbm, wd), (wu_hbm, wu), (m_hbm, m_v), (wo_hbm, wo)]
        loads = [copies.here(lambda a=a, b=b: (a, b)) for a, b in pairs]
        at_e = copies.locals
        at_g = at_e + chunks
        at_gu = at_g + chunks
        copies.locals += 3 * chunks

        def fetch_e(f):
            return pltpu.make_async_copy(
                e_hbm.at[:, columns(f * width, width)], e_v.at[lax.rem(f, 2)], copies.local.at[at_e + f])

        def fetch_g(f):
            return pltpu.make_async_copy(g_hbm.at[f], g_v.at[lax.rem(f, 2)], copies.local.at[at_g + f])

        def put(f):
            return pltpu.make_async_copy(
                gu_v.at[lax.rem(f, 2)], gu.at[lax.rem(f, 2), f // 2], copies.local.at[at_gu + f])

        loads[0].start()
        fetch_e(0).start()
        fetch_e(1).start()
        for copy in loads[1:]:
            copy.start()
        fetch_g(0).start()
        moves, steps = [], []
        if direct:
            p = Place(img_size)
            announce(p.partners())
            moves = [Move(p, copies, a, b, False) for a, b in zip(wh, blocks)]
            scatter = Scatter(p, copies, None, gd, scr[16:23], cut)
            units = scatter.units(y_first, True)
            over_c = [
                copies.remote(lambda f=f: (scatter.stage.at[:, f], scatter.from_c.at[:, f], p.at(c=1 - p.c)))
                for f in range(chunks)
            ]
            steps = [in_turn(*[copy.wait_recv for copy in over_c], units[0][1], units[1][1])]
            steps += [units[2][1], in_turn(units[0][2], units[1][2]), in_turn(units[0][3], units[1][3], units[2][2])]
            steps += [units[2][3], in_turn(*[unit[4] for unit in units])]
        loads[0].wait()

        def down(f):
            fetch_e(f).wait()
            gd_v[...] = dot(e_v[lax.rem(f, 2)], dr_v[...], TN).astype(BF)
            if direct:
                for to, c in ((scatter.own, p.c), (scatter.stage, 1 - p.c)):
                    got = gd_v[:, columns(c * wide, wide)].reshape(2, 2, cut, tall, wide)
                    for r in range(cut):
                        to[r, f] = got[:, :, r]
            else:
                for c in range(2):
                    gd[0, c, f] = gd_v[:, c * wide:(c + 1) * wide].reshape(2, 2, k2, wide)

            if f + 2 < chunks:
                fetch_e(f + 2).start()
            if direct:
                if f == 0:
                    await_partners(p.partners())
                    for m in moves:
                        m.start()
                over_c[f].start()

        for f in range(chunks):
            down(f)
        for step in steps[:1]:
            step()
        late = [copies.here(lambda: (att_hbm, e_v.at[0])), copies.here(lambda: (dy_hbm, e_v.at[1]))]
        for copy in late:
            copy.start()
        for copy in loads[1:4]:
            copy.wait()
        nt_v[...] = n2_v[...].T
        dn[...] = jnp.zeros_like(dn)
        g2, s1, b2, bo = (vec[i:i + 1, :] for i in (1, 2, 5, 8))
        points = {t + 1: step for t, step in enumerate(steps[1:])}

        def chunk(f, carry):
            run_point(points, f, 0, 1, chunks)
            slot = lax.rem(f, 2)
            fetch_g(f).wait()

            @pl.when(f + 1 < chunks)
            def _():
                fetch_g(f + 1).start()

            @pl.when(f >= 2)
            def _():
                put(f - 2).wait()

            w1 = wu[slot, f // 2].reshape(width, width)
            w2 = jnp.concatenate([wd[0, c, f].reshape(width, wide) for c in range(2)], 1)
            total = jnp.zeros((8, width), F32)
            for i in range(2):
                at = slice(i * half, (i + 1) * half)
                de = dot(dr_v[at, :], w2, NT)
                du = (de * g_v[slot, at, :].astype(F32)).astype(BF)
                du_v[at, :] = du
                total += fold8(du.astype(F32))
            up_acc[f] = total
            dn[...] += dot(du_v[...], w1, NT)
            gu_v[slot] = dot(nt_v[...], du_v[...], NN).astype(BF).reshape(gu_v.shape[1:])
            put(f).start()
            return carry

        lax.fori_loop(0, chunks, chunk, 0)
        for copy in loads[4:] + late:
            copy.wait()
        acc[...] = jnp.zeros_like(acc)
        run_some = [points[t] for t in sorted(points) if t >= chunks]
        for step in run_some[:1]:
            step()

        def norm(start, size):
            at = pl.ds(start, size)
            hat, scale = norm_parts(m_v[at, :])
            d = dn[at, :]
            acc[0] += fold8(d * hat)
            acc[1] += fold8(d)
            dm = e_v[1, at, :].astype(F32) + norm_back(d, hat, scale, g2)
            da = (s1 * dm).astype(BF)
            acc[2] += fold8(da.astype(F32))
            m_v[at, :] = dm
            du_v[at, :] = da

        row_tiles(rows, 96, norm)
        out = [copies.here(lambda: (m_v, dm_hbm))]
        out[0].start()
        for step in run_some[1:]:
            step()
        w = joined(wo, 0)
        got = dot(e_v[0], du_v[...], TN).astype(BF)
        for c in range(2):
            go_v[c] = got[:, c * (width // 2):(c + 1) * (width // 2)].reshape(go_v.shape[1:])
        out.append(copies.here(lambda: (go_v, go.at[0])))
        out[1].start()
        for i in range(2):
            at = slice(i * half, (i + 1) * half)
            n2_v[at, :] = dot(du_v[at, :], w, NT).astype(BF)
            a = dot(e_v[0, at, :], w, NN) + bo
            acc[3] += fold8(a * m_v[at, :])
        out.append(copies.here(lambda: (n2_v, da_hbm)))
        out[2].start()
        sums[...] = jnp.zeros_like(sums)
        for i, (part, row) in enumerate(((0, 1), (0, 5), (1, 0), (0, 2))):
            sums[part, row:row + 1, :] = jnp.sum(acc[i], 0, keepdims=True)
        sums[0, 3:4, :] = s_in[0:1, :]
        sums[1, 1:2, :] = s_in[1:2, :]
        for f in range(chunks):
            sums[1, 2 + f:3 + f, :] = jnp.sum(up_acc[f], 0, keepdims=True)
        for f in (chunks - 2, chunks - 1):
            put(f).wait()
        if direct:
            for copy in over_c:
                copy.wait_send()
            scatter.end()
        for copy in moves:
            copy.finish()
        for copy in out:
            copy.wait()

    bf = lambda *s: jax.ShapeDtypeStruct(s, BF)
    f32 = lambda *s: jax.ShapeDtypeStruct(s, F32)
    vm = pltpu.VMEM
    flat = vm((rows, width), BF)
    scratch = [
        vm((rows, width), F32), flat, vm((width, rows), BF), vm((2, rows, width), BF),
        vm((2, rows, width), BF), flat, vm(w_out.shape, BF), vm(w_up.shape, BF), vm(w_down.shape, BF),
        vm((rows, width), F32), flat, vm((width, width), BF), vm((2,) + w_up.shape[2:], BF),
        vm(w_out.shape[1:], BF), vm((4, 8, width), F32), vm((chunks, 8, width), F32),
    ]
    if direct:
        scratch += Scatter.scratch(zs, k2 // 2, cols, 1, cut, True)
    scratch += semaphores(max(1, 3 * nw + Scatter.remotes(zs, 1, cut) + chunks), 6 + 3 * chunks + 2 + 3 + nw + 1)
    remote = dict(collective_id=4, has_side_effects=True) if direct else {}
    return pl.pallas_call(
        kernel,
        out_shape=[bf(*w_out.shape), bf(*w_up.shape), f32(k2 // 2, cols) if direct else bf(*w_down.shape),
                   f32(rows, width), bf(rows, width), f32(2, 8, width)]
        + [bf(w.shape[0] * 4, *w.shape[2:]) for w in wholes],
        in_specs=[ANY] * 10 + [VMEM, VMEM] + [ANY] * nw,
        out_specs=[ANY, ANY, ANY if direct else VMEM, ANY, ANY, VMEM] + [ANY] * nw,
        scratch_shapes=scratch,
        compiler_params=pltpu.CompilerParams(vmem_limit_bytes=61 * MIB, **remote),
        name="backward_head",
    )(att, m, n2, e, g, dr, dy, w_out, w_up, w_down, vectors, sums_in, *wholes)


def project_in(x_l, x_s, w_qkv, vectors, merged_bias):
    large, small = x_l.shape[0], x_s.shape[0]
    rows, width = large * LEN_L + small * LEN_S, x_l.shape[3]
    panels, wide = w_qkv.shape[0], w_qkv.shape[-1]

    def kernel(xl_hbm, xs_hbm, w_hbm, vec, bias, out, flat, four, w_v, local):
        copies = Copies(None, None, local)
        loads = load_tokens(copies, xl_hbm, xs_hbm, flat, four) + [copies.here(lambda: (w_hbm, w_v))]
        for copy in loads:
            copy.start()
        for copy in loads[:-1]:
            copy.wait()
        join_small(flat, four, large)

        def normed(start, size):
            at = pl.ds(start, size)
            hat, _ = norm_parts(flat[at, :].astype(F32))
            flat[at, :] = (hat * vec[0:1, :] + vec[4:5, :]).astype(BF)

        row_tiles(rows, 96, normed)
        loads[-1].wait()
        for u in range(panels):
            for c in range(2):
                cols = slice((c * panels + u) * wide, (c * panels + u + 1) * wide)
                got = dot(flat[...], w_v[u, c].reshape(width, wide), NN) + bias[:, cols]
                out[:, cols] = got.astype(BF)

    return pl.pallas_call(
        kernel,
        out_shape=jax.ShapeDtypeStruct((rows, 3 * width), BF),
        in_specs=[ANY] * 3 + [VMEM, VMEM],
        out_specs=VMEM,
        scratch_shapes=[pltpu.VMEM((rows, width), BF), pltpu.VMEM(x_s.shape, BF), pltpu.VMEM(w_qkv.shape, BF),
                        pltpu.SemaphoreType.DMA((4 * large + 2,))],
        compiler_params=pltpu.CompilerParams(vmem_limit_bytes=40 * MIB),
        name="project_in",
    )(x_l, x_s, w_qkv, vectors, merged_bias)


def head_columns(rows, at):
    return pl.BlockSpec((rows, 128), lambda g: (0, g + at))


def attend(qkv, rows_l, rows_s, large, small):
    rows = qkv.shape[0]
    return pl.pallas_call(
        functools.partial(attend_kernel, large, small),
        grid=(H // 2,),
        out_shape=[jax.ShapeDtypeStruct((rows, 64 * H), BF),
                   jax.ShapeDtypeStruct((large + small, 16, 640), F32)],
        in_specs=[head_columns(rows, H // 2 * i) for i in range(3)]
        + [pl.BlockSpec((2, 8, WIDE_L), lambda g: (g, 0, 0)), pl.BlockSpec((2, 8, WIDE_S), lambda g: (g, 0, 0))],
        out_specs=[head_columns(rows, 0), pl.BlockSpec((large + small, 16, 640), lambda g: (0, 0, 0))],
        scratch_shapes=[pltpu.VMEM((2, LEN_L, LEN_L), F32), pltpu.VMEM((2, LEN_S, LEN_S), F32)],
        compiler_params=pltpu.CompilerParams(vmem_limit_bytes=56 * MIB),
        name="attend",
    )(qkv, qkv, qkv, rows_l, rows_s)


def layer_norm(values, gain, shift):
    average = jnp.mean(values, -1, keepdims=True)
    centered = values - average
    variance = jnp.mean(centered * centered, -1, keepdims=True)
    return centered * lax.rsqrt(variance + 1e-06) * gain + shift


def table_sums(rows, side, blocks):
    span = 2 * side - 1
    rows = jnp.roll(rows[:, :H], side - -(-side // 8) * 8, 2)
    low, high = rows[:, :, :(blocks + 1) * side].reshape(2, H, blocks + 1, side)
    square = jnp.concatenate([low[:, :blocks], high[:, 1:, :side - 1]], 2)
    square = jnp.concatenate([square[:, :span - 1], jnp.sum(square[:, span - 1:], 1, keepdims=True)], 1)
    return square.reshape(H, span * span)


def to_images(blocks):
    n = blocks.shape[0] // 4
    got = lax.all_to_all(blocks.reshape((4, n) + blocks.shape[1:]), "rows", 0, 0)
    return jnp.swapaxes(got, 0, 1)


def to_blocks(whole):
    got = lax.all_to_all(jnp.swapaxes(whole, 0, 1), "rows", 0, 0)
    return got.reshape((-1,) + got.shape[2:])


def to_panels(full, panels):
    rows, cols = full.shape
    split = full.reshape(4, 2, 2, rows // 16, 2, panels, cols // 2 // panels)
    return split.transpose(5, 4, 0, 1, 2, 3, 6)


def from_panels(split):
    rows, cols = 16 * split.shape[5], split.shape[0] * 2 * split.shape[6]
    return split.transpose(2, 3, 4, 5, 1, 0, 6).reshape(rows, cols)


CUTS = ((3, 1), (1, 1), (2, 3), (1, 3))


def on_device(img_size, small_images, large_images, w_qkv, w_out, w_up, w_down, gains, biases, up_bias,
              small_table, large_table, small_cotangent, large_cotangent):
    width = small_images.shape[2]
    axes = ("img", "rows")
    own = gains.shape[0]
    own_up = up_bias.shape[0]
    table_l, table_s = padded_table(large_table, TABLE_L), padded_table(small_table, TABLE_S)
    direct = own % 8 == 0
    if direct:
        block = jnp.concatenate([gains.T, biases.T], 0)
        block = jnp.pad(block, ((0, 0), (0, own_up - own)))
        block = jnp.pad(jnp.concatenate([block, up_bias[None]], 0), ((0, 5), (0, 128 - own_up)))
        large_x, small_x, large_ct, small_ct, qkv_w, up_w, out_w, down_w, qkv, n1, attended, lse, vectors, up_vec = front(
            img_size, [large_images, small_images, large_cotangent, small_cotangent], block, [w_qkv, w_up, w_out, w_down],
            [CUTS[i] for i in (0, 2, 1, 3)], [(4, 5), (0,)], table_l, table_s)
        large, small = large_x.shape[0], small_x.shape[0]
        large_y, small_y, m, n2, e, g, dr, dy, sums, down_w, _ = forward_tail(
            img_size, attended, large_x, small_x, large_cotangent, small_ct, large_ct, out_w, up_w, down_w, CUTS[3],
            vectors, up_vec)
        grad_out, grad_up, own_down, dm, d_att, sums = backward_head(
            img_size, attended, m, n2, e, g, dr, dy, out_w, up_w, down_w, CUTS[3][1], (1,), vectors,
            sums, [])
        df, large_sums, small_sums, own_out, own_up_w, large_out, small_out = attention_back(
            img_size, qkv, d_att, attended, lse, table_l, table_s, [grad_out, grad_up], [1, 1],
            [large_y, small_y], large, small)
        large_grad, small_grad, own_qkv, sums, grad_large_table, grad_small_table = projection_back(
            img_size, df, dm, n1, large_x, small_x, qkv_w, vectors, sums, [large_sums, small_sums], large, small)
    else:
        large_x, small_x, large_ct, small_ct = [
            to_images(a) for a in (large_images, small_images, large_cotangent, small_cotangent)]
        large, small = large_x.shape[0], small_x.shape[0]
        qkv_w, out_w, up_w, down_w = [
            to_panels(lax.all_gather(s.astype(BF), axes, axis=0, tiled=True), c[0])
            for s, c in zip((w_qkv, w_out, w_up, w_down), CUTS)]
        vectors = lax.all_gather(jnp.concatenate([gains, biases], 1).astype(BF), axes, axis=0, tiled=True)
        vectors = jnp.pad(vectors.astype(F32).T, ((0, 6), (0, 0)))
        up_vec = lax.all_gather(up_bias.astype(BF), axes, axis=0, tiled=True).astype(F32).reshape(-1, width)
        merged_bias = jnp.concatenate([vectors[6:7], jnp.zeros((1, width), F32), vectors[7:8]], 1)
        qkv = project_in(large_x, small_x, qkv_w, vectors, merged_bias)
        attended, lse = attend(
            qkv, table_rows(large_table, SIDE_L, 47, WIDE_L), table_rows(small_table, SIDE_S, 29, WIDE_S), large, small)
        large_y, small_y, m, n2, e, g, dr, dy, sums = forward_tail(
            None, attended, large_x, small_x, large_ct, small_ct, None, out_w, up_w, down_w, (1, 1), vectors, up_vec)
        grad_out, grad_up, grad_down, dm, d_att, sums = backward_head(
            None, attended, m, n2, e, g, dr, dy, out_w, up_w, down_w, 1, (), vectors, sums, [])
        df, large_sums, small_sums = attention_back(
            img_size, qkv, d_att, attended, lse, table_l, table_s, [], [], [], large, small)
        split_at = large * LEN_L
        tokens = jnp.concatenate([large_x.reshape(-1, width), small_x.reshape(-1, width)], 0).astype(F32)
        normed, pull = jax.vjp(layer_norm, tokens, vectors[0], vectors[4])
        grad_qkv = jnp.einsum("rd,re->de", normed.astype(BF), df, preferred_element_type=F32)
        d_normed = jnp.einsum("re,de->rd", df, from_panels(qkv_w), preferred_element_type=F32)
        d_tokens, grad_gain, grad_shift = pull(d_normed)
        d_tokens = (dm + d_tokens).astype(BF)
        grad_q = jnp.sum(df[:, :width].astype(F32), 0)
        grad_v = jnp.sum(df[:, 2 * width:].astype(F32), 0)
        for row, value in ((0, grad_gain), (4, grad_shift), (6, grad_q), (7, grad_v)):
            sums = sums.at[0, row].set(value)
        sums, large_sums, small_sums = lax.psum((sums, large_sums, small_sums), axes)
        grad_large_table = table_sums(large_sums, SIDE_L, 47)
        grad_small_table = table_sums(small_sums, SIDE_S, 29)
        large_grad = to_blocks(d_tokens[:split_at].reshape(large_x.shape))
        small_grad = to_blocks(d_tokens[split_at:].reshape(small_x.shape))
        large_out, small_out = to_blocks(large_y), to_blocks(small_y)
        grads = [grad_qkv] + [from_panels(g).astype(F32) for g in (grad_out, grad_up, grad_down)]
        own_qkv, own_out, own_up_w, own_down = [
            lax.psum_scatter(g, axes, scatter_dimension=0, tiled=True) for g in grads]

    index = lax.axis_index("img") * 4 + lax.axis_index("rows")
    flat_sums = sums.reshape(16, width)
    own_columns = lax.dynamic_slice(flat_sums, (0, index * own), (10, own)).T
    own_up_sums = lax.dynamic_slice(flat_sums[10:14].reshape(-1), (index * own_up,), (own_up,))
    return (
        small_out, large_out, small_grad, large_grad, own_qkv, own_out, own_up_w, own_down,
        own_columns[:, :4], own_columns[:, 4:], own_up_sums, grad_small_table, grad_large_table,
    )


def solution(mesh):
    images = P("img", "rows", None)
    matrix = P(("img", "rows"), None)
    vector = P(("img", "rows"))
    in_specs = (images, images) + (matrix,) * 6 + (vector, P(), P(), images, images)
    out_specs = (images,) * 4 + (matrix,) * 6 + (vector, P(), P())
    return jax.shard_map(
        functools.partial(on_device, mesh.shape["img"]),
        mesh=mesh, in_specs=in_specs, out_specs=out_specs, check_vma=False,
    )
```
